32 devices in a mesh: section: 4 (over x, core), seq: 2 (over y), dp: 4 (over z).
Axes of the slice: x: 2, y: 2, z: 4, core: 2. Of those that a mesh axis runs over, the one named last changes fastest.
Arguments:
- main_hidden: bfloat16 [4, 4, 256, 7168], P('section', 'dp', 'seq'), may hold values from -6 to 6
- embedded: bfloat16 [4, 4, 256, 7168], P('section', 'dp', 'seq'), may hold values from -6 to 6
- cotangent: bfloat16 [4, 4, 256, 7168], P('section', 'dp', 'seq'), may hold values from -6 to 6
- slot_token: int32 [4, 4, 2, 12], P('section', 'dp', None, 'seq'), may hold values from 0 to 127, as said below
- slot_count: int32 [4, 4, 2, 2], P('section', 'dp', None, 'seq'), may hold values from 1 to 6, as said below
- route_gate: float32 [4, 4, 2, 12], P('section', 'dp', None, 'seq'), may hold values from 0.2 to 2
- norm_gain: float32 [2, 2, 7168], replicated, may hold values from 0.5 to 1.5
- expert_weight: bfloat16 [2, 3, 7168, 2048], P(None, None, 'seq', 'dp'), may hold values from -0.0625 to 0.0625
Outputs:
- hidden_grad: bfloat16 [4, 4, 256, 7168], P('section', 'dp', 'seq')
- expert_grad: bfloat16 [4, 2, 3, 7168, 2048], P('section', None, None, 'seq', 'dp')
- gain_grad: float32 [4, 2, 2, 7168], P('section', None, None, ('seq', 'dp'))
The draws below stay inside these ranges and needn't reach their ends.
Inputs may be any that keep to these rules, and one draw needn't show every extreme that they name: `slot_token`: the slots of one device and depth name distinct positions of that device's block. `slot_count`: in every micro-batch, sequence and depth some device has all 6 slots live.
All inputs are finite; a program needn't handle non-finite values.
Results may differ from the reference program's by a relative error of at most 0.0077.
Values may be sent and summed in bfloat16 or wider, within the bound.
No kernel may reach another device: no remote copies, remote signals or barrier semaphores. Data moves between devices by JAX's collectives and lax.ppermute only.
A program may use at most 128 MiB of HBM per device.

```python
import math
import jax
import jax.numpy as jnp
from jax import lax

D = 7168
H = 2048
TOK_DEV = 128
CAP = 6
DEPTHS = 2
SECTIONS = 4
BATCH = 4
SEQ_SHARDS = 2
LENGTH = 256
SLOTS = 12


def draw_slot_token(key, part):
    blocks = SECTIONS * BATCH * DEPTHS * SEQ_SHARDS
    keys = jax.random.split(jax.random.fold_in(key, 11), blocks)
    chosen = jax.vmap(lambda single: jax.random.permutation(single, TOK_DEV))(keys)[:, :CAP]
    return chosen.reshape(SECTIONS, BATCH, DEPTHS, SLOTS).astype(jnp.int32)


def draw_slot_count(key, part):
    first, second = jax.random.split(jax.random.fold_in(key, 23))
    counts = jax.random.randint(first, (SECTIONS, BATCH, DEPTHS, SEQ_SHARDS), 1, CAP + 1)
    full = jax.random.randint(second, (SECTIONS, BATCH, DEPTHS, 1), 0, SEQ_SHARDS)
    places = jnp.arange(SEQ_SHARDS, dtype=jnp.int32)
    return jnp.where(places == full, CAP, counts).astype(jnp.int32)


def steps_of(rng, dims, cuts, smallest, top_value):
    def one(axis_at, parts):
        draws = jax.random.uniform(jax.random.fold_in(jax.random.fold_in(rng, 6), axis_at), (parts,), jnp.float32, smallest / len(cuts), top_value / len(cuts))
        return jnp.repeat(jnp.exp(draws), dims[axis_at] // parts).reshape((-1,) + (1,) * (len(dims) - axis_at - 1))

    level = one(*cuts[0])
    for cut in cuts[1:]:
        level = level * one(*cut)
    return level


def bell_draw(stream_key, extent, deviation, most, shards=(), held_as=jnp.bfloat16):
    entries = deviation * jax.random.normal(stream_key, extent, jnp.float32)
    if shards:
        entries = entries * steps_of(stream_key, extent, shards, -0.22, 0.18)
    return jnp.clip(entries, -most, most).astype(held_as)


def setup_inputs(seed: int = 0) -> dict:
    streams_of = jax.random.split(jax.random.key(seed), 9)
    main_hidden = bell_draw(streams_of[0], (SECTIONS, BATCH, LENGTH, D), 1.0, 6.0, ((0, 4), (1, 4), (2, 2)))
    embedded = bell_draw(streams_of[1], (SECTIONS, BATCH, LENGTH, D), 1.0, 6.0, ((0, 4), (1, 4), (2, 2)))
    cotangent = bell_draw(streams_of[2], (SECTIONS, BATCH, LENGTH, D), 1.0, 6.0, ((0, 4), (1, 4), (2, 2)))
    slot_token = draw_slot_token(jax.random.fold_in(streams_of[8], 71), 0)
    slot_count = draw_slot_count(jax.random.fold_in(streams_of[8], 71), 0)
    route_gate = jnp.clip(jnp.exp(math.log(2.0) - 2.3025851 * jax.random.uniform(streams_of[5], (SECTIONS, BATCH, DEPTHS, SLOTS), jnp.float32) ** steps_of(streams_of[5], (SECTIONS, BATCH, DEPTHS, SLOTS), ((0, 4), (1, 4), (3, 2)), -0.2, 0.2)), 0.2, 2.0)
    norm_gain = jnp.clip(1.0 + 0.1 * jax.random.normal(streams_of[6], (DEPTHS, 2, D), jnp.float32), 0.5, 1.5)
    expert_weight = bell_draw(streams_of[7], (DEPTHS, 3, D, H), D ** -0.5, 0.0625, ((2, 2), (3, 4)))
    return dict(main_hidden=main_hidden, embedded=embedded, cotangent=cotangent, slot_token=slot_token, slot_count=slot_count, route_gate=route_gate, norm_gain=norm_gain, expert_weight=expert_weight)


eps_norm = 1e-06

def normed(value):
    wide = value.astype(jnp.float32)
    scale = lax.rsqrt(lax.optimization_barrier(jnp.mean(wide * wide, axis=-1, keepdims=True)) + eps_norm)
    return (wide * scale, scale)

def norm_back(grad, unit, scale):
    inner = lax.optimization_barrier(jnp.mean(grad * unit, axis=-1, keepdims=True))
    return (grad - unit * inner) * scale

def contract_rows(left, right):
    return lax.dot_general(left, right, (((0,), (0,)), ((), ())), preferred_element_type=jnp.float32)

def contract_last(left, right):
    return lax.dot_general(left, right, (((1,), (1,)), ((), ())), preferred_element_type=jnp.float32)

def one_sequence(hidden, embedded, cotangent, slots, counts, gates, norm_gain, expert_weight):
    order = jnp.arange(SLOTS, dtype=jnp.int32)
    padded = jnp.concatenate([embedded, jnp.zeros((DEPTHS, D), jnp.bfloat16)], 0)
    current = hidden
    saved = []
    for depth in range(DEPTHS):
        shifted = padded[depth + 1:depth + 1 + LENGTH]
        unit_h, scale_h = normed(current)
        unit_e, scale_e = normed(shifted)
        mixed = (unit_h * norm_gain[depth, 0] + unit_e * norm_gain[depth, 1]).astype(jnp.bfloat16)
        tokens = (order // CAP * TOK_DEV + slots[depth]).astype(jnp.int32)
        live = order % CAP < counts[depth][order // CAP]
        weight = gates[depth] * live.astype(jnp.float32)
        rows = mixed[tokens] * live[:, None].astype(jnp.bfloat16)
        gate_in = jnp.dot(rows, expert_weight[depth, 0], preferred_element_type=jnp.float32)
        up_in = jnp.dot(rows, expert_weight[depth, 1], preferred_element_type=jnp.float32)
        act = (jax.nn.silu(gate_in) * up_in).astype(jnp.bfloat16)
        result = contract_last(act, expert_weight[depth, 2])
        current = mixed.astype(jnp.float32).at[tokens].add(result * weight[:, None]).astype(jnp.bfloat16)
        saved.append((unit_h, scale_h, unit_e, tokens, live, weight, rows, gate_in, up_in, act))
    grad = cotangent.astype(jnp.float32)
    weight_grads = [None] * DEPTHS
    gain_terms = [None] * DEPTHS
    for depth in reversed(range(DEPTHS)):
        unit_h, scale_h, unit_e, tokens, live, weight, rows, gate_in, up_in, act = saved[depth]
        dout = (grad[tokens] * weight[:, None]).astype(jnp.bfloat16)
        d_act = jnp.dot(dout, expert_weight[depth, 2], preferred_element_type=jnp.float32)
        down_grad = contract_rows(dout, act)
        sig = jax.nn.sigmoid(gate_in)
        d_gate = (d_act * up_in * sig * (1.0 + gate_in * (1.0 - sig))).astype(jnp.bfloat16)
        d_up = (d_act * jax.nn.silu(gate_in)).astype(jnp.bfloat16)
        gate_grad = contract_rows(rows, d_gate)
        up_grad = contract_rows(rows, d_up)
        d_rows = contract_last(d_gate, expert_weight[depth, 0]) + contract_last(d_up, expert_weight[depth, 1])
        d_mixed = grad.at[tokens].add(d_rows * live[:, None].astype(jnp.float32))
        gain_terms[depth] = jnp.stack([lax.optimization_barrier(jnp.sum(d_mixed * unit_h, 0)), lax.optimization_barrier(jnp.sum(d_mixed * unit_e, 0))])
        weight_grads[depth] = jnp.stack([gate_grad, up_grad, down_grad])
        grad = norm_back(d_mixed * norm_gain[depth, 0], unit_h, scale_h)
    return (grad.astype(jnp.bfloat16), jnp.stack(weight_grads), jnp.stack(gain_terms))

def one_section(items, norm_gain, expert_weight):
    hidden, embedded, cotangent, slots, counts, gates = items
    grads = []
    weight_total = jnp.zeros((DEPTHS, 3, D, H), jnp.float32)
    gain_total = jnp.zeros((DEPTHS, 2, D), jnp.float32)
    for batch in range(BATCH):
        grad, weight_grad, gain_grad = one_sequence(hidden[batch], embedded[batch], cotangent[batch], slots[batch], counts[batch], gates[batch], norm_gain, expert_weight)
        grads.append(grad)
        weight_total = weight_total + weight_grad
        gain_total = gain_total + gain_grad
    return (jnp.stack(grads), weight_total.astype(jnp.bfloat16), gain_total)

def reference(main_hidden, embedded, cotangent, slot_token, slot_count, route_gate, norm_gain, expert_weight):
    started = jnp.roll(main_hidden, 1, axis=0)
    grads, expert_grad, gain_grad = lax.map(lambda items: one_section(items, norm_gain, expert_weight), (started, embedded, cotangent, slot_token, slot_count, route_gate))
    hidden_grad = jnp.roll(grads, -1, axis=0)
    return (hidden_grad, expert_grad, gain_grad)
```

```python
import functools

import jax
import jax.numpy as jnp
from jax import lax
from jax.experimental import pallas as pl
from jax.experimental.pallas import tpu as pltpu
from jax.sharding import PartitionSpec as P

eps_norm = 1e-06
lanes = 128
absent = -1000
f32 = jnp.float32
bf16 = jnp.bfloat16


def ring(value, axis, steps):
    count = lax.axis_size(axis)
    return lax.ppermute(value, axis, [(i, (i + steps) % count) for i in range(count)])


def from_after(array, axis, by):
    size = lax.axis_size(axis)
    return lax.ppermute(array, axis, [(i, i - by) for i in range(by, size)])


def hop(value, section_step, seq_step):
    sections, seqs = lax.axis_size("section"), lax.axis_size("seq")
    pairs = [
        (c * seqs + s, (c + section_step) % sections * seqs + (s + seq_step) % seqs)
        for c in range(sections)
        for s in range(seqs)
    ]
    return lax.ppermute(value, ("section", "seq"), pairs)


def trade_seq(pieces, section_step=0):
    if section_step == 0:
        return [pieces[0]] + [ring(pieces[o], "seq", o) for o in range(1, len(pieces))]
    return [hop(piece, section_step, o) for o, piece in enumerate(pieces)]


def gather_dp(block):
    return [block] + [ring(block, "dp", i) for i in range(1, lax.axis_size("dp"))]


def return_dp(blocks):
    return [blocks[0]] + [ring(blocks[i], "dp", -i) for i in range(1, len(blocks))]


def pair_seq(own, send):
    if lax.axis_size("seq") == 2:
        return own, ring(send, "seq", 1)
    return lax.psum(own, "seq"), jnp.zeros_like(send)


def one_hot(column, width):
    return (column == lax.broadcasted_iota(jnp.int32, (column.shape[0], width), 1)).astype(bf16)


def pick(column, table):
    return jnp.dot(one_hot(column, table.shape[0]), table, preferred_element_type=f32)


def inv_rms(value):
    return lax.rsqrt(jnp.mean(value * value, axis=-1, keepdims=True) + eps_norm)


def coded(column):
    high = column.astype(bf16).astype(f32)
    mid = (column - high).astype(bf16).astype(f32)
    low = column - high - mid
    lane = lax.broadcasted_iota(jnp.int32, (column.shape[0], lanes), 1)
    return jnp.where(
        lane == 0, high, jnp.where(lane == 1, mid, jnp.where(lane == 2, low, 0.0))
    )


def decoded(block):
    return jnp.sum(block.astype(f32), axis=1, keepdims=True)


def piece_of(value, place, count, step):
    width = value.shape[1] // count
    want = lax.rem(place + step, count)
    out = value[:, :width]
    for p in range(1, count):
        out = jnp.where(want == p, value[:, p * width : (p + 1) * width], out)
    return out


def pieces_of(value, place, count):
    return [piece_of(value, place, count, o) for o in range(count)]


def from_block(got, place, block):
    count = len(got)
    out = got[0]
    for o in range(1, count):
        out = jnp.where(lax.rem(place - o + count, count) == block, got[o], out)
    return out


def in_order(got, place, axis):
    return jnp.concatenate([from_block(got, place, j) for j in range(len(got))], axis)


def call(fn, outs, *args, flops=0):
    shapes = [jax.ShapeDtypeStruct(shape, kind) for shape, kind in outs]
    scalars = [a.ndim == 1 and a.dtype == jnp.int32 for a in args]
    count = len(args)

    def body(*refs):
        values = [r if s else r[...] for r, s in zip(refs[:count], scalars)]
        for ref, value in zip(refs[count:], fn(*values)):
            ref[...] = value.astype(ref.dtype)

    size = sum(a.size * a.dtype.itemsize for a in list(args) + shapes)
    return pl.pallas_call(
        body,
        out_shape=shapes,
        in_specs=[
            pl.BlockSpec(memory_space=pltpu.SMEM if s else pltpu.VMEM) for s in scalars
        ],
        out_specs=[pl.BlockSpec(memory_space=pltpu.VMEM) for _ in shapes],
        compiler_params=pltpu.CompilerParams(vmem_limit_bytes=min(48 << 20, 8 * size + (8 << 20))),
        cost_estimate=pl.CostEstimate(flops=flops, bytes_accessed=size, transcendentals=0),
    )(*args)


def chunk_of(width):
    for step in (896, 512, 256, 128):
        if width % step == 0:
            return step
    return width


def project(blocks, weight, depth, kinds, select=None, gain=None, mates=None):
    rows, width = blocks[0].shape
    hidden = weight.shape[3]
    total, many = rows * len(blocks), len(kinds) * hidden
    step = chunk_of(width)
    steps = width // step
    marked = select is not None or mates is not None
    extra = lanes if marked else 0

    def body(*refs):
        refs = list(refs)
        x_refs = [refs.pop(0) for _ in blocks]
        w_refs = [refs.pop(0) for _ in kinds]
        select_ref, gain_ref = (refs.pop(0), refs.pop(0)) if select is not None else (None, None)
        mate_refs = [refs.pop(0) for _ in mates] if mates is not None else None
        own_ref, send_ref = refs.pop(0), refs.pop(0)
        kept_ref = refs.pop(0) if select is not None else None
        at = pl.program_id(0)

        @pl.when(at == 0)
        def _():
            own_ref[...] = jnp.zeros_like(own_ref)

        x = jnp.concatenate([r[...] for r in x_refs], 0)
        if marked:
            wide = x.astype(f32)
            if mates is not None:
                mate = jnp.concatenate([r[...] for r in mate_refs], 0).astype(f32)
            else:
                mate = wide
            lane = lax.broadcasted_iota(jnp.int32, (total, lanes), 1)
            mark = jnp.sum(wide * mate, axis=1, keepdims=True)
            own_ref[:, many:] += jnp.where(lane == 0, mark, 0.0)
        if select is not None:
            chosen = jnp.dot(select_ref[...], x, preferred_element_type=f32)
            x = (chosen * gain_ref[...]).astype(bf16)
            kept_ref[...] = x
        for k, w_ref in enumerate(w_refs):
            own_ref[:, k * hidden : (k + 1) * hidden] += jnp.dot(
                x, w_ref[0, 0], preferred_element_type=f32
            )

        @pl.when(at == steps - 1)
        def _():
            send_ref[:, :many] = own_ref[:, :many].astype(bf16)
            if marked:
                send_ref[:, many:] = coded(own_ref[:, many : many + 1]).astype(bf16)

    row_spec = pl.BlockSpec((rows, step), lambda i: (0, i))
    args = list(blocks) + [weight] * len(kinds)
    specs = [row_spec] * len(blocks) + [
        pl.BlockSpec((1, 1, step, hidden), lambda i, k=k: (depth, k, i, 0)) for k in kinds
    ]
    outs = [
        jax.ShapeDtypeStruct((total, many + extra), f32),
        jax.ShapeDtypeStruct((total, many + extra), bf16),
    ]
    out_specs = [pl.BlockSpec((total, many + extra), lambda i: (0, 0))] * 2
    if select is not None:
        args += [select, gain]
        specs += [
            pl.BlockSpec(select.shape, lambda i: (0, 0)),
            pl.BlockSpec((1, step), lambda i: (0, i)),
        ]
        outs.append(jax.ShapeDtypeStruct((total, width), bf16))
        out_specs.append(pl.BlockSpec((total, step), lambda i: (0, i)))
    if mates is not None:
        args += list(mates)
        specs += [row_spec] * len(mates)
    size = len(kinds) * width * hidden * 2
    return pl.pallas_call(
        body,
        grid=(steps,),
        in_specs=specs,
        out_specs=out_specs,
        out_shape=outs,
        compiler_params=pltpu.CompilerParams(vmem_limit_bytes=32 << 20),
        cost_estimate=pl.CostEstimate(
            flops=2 * total * width * many, bytes_accessed=size, transcendentals=0
        ),
    )(*args)


def expand(prepare, args, saved, weight, depth, kinds, groups):
    width, hidden = weight.shape[2], weight.shape[3]
    total = saved[0][0][0]
    rows = total // groups
    step = chunk_of(width)
    count, kept = len(args), len(saved)

    def body(*refs):
        refs = list(refs)
        in_refs = [refs.pop(0) for _ in range(count)]
        w_refs = [refs.pop(0) for _ in kinds]
        saved_refs = [refs.pop(0) for _ in range(kept)]
        block_refs = [refs.pop(0) for _ in range(groups)]
        left_refs = saved_refs[: len(kinds)]

        @pl.when(pl.program_id(0) == 0)
        def _():
            for ref, value in zip(saved_refs, prepare(*[r[...] for r in in_refs])):
                ref[...] = value.astype(ref.dtype)

        out = 0.0
        for left_ref, w_ref in zip(left_refs, w_refs):
            out += lax.dot_general(
                left_ref[...], w_ref[0, 0], (((1,), (1,)), ((), ())), preferred_element_type=f32
            )
        for g, ref in enumerate(block_refs):
            ref[...] = out[g * rows : (g + 1) * rows].astype(ref.dtype)

    size = len(kinds) * width * hidden * 2
    results = pl.pallas_call(
        body,
        grid=(width // step,),
        in_specs=[pl.BlockSpec(a.shape, lambda i: (0, 0)) for a in args]
        + [pl.BlockSpec((1, 1, step, hidden), lambda i, k=k: (depth, k, i, 0)) for k in kinds],
        out_specs=[pl.BlockSpec(shape, lambda i: (0, 0)) for shape, _ in saved]
        + [pl.BlockSpec((rows, step), lambda i: (0, i))] * groups,
        out_shape=[jax.ShapeDtypeStruct(shape, kind) for shape, kind in saved]
        + [jax.ShapeDtypeStruct((rows, width), f32 if g == 0 else bf16) for g in range(groups)],
        compiler_params=pltpu.CompilerParams(vmem_limit_bytes=32 << 20),
        cost_estimate=pl.CostEstimate(
            flops=2 * total * width * hidden * len(kinds), bytes_accessed=size, transcendentals=0
        ),
    )(*args, *([weight] * len(kinds)))
    return results[:kept], results[kept:]


def outer(depth, depths, build, row_args, column_args, d_gate, d_up, act, before):
    total, hidden = act.shape
    width = row_args[0].shape[1]
    step = chunk_of(width)
    n_rows, n_columns = len(row_args), len(column_args)

    def contract(left, right):
        return lax.dot_general(left, right, (((0,), (0,)), ((), ())), preferred_element_type=f32)

    def body(*refs):
        row_refs, refs = refs[:n_rows], refs[n_rows:]
        column_refs, refs = refs[:n_columns], refs[n_columns:]
        gate_ref, up_ref, act_ref = refs[:3]
        out_ref = refs[-1]
        rows, dout = build([r[...] for r in row_refs], [r[...] for r in column_refs])
        out_ref[0, 0, 0] = contract(rows, gate_ref[...]).astype(bf16)
        out_ref[0, 0, 1] = contract(rows, up_ref[...]).astype(bf16)
        out_ref[0, 0, 2] = contract(dout, act_ref[...]).astype(bf16)

    whole = lambda i: (0, 0)
    args = list(row_args) + list(column_args) + [d_gate, d_up, act]
    specs = [pl.BlockSpec((a.shape[0], step), lambda i: (0, i)) for a in row_args]
    specs += [pl.BlockSpec(a.shape, whole) for a in args[n_rows:]]
    alias = {}
    if before is not None:
        alias = {len(args): 0}
        args.append(before)
        specs.append(pl.BlockSpec(memory_space=pl.ANY))
    return pl.pallas_call(
        body,
        grid=(width // step,),
        in_specs=specs,
        out_specs=pl.BlockSpec((1, 1, 3, step, hidden), lambda i: (0, depth, 0, i, 0)),
        out_shape=jax.ShapeDtypeStruct((1, depths, 3, width, hidden), bf16),
        input_output_aliases=alias,
        compiler_params=pltpu.CompilerParams(vmem_limit_bytes=40 << 20),
        cost_estimate=pl.CostEstimate(
            flops=6 * total * width * hidden, bytes_accessed=6 * width * hidden, transcendentals=0
        ),
    )(*args)


def backward_rows(hidden, ahead_1, ahead_2, d_mixed_2, keep, gain):
    scale_1 = inv_rms(hidden)
    unit_1 = hidden * scale_1
    unit_e1 = ahead_1 * inv_rms(ahead_1)
    unit_e2 = ahead_2 * inv_rms(ahead_2)
    mixed = (unit_1 * gain[0:1] + unit_e1 * gain[1:2]).astype(bf16).astype(f32)
    scale_2 = inv_rms(mixed)
    unit_2 = mixed * scale_2
    u = d_mixed_2 * gain[2:3]
    grad_1 = (u - unit_2 * jnp.mean(u * unit_2, axis=-1, keepdims=True)) * scale_2
    v = grad_1 * gain[0:1]
    grad_0 = (v - unit_1 * jnp.mean(v * unit_1, axis=-1, keepdims=True)) * scale_1
    kept_1, kept_2 = grad_1 * keep, d_mixed_2 * keep
    terms = [
        jnp.sum(a * b, axis=0, keepdims=True)
        for a, b in ((kept_1, unit_1), (kept_1, unit_e1), (kept_2, unit_2), (kept_2, unit_e2))
    ]
    return grad_0.astype(bf16), jnp.concatenate(terms, 0)


def dense_rows(hidden, padded, cotangent, keep, gain):
    tokens, width = hidden.shape
    step = 16

    def body(hidden_ref, now_ref, next_ref, cot_ref, keep_ref, gain_ref, out_ref, terms_ref):
        @pl.when(pl.program_id(0) == 0)
        def _():
            terms_ref[...] = jnp.zeros_like(terms_ref)

        both = jnp.concatenate([now_ref[...].astype(f32), next_ref[...].astype(f32)[:8]], 0)
        grad, terms = backward_rows(
            hidden_ref[...].astype(f32),
            both[1 : step + 1],
            both[2 : step + 2],
            cot_ref[...].astype(f32),
            keep_ref[...],
            gain_ref[...],
        )
        out_ref[...] = grad
        terms_ref[...] += terms

    rows = pl.BlockSpec((step, width), lambda i: (i, 0))
    return pl.pallas_call(
        body,
        grid=(tokens // step,),
        in_specs=[
            rows,
            rows,
            pl.BlockSpec((step, width), lambda i: (i + 1, 0)),
            rows,
            pl.BlockSpec((step, 1), lambda i: (i, 0)),
            pl.BlockSpec((4, width), lambda i: (0, 0)),
        ],
        out_specs=[rows, pl.BlockSpec((4, width), lambda i: (0, 0))],
        out_shape=[
            jax.ShapeDtypeStruct((tokens, width), bf16),
            jax.ShapeDtypeStruct((4, width), f32),
        ],
        compiler_params=pltpu.CompilerParams(vmem_limit_bytes=32 << 20),
        cost_estimate=pl.CostEstimate(
            flops=60 * tokens * width, bytes_accessed=10 * tokens * width, transcendentals=0
        ),
    )(hidden, padded, padded, cotangent, keep, gain)


def local(
    main_hidden, embedded, cotangent, slot_token, slot_count, route_gate, norm_gain, expert_weight
):
    depths, _, features = norm_gain.shape
    tokens = main_hidden.shape[2]
    capacity = slot_token.shape[3]
    seqs, groups = lax.axis_size("seq"), lax.axis_size("dp")
    slots = -(-capacity // 8) * 8
    rows = seqs * slots
    total = groups * rows
    width = features // seqs
    hidden_units = expert_weight.shape[3]
    place = lax.axis_index("seq").astype(jnp.int32)
    spot = place[None]
    source, embed, cot = main_hidden[0, 0], embedded[0, 0], cotangent[0, 0]
    gain = norm_gain.reshape(2 * depths, features)
    gain_part = lax.dynamic_slice(gain, (0, place * width), (2 * depths, width))

    pad = ((0, 0), (0, slots - capacity))
    token = jnp.pad(slot_token[0, 0], pad, constant_values=absent)
    live = jnp.pad(
        (jnp.arange(capacity, dtype=jnp.int32) < slot_count[0, 0]).astype(f32), pad
    )
    weight = jnp.pad(route_gate[0, 0], pad) * live
    token_1, token_2 = token[0][:, None], token[1][:, None]
    live_1, live_2 = live[0][:, None], live[1][:, None]

    asked = ring(jnp.stack([token[0], token[1], (live[0]).astype(jnp.int32)]), "section", -1)
    asked_token, asked_live = asked[0][:, None], asked[2][:, None]

    def source_rows(spot, first, second, table):
        rows_1 = pick(first, table)
        scale = coded(inv_rms(rows_1))
        parts = pieces_of(rows_1, spot[0], seqs)
        return [jnp.concatenate([p, scale], 1) for p in parts] + [rows_1, pick(second, table)]

    *sent, asked_rows, second_rows = call(
        source_rows,
        [((slots, width + lanes), bf16)] * seqs + [((slots, features), bf16)] * 2,
        spot, asked_token, asked[1][:, None], source,
    )
    start_got = trade_seq(sent, 1)
    start_2 = ring(second_rows, "section", 1)

    next_rows = from_after(embed[:depths], "seq", 1)
    padded = jnp.concatenate(
        [embed, next_rows, jnp.zeros((16 - depths, features), bf16)], 0
    )

    facts = jnp.stack([token[0].astype(f32), token[1].astype(f32), live[0], live[1], weight[0], weight[1]], 1)
    if seqs == 2:
        facts_got = trade_seq([facts, facts])
        facts = in_order(facts_got, place, 0)
    else:
        facts = lax.all_gather(facts, "seq", axis=0, tiled=True)
    facts = jnp.concatenate(gather_dp(facts), 0)
    base = (jnp.arange(total, dtype=f32) // slots * tokens)[:, None]
    keys = facts[:, 0:2] + base
    all_live = facts[:, 2:4]
    all_weight = facts[:, 4:6]
    same = (
        (keys[:, 1:2] == keys[:, 0:1].T) & (all_live[:, 1:2] > 0) & (all_live[:, 0:1].T > 0)
    )
    same = same.astype(f32)
    same_16 = same.astype(bf16)
    same_own = same[:rows, :rows]
    weight_1 = all_weight[:, 0:1]
    met = (token_2 == token_1.T) & (live_1.T > 0)
    met = jnp.any(met, axis=1, keepdims=True).astype(f32)
    where_1 = (token_1 == jnp.arange(tokens)[None, :]).astype(f32) * live_1
    where_2 = (token_2 == jnp.arange(tokens)[None, :]).astype(f32) * live_2
    keep = 1.0 - jnp.maximum(jnp.max(where_1, 0), jnp.max(where_2, 0))[:, None]

    def local_rows(spot, first, second, weight_2, table, cot):
        ahead_11, ahead_12 = pick(first + 1, table), pick(first + 2, table)
        block = jnp.concatenate(
            [ahead_11, ahead_12, pick(first, cot), pick(second, cot) * weight_2], 0
        )
        none = jnp.zeros((2 * slots, lanes), f32)
        scale = jnp.concatenate([coded(inv_rms(ahead_11)), coded(inv_rms(ahead_12)), none], 0)
        return [jnp.concatenate([p, scale], 1) for p in pieces_of(block, spot[0], seqs)]

    local_got = trade_seq(
        call(
            local_rows,
            [((4 * slots, width + lanes), bf16)] * seqs,
            spot, token_1, token_2, weight[1][:, None], padded, cot,
        )
    )

    def local_parts(spot, *got):
        parts = []
        for k in range(4):
            mine = [g[k * slots : (k + 1) * slots].astype(f32) for g in got]
            block = in_order(mine, spot[0], 0)
            body = block[:, :width]
            parts.append(body * decoded(block[:, width:]) if k < 2 else body)
        return parts

    unit_e1, unit_e2, cot_1, dout_2 = call(
        local_parts,
        [((rows, width), f32)] * 3 + [((rows, width), bf16)],
        spot, *local_got,
    )
    dout_2_all = gather_dp(dout_2)

    def first_mixed(spot, unit_e1, live_1, gain, *got):
        block = in_order([g.astype(f32) for g in got], spot[0], 0)
        unit = block[:, :width] * decoded(block[:, width:])
        mixed = (unit * gain[0:1] + unit_e1 * gain[1:2]).astype(bf16).astype(f32)
        return mixed * live_1, unit

    rows_1, unit_1 = call(
        first_mixed,
        [((rows, width), bf16), ((rows, width), f32)],
        spot, unit_e1, all_live[:rows, 0:1], gain_part, *start_got,
    )
    rows_1_all = gather_dp(rows_1)

    def second_base(spot, start, second, met, live_2, table, gain):
        start = start.astype(f32)
        ahead_1, ahead_2 = pick(second + 1, table), pick(second + 2, table)
        unit = start * inv_rms(start)
        mixed = unit * gain[0:1] + ahead_1 * inv_rms(ahead_1) * gain[1:2]
        mixed = mixed.astype(bf16).astype(f32)
        own = mixed * inv_rms(mixed) * gain[2:3] * (1.0 - met)
        out = (own + ahead_2 * inv_rms(ahead_2) * gain[3:4]) * live_2
        return pieces_of(out, spot[0], seqs) + [ahead_1, ahead_2]

    *base_parts, ahead_21, ahead_22 = call(
        second_base,
        [((slots, width), bf16)] * seqs + [((slots, features), bf16)] * 2,
        spot, start_2, token_2, met, live_2, padded, gain,
    )
    base_got = trade_seq(base_parts)
    (base_2,) = call(
        lambda spot, *got: [in_order([g.astype(f32) for g in got], spot[0], 0)],
        [((rows, width), bf16)],
        spot, *base_got,
    )

    first = pair_seq(*project(rows_1_all, expert_weight, 0, (0, 1)))
    base_2_all = gather_dp(base_2)

    def forward_1(own, other):
        both = own + other.astype(f32)
        gate, up = both[:, :hidden_units], both[:, hidden_units:]
        return jax.nn.silu(gate) * up, both

    (act_1, both_1), out_blocks = expand(
        forward_1,
        first,
        [((total, hidden_units), bf16), ((total, 2 * hidden_units), f32)],
        expert_weight, 0, (2,), groups,
    )
    out_got = return_dp(out_blocks)

    def second_prev(rows_1, weight_1, *got):
        out = sum(g.astype(f32) for g in got)
        return [rows_1.astype(f32) + out * weight_1]

    (prev,) = call(
        second_prev, [((rows, width), bf16)], rows_1, weight_1[:rows], *out_got
    )
    prev_all = gather_dp(prev)
    base_own, base_send = project(base_2_all, expert_weight, 1, (0, 1))
    back_own, back_send = project(dout_2_all, expert_weight, 1, (2,))
    base_pair = pair_seq(base_own, base_send)
    back_pair = pair_seq(back_own, back_send)

    mixed_own, mixed_send, chosen = project(
        prev_all, expert_weight, 1, (0, 1), select=same_16, gain=gain_part[2:3]
    )
    second = pair_seq(mixed_own, mixed_send)
    prev_pair = pair_seq(*project(prev_all, expert_weight, 0, (2,)))

    def gates_back(gate, up, d_act):
        sig = jax.nn.sigmoid(gate)
        d_gate = d_act * up * sig * (1.0 + gate * (1.0 - sig))
        return d_gate, d_act * gate * sig

    def backward_2(own, other, base_own, base_other, back_own, back_other, same):
        many = 2 * hidden_units
        square = own[:, many : many + 1] + decoded(other[:, many:])
        scale = lax.rsqrt(square / features + eps_norm)
        row = jnp.sum(jnp.where(same > 0, jnp.transpose(jnp.broadcast_to(scale, same.shape)), 0.0), axis=1, keepdims=True)
        both = (own[:, :many] + other[:, :many].astype(f32)) * row
        both = both + base_own + base_other.astype(f32)
        gate, up = both[:, :hidden_units], both[:, hidden_units:]
        d_gate, d_up = gates_back(gate, up, back_own + back_other.astype(f32))
        return d_gate, d_up, jax.nn.silu(gate) * up, scale, row

    units = ((total, hidden_units), bf16)
    (d_gate_2, d_up_2, act_2, scale_2, row_2), d_rows_blocks = expand(
        backward_2,
        second + base_pair + back_pair + (same,),
        [units, units, units, ((total, 1), f32), ((total, 1), f32)],
        expert_weight, 1, (0, 1), groups,
    )
    d_rows_got = return_dp(d_rows_blocks)

    def first_grad(spot, cot, same, gain, *got):
        d_rows = sum(g.astype(f32) for g in got)
        added = lax.dot_general(
            same, d_rows, (((0,), (0,)), ((), ())),
            precision=lax.Precision.HIGHEST, preferred_element_type=f32,
        )
        d_mixed = cot + added
        back = []
        for o in range(seqs):
            block = d_rows[:slots]
            for j in range(1, seqs):
                want = lax.rem(spot[0] + o, seqs) == j
                block = jnp.where(want, d_rows[j * slots : (j + 1) * slots], block)
            back.append(block)
        return [d_mixed * gain[2:3], d_mixed] + back

    u, d_mixed_2, *d_rows_back = call(
        first_grad,
        [((rows, width), bf16), ((rows, width), f32)] + [((slots, width), bf16)] * seqs,
        spot, cot_1, same_own, gain_part, *d_rows_got,
    )
    u_all = gather_dp(u)
    own_back = trade_seq(d_rows_back)

    def build_2(row_values, column_values):
        chosen, *rest = row_values
        base = jnp.concatenate(rest[:groups], 0).astype(f32)
        dout = jnp.concatenate(rest[groups:], 0)
        (row,) = column_values
        return (chosen.astype(f32) * row + base).astype(bf16), dout

    weight_grad = outer(
        1, depths, build_2, [chosen] + base_2_all + dout_2_all, [row_2], d_gate_2, d_up_2, act_2, None
    )

    hidden, _ = lax.optimization_barrier((source, start_2))
    hidden = ring(hidden, "section", 1)
    dense_grad, dense_terms = dense_rows(hidden, padded, cot, keep, gain)
    dense_grad = ring(dense_grad, "section", -1)

    def second_grad(spot, start, ahead_1, ahead_2, second, keep, cot, gain, terms, *got):
        d_rows = in_order([g.astype(f32) for g in got], spot[0], 1)
        grad, more = backward_rows(
            start.astype(f32), ahead_1.astype(f32), ahead_2.astype(f32),
            pick(second, cot) + d_rows, keep, gain,
        )
        terms = terms + more
        return [grad] + pieces_of(terms, spot[0], seqs)

    grad_2, *terms_parts = call(
        second_grad,
        [((slots, features), bf16)] + [((2 * depths, width), f32)] * seqs,
        spot, start_2, ahead_21, ahead_22, token_2, live_2 * (1.0 - met), cot, gain, dense_terms, *own_back,
    )
    asked_2 = ring(jnp.stack([token[1], (live_2 * (1.0 - met))[:, 0].astype(jnp.int32)]), "section", -1)
    grad_2 = ring(grad_2, "section", -1)
    terms_got = trade_seq(terms_parts)

    back_1 = pair_seq(*project(u_all, expert_weight, 0, (2,), mates=prev_all))

    def backward_1(own, other, prev_own, prev_other, both, scale, weight_1):
        inner = own[:, hidden_units : hidden_units + 1] + decoded(other[:, hidden_units:])
        d_act = own[:, :hidden_units] + other[:, :hidden_units].astype(f32)
        through = scale * scale * inner / features
        d_act = d_act - through * (prev_own + prev_other.astype(f32))
        d_act = d_act * (weight_1 * scale)
        d_gate, d_up = gates_back(both[:, :hidden_units], both[:, hidden_units:], d_act)
        return d_gate, d_up, through

    (d_gate_1, d_up_1, through_1), d_rows_blocks = expand(
        backward_1,
        back_1 + prev_pair + (both_1, scale_2, weight_1),
        [units, units, ((total, 1), f32)],
        expert_weight, 0, (0, 1), groups,
    )
    d_rows_got = return_dp(d_rows_blocks)

    def build_1(row_values, column_values):
        first, u, prev = (
            jnp.concatenate(row_values[k * groups : (k + 1) * groups], 0) for k in range(3)
        )
        through, factor = column_values
        dout = (u.astype(f32) - through * prev.astype(f32)) * factor
        return first, dout.astype(bf16)

    weight_grad = outer(
        0, depths, build_1, rows_1_all + u_all + prev_all, [through_1, weight_1 * scale_2],
        d_gate_1, d_up_1, act_1, weight_grad,
    )

    def last_grad(spot, d_mixed_2, prev, scale, through, unit_1, unit_e1, unit_e2, live_1, gain, *got):
        terms, got = got[:seqs], got[seqs:]
        d_rows = sum(g.astype(f32) for g in got)
        prev = prev.astype(f32)
        grad_1 = (d_mixed_2 * gain[2:3] - through * prev) * scale
        d_mixed_1 = grad_1 + d_rows
        kept_1, kept_2 = d_mixed_1 * live_1, d_mixed_2 * live_1
        sums = [
            jnp.sum(a * b, axis=0, keepdims=True)
            for a, b in ((kept_1, unit_1), (kept_1, unit_e1), (kept_2, prev * scale), (kept_2, unit_e2))
        ]
        sums = jnp.concatenate(sums, 0) + sum(terms)
        out = d_mixed_1 * gain[0:1]
        back = []
        for o in range(seqs):
            block = out[:slots]
            for j in range(1, seqs):
                want = lax.rem(spot[0] + o, seqs) == j
                block = jnp.where(want, out[j * slots : (j + 1) * slots], block)
            back.append(block)
        return [sums] + back

    sums, *last_parts = call(
        last_grad,
        [((2 * depths, width), f32)] + [((slots, width), bf16)] * seqs,
        spot, d_mixed_2, prev, scale_2[:rows], through_1[:rows], unit_1, unit_e1, unit_e2,
        all_live[:rows, 0:1], gain_part, *terms_got, *d_rows_got,
    )
    last_got = trade_seq(last_parts, -1)

    mine = lax.axis_index("dp")
    share = width // groups

    def columns(i):
        return lax.dynamic_slice(sums, (0, lax.rem(mine - i + groups, groups) * share), (2 * depths, share))

    gain_grad = sum(return_dp([columns(i) for i in range(groups)]))

    def finish(spot, dense, first, kept_1, rows, second, kept_2, grad_2, *got):
        part = in_order([g.astype(f32) for g in got], spot[0], 1)
        rows = rows.astype(f32)
        scale = inv_rms(rows)
        unit = rows * scale
        grad_1 = (part - unit * jnp.mean(part * unit, axis=-1, keepdims=True)) * scale
        lane = lax.broadcasted_iota(jnp.int32, (slots, tokens), 1)
        chosen = jnp.concatenate(
            [((first == lane) & (kept_1 > 0)).astype(f32), ((second == lane) & (kept_2 > 0)).astype(f32)], 0
        )
        placed = lax.dot_general(
            chosen.astype(bf16), jnp.concatenate([grad_1, grad_2.astype(f32)], 0).astype(bf16),
            (((0,), (0,)), ((), ())), preferred_element_type=f32,
        )
        taken = lax.dot_general(
            chosen, jnp.ones((2 * slots, lanes), f32), (((0,), (0,)), ((), ())), preferred_element_type=f32
        )[:, 0:1]
        return [jnp.where(taken > 0, placed, dense.astype(f32))]

    (hidden_grad,) = call(
        finish,
        [((tokens, features), bf16)],
        spot, dense_grad, asked_token, asked_live, asked_rows, asked_2[0][:, None], asked_2[1][:, None],
        grad_2, *last_got,
    )
    return (
        hidden_grad[None, None],
        weight_grad,
        gain_grad.reshape(1, depths, 2, share),
    )


def solution(mesh):
    return jax.shard_map(
        local,
        mesh=mesh,
        in_specs=(
            P("section", "dp", "seq", None),
            P("section", "dp", "seq", None),
            P("section", "dp", "seq", None),
            P("section", "dp", None, "seq"),
            P("section", "dp", None, "seq"),
            P("section", "dp", None, "seq"),
            P(),
            P(None, None, "seq", "dp"),
        ),
        out_specs=(
            P("section", "dp", "seq", None),
            P("section", None, None, "seq", "dp"),
            P("section", None, None, ("seq", "dp")),
        ),
        check_vma=False,
    )
```

```python
import jax
import jax.numpy as jnp
from jax import lax
from jax.experimental import pallas as pl
from jax.experimental.pallas import tpu as pltpu
from jax.sharding import PartitionSpec as P

eps_norm = 1e-06
lanes = 128
f32 = jnp.float32
bf16 = jnp.bfloat16
vmem = pl.BlockSpec(memory_space=pltpu.VMEM)
smem = pl.BlockSpec(memory_space=pltpu.SMEM)
anywhere = pl.BlockSpec(memory_space=pl.ANY)


def ring(value, axis, steps):
    count = lax.axis_size(axis)
    return lax.ppermute(value, axis, [(i, (i + steps) % count) for i in range(count)])


def from_after(array, axis, by):
    size = lax.axis_size(axis)
    return lax.ppermute(array, axis, [(i, i - by) for i in range(by, size)])


def hop(value, section_step, seq_step):
    sections, seqs = lax.axis_size("section"), lax.axis_size("seq")
    pairs = [
        (c * seqs + s, (c + section_step) % sections * seqs + (s + seq_step) % seqs)
        for c in range(sections)
        for s in range(seqs)
    ]
    return lax.ppermute(value, ("section", "seq"), pairs)


def trade_seq(pieces, section_step=0):
    if section_step == 0:
        return [pieces[0]] + [ring(pieces[o], "seq", o) for o in range(1, len(pieces))]
    return [hop(piece, section_step, o) for o, piece in enumerate(pieces)]


def swap_dp(blocks):
    return lax.all_to_all(blocks, "dp", split_axis=0, concat_axis=0, tiled=True)


def pair_seq(own, send):
    if lax.axis_size("seq") == 2:
        return own, ring(send, "seq", 1)
    return lax.psum(own, "seq"), jnp.zeros_like(send)


def inv_rms(value):
    return lax.rsqrt(jnp.mean(value * value, axis=-1, keepdims=True) + eps_norm)


def iota(shape, dim):
    return lax.broadcasted_iota(jnp.int32, shape, dim)


def token_column(token, depth):
    capacity = token.shape[3]
    out = jnp.full((capacity, 1), token[0, 0, depth, 0], jnp.int32)
    for c in range(1, capacity):
        out = jnp.where(iota((capacity, 1), 0) == c, token[0, 0, depth, c], out)
    return out


def gate_column(gate, depth):
    capacity = gate.shape[3]
    out = jnp.full((capacity, 1), gate[0, 0, depth, 0], f32)
    for c in range(1, capacity):
        out = jnp.where(iota((capacity, 1), 0) == c, gate[0, 0, depth, c], out)
    return out


def live_column(count, depth, capacity):
    return (iota((capacity, 1), 0) < count[0, 0, depth, 0]).astype(f32)


def met_column(token, count):
    capacity = token.shape[3]
    second = token_column(token, 1)
    out = jnp.zeros((capacity, 1), f32)
    for c in range(capacity):
        out += ((second == token[0, 0, 0, c]) & (c < count[0, 0, 0, 0])).astype(f32)
    return jnp.minimum(out, 1.0)


def pick(column, table):
    hot = (column == iota((column.shape[0], table.shape[0]), 1)).astype(bf16)
    return jnp.dot(hot, table, preferred_element_type=f32)


def pick_ahead(column, table, after):
    out = pick(column, table)
    for k in range(after.shape[0]):
        row = after[k : k + 1].astype(f32)
        out += jnp.where(column == table.shape[0] + k, row, 0.0)
    return out


def thirds(column):
    high = column.astype(bf16).astype(f32)
    mid = (column - high).astype(bf16).astype(f32)
    return [high, mid, column - high - mid]


def in_lanes(columns):
    lane = iota((columns[0].shape[0], lanes), 1)
    out = jnp.zeros(lane.shape, f32)
    for k, column in enumerate(columns):
        out = jnp.where(lane == k, column, out)
    return out


def coded(column):
    return in_lanes(thirds(column))


def decoded(block, first=0):
    lane = iota(block.shape, 1)
    inside = (lane >= first) & (lane < first + 3)
    return jnp.sum(jnp.where(inside, block.astype(f32), 0.0), axis=1, keepdims=True)


def piece_of(value, place, count, step):
    width = value.shape[-1] // count
    want = lax.rem(place + step, count)
    out = value[:, :width]
    for p in range(1, count):
        out = jnp.where(want == p, value[:, p * width : (p + 1) * width], out)
    return out


def pieces_of(value, place, count):
    return [piece_of(value, place, count, o) for o in range(count)]


def blocks_of(value, place, count):
    size = value.shape[0] // count
    out = []
    for o in range(count):
        block = value[:size]
        for j in range(1, count):
            want = lax.rem(place + o, count) == j
            block = jnp.where(want, value[j * size : (j + 1) * size], block)
        out.append(block)
    return out


def in_order(got, place, axis):
    count = len(got)
    out = []
    for j in range(count):
        block = got[0]
        for o in range(1, count):
            block = jnp.where(lax.rem(place - o + count, count) == j, got[o], block)
        out.append(block)
    return jnp.concatenate(out, axis)


def own_rows(value, place, count):
    size = value.shape[0] // count
    out = value[:size]
    for z in range(1, count):
        out = jnp.where(place == z, value[z * size : (z + 1) * size], out)
    return out


def as_row(column):
    size = column.shape[0]
    here = iota((size, size), 0) == iota((size, size), 1)
    return jnp.sum(jnp.where(here, column, 0.0), axis=0, keepdims=True)


def folds(rows, width):
    for count in (1, 2, 4, 8):
        if rows * count % 16 == 0 and width % (count * lanes) == 0:
            return count
    return 1


def folded(value, count):
    step = value.shape[1] // count
    return jnp.concatenate([value[:, g * step : (g + 1) * step] for g in range(count)], 0)


def unfolded(value, count):
    rows = value.shape[0] // count
    return jnp.concatenate([value[g * rows : (g + 1) * rows] for g in range(count)], 1)


def column_part(blocks, rows, g):
    step = blocks.shape[2]
    return jnp.concatenate(
        [blocks[z][g * rows : (g + 1) * rows].astype(f32) for z in range(blocks.shape[0])], 0
    ).astype(bf16)


def repeated(value, count):
    return jnp.stack([value] * count)


def call(name, fn, outs, small, *args, after=(), flops=0, limit=12):
    shapes = [jax.ShapeDtypeStruct(shape, kind) for shape, kind in outs]
    n_small, n_args, n_after = len(small), len(args), len(after)

    def body(*refs):
        values = list(refs[:n_small]) + [r[...] for r in refs[n_small : n_small + n_args]]
        for ref, value in zip(refs[n_small + n_args + n_after :], fn(*values)):
            ref[...] = value.astype(ref.dtype)

    size = sum(a.size * a.dtype.itemsize for a in list(args) + shapes)
    return pl.pallas_call(
        body,
        name=name,
        out_shape=shapes,
        in_specs=[smem] * n_small + [vmem] * n_args + [anywhere] * n_after,
        out_specs=[vmem] * len(shapes),
        compiler_params=pltpu.CompilerParams(vmem_limit_bytes=limit << 20),
        cost_estimate=pl.CostEstimate(flops=flops, bytes_accessed=size, transcendentals=0),
    )(*small, *args, *after)


def fetch(weight_ref, depth, kinds, buffer, sems, parts):
    step = weight_ref.shape[2] // parts
    copies = []
    for g in range(parts):
        row = []
        for k, kind in enumerate(kinds):
            copy = pltpu.make_async_copy(
                weight_ref.at[depth, kind, pl.ds(g * step, step)],
                buffer.at[g, k],
                sems.at[g, k],
            )
            copy.start()
            row.append(copy)
        copies.append(row)
    return copies


def fetched(weight, kinds, parts):
    hidden = weight.shape[3]
    return [
        pltpu.VMEM((parts, len(kinds), weight.shape[2] // parts, hidden), bf16),
        pltpu.SemaphoreType.DMA((parts, len(kinds))),
    ]


def project(name, blocks, weight, depth, kinds, parts, select=None, gain=None, mates=None, after=()):
    groups, folded_rows, _ = blocks.shape
    rows = folded_rows // parts
    width, hidden = weight.shape[2:]
    step = width // parts
    total, many = rows * groups, len(kinds) * hidden
    marked = select is not None or mates is not None
    extra = lanes if marked else 0

    def body(*refs):
        refs = list(refs)
        if select is not None:
            where_ref, x_ref, w_ref, select_ref, gain_ref = (refs.pop(0) for _ in range(5))
        else:
            x_ref, w_ref = refs.pop(0), refs.pop(0)
        mate_ref = refs.pop(0) if mates is not None else None
        refs = refs[len(after) :]
        own_ref, send_ref = refs.pop(0), refs.pop(0)
        kept_ref = refs.pop(0) if select is not None else None
        buffer, sems = refs
        copies = fetch(w_ref, depth, kinds, buffer, sems, parts)
        x_all = x_ref[...]
        mate_all = mate_ref[...] if mates is not None else x_all
        if select is not None:
            gain_all = piece_of(gain_ref[1, 0:1, :], where_ref[0], gain.shape[2] // width, 0)
        sums = [jnp.zeros((total, hidden), f32) for _ in kinds]
        mark = jnp.zeros((total, 1), f32)
        for g in range(parts):
            x = column_part(x_all, rows, g)
            if marked:
                mate = x if mates is None else column_part(mate_all, rows, g)
                mark += jnp.sum(x.astype(f32) * mate.astype(f32), axis=1, keepdims=True)
            if select is not None:
                chosen = jnp.dot(select_ref[...], x, preferred_element_type=f32)
                x = (chosen * gain_all[:, g * step : (g + 1) * step]).astype(bf16)
                kept_ref[:, g * step : (g + 1) * step] = x
            for k in range(len(kinds)):
                copies[g][k].wait()
                sums[k] += jnp.dot(x, buffer[g, k], preferred_element_type=f32)
        for k in range(len(kinds)):
            own_ref[:, k * hidden : (k + 1) * hidden] = sums[k]
            send_ref[:, k * hidden : (k + 1) * hidden] = sums[k].astype(bf16)
        if marked:
            own_ref[:, many:] = in_lanes([mark])
            send_ref[:, many:] = coded(mark).astype(bf16)

    args, specs = [blocks, pltpu.with_memory_space_constraint(weight, pltpu.HBM)], [vmem, anywhere]
    outs = [
        jax.ShapeDtypeStruct((total, many + extra), f32),
        jax.ShapeDtypeStruct((total, many + extra), bf16),
    ]
    if select is not None:
        where, table = select
        args, specs = [where] + args + [table, gain], [smem] + specs + [vmem, vmem]
        outs.append(jax.ShapeDtypeStruct((total, width), bf16))
    if mates is not None:
        args, specs = args + [mates], specs + [vmem]
    return pl.pallas_call(
        body,
        name=name,
        in_specs=specs + [anywhere] * len(after),
        out_specs=[vmem] * len(outs),
        out_shape=outs,
        scratch_shapes=fetched(weight, kinds, parts),
        compiler_params=pltpu.CompilerParams(vmem_limit_bytes=16 << 20),
        cost_estimate=pl.CostEstimate(
            flops=2 * total * width * many, bytes_accessed=2 * width * many, transcendentals=0
        ),
    )(*args, *after)


def expand(name, prepare, args, saved, weight, depth, kinds, groups, parts, after=()):
    width, hidden = weight.shape[2:]
    total = saved[0][0][0]
    rows, step = total // groups, width // parts
    count, kept = len(args), len(saved)

    def body(*refs):
        in_refs, w_ref = refs[:count], refs[count]
        refs = refs[count + 1 + len(after) :]
        saved_refs, out_ref, buffer, sems = refs[:kept], refs[kept], refs[kept + 1], refs[kept + 2]
        copies = fetch(w_ref, depth, kinds, buffer, sems, parts)
        for ref, value in zip(saved_refs, prepare(*[r[...] for r in in_refs])):
            ref[...] = value.astype(ref.dtype)
        out = []
        for g in range(parts):
            part = jnp.zeros((total, step), f32)
            for k in range(len(kinds)):
                copies[g][k].wait()
                part += lax.dot_general(
                    saved_refs[k][...], buffer[g, k], (((1,), (1,)), ((), ())),
                    preferred_element_type=f32,
                )
            out.append(part)
        for z in range(groups):
            block = jnp.concatenate([part[z * rows : (z + 1) * rows] for part in out], 0)
            out_ref[z] = block.astype(bf16)

    results = pl.pallas_call(
        body,
        name=name,
        in_specs=[vmem] * count + [anywhere] * (1 + len(after)),
        out_specs=[vmem] * (kept + 1),
        out_shape=[jax.ShapeDtypeStruct(shape, kind) for shape, kind in saved]
        + [jax.ShapeDtypeStruct((groups, rows * parts, step), bf16)],
        scratch_shapes=fetched(weight, kinds, parts),
        compiler_params=pltpu.CompilerParams(vmem_limit_bytes=16 << 20),
        cost_estimate=pl.CostEstimate(
            flops=2 * total * width * hidden * len(kinds),
            bytes_accessed=2 * width * hidden * len(kinds),
            transcendentals=0,
        ),
    )(*args, pltpu.with_memory_space_constraint(weight, pltpu.HBM), *after)
    return results[:kept], results[kept]


def outer(name, depth, depths, build, args, d_gate, d_up, act, width, parts, before, after=()):
    total, hidden = act.shape
    step = width // parts
    count = len(args)
    earlier = [] if before is None else [before]

    def contract(left, right):
        return lax.dot_general(left, right, (((0,), (0,)), ((), ())), preferred_element_type=f32)

    def body(*refs):
        values = [r[...] for r in refs[:count]]
        gate_ref, up_ref, act_ref = refs[count : count + 3]
        out_ref, buffer, sems = refs[-3:]
        copies = []
        for g in range(parts):
            rows, dout = build(values, g)
            pairs = ((rows, gate_ref), (rows, up_ref), (dout, act_ref))
            for k, (left, right_ref) in enumerate(pairs):
                buffer[g, k] = contract(left, right_ref[...]).astype(bf16)
                copy = pltpu.make_async_copy(
                    buffer.at[g, k],
                    out_ref.at[0, depth, k, pl.ds(g * step, step)],
                    sems.at[g, k],
                )
                copy.start()
                copies.append(copy)
        for copy in copies:
            copy.wait()

    return pl.pallas_call(
        body,
        name=name,
        in_specs=[vmem] * (count + 3) + [anywhere] * (len(earlier) + len(after)),
        out_specs=anywhere,
        out_shape=jax.ShapeDtypeStruct((1, depths, 3, width, hidden), bf16),
        input_output_aliases={} if before is None else {count + 3: 0},
        scratch_shapes=[
            pltpu.VMEM((parts, 3, step, hidden), bf16),
            pltpu.SemaphoreType.DMA((parts, 3)),
        ],
        compiler_params=pltpu.CompilerParams(vmem_limit_bytes=24 << 20),
        cost_estimate=pl.CostEstimate(
            flops=6 * total * width * hidden, bytes_accessed=6 * width * hidden, transcendentals=0
        ),
    )(*args, d_gate, d_up, act, *earlier, *after)


def backward_rows(hidden, ahead_1, ahead_2, d_mixed_2, keep, gain):
    scale_1 = inv_rms(hidden)
    unit_1 = hidden * scale_1
    unit_e1 = ahead_1 * inv_rms(ahead_1)
    unit_e2 = ahead_2 * inv_rms(ahead_2)
    mixed = (unit_1 * gain[0, 0:1] + unit_e1 * gain[0, 1:2]).astype(bf16).astype(f32)
    scale_2 = inv_rms(mixed)
    unit_2 = mixed * scale_2
    u = d_mixed_2 * gain[1, 0:1]
    grad_1 = (u - unit_2 * jnp.mean(u * unit_2, axis=-1, keepdims=True)) * scale_2
    v = grad_1 * gain[0, 0:1]
    grad_0 = (v - unit_1 * jnp.mean(v * unit_1, axis=-1, keepdims=True)) * scale_1
    kept_1, kept_2 = grad_1 * keep, d_mixed_2 * keep
    terms = [
        jnp.sum(a * b, axis=0, keepdims=True)
        for a, b in ((kept_1, unit_1), (kept_1, unit_e1), (kept_2, unit_2), (kept_2, unit_e2))
    ]
    return grad_0.astype(bf16), jnp.concatenate(terms, 0)


def dense_rows(name, token, count, hidden, embed, next_rows, cotangent, gain, before, half, halves, after=()):
    tokens, width = hidden.shape
    step = 16
    steps = tokens // step // halves
    first, last = half * steps, tokens // step - 1
    capacity = token.shape[3]
    earlier = [] if before is None else [before]

    def body(token_ref, count_ref, hidden_ref, now_ref, next_ref, after_ref, cot_ref, gain_ref, *refs):
        out_ref, terms_ref = refs[-2:]
        block = first + pl.program_id(0)

        @pl.when(pl.program_id(0) == 0)
        def _():
            terms_ref[...] = refs[0][...] if earlier else jnp.zeros_like(terms_ref)

        here = iota((step, 1), 0) + block * step
        keep = jnp.ones((step, 1), f32)
        for k in range(2):
            for c in range(capacity):
                out = (here == token_ref[0, 0, k, c]) & (c < count_ref[0, 0, k, 0])
                keep = jnp.where(out, 0.0, keep)
        follow = jnp.where(
            block == last,
            jnp.concatenate([after_ref[...].astype(f32)] * (8 // after_ref.shape[0]), 0),
            next_ref[...].astype(f32)[:8],
        )
        both = jnp.concatenate([now_ref[...].astype(f32), follow], 0)
        grad, terms = backward_rows(
            hidden_ref[...].astype(f32),
            both[1 : step + 1],
            both[2 : step + 2],
            cot_ref[...].astype(f32),
            keep,
            gain_ref[...],
        )
        out_ref[...] = grad
        terms_ref[...] += terms

    rows = pl.BlockSpec((step, width), lambda i: (first + i, 0))
    terms = pl.BlockSpec((4, width), lambda i: (0, 0))
    return pl.pallas_call(
        body,
        name=name,
        grid=(steps,),
        in_specs=[
            smem,
            smem,
            rows,
            rows,
            pl.BlockSpec((step, width), lambda i: (jnp.minimum(first + i + 1, last), 0)),
            pl.BlockSpec(next_rows.shape, lambda i: (0, 0)),
            rows,
            pl.BlockSpec(gain.shape, lambda i: (0, 0, 0)),
        ]
        + [terms] * len(earlier)
        + [anywhere] * len(after),
        out_specs=[pl.BlockSpec((step, width), lambda i: (i, 0)), terms],
        out_shape=[
            jax.ShapeDtypeStruct((tokens // halves, width), bf16),
            jax.ShapeDtypeStruct((4, width), f32),
        ],
        compiler_params=pltpu.CompilerParams(vmem_limit_bytes=20 << 20),
        cost_estimate=pl.CostEstimate(
            flops=60 * tokens * width // halves,
            bytes_accessed=10 * tokens * width // halves,
            transcendentals=0,
        ),
    )(token, count, hidden, embed, embed, next_rows, cotangent, gain, *earlier, *after)


def local(
    main_hidden, embedded, cotangent, slot_token, slot_count, route_gate, norm_gain, expert_weight
):
    depths, _, features = norm_gain.shape
    tokens = main_hidden.shape[2]
    slots = slot_token.shape[3]
    seqs, groups = lax.axis_size("seq"), lax.axis_size("dp")
    rows = seqs * slots
    total = groups * rows
    width = features // seqs
    share = width // groups
    hidden_units = expert_weight.shape[3]
    parts = folds(rows, width)
    where = jnp.stack([lax.axis_index("seq"), lax.axis_index("dp")]).astype(jnp.int32)
    source, embed, cot = main_hidden[0, 0], embedded[0, 0], cotangent[0, 0]
    facts = (slot_token, slot_count)
    packed = ((groups, rows * parts, width // parts), bf16)
    part_rows = ((rows, width), f32)

    def payload(value):
        return repeated(folded(value, parts), groups)

    asked_token = ring(slot_token, "section", -1)
    next_rows = from_after(embed[:depths], "seq", 1)

    def cot_rows(where, token, count, gate, cot):
        first, second = token_column(token, 0), token_column(token, 1)
        live_1, live_2 = (live_column(count, k, slots) for k in range(2))
        weight_1, weight_2 = gate_column(gate, 0) * live_1, gate_column(gate, 1) * live_2
        facts = in_lanes(
            [first.astype(f32), second.astype(f32), live_1, live_2]
            + thirds(weight_1)
            + thirds(weight_2)
        )
        cot_1, dout = pick(first, cot), pick(second, cot) * weight_2
        return [
            jnp.concatenate(
                [
                    jnp.concatenate([piece_of(cot_1, where[0], seqs, o), facts], 1),
                    jnp.concatenate([piece_of(dout, where[0], seqs, o), facts], 1),
                ],
                0,
            )
            for o in range(seqs)
        ]

    cot_got = trade_seq(
        call(
            "cot_rows", cot_rows, [((2 * slots, width + lanes), bf16)] * seqs,
            (where, slot_token, slot_count, route_gate), cot,
        )
    )

    def cot_parts(where, *got):
        parts_1, parts_2 = (
            in_order([g[k * slots : (k + 1) * slots].astype(f32) for g in got], where[0], 0)
            for k in range(2)
        )
        facts = parts_1[:, width:]
        out = folded(parts_2[:, :width], parts)
        none = jnp.zeros(((parts - 1) * rows, lanes), f32)
        tail = facts if parts == 1 else jnp.concatenate([facts, none], 0)
        return parts_1[:, :width], repeated(jnp.concatenate([out, tail], 1), groups), facts

    cot_1, dout_2, own_facts = call(
        "cot_parts", cot_parts,
        [part_rows, ((groups, rows * parts, width // parts + lanes), bf16), ((rows, lanes), f32)],
        (where,), *cot_got,
    )
    dout_2_all = swap_dp(dout_2)

    def source_rows(where, token, table):
        first = pick(token_column(token, 0), table)
        second = pick(token_column(token, 1), table)
        scale = coded(inv_rms(first))
        sent = [jnp.concatenate([p, scale], 1) for p in pieces_of(first, where[0], seqs)]
        return sent + [first, second]

    *sent, asked_rows, second_rows = call(
        "source_rows", source_rows,
        [((slots, width + lanes), bf16)] * seqs + [((slots, features), bf16)] * 2,
        (where, asked_token), source,
    )
    start_got = trade_seq(sent, 1)
    start_2 = ring(second_rows, "section", 1)

    def ahead_rows(where, token, table, after):
        first = token_column(token, 0)
        out = []
        for k in range(2):
            ahead = pick_ahead(first + k + 1, table, after)
            scale = coded(inv_rms(ahead))
            out.append([jnp.concatenate([p, scale], 1) for p in pieces_of(ahead, where[0], seqs)])
        return [jnp.concatenate(both, 0) for both in zip(*out)]

    ahead_got = trade_seq(
        call(
            "ahead_rows", ahead_rows, [((2 * slots, width + lanes), bf16)] * seqs,
            (where, slot_token), embed, next_rows,
        )
    )

    def first_mixed(where, own_facts, gain, *got):
        ahead_got, start_got = got[:seqs], got[seqs:]
        ahead_1, ahead_2 = (
            in_order([g[k * slots : (k + 1) * slots].astype(f32) for g in ahead_got], where[0], 0)
            for k in range(2)
        )
        start = in_order([g.astype(f32) for g in start_got], where[0], 0)
        unit, unit_1, unit_2 = (
            block[:, :width] * decoded(block[:, width:]) for block in (start, ahead_1, ahead_2)
        )
        gain_h, gain_e = (piece_of(gain[0, k : k + 1], where[0], seqs, 0) for k in range(2))
        mixed = (unit * gain_h + unit_1 * gain_e).astype(bf16).astype(f32)
        return payload(mixed * own_facts[:, 2:3]), unit, unit_1, unit_2

    rows_1, unit_1, unit_e1, unit_e2 = call(
        "first_mixed", first_mixed, [packed] + [part_rows] * 3,
        (where,), own_facts, norm_gain, *ahead_got, *start_got,
    )
    rows_1_all = swap_dp(rows_1)

    def second_base(where, token, count, start, table, after, gain):
        second = token_column(token, 1)
        start = start.astype(f32)
        ahead_1 = pick_ahead(second + 1, table, after)
        ahead_2 = pick_ahead(second + 2, table, after)
        unit = start * inv_rms(start)
        mixed = unit * gain[0, 0:1] + ahead_1 * inv_rms(ahead_1) * gain[0, 1:2]
        mixed = mixed.astype(bf16).astype(f32)
        own = mixed * inv_rms(mixed) * gain[1, 0:1] * (1.0 - met_column(token, count))
        out = (own + ahead_2 * inv_rms(ahead_2) * gain[1, 1:2]) * live_column(count, 1, slots)
        return pieces_of(out, where[0], seqs) + [ahead_1, ahead_2]

    *base_parts, ahead_21, ahead_22 = call(
        "second_base", second_base,
        [((slots, width), bf16)] * seqs + [((slots, features), bf16)] * 2,
        (where, *facts), start_2, embed, next_rows, norm_gain, after=(rows_1,),
    )
    base_got = trade_seq(base_parts)

    first_own, first_send = project(
        "gate_up_1", rows_1_all, expert_weight, 0, (0, 1), parts, after=(ahead_21,)
    )
    first = pair_seq(first_own, first_send)

    def base_order(where, *got):
        return [payload(in_order([g.astype(f32) for g in got], where[0], 0))]

    (base_2,) = call("base_order", base_order, [packed], (where,), *base_got, after=(first_send,))
    base_2_all = swap_dp(base_2)

    def forward_1(own, other):
        both = own + other.astype(f32)
        gate, up = both[:, :hidden_units], both[:, hidden_units:]
        return gate * jax.nn.sigmoid(gate) * up, both

    (act_1, both_1), out_blocks = expand(
        "down_1", forward_1, first,
        [((total, hidden_units), bf16), ((total, 2 * hidden_units), f32)],
        expert_weight, 0, (2,), groups, parts, after=(base_2,),
    )
    out_got = swap_dp(out_blocks)

    def slot_facts(where, blocks):
        facts = jnp.concatenate(
            [blocks[z][:rows].astype(f32)[:, width // parts :] for z in range(groups)], 0
        )
        base = (iota((total, 1), 0) // slots * tokens).astype(f32)
        first, second = facts[:, 0:1] + base, facts[:, 1:2] + base
        live = (facts[:, 3:4] > 0) & (as_row(facts[:, 2:3]) > 0)
        same = ((second == as_row(first)) & live).astype(f32)
        own = own_rows(same, where[1], groups)
        own = sum(
            jnp.where(where[1] == z, own[:, z * rows : (z + 1) * rows], 0.0) for z in range(groups)
        )
        return same, same, own, decoded(facts, 4)

    same, same_16, same_own, weight_1 = call(
        "slot_facts", slot_facts,
        [((total, total), f32), ((total, total), bf16), ((rows, rows), f32), ((total, 1), f32)],
        (where,), dout_2_all, after=(out_blocks,),
    )
    base_own, base_send = project(
        "base_gate_up", base_2_all, expert_weight, 1, (0, 1), parts, after=(same_own,)
    )
    back_own, back_send = project(
        "back_2", dout_2_all[:, :, : width // parts], expert_weight, 1, (2,), parts, after=(base_own,)
    )
    base_pair = pair_seq(base_own, base_send)
    back_pair = pair_seq(back_own, back_send)

    def second_prev(where, own_facts, rows_1, got, *_):
        out = unfolded(sum(got[z].astype(f32) for z in range(groups)), parts)
        value = unfolded(rows_1[0].astype(f32), parts) + out * decoded(own_facts, 4)
        return payload(value), value.astype(bf16)

    prev, prev_own = call(
        "second_prev", second_prev, [packed, ((rows, width), bf16)],
        (where,), own_facts, rows_1, out_got, after=(back_own,),
    )
    prev_all = swap_dp(prev)

    hidden, _ = lax.optimization_barrier((source, start_2))
    hidden = ring(hidden, "section", 1)
    dense_a, terms_a = dense_rows(
        "dense_a", *facts, hidden, embed, next_rows, cot, norm_gain, None, 0, 2, after=(prev,)
    )
    dense_a = ring(dense_a, "section", -1)

    mixed_own, mixed_send, chosen = project(
        "gate_up_2", prev_all, expert_weight, 1, (0, 1), parts,
        select=(where, same_16), gain=norm_gain, after=(terms_a,),
    )
    second = pair_seq(mixed_own, mixed_send)
    prev_w_own, prev_w_send = project(
        "prev_down", prev_all, expert_weight, 0, (2,), parts, after=(mixed_send,)
    )
    prev_pair = pair_seq(prev_w_own, prev_w_send)

    def gates_back(gate, up, d_act):
        sig = jax.nn.sigmoid(gate)
        d_gate = d_act * up * sig * (1.0 + gate * (1.0 - sig))
        return d_gate, d_act * gate * sig

    def backward_2(own, other, base_own, base_other, back_own, back_other, same):
        many = 2 * hidden_units
        square = own[:, many : many + 1] + decoded(other[:, many:])
        scale = lax.rsqrt(square / features + eps_norm)
        row = jnp.sum(same * as_row(scale), axis=1, keepdims=True)
        both = (own[:, :many] + other[:, :many].astype(f32)) * row
        both = both + base_own + base_other.astype(f32)
        gate, up = both[:, :hidden_units], both[:, hidden_units:]
        d_gate, d_up = gates_back(gate, up, back_own + back_other.astype(f32))
        return d_gate, d_up, gate * jax.nn.sigmoid(gate) * up, scale, row

    units = ((total, hidden_units), bf16)
    (d_gate_2, d_up_2, act_2, scale_2, row_2), d_rows_blocks = expand(
        "back_rows_2", backward_2,
        second + base_pair + back_pair + (same,),
        [units, units, units, ((total, 1), f32), ((total, 1), f32)],
        expert_weight, 1, (0, 1), groups, parts, after=(prev_w_own,),
    )
    d_rows_got = swap_dp(d_rows_blocks)
    dense_b, dense_terms = dense_rows(
        "dense_b", *facts, hidden, embed, next_rows, cot, norm_gain, terms_a, 1, 2, after=(d_rows_blocks,)
    )
    dense_b = ring(dense_b, "section", -1)

    def first_grad(where, cot, same, gain, got):
        d_rows = unfolded(sum(got[z].astype(f32) for z in range(groups)), parts)
        added = lax.dot_general(
            same, d_rows, (((0,), (0,)), ((), ())),
            precision=lax.Precision.HIGHEST, preferred_element_type=f32,
        )
        d_mixed = cot + added
        u = d_mixed * piece_of(gain[1, 0:1], where[0], seqs, 0)
        return [payload(u), d_mixed] + blocks_of(d_rows, where[0], seqs)

    u, d_mixed_2, *d_rows_back = call(
        "first_grad", first_grad, [packed, part_rows] + [((slots, width), bf16)] * seqs,
        (where,), cot_1, same_own, norm_gain, d_rows_got, after=(dense_terms,),
    )
    u_all = swap_dp(u)
    back_got = trade_seq(d_rows_back)

    def build_2(values, g):
        chosen, base, dout, row = values
        step = width // parts
        first = chosen[:, g * step : (g + 1) * step].astype(f32) * row
        first = first + column_part(base, rows, g).astype(f32)
        return first.astype(bf16), column_part(dout[:, :, :step], rows, g)

    weight_grad = outer(
        "weight_grad_2", 1, depths, build_2, [chosen, base_2_all, dout_2_all, row_2],
        d_gate_2, d_up_2, act_2, width, parts, None, after=(u,),
    )

    back_1_own, back_1_send = project(
        "back_1", u_all, expert_weight, 0, (2,), parts, mates=prev_all, after=(weight_grad,)
    )
    back_1 = pair_seq(back_1_own, back_1_send)

    def second_grad(where, token, count, start, ahead_1, ahead_2, cot, gain, terms, *got):
        d_rows = in_order([g.astype(f32) for g in got], where[0], 1)
        keep = live_column(count, 1, slots) * (1.0 - met_column(token, count))
        grad, more = backward_rows(
            start.astype(f32), ahead_1.astype(f32), ahead_2.astype(f32),
            pick(token_column(token, 1), cot) + d_rows, keep, gain,
        )
        return [grad] + pieces_of(terms + more, where[0], seqs)

    grad_2, *terms_parts = call(
        "second_grad", second_grad,
        [((slots, features), bf16)] + [((2 * depths, width), f32)] * seqs,
        (where, *facts), start_2, ahead_21, ahead_22, cot, norm_gain, dense_terms, *back_got,
        after=(back_1_send,),
    )
    grad_2 = ring(grad_2, "section", -1)
    asked_count = ring(slot_count, "section", -1)
    terms_got = trade_seq(terms_parts)

    def backward_1(own, other, prev_own, prev_other, both, scale, weight_1):
        inner = own[:, hidden_units : hidden_units + 1] + decoded(other[:, hidden_units:])
        d_act = own[:, :hidden_units] + other[:, :hidden_units].astype(f32)
        through = scale * scale * inner / features
        d_act = d_act - through * (prev_own + prev_other.astype(f32))
        d_act = d_act * (weight_1 * scale)
        d_gate, d_up = gates_back(both[:, :hidden_units], both[:, hidden_units:], d_act)
        return d_gate, d_up, through

    (d_gate_1, d_up_1, through_1), d_rows_blocks = expand(
        "back_rows_1", backward_1,
        back_1 + prev_pair + (both_1, scale_2, weight_1),
        [units, units, ((total, 1), f32)],
        expert_weight, 0, (0, 1), groups, parts, after=(terms_parts[0],),
    )
    d_rows_got = swap_dp(d_rows_blocks)

    def build_1(values, g):
        first, u, prev, through, scale, weight = values
        dout = column_part(u, rows, g).astype(f32) - through * column_part(prev, rows, g).astype(f32)
        return column_part(first, rows, g), (dout * (weight * scale)).astype(bf16)

    weight_grad = outer(
        "weight_grad_1", 0, depths, build_1,
        [rows_1_all, u_all, prev_all, through_1, scale_2, weight_1],
        d_gate_1, d_up_1, act_1, width, parts, weight_grad, after=(d_rows_blocks,),
    )

    def last_grad(where, d_mixed_2, prev, scale, through, unit_1, unit_e1, unit_e2, own_facts, gain, got, *terms):
        d_rows = unfolded(sum(got[z].astype(f32) for z in range(groups)), parts)
        gain_1, gain_2 = (piece_of(gain[k, 0:1], where[0], seqs, 0) for k in range(2))
        scale, through = (own_rows(value, where[1], groups) for value in (scale, through))
        live = own_facts[:, 2:3]
        prev = prev.astype(f32)
        grad_1 = (d_mixed_2 * gain_2 - through * prev) * scale
        d_mixed_1 = grad_1 + d_rows
        kept_1, kept_2 = d_mixed_1 * live, d_mixed_2 * live
        sums = [
            jnp.sum(a * b, axis=0, keepdims=True)
            for a, b in ((kept_1, unit_1), (kept_1, unit_e1), (kept_2, prev * scale), (kept_2, unit_e2))
        ]
        sums = jnp.concatenate(sums, 0) + sum(terms)
        cut = jnp.stack([sums[:, z * share : (z + 1) * share] for z in range(groups)])
        return [cut] + blocks_of(d_mixed_1 * gain_1, where[0], seqs)

    sums, *last_parts = call(
        "last_grad", last_grad,
        [((groups, 2 * depths, share), f32)] + [((slots, width), bf16)] * seqs,
        (where,), d_mixed_2, prev_own, scale_2, through_1, unit_1, unit_e1, unit_e2,
        own_facts, norm_gain, d_rows_got, *terms_got,
    )
    last_got = trade_seq(last_parts, -1)
    gain_grad = jnp.sum(swap_dp(sums), 0)

    def finish(where, token, count, dense_a, dense_b, asked_rows, grad_2, *got):
        part = in_order([g.astype(f32) for g in got], where[0], 1)
        asked_rows = asked_rows.astype(f32)
        scale = inv_rms(asked_rows)
        unit = asked_rows * scale
        grad_1 = (part - unit * jnp.mean(part * unit, axis=-1, keepdims=True)) * scale
        grad_1, grad_2 = grad_1.astype(bf16).astype(f32), grad_2.astype(f32)
        dense = jnp.concatenate([dense_a, dense_b], 0).astype(f32)
        here = iota((tokens, 1), 0)
        for k, grad in ((1, grad_2), (0, grad_1)):
            for c in range(slots):
                chosen = (here == token[0, 0, k, c]) & (c < count[0, 0, k, 0])
                dense = jnp.where(chosen, grad[c : c + 1], dense)
        return [dense]

    (hidden_grad,) = call(
        "finish", finish, [((tokens, features), bf16)],
        (where, asked_token, asked_count), dense_a, dense_b, asked_rows, grad_2, *last_got, limit=24,
    )
    return (
        hidden_grad[None, None],
        weight_grad,
        gain_grad.reshape(1, depths, 2, share),
    )


def solution(mesh):
    return jax.shard_map(
        local,
        mesh=mesh,
        in_specs=(
            P("section", "dp", "seq", None),
            P("section", "dp", "seq", None),
            P("section", "dp", "seq", None),
            P("section", "dp", None, "seq"),
            P("section", "dp", None, "seq"),
            P("section", "dp", None, "seq"),
            P(),
            P(None, None, "seq", "dp"),
        ),
        out_specs=(
            P("section", "dp", "seq", None),
            P("section", None, None, "seq", "dp"),
            P("section", None, None, ("seq", "dp")),
        ),
        check_vma=False,
    )
```

```python
import jax
import jax.numpy as jnp
from jax import lax
from jax.experimental import pallas as pl
from jax.experimental.pallas import tpu as pltpu
from jax.sharding import PartitionSpec as P

eps_norm = 1e-06
lanes = 128
f32 = jnp.float32
bf16 = jnp.bfloat16
vmem = pl.BlockSpec(memory_space=pltpu.VMEM)
smem = pl.BlockSpec(memory_space=pltpu.SMEM)
anywhere = pl.BlockSpec(memory_space=pl.ANY)


def ring(value, axis, steps):
    count = lax.axis_size(axis)
    return lax.ppermute(value, axis, [(i, (i + steps) % count) for i in range(count)])


def from_after(array, axis, by):
    size = lax.axis_size(axis)
    return lax.ppermute(array, axis, [(i, i - by) for i in range(by, size)])


def hop(value, section_step, seq_step):
    sections, seqs = lax.axis_size("section"), lax.axis_size("seq")
    pairs = [
        (c * seqs + s, (c + section_step) % sections * seqs + (s + seq_step) % seqs)
        for c in range(sections)
        for s in range(seqs)
    ]
    return lax.ppermute(value, ("section", "seq"), pairs)


def trade_seq(pieces, section_step=0):
    if section_step == 0:
        return [pieces[0]] + [ring(pieces[o], "seq", o) for o in range(1, len(pieces))]
    return [hop(piece, section_step, o) for o, piece in enumerate(pieces)]


def gather_dp(block):
    return [block] + [ring(block, "dp", i) for i in range(1, lax.axis_size("dp"))]


def return_dp(blocks):
    return [blocks[0]] + [ring(blocks[i], "dp", -i) for i in range(1, len(blocks))]


def pair_seq(own, send):
    if lax.axis_size("seq") == 2:
        return own, ring(send, "seq", 1)
    return lax.psum(own, "seq"), jnp.zeros_like(send)


def inv_rms(value):
    return lax.rsqrt(jnp.mean(value * value, axis=-1, keepdims=True) + eps_norm)


def iota(shape, dim):
    return lax.broadcasted_iota(jnp.int32, shape, dim)


def token_column(token, depth):
    capacity = token.shape[3]
    out = jnp.full((capacity, 1), token[0, 0, depth, 0], jnp.int32)
    for c in range(1, capacity):
        out = jnp.where(iota((capacity, 1), 0) == c, token[0, 0, depth, c], out)
    return out


def gate_column(gate, depth):
    capacity = gate.shape[3]
    out = jnp.full((capacity, 1), gate[0, 0, depth, 0], f32)
    for c in range(1, capacity):
        out = jnp.where(iota((capacity, 1), 0) == c, gate[0, 0, depth, c], out)
    return out


def live_column(count, depth, capacity):
    return (iota((capacity, 1), 0) < count[0, 0, depth, 0]).astype(f32)


def met_column(token, count):
    capacity = token.shape[3]
    second = token_column(token, 1)
    out = jnp.zeros((capacity, 1), f32)
    for c in range(capacity):
        out += ((second == token[0, 0, 0, c]) & (c < count[0, 0, 0, 0])).astype(f32)
    return jnp.minimum(out, 1.0)


def pick(column, table):
    hot = (column == iota((column.shape[0], table.shape[0]), 1)).astype(bf16)
    return jnp.dot(hot, table, preferred_element_type=f32)


def pick_ahead(column, table, after):
    out = pick(column, table)
    for k in range(after.shape[0]):
        row = after[k : k + 1].astype(f32)
        out += jnp.where(column == table.shape[0] + k, row, 0.0)
    return out


def thirds(column):
    high = column.astype(bf16).astype(f32)
    mid = (column - high).astype(bf16).astype(f32)
    return [high, mid, column - high - mid]


def in_lanes(columns):
    lane = iota((columns[0].shape[0], lanes), 1)
    out = jnp.zeros(lane.shape, f32)
    for k, column in enumerate(columns):
        out = jnp.where(lane == k, column, out)
    return out


def coded(column):
    return in_lanes(thirds(column))


def decoded(block, first=0):
    lane = iota(block.shape, 1)
    inside = (lane >= first) & (lane < first + 3)
    return jnp.sum(jnp.where(inside, block.astype(f32), 0.0), axis=1, keepdims=True)


def piece_of(value, place, count, step):
    width = value.shape[-1] // count
    want = lax.rem(place + step, count)
    out = value[:, :width]
    for p in range(1, count):
        out = jnp.where(want == p, value[:, p * width : (p + 1) * width], out)
    return out


def pieces_of(value, place, count):
    return [piece_of(value, place, count, o) for o in range(count)]


def blocks_of(value, place, count):
    size = value.shape[0] // count
    out = []
    for o in range(count):
        block = value[:size]
        for j in range(1, count):
            want = lax.rem(place + o, count) == j
            block = jnp.where(want, value[j * size : (j + 1) * size], block)
        out.append(block)
    return out


def in_order(got, place, axis):
    count = len(got)
    out = []
    for j in range(count):
        block = got[0]
        for o in range(1, count):
            block = jnp.where(lax.rem(place - o + count, count) == j, got[o], block)
        out.append(block)
    return jnp.concatenate(out, axis)


def as_row(column):
    size = column.shape[0]
    here = iota((size, size), 0) == iota((size, size), 1)
    return jnp.sum(jnp.where(here, column, 0.0), axis=0, keepdims=True)


def folds(rows, width):
    for count in (1, 2, 4, 8):
        if rows * count % 16 == 0 and width % (count * lanes) == 0:
            return count
    return 1


def folded(value, count):
    step = value.shape[1] // count
    return jnp.concatenate([value[:, g * step : (g + 1) * step] for g in range(count)], 0)


def unfolded(value, count):
    rows = value.shape[0] // count
    return jnp.concatenate([value[g * rows : (g + 1) * rows] for g in range(count)], 1)


def column_part(blocks, rows, g):
    return jnp.concatenate(
        [block[g * rows : (g + 1) * rows].astype(f32) for block in blocks], 0
    ).astype(bf16)


def summed(got, parts):
    return unfolded(sum(g.astype(f32) for g in got), parts)


def chunk_of(width):
    for step in (1024, 896, 512, 256, 128):
        if width % step == 0:
            return step
    return width


def call(name, fn, outs, small, *args, after=(), flops=0, limit=12):
    shapes = [jax.ShapeDtypeStruct(shape, kind) for shape, kind in outs]
    n_small, n_args, n_after = len(small), len(args), len(after)

    def body(*refs):
        values = list(refs[:n_small]) + [r[...] for r in refs[n_small : n_small + n_args]]
        for ref, value in zip(refs[n_small + n_args + n_after :], fn(*values)):
            ref[...] = value.astype(ref.dtype)

    size = sum(a.size * a.dtype.itemsize for a in list(args) + shapes)
    return pl.pallas_call(
        body,
        name=name,
        out_shape=shapes,
        in_specs=[smem] * n_small + [vmem] * n_args + [anywhere] * n_after,
        out_specs=[vmem] * len(shapes),
        compiler_params=pltpu.CompilerParams(vmem_limit_bytes=limit << 20),
        cost_estimate=pl.CostEstimate(flops=flops, bytes_accessed=size, transcendentals=0),
    )(*small, *args, *after)


def fetch(weight_ref, depth, kinds, buffer, sems, parts):
    step = weight_ref.shape[2] // parts
    copies = []
    for g in range(parts):
        row = []
        for k, kind in enumerate(kinds):
            copy = pltpu.make_async_copy(
                weight_ref.at[depth, kind, pl.ds(g * step, step)],
                buffer.at[g, k],
                sems.at[g, k],
            )
            copy.start()
            row.append(copy)
        copies.append(row)
    return copies


def fetched(weight, kinds, parts):
    hidden = weight.shape[3]
    return [
        pltpu.VMEM((parts, len(kinds), weight.shape[2] // parts, hidden), bf16),
        pltpu.SemaphoreType.DMA((parts, len(kinds))),
    ]


def project(name, blocks, weight, depth, kinds, parts, select=None, gain=None, mates=None, after=()):
    groups = len(blocks)
    rows = blocks[0].shape[0] // parts
    width, hidden = weight.shape[2:]
    step = width // parts
    total, many = rows * groups, len(kinds) * hidden
    marked = select is not None or mates is not None
    extra = lanes if marked else 0

    def body(*refs):
        refs = list(refs)
        where_ref = refs.pop(0) if select is not None else None
        x_refs, w_ref, refs = refs[:groups], refs[groups], refs[groups + 1 :]
        if select is not None:
            select_ref, gain_ref = refs.pop(0), refs.pop(0)
        if mates is not None:
            mate_refs, refs = refs[:groups], refs[groups:]
        refs = refs[len(after) :]
        own_ref, send_ref = refs.pop(0), refs.pop(0)
        kept_ref = refs.pop(0) if select is not None else None
        buffer, sems = refs
        copies = fetch(w_ref, depth, kinds, buffer, sems, parts)
        x_all = [r[...] for r in x_refs]
        mate_all = [r[...] for r in mate_refs] if mates is not None else x_all
        if select is not None:
            gain_all = piece_of(gain_ref[1, 0:1, :], where_ref[0], gain.shape[2] // width, 0)
        sums = [jnp.zeros((total, hidden), f32) for _ in kinds]
        mark = jnp.zeros((total, 1), f32)
        for g in range(parts):
            x = column_part(x_all, rows, g)[:, :step]
            if marked:
                mate = x if mates is None else column_part(mate_all, rows, g)
                mark += jnp.sum(x.astype(f32) * mate.astype(f32), axis=1, keepdims=True)
            if select is not None:
                chosen = jnp.dot(select_ref[...], x, preferred_element_type=f32)
                x = (chosen * gain_all[:, g * step : (g + 1) * step]).astype(bf16)
                kept_ref[:, g * step : (g + 1) * step] = x
            for k in range(len(kinds)):
                copies[g][k].wait()
                sums[k] += jnp.dot(x, buffer[g, k], preferred_element_type=f32)
        for k in range(len(kinds)):
            own_ref[:, k * hidden : (k + 1) * hidden] = sums[k]
            send_ref[:, k * hidden : (k + 1) * hidden] = sums[k].astype(bf16)
        if marked:
            own_ref[:, many:] = in_lanes([mark])
            send_ref[:, many:] = coded(mark).astype(bf16)

    args = list(blocks) + [pltpu.with_memory_space_constraint(weight, pltpu.HBM)]
    specs = [vmem] * groups + [anywhere]
    outs = [
        jax.ShapeDtypeStruct((total, many + extra), f32),
        jax.ShapeDtypeStruct((total, many + extra), bf16),
    ]
    if select is not None:
        where, table = select
        args, specs = [where] + args + [table, gain], [smem] + specs + [vmem, vmem]
        outs.append(jax.ShapeDtypeStruct((total, width), bf16))
    if mates is not None:
        args, specs = args + list(mates), specs + [vmem] * groups
    return pl.pallas_call(
        body,
        name=name,
        in_specs=specs + [anywhere] * len(after),
        out_specs=[vmem] * len(outs),
        out_shape=outs,
        scratch_shapes=fetched(weight, kinds, parts),
        compiler_params=pltpu.CompilerParams(vmem_limit_bytes=16 << 20),
        cost_estimate=pl.CostEstimate(
            flops=2 * total * width * many, bytes_accessed=2 * width * many, transcendentals=0
        ),
    )(*args, *after)


def expand(name, prepare, args, saved, weight, depth, kinds, groups, parts, after=()):
    width, hidden = weight.shape[2:]
    total = saved[0][0][0]
    rows, step = total // groups, width // parts
    count, kept = len(args), len(saved)

    def body(*refs):
        in_refs, w_ref = refs[:count], refs[count]
        refs = refs[count + 1 + len(after) :]
        saved_refs, out_refs, (buffer, sems) = refs[:kept], refs[kept:-2], refs[-2:]
        copies = fetch(w_ref, depth, kinds, buffer, sems, parts)
        for ref, value in zip(saved_refs, prepare(*[r[...] for r in in_refs])):
            ref[...] = value.astype(ref.dtype)
        out = []
        for g in range(parts):
            part = jnp.zeros((total, step), f32)
            for k in range(len(kinds)):
                copies[g][k].wait()
                part += lax.dot_general(
                    saved_refs[k][...], buffer[g, k], (((1,), (1,)), ((), ())),
                    preferred_element_type=f32,
                )
            out.append(part)
        for z in range(groups):
            block = jnp.concatenate([part[z * rows : (z + 1) * rows] for part in out], 0)
            out_refs[z][...] = block.astype(bf16)

    results = pl.pallas_call(
        body,
        name=name,
        in_specs=[vmem] * count + [anywhere] * (1 + len(after)),
        out_specs=[vmem] * (kept + groups),
        out_shape=[jax.ShapeDtypeStruct(shape, kind) for shape, kind in saved]
        + [jax.ShapeDtypeStruct((rows * parts, step), bf16)] * groups,
        scratch_shapes=fetched(weight, kinds, parts),
        compiler_params=pltpu.CompilerParams(vmem_limit_bytes=16 << 20),
        cost_estimate=pl.CostEstimate(
            flops=2 * total * width * hidden * len(kinds),
            bytes_accessed=2 * width * hidden * len(kinds),
            transcendentals=0,
        ),
    )(*args, pltpu.with_memory_space_constraint(weight, pltpu.HBM), *after)
    return results[:kept], results[kept:]


def outer(name, depth, depths, build, args, d_gate, d_up, act, width, parts, before, after=()):
    total, hidden = act.shape
    step = width // parts
    count = len(args)
    earlier = [] if before is None else [pltpu.with_memory_space_constraint(before, pltpu.HBM)]

    def contract(left, right):
        return lax.dot_general(left, right, (((0,), (0,)), ((), ())), preferred_element_type=f32)

    def body(*refs):
        values = [r[...] for r in refs[:count]]
        gate_ref, up_ref, act_ref = refs[count : count + 3]
        out_ref, tick_ref, buffer, sems = refs[-4:]
        tick_ref[...] = jnp.zeros_like(tick_ref)
        copies = []
        for g in range(parts):
            rows, dout = build(values, g)
            pairs = ((rows, gate_ref), (rows, up_ref), (dout, act_ref))
            for k, (left, right_ref) in enumerate(pairs):
                buffer[g, k] = contract(left, right_ref[...]).astype(bf16)
                copy = pltpu.make_async_copy(
                    buffer.at[g, k],
                    out_ref.at[0, depth, k, pl.ds(g * step, step)],
                    sems.at[g, k],
                )
                copy.start()
                copies.append(copy)
        for copy in copies:
            copy.wait()

    return pl.pallas_call(
        body,
        name=name,
        in_specs=[vmem] * (count + 3) + [anywhere] * (len(earlier) + len(after)),
        out_specs=[anywhere, vmem],
        out_shape=[
            jax.ShapeDtypeStruct((1, depths, 3, width, hidden), bf16),
            jax.ShapeDtypeStruct((8, lanes), f32),
        ],
        input_output_aliases={} if before is None else {count + 3: 0},
        scratch_shapes=[
            pltpu.VMEM((parts, 3, step, hidden), bf16),
            pltpu.SemaphoreType.DMA((parts, 3)),
        ],
        compiler_params=pltpu.CompilerParams(vmem_limit_bytes=24 << 20),
        cost_estimate=pl.CostEstimate(
            flops=6 * total * width * hidden, bytes_accessed=6 * width * hidden, transcendentals=0
        ),
    )(*args, d_gate, d_up, act, *earlier, *after)


def backward_rows(hidden, ahead_1, ahead_2, d_mixed_2, keep, gain):
    scale_1 = inv_rms(hidden)
    unit_1 = hidden * scale_1
    unit_e1 = ahead_1 * inv_rms(ahead_1)
    unit_e2 = ahead_2 * inv_rms(ahead_2)
    mixed = (unit_1 * gain[0, 0:1] + unit_e1 * gain[0, 1:2]).astype(bf16).astype(f32)
    scale_2 = inv_rms(mixed)
    unit_2 = mixed * scale_2
    u = d_mixed_2 * gain[1, 0:1]
    grad_1 = (u - unit_2 * jnp.mean(u * unit_2, axis=-1, keepdims=True)) * scale_2
    v = grad_1 * gain[0, 0:1]
    grad_0 = (v - unit_1 * jnp.mean(v * unit_1, axis=-1, keepdims=True)) * scale_1
    kept_1, kept_2 = grad_1 * keep, d_mixed_2 * keep
    terms = [
        jnp.sum(a * b, axis=0, keepdims=True)
        for a, b in ((kept_1, unit_1), (kept_1, unit_e1), (kept_2, unit_2), (kept_2, unit_e2))
    ]
    return grad_0.astype(bf16), jnp.concatenate(terms, 0)


def dense_rows(name, token, count, hidden, embed, next_rows, cotangent, gain, before, half, halves, after=()):
    tokens, width = hidden.shape
    step = 16
    steps = tokens // step // halves
    first, last = half * steps, tokens // step - 1
    capacity = token.shape[3]
    earlier = [] if before is None else [before]

    def body(token_ref, count_ref, hidden_ref, now_ref, next_ref, after_ref, cot_ref, gain_ref, *refs):
        out_ref, terms_ref = refs[-2:]
        block = first + pl.program_id(0)

        @pl.when(pl.program_id(0) == 0)
        def _():
            terms_ref[...] = refs[0][...] if earlier else jnp.zeros_like(terms_ref)

        here = iota((step, 1), 0) + block * step
        keep = jnp.ones((step, 1), f32)
        for k in range(2):
            for c in range(capacity):
                out = (here == token_ref[0, 0, k, c]) & (c < count_ref[0, 0, k, 0])
                keep = jnp.where(out, 0.0, keep)
        follow = jnp.where(
            block == last,
            jnp.concatenate([after_ref[...].astype(f32)] * (8 // after_ref.shape[0]), 0),
            next_ref[...].astype(f32)[:8],
        )
        both = jnp.concatenate([now_ref[...].astype(f32), follow], 0)
        grad, terms = backward_rows(
            hidden_ref[...].astype(f32),
            both[1 : step + 1],
            both[2 : step + 2],
            cot_ref[...].astype(f32),
            keep,
            gain_ref[...],
        )
        out_ref[...] = grad
        terms_ref[...] += terms

    rows = pl.BlockSpec((step, width), lambda i: (first + i, 0))
    terms = pl.BlockSpec((4, width), lambda i: (0, 0))
    return pl.pallas_call(
        body,
        name=name,
        grid=(steps,),
        in_specs=[
            smem,
            smem,
            rows,
            rows,
            pl.BlockSpec((step, width), lambda i: (jnp.minimum(first + i + 1, last), 0)),
            pl.BlockSpec(next_rows.shape, lambda i: (0, 0)),
            rows,
            pl.BlockSpec(gain.shape, lambda i: (0, 0, 0)),
        ]
        + [terms] * len(earlier)
        + [anywhere] * len(after),
        out_specs=[pl.BlockSpec((step, width), lambda i: (i, 0)), terms],
        out_shape=[
            jax.ShapeDtypeStruct((tokens // halves, width), bf16),
            jax.ShapeDtypeStruct((4, width), f32),
        ],
        compiler_params=pltpu.CompilerParams(vmem_limit_bytes=20 << 20),
        cost_estimate=pl.CostEstimate(
            flops=60 * tokens * width // halves,
            bytes_accessed=10 * tokens * width // halves,
            transcendentals=0,
        ),
    )(token, count, hidden, embed, embed, next_rows, cotangent, gain, *earlier, *after)


def local(
    main_hidden, embedded, cotangent, slot_token, slot_count, route_gate, norm_gain, expert_weight
):
    depths, _, features = norm_gain.shape
    tokens = main_hidden.shape[2]
    slots = slot_token.shape[3]
    seqs, groups = lax.axis_size("seq"), lax.axis_size("dp")
    rows = seqs * slots
    total = groups * rows
    width = features // seqs
    share = width // groups
    hidden_units = expert_weight.shape[3]
    parts = folds(rows, width)
    where = jnp.stack([lax.axis_index("seq"), lax.axis_index("dp")]).astype(jnp.int32)
    source, embed, cot = main_hidden[0, 0], embedded[0, 0], cotangent[0, 0]
    facts = (slot_token, slot_count)
    packed = ((rows * parts, width // parts), bf16)
    part_rows = ((rows, width), f32)

    def payload(value):
        return folded(value, parts)

    asked_token = ring(slot_token, "section", -1)
    next_rows = from_after(embed[:depths], "seq", 1)

    def cot_rows(where, token, count, gate, cot):
        first, second = token_column(token, 0), token_column(token, 1)
        live_1, live_2 = (live_column(count, k, slots) for k in range(2))
        weight_1, weight_2 = gate_column(gate, 0) * live_1, gate_column(gate, 1) * live_2
        facts = in_lanes(
            [first.astype(f32), second.astype(f32), live_1, live_2]
            + thirds(weight_1)
            + thirds(weight_2)
        )
        cot_1, dout = pick(first, cot), pick(second, cot) * weight_2
        return [
            jnp.concatenate(
                [
                    jnp.concatenate([piece_of(cot_1, where[0], seqs, o), facts], 1),
                    jnp.concatenate([piece_of(dout, where[0], seqs, o), facts], 1),
                ],
                0,
            )
            for o in range(seqs)
        ]

    cot_sent = call(
        "cot_rows", cot_rows, [((2 * slots, width + lanes), bf16)] * seqs,
        (where, slot_token, slot_count, route_gate), cot,
    )
    cot_got = trade_seq(cot_sent)

    def cot_parts(where, *got):
        parts_1, parts_2 = (
            in_order([g[k * slots : (k + 1) * slots].astype(f32) for g in got], where[0], 0)
            for k in range(2)
        )
        facts = parts_1[:, width:]
        out = folded(parts_2[:, :width], parts)
        none = jnp.zeros(((parts - 1) * rows, lanes), f32)
        tail = facts if parts == 1 else jnp.concatenate([facts, none], 0)
        return parts_1[:, :width], jnp.concatenate([out, tail], 1), facts

    cot_1, dout_2, own_facts = call(
        "cot_parts", cot_parts,
        [part_rows, ((rows * parts, width // parts + lanes), bf16), ((rows, lanes), f32)],
        (where,), *cot_got,
    )
    dout_2_all = gather_dp(dout_2)

    def first_rows(where, asked, token, source, table, after):
        first = pick(token_column(asked, 0), source)
        second = pick(token_column(asked, 1), source)
        scale = coded(inv_rms(first))
        sent = [jnp.concatenate([p, scale], 1) for p in pieces_of(first, where[0], seqs)]
        first_own = token_column(token, 0)
        out = []
        for k in range(2):
            ahead = pick_ahead(first_own + k + 1, table, after)
            scale = coded(inv_rms(ahead))
            out.append([jnp.concatenate([p, scale], 1) for p in pieces_of(ahead, where[0], seqs)])
        return sent + [jnp.concatenate(both, 0) for both in zip(*out)] + [first, second]

    *sent, asked_rows, second_rows = call(
        "first_rows", first_rows,
        [((slots, width + lanes), bf16)] * seqs
        + [((2 * slots, width + lanes), bf16)] * seqs
        + [((slots, features), bf16)] * 2,
        (where, asked_token, slot_token), source, embed, next_rows, after=(cot_sent[0],),
    )
    start_got = trade_seq(sent[:seqs], 1)
    ahead_got = trade_seq(sent[seqs:])
    start_2 = ring(second_rows, "section", 1)

    def first_mixed(where, own_facts, gain, *got):
        ahead_got, start_got = got[:seqs], got[seqs:]
        ahead_1, ahead_2 = (
            in_order([g[k * slots : (k + 1) * slots].astype(f32) for g in ahead_got], where[0], 0)
            for k in range(2)
        )
        start = in_order([g.astype(f32) for g in start_got], where[0], 0)
        unit, unit_1, unit_2 = (
            block[:, :width] * decoded(block[:, width:]) for block in (start, ahead_1, ahead_2)
        )
        gain_h, gain_e = (piece_of(gain[0, k : k + 1], where[0], seqs, 0) for k in range(2))
        mixed = (unit * gain_h + unit_1 * gain_e).astype(bf16).astype(f32)
        return payload(mixed * own_facts[:, 2:3]), unit, unit_1, unit_2

    rows_1, unit_1, unit_e1, unit_e2 = call(
        "first_mixed", first_mixed, [packed] + [part_rows] * 3,
        (where,), own_facts, norm_gain, *ahead_got, *start_got,
    )
    rows_1_all = gather_dp(rows_1)

    def second_base(where, token, count, start, table, after, gain):
        second = token_column(token, 1)
        start = start.astype(f32)
        ahead_1 = pick_ahead(second + 1, table, after)
        ahead_2 = pick_ahead(second + 2, table, after)
        unit = start * inv_rms(start)
        mixed = unit * gain[0, 0:1] + ahead_1 * inv_rms(ahead_1) * gain[0, 1:2]
        mixed = mixed.astype(bf16).astype(f32)
        own = mixed * inv_rms(mixed) * gain[1, 0:1] * (1.0 - met_column(token, count))
        out = (own + ahead_2 * inv_rms(ahead_2) * gain[1, 1:2]) * live_column(count, 1, slots)
        return pieces_of(out, where[0], seqs) + [ahead_1, ahead_2]

    *base_parts, ahead_21, ahead_22 = call(
        "second_base", second_base,
        [((slots, width), bf16)] * seqs + [((slots, features), bf16)] * 2,
        (where, *facts), start_2, embed, next_rows, norm_gain, after=(rows_1,),
    )
    base_got = trade_seq(base_parts)

    first_own, first_send = project(
        "gate_up_1", rows_1_all, expert_weight, 0, (0, 1), parts, after=(ahead_21,)
    )
    first = pair_seq(first_own, first_send)

    def base_order(where, *got):
        return [payload(in_order([g.astype(f32) for g in got], where[0], 0))]

    (base_2,) = call("base_order", base_order, [packed], (where,), *base_got, after=(first_send,))
    base_2_all = gather_dp(base_2)

    def forward_1(own, other):
        both = own + other.astype(f32)
        gate, up = both[:, :hidden_units], both[:, hidden_units:]
        return gate * jax.nn.sigmoid(gate) * up, both

    (act_1, both_1), out_blocks = expand(
        "down_1", forward_1, first,
        [((total, hidden_units), bf16), ((total, 2 * hidden_units), f32)],
        expert_weight, 0, (2,), groups, parts, after=(base_2,),
    )
    out_got = return_dp(out_blocks)

    def slot_facts(*blocks):
        facts = jnp.concatenate(
            [block[:rows].astype(f32)[:, width // parts :] for block in blocks], 0
        )
        base = (iota((total, 1), 0) // slots * tokens).astype(f32)
        first, second = facts[:, 0:1] + base, facts[:, 1:2] + base
        live = (facts[:, 3:4] > 0) & (as_row(facts[:, 2:3]) > 0)
        same = ((second == as_row(first)) & live).astype(f32)
        return same, same, same[:rows, :rows], decoded(facts, 4)

    same, same_16, same_own, weight_1 = call(
        "slot_facts", slot_facts,
        [((total, total), f32), ((total, total), bf16), ((rows, rows), f32), ((total, 1), f32)],
        (), *dout_2_all, after=(out_blocks[0],),
    )
    base_own, base_send = project(
        "base_gate_up", base_2_all, expert_weight, 1, (0, 1), parts, after=(same_own,)
    )
    back_own, back_send = project(
        "back_2", dout_2_all, expert_weight, 1, (2,), parts, after=(base_own,)
    )
    base_pair = pair_seq(base_own, base_send)
    back_pair = pair_seq(back_own, back_send)

    def second_prev(own_facts, rows_1, *got):
        value = unfolded(rows_1.astype(f32), parts) + summed(got, parts) * decoded(own_facts, 4)
        return payload(value), value.astype(bf16)

    prev, prev_own = call(
        "second_prev", second_prev, [packed, ((rows, width), bf16)],
        (), own_facts, rows_1, *out_got, after=(back_own,),
    )
    prev_all = gather_dp(prev)

    hidden, _ = lax.optimization_barrier((source, start_2))
    hidden = ring(hidden, "section", 1)
    dense_a, terms_a = dense_rows(
        "dense_a", *facts, hidden, embed, next_rows, cot, norm_gain, None, 0, 2, after=(prev,)
    )
    dense_a = ring(dense_a, "section", -1)

    mixed_own, mixed_send, chosen = project(
        "gate_up_2", prev_all, expert_weight, 1, (0, 1), parts,
        select=(where, same_16), gain=norm_gain, after=(terms_a,),
    )
    second = pair_seq(mixed_own, mixed_send)
    prev_w_own, prev_w_send = project(
        "prev_down", prev_all, expert_weight, 0, (2,), parts, after=(mixed_send,)
    )
    prev_pair = pair_seq(prev_w_own, prev_w_send)

    def gates_back(gate, up, d_act):
        sig = jax.nn.sigmoid(gate)
        d_gate = d_act * up * sig * (1.0 + gate * (1.0 - sig))
        return d_gate, d_act * gate * sig

    def backward_2(own, other, base_own, base_other, back_own, back_other, same):
        many = 2 * hidden_units
        square = own[:, many : many + 1] + decoded(other[:, many:])
        scale = lax.rsqrt(square / features + eps_norm)
        row = jnp.sum(same * as_row(scale), axis=1, keepdims=True)
        both = (own[:, :many] + other[:, :many].astype(f32)) * row
        both = both + base_own + base_other.astype(f32)
        gate, up = both[:, :hidden_units], both[:, hidden_units:]
        d_gate, d_up = gates_back(gate, up, back_own + back_other.astype(f32))
        return d_gate, d_up, gate * jax.nn.sigmoid(gate) * up, scale, row

    units = ((total, hidden_units), bf16)
    (d_gate_2, d_up_2, act_2, scale_2, row_2), d_rows_blocks = expand(
        "back_rows_2", backward_2,
        second + base_pair + back_pair + (same,),
        [units, units, units, ((total, 1), f32), ((total, 1), f32)],
        expert_weight, 1, (0, 1), groups, parts, after=(prev_w_own,),
    )
    d_rows_got = return_dp(d_rows_blocks)
    dense_b, dense_terms = dense_rows(
        "dense_b", *facts, hidden, embed, next_rows, cot, norm_gain, terms_a, 1, 2, after=(d_rows_blocks[0],)
    )
    dense_b = ring(dense_b, "section", -1)

    def first_grad(where, cot, same, gain, *got):
        d_rows = summed(got, parts)
        added = lax.dot_general(
            same, d_rows, (((0,), (0,)), ((), ())),
            precision=lax.Precision.HIGHEST, preferred_element_type=f32,
        )
        d_mixed = cot + added
        u = d_mixed * piece_of(gain[1, 0:1], where[0], seqs, 0)
        return [payload(u), d_mixed] + blocks_of(d_rows, where[0], seqs)

    u, d_mixed_2, *d_rows_back = call(
        "first_grad", first_grad, [packed, part_rows] + [((slots, width), bf16)] * seqs,
        (where,), cot_1, same_own, norm_gain, *d_rows_got, after=(dense_terms,),
    )
    u_all = gather_dp(u)
    back_got = trade_seq(d_rows_back)

    def build_2(values, g):
        chosen, row, base, dout = values[0], values[1], values[2 : 2 + groups], values[2 + groups :]
        step = width // parts
        first = chosen[:, g * step : (g + 1) * step].astype(f32) * row
        first = first + column_part(base, rows, g).astype(f32)
        return first.astype(bf16), column_part(dout, rows, g)[:, :step]

    weight_grad, tick_2 = outer(
        "weight_grad_2", 1, depths, build_2, [chosen, row_2] + base_2_all + dout_2_all,
        d_gate_2, d_up_2, act_2, width, parts, None, after=(u,),
    )

    back_1_own, back_1_send = project(
        "back_1", u_all, expert_weight, 0, (2,), parts, mates=prev_all, after=(tick_2,)
    )
    back_1 = pair_seq(back_1_own, back_1_send)

    def second_grad(where, token, count, start, ahead_1, ahead_2, cot, gain, terms, *got):
        d_rows = in_order([g.astype(f32) for g in got], where[0], 1)
        keep = live_column(count, 1, slots) * (1.0 - met_column(token, count))
        grad, more = backward_rows(
            start.astype(f32), ahead_1.astype(f32), ahead_2.astype(f32),
            pick(token_column(token, 1), cot) + d_rows, keep, gain,
        )
        return [grad] + pieces_of(terms + more, where[0], seqs)

    grad_2, *terms_parts = call(
        "second_grad", second_grad,
        [((slots, features), bf16)] + [((2 * depths, width), f32)] * seqs,
        (where, *facts), start_2, ahead_21, ahead_22, cot, norm_gain, dense_terms, *back_got,
        after=(back_1_send,),
    )
    grad_2 = ring(grad_2, "section", -1)
    asked_count = ring(slot_count, "section", -1)
    terms_got = trade_seq(terms_parts)

    def backward_1(own, other, prev_own, prev_other, both, scale, weight_1):
        inner = own[:, hidden_units : hidden_units + 1] + decoded(other[:, hidden_units:])
        d_act = own[:, :hidden_units] + other[:, :hidden_units].astype(f32)
        through = scale * scale * inner / features
        d_act = d_act - through * (prev_own + prev_other.astype(f32))
        d_act = d_act * (weight_1 * scale)
        d_gate, d_up = gates_back(both[:, :hidden_units], both[:, hidden_units:], d_act)
        return d_gate, d_up, through

    (d_gate_1, d_up_1, through_1), d_rows_blocks = expand(
        "back_rows_1", backward_1,
        back_1 + prev_pair + (both_1, scale_2, weight_1),
        [units, units, ((total, 1), f32)],
        expert_weight, 0, (0, 1), groups, parts, after=(terms_parts[0],),
    )
    d_rows_got = return_dp(d_rows_blocks)

    def build_1(values, g):
        through, scale, weight = values[:3]
        first, u, prev = (values[3 + k * groups : 3 + (k + 1) * groups] for k in range(3))
        dout = column_part(u, rows, g).astype(f32) - through * column_part(prev, rows, g).astype(f32)
        return column_part(first, rows, g), (dout * (weight * scale)).astype(bf16)

    weight_grad, tick_1 = outer(
        "weight_grad_1", 0, depths, build_1,
        [through_1, scale_2, weight_1] + rows_1_all + u_all + prev_all,
        d_gate_1, d_up_1, act_1, width, parts, weight_grad, after=(d_rows_blocks[0],),
    )

    def last_grad(where, d_mixed_2, prev, scale, through, unit_1, unit_e1, unit_e2, own_facts, gain, *got):
        got, terms = got[:groups], got[groups:]
        d_rows = summed(got, parts)
        gain_1, gain_2 = (piece_of(gain[k, 0:1], where[0], seqs, 0) for k in range(2))
        scale, through = scale[:rows], through[:rows]
        live = own_facts[:, 2:3]
        prev = prev.astype(f32)
        grad_1 = (d_mixed_2 * gain_2 - through * prev) * scale
        d_mixed_1 = grad_1 + d_rows
        kept_1, kept_2 = d_mixed_1 * live, d_mixed_2 * live
        sums = [
            jnp.sum(a * b, axis=0, keepdims=True)
            for a, b in ((kept_1, unit_1), (kept_1, unit_e1), (kept_2, prev * scale), (kept_2, unit_e2))
        ]
        sums = jnp.concatenate(sums, 0) + sum(terms)
        cut = []
        for i in range(groups):
            want = lax.rem(where[1] - i + groups, groups)
            block = sums[:, :share]
            for z in range(1, groups):
                block = jnp.where(want == z, sums[:, z * share : (z + 1) * share], block)
            cut.append(block)
        return cut + blocks_of(d_mixed_1 * gain_1, where[0], seqs)

    last = call(
        "last_grad", last_grad,
        [((2 * depths, share), f32)] * groups + [((slots, width), bf16)] * seqs,
        (where,), d_mixed_2, prev_own, scale_2, through_1, unit_1, unit_e1, unit_e2,
        own_facts, norm_gain, *d_rows_got, *terms_got, after=(tick_1,),
    )
    last_got = trade_seq(last[groups:], -1)
    sums_got = return_dp(last[:groups])

    def finish(where, token, count, dense_a, dense_b, asked_rows, grad_2, *got):
        got, sums = got[:seqs], sum(got[seqs:])
        part = in_order([g.astype(f32) for g in got], where[0], 1)
        asked_rows = asked_rows.astype(f32)
        scale = inv_rms(asked_rows)
        unit = asked_rows * scale
        grad_1 = (part - unit * jnp.mean(part * unit, axis=-1, keepdims=True)) * scale
        grads = jnp.concatenate([grad_1, grad_2.astype(f32)], 0).astype(bf16)
        lane = iota((slots, tokens), 1)
        live_1 = live_column(count, 0, slots)
        live_2 = live_column(count, 1, slots) * (1.0 - met_column(token, count))
        chosen = jnp.concatenate(
            [
                jnp.where(lane == token_column(token, k), live, 0.0)
                for k, live in ((0, live_1), (1, live_2))
            ],
            0,
        ).astype(bf16)
        here = iota((tokens, 1), 0)
        taken = jnp.zeros((tokens, 1), f32)
        for k in range(2):
            for c in range(slots):
                match = (here == token[0, 0, k, c]) & (c < count[0, 0, k, 0])
                taken = jnp.where(match, 1.0, taken)
        out = []
        step = chunk_of(features)
        for at in range(0, features, step):
            placed = lax.dot_general(
                chosen, grads[:, at : at + step], (((0,), (0,)), ((), ())),
                preferred_element_type=f32,
            )
            dense = jnp.concatenate([d[:, at : at + step] for d in (dense_a, dense_b)], 0)
            out.append(jnp.where(taken > 0, placed, dense.astype(f32)).astype(bf16))
        return [jnp.concatenate(out, 1), jnp.stack([sums[2 * k : 2 * k + 2] for k in range(depths)])[None]]

    hidden_grad, gain_grad = call(
        "finish", finish, [((tokens, features), bf16), ((1, depths, 2, share), f32)],
        (where, asked_token, asked_count),
        dense_a, dense_b, asked_rows, grad_2, *last_got, *sums_got, limit=20,
    )
    return (
        hidden_grad[None, None],
        weight_grad,
        gain_grad,
    )


def solution(mesh):
    return jax.shard_map(
        local,
        mesh=mesh,
        in_specs=(
            P("section", "dp", "seq", None),
            P("section", "dp", "seq", None),
            P("section", "dp", "seq", None),
            P("section", "dp", None, "seq"),
            P("section", "dp", None, "seq"),
            P("section", "dp", None, "seq"),
            P(),
            P(None, None, "seq", "dp"),
        ),
        out_specs=(
            P("section", "dp", "seq", None),
            P("section", None, None, "seq", "dp"),
            P("section", None, None, ("seq", "dp")),
        ),
        check_vma=False,
    )
```

```python
import jax
import jax.numpy as jnp
from jax import lax
from jax.experimental import pallas as pl
from jax.experimental.pallas import tpu as pltpu
from jax.sharding import PartitionSpec as P

eps_norm = 1e-06
lanes = 128
f32 = jnp.float32
bf16 = jnp.bfloat16
vmem = pl.BlockSpec(memory_space=pltpu.VMEM)
smem = pl.BlockSpec(memory_space=pltpu.SMEM)
anywhere = pl.BlockSpec(memory_space=pl.ANY)


def ring(value, axis, steps):
    count = lax.axis_size(axis)
    return lax.ppermute(value, axis, [(i, (i + steps) % count) for i in range(count)])


def hop(value, section_step, seq_step):
    sections, seqs = lax.axis_size("section"), lax.axis_size("seq")
    pairs = [
        (c * seqs + s, (c + section_step) % sections * seqs + (s + seq_step) % seqs)
        for c in range(sections)
        for s in range(seqs)
    ]
    return lax.ppermute(value, ("section", "seq"), pairs)


def trade_seq(pieces, section_step=0):
    if section_step == 0:
        return [pieces[0]] + [ring(pieces[o], "seq", o) for o in range(1, len(pieces))]
    return [hop(piece, section_step, o) for o, piece in enumerate(pieces)]


def gather_dp(block):
    return [block] + [ring(block, "dp", i) for i in range(1, lax.axis_size("dp"))]


def return_dp(blocks):
    return [blocks[0]] + [ring(blocks[i], "dp", -i) for i in range(1, len(blocks))]


def pair_seq(own, send):
    if lax.axis_size("seq") == 2:
        return own, ring(send, "seq", 1)
    return lax.psum(own, "seq"), jnp.zeros_like(send)


def inv_rms(value):
    return lax.rsqrt(jnp.mean(value * value, axis=-1, keepdims=True) + eps_norm)


def iota(shape, dim):
    return lax.broadcasted_iota(jnp.int32, shape, dim)


def token_column(token, depth):
    capacity = token.shape[3]
    out = jnp.full((capacity, 1), token[0, 0, depth, 0], jnp.int32)
    for c in range(1, capacity):
        out = jnp.where(iota((capacity, 1), 0) == c, token[0, 0, depth, c], out)
    return out


def gate_column(gate, depth):
    capacity = gate.shape[3]
    out = jnp.full((capacity, 1), gate[0, 0, depth, 0], f32)
    for c in range(1, capacity):
        out = jnp.where(iota((capacity, 1), 0) == c, gate[0, 0, depth, c], out)
    return out


def live_column(count, depth, capacity):
    return (iota((capacity, 1), 0) < count[0, 0, depth, 0]).astype(f32)


def met_column(token, count):
    capacity = token.shape[3]
    second = token_column(token, 1)
    out = jnp.zeros((capacity, 1), f32)
    for c in range(capacity):
        out += ((second == token[0, 0, 0, c]) & (c < count[0, 0, 0, 0])).astype(f32)
    return jnp.minimum(out, 1.0)


def pick(column, table):
    hot = (column == iota((column.shape[0], table.shape[0]), 1)).astype(bf16)
    return jnp.dot(hot, table, preferred_element_type=f32)


def pick_ahead(column, table, after):
    out = pick(column, table)
    for k in range(after.shape[0]):
        row = after[k : k + 1].astype(f32)
        out += jnp.where(column == table.shape[0] + k, row, 0.0)
    return out


def thirds(column):
    high = column.astype(bf16).astype(f32)
    mid = (column - high).astype(bf16).astype(f32)
    return [high, mid, column - high - mid]


def in_lanes(columns):
    lane = iota((columns[0].shape[0], lanes), 1)
    out = jnp.zeros(lane.shape, f32)
    for k, column in enumerate(columns):
        out = jnp.where(lane == k, column, out)
    return out


def coded(column):
    return in_lanes(thirds(column))


def decoded(block, first=0):
    lane = iota(block.shape, 1)
    inside = (lane >= first) & (lane < first + 3)
    return jnp.sum(jnp.where(inside, block.astype(f32), 0.0), axis=1, keepdims=True)


def piece_of(value, place, count, step):
    width = value.shape[-1] // count
    want = lax.rem(place + step, count)
    out = value[:, :width]
    for p in range(1, count):
        out = jnp.where(want == p, value[:, p * width : (p + 1) * width], out)
    return out


def pieces_of(value, place, count):
    return [piece_of(value, place, count, o) for o in range(count)]


def blocks_of(value, place, count):
    size = value.shape[0] // count
    out = []
    for o in range(count):
        block = value[:size]
        for j in range(1, count):
            want = lax.rem(place + o, count) == j
            block = jnp.where(want, value[j * size : (j + 1) * size], block)
        out.append(block)
    return out


def in_order(got, place, axis):
    count = len(got)
    out = []
    for j in range(count):
        block = got[0]
        for o in range(1, count):
            block = jnp.where(lax.rem(place - o + count, count) == j, got[o], block)
        out.append(block)
    return jnp.concatenate(out, axis)


def as_row(column):
    size = column.shape[0]
    here = iota((size, size), 0) == iota((size, size), 1)
    return jnp.sum(jnp.where(here, column, 0.0), axis=0, keepdims=True)


def folds(rows, width):
    for count in (1, 2, 4, 8):
        if rows * count % 16 == 0 and width % (count * lanes) == 0:
            return count
    return 1


def folded(value, count):
    step = value.shape[1] // count
    return jnp.concatenate([value[:, g * step : (g + 1) * step] for g in range(count)], 0)


def unfolded(value, count):
    rows = value.shape[0] // count
    return jnp.concatenate([value[g * rows : (g + 1) * rows] for g in range(count)], 1)


def column_part(blocks, rows, g):
    return jnp.concatenate(
        [block[g * rows : (g + 1) * rows].astype(f32) for block in blocks], 0
    ).astype(bf16)


def summed(got, parts):
    return unfolded(sum(g.astype(f32) for g in got), parts)


def chunk_of(width):
    for step in (1024, 896, 512, 256, 128):
        if width % step == 0:
            return step
    return width


def call(name, fn, outs, small, *args, after=(), flops=0, limit=12):
    shapes = [jax.ShapeDtypeStruct(shape, kind) for shape, kind in outs]
    n_small, n_args, n_after = len(small), len(args), len(after)

    def body(*refs):
        values = list(refs[:n_small]) + [r[...] for r in refs[n_small : n_small + n_args]]
        for ref, value in zip(refs[n_small + n_args + n_after :], fn(*values)):
            ref[...] = value.astype(ref.dtype)

    size = sum(a.size * a.dtype.itemsize for a in list(args) + shapes)
    return pl.pallas_call(
        body,
        name=name,
        out_shape=shapes,
        in_specs=[smem] * n_small + [vmem] * n_args + [anywhere] * n_after,
        out_specs=[vmem] * len(shapes),
        compiler_params=pltpu.CompilerParams(vmem_limit_bytes=limit << 20),
        cost_estimate=pl.CostEstimate(flops=flops, bytes_accessed=size, transcendentals=0),
    )(*small, *args, *after)


def fetch(weight_ref, depth, kinds, buffer, sems, parts):
    step = weight_ref.shape[2] // parts
    copies = []
    for g in range(parts):
        row = []
        for k, kind in enumerate(kinds):
            copy = pltpu.make_async_copy(
                weight_ref.at[depth, kind, pl.ds(g * step, step)],
                buffer.at[g, k],
                sems.at[g, k],
            )
            copy.start()
            row.append(copy)
        copies.append(row)
    return copies


def fetched(weight, kinds, parts):
    hidden = weight.shape[3]
    return [
        pltpu.VMEM((parts, len(kinds), weight.shape[2] // parts, hidden), bf16),
        pltpu.SemaphoreType.DMA((parts, len(kinds))),
    ]


def project(name, blocks, weight, depth, kinds, parts, others=None, select=None, gain=None, mates=None, after=()):
    groups = len(blocks)
    rows = blocks[0].shape[0] // parts
    width, hidden = weight.shape[2:]
    step = width // parts
    other_blocks, other_kinds = others if others is not None else ([], ())
    first_kinds, kinds = kinds, kinds + other_kinds
    total, many = rows * groups, len(kinds) * hidden
    marked = select is not None or mates is not None
    extra = lanes if marked else 0

    def body(*refs):
        refs = list(refs)
        where_ref = refs.pop(0) if select is not None else None
        x_refs, w_ref, refs = refs[:groups], refs[groups], refs[groups + 1 :]
        other_refs, refs = refs[: len(other_blocks)], refs[len(other_blocks) :]
        if select is not None:
            select_ref, gain_ref = refs.pop(0), refs.pop(0)
        if mates is not None:
            mate_refs, refs = refs[:groups], refs[groups:]
        refs = refs[len(after) :]
        own_ref, send_ref = refs.pop(0), refs.pop(0)
        kept_ref = refs.pop(0) if select is not None else None
        buffer, sems = refs
        copies = fetch(w_ref, depth, kinds, buffer, sems, parts)
        x_all = [r[...] for r in x_refs]
        mate_all = [r[...] for r in mate_refs] if mates is not None else x_all
        if select is not None:
            gain_all = piece_of(gain_ref[1, 0:1, :], where_ref[0], gain.shape[2] // width, 0)
        sums = [jnp.zeros((total, hidden), f32) for _ in kinds]
        mark = jnp.zeros((total, 1), f32)
        for g in range(parts):
            x = column_part(x_all, rows, g)
            if marked:
                mate = x if mates is None else column_part(mate_all, rows, g)
                mark += jnp.sum(x.astype(f32) * mate.astype(f32), axis=1, keepdims=True)
            if select is not None:
                chosen = jnp.dot(select_ref[...], x, preferred_element_type=f32)
                x = (chosen * gain_all[:, g * step : (g + 1) * step]).astype(bf16)
                kept_ref[:, g * step : (g + 1) * step] = x
            for k in range(len(kinds)):
                if k == len(first_kinds):
                    x = column_part([r[...] for r in other_refs], rows, g)[:, :step]
                copies[g][k].wait()
                sums[k] += jnp.dot(x, buffer[g, k], preferred_element_type=f32)
        for k in range(len(kinds)):
            own_ref[:, k * hidden : (k + 1) * hidden] = sums[k]
            send_ref[:, k * hidden : (k + 1) * hidden] = sums[k].astype(bf16)
        if marked:
            own_ref[:, many:] = in_lanes([mark])
            send_ref[:, many:] = coded(mark).astype(bf16)

    args = list(blocks) + [pltpu.with_memory_space_constraint(weight, pltpu.HBM)]
    args, specs = args + list(other_blocks), [vmem] * groups + [anywhere] + [vmem] * len(other_blocks)
    outs = [
        jax.ShapeDtypeStruct((total, many + extra), f32),
        jax.ShapeDtypeStruct((total, many + extra), bf16),
    ]
    if select is not None:
        where, table = select
        args, specs = [where] + args + [table, gain], [smem] + specs + [vmem, vmem]
        outs.append(jax.ShapeDtypeStruct((total, width), bf16))
    if mates is not None:
        args, specs = args + list(mates), specs + [vmem] * groups
    return pl.pallas_call(
        body,
        name=name,
        in_specs=specs + [anywhere] * len(after),
        out_specs=[vmem] * len(outs),
        out_shape=outs,
        scratch_shapes=fetched(weight, kinds, parts),
        compiler_params=pltpu.CompilerParams(vmem_limit_bytes=16 << 20),
        cost_estimate=pl.CostEstimate(
            flops=2 * total * width * many, bytes_accessed=2 * width * many, transcendentals=0
        ),
    )(*args, *after)


def expand(name, prepare, args, saved, weight, depth, kinds, groups, parts, after=()):
    width, hidden = weight.shape[2:]
    total = saved[0][0][0]
    rows, step = total // groups, width // parts
    count, kept = len(args), len(saved)

    def body(*refs):
        in_refs, w_ref = refs[:count], refs[count]
        refs = refs[count + 1 + len(after) :]
        saved_refs, out_refs, (buffer, sems) = refs[:kept], refs[kept:-2], refs[-2:]
        copies = fetch(w_ref, depth, kinds, buffer, sems, parts)
        for ref, value in zip(saved_refs, prepare(*[r[...] for r in in_refs])):
            ref[...] = value.astype(ref.dtype)
        out = []
        for g in range(parts):
            part = jnp.zeros((total, step), f32)
            for k in range(len(kinds)):
                copies[g][k].wait()
                part += lax.dot_general(
                    saved_refs[k][...], buffer[g, k], (((1,), (1,)), ((), ())),
                    preferred_element_type=f32,
                )
            out.append(part)
        for z in range(groups):
            block = jnp.concatenate([part[z * rows : (z + 1) * rows] for part in out], 0)
            out_refs[z][...] = block.astype(bf16)

    results = pl.pallas_call(
        body,
        name=name,
        in_specs=[vmem] * count + [anywhere] * (1 + len(after)),
        out_specs=[vmem] * (kept + groups),
        out_shape=[jax.ShapeDtypeStruct(shape, kind) for shape, kind in saved]
        + [jax.ShapeDtypeStruct((rows * parts, step), bf16)] * groups,
        scratch_shapes=fetched(weight, kinds, parts),
        compiler_params=pltpu.CompilerParams(vmem_limit_bytes=16 << 20),
        cost_estimate=pl.CostEstimate(
            flops=2 * total * width * hidden * len(kinds),
            bytes_accessed=2 * width * hidden * len(kinds),
            transcendentals=0,
        ),
    )(*args, pltpu.with_memory_space_constraint(weight, pltpu.HBM), *after)
    return results[:kept], results[kept:]


def outer(name, depth, depths, build, args, d_gate, d_up, act, width, parts, before, after=()):
    total, hidden = act.shape
    step = width // parts
    count = len(args)
    earlier = [] if before is None else [pltpu.with_memory_space_constraint(before, pltpu.HBM)]

    def contract(left, right):
        return lax.dot_general(left, right, (((0,), (0,)), ((), ())), preferred_element_type=f32)

    def body(*refs):
        values = [r[...] for r in refs[:count]]
        gate_ref, up_ref, act_ref = refs[count : count + 3]
        out_ref, tick_ref, buffer, sems = refs[-4:]
        tick_ref[...] = jnp.zeros_like(tick_ref)
        copies = []
        for g in range(parts):
            rows, dout = build(values, g)
            pairs = ((rows, gate_ref), (rows, up_ref), (dout, act_ref))
            for k, (left, right_ref) in enumerate(pairs):
                buffer[g, k] = contract(left, right_ref[...]).astype(bf16)
                copy = pltpu.make_async_copy(
                    buffer.at[g, k],
                    out_ref.at[0, depth, k, pl.ds(g * step, step)],
                    sems.at[g, k],
                )
                copy.start()
                copies.append(copy)
        for copy in copies:
            copy.wait()

    return pl.pallas_call(
        body,
        name=name,
        in_specs=[vmem] * (count + 3) + [anywhere] * (len(earlier) + len(after)),
        out_specs=[anywhere, vmem],
        out_shape=[
            jax.ShapeDtypeStruct((1, depths, 3, width, hidden), bf16),
            jax.ShapeDtypeStruct((8, lanes), f32),
        ],
        input_output_aliases={} if before is None else {count + 3: 0},
        scratch_shapes=[
            pltpu.VMEM((parts, 3, step, hidden), bf16),
            pltpu.SemaphoreType.DMA((parts, 3)),
        ],
        compiler_params=pltpu.CompilerParams(vmem_limit_bytes=24 << 20),
        cost_estimate=pl.CostEstimate(
            flops=6 * total * width * hidden, bytes_accessed=6 * width * hidden, transcendentals=0
        ),
    )(*args, d_gate, d_up, act, *earlier, *after)


def backward_rows(hidden, ahead_1, ahead_2, d_mixed_2, keep, gain):
    scale_1 = inv_rms(hidden)
    unit_1 = hidden * scale_1
    unit_e1 = ahead_1 * inv_rms(ahead_1)
    unit_e2 = ahead_2 * inv_rms(ahead_2)
    mixed = (unit_1 * gain[0, 0:1] + unit_e1 * gain[0, 1:2]).astype(bf16).astype(f32)
    scale_2 = inv_rms(mixed)
    unit_2 = mixed * scale_2
    u = d_mixed_2 * gain[1, 0:1]
    grad_1 = (u - unit_2 * jnp.mean(u * unit_2, axis=-1, keepdims=True)) * scale_2
    v = grad_1 * gain[0, 0:1]
    grad_0 = (v - unit_1 * jnp.mean(v * unit_1, axis=-1, keepdims=True)) * scale_1
    kept_1, kept_2 = grad_1 * keep, d_mixed_2 * keep
    terms = [
        jnp.sum(a * b, axis=0, keepdims=True)
        for a, b in ((kept_1, unit_1), (kept_1, unit_e1), (kept_2, unit_2), (kept_2, unit_e2))
    ]
    return grad_0.astype(bf16), jnp.concatenate(terms, 0)


def dense_rows(name, token, count, hidden, embed, next_rows, cotangent, gain, before, half, halves, after=()):
    tokens, width = hidden.shape
    step, lane_step = 16, 256 if width % 256 == 0 else lanes
    steps, chunks = tokens // step // halves, width // lane_step
    first, last = half * steps, tokens // step - 1
    capacity = token.shape[3]
    earlier = []
    if before is not None:
        earlier = [pltpu.with_memory_space_constraint(before[0], pltpu.HBM), before[1]]

    def body(token_ref, count_ref, hidden_ref, now_ref, next_ref, after_ref, cot_ref, gain_ref, *refs):
        out_ref, terms_ref, sums_ref = refs[-3:]
        block = first + pl.program_id(0)

        @pl.when(pl.program_id(0) == 0)
        def _():
            sums_ref[...] = jnp.zeros_like(sums_ref)

        here = iota((step, 1), 0) + block * step
        keep = jnp.ones((step, 1), f32)
        for k in range(2):
            for c in range(capacity):
                out = (here == token_ref[0, 0, k, c]) & (c < count_ref[0, 0, k, 0])
                keep = jnp.where(out, 0.0, keep)
        depths = after_ref.shape[0]

        def at(i):
            return pl.ds(pl.multiple_of(i * lane_step, lane_step), lane_step)

        def embeds(i):
            tail = jnp.concatenate([after_ref[:, at(i)].astype(f32)] * (8 // depths), 0)
            follow = jnp.where(block == last, tail, next_ref[:, at(i)].astype(f32)[:8])
            return jnp.concatenate([now_ref[:, at(i)].astype(f32), follow], 0)

        def total(value):
            return jnp.sum(value, axis=1, keepdims=True) / width

        def squares(i, carry):
            h, e = hidden_ref[:, at(i)].astype(f32), embeds(i)
            return carry[0] + h * h, carry[1] + e * e

        sums = lax.fori_loop(
            0, chunks, squares,
            (jnp.zeros((step, lane_step), f32), jnp.zeros((step + 8, lane_step), f32)),
        )
        scale_1 = lax.rsqrt(total(sums[0]) + eps_norm)
        scale_e = lax.rsqrt(total(sums[1]) + eps_norm)
        scale_e1, scale_e2 = scale_e[1 : step + 1], scale_e[2 : step + 2]

        def units(i):
            both = embeds(i)
            unit_1 = hidden_ref[:, at(i)].astype(f32) * scale_1
            unit_e1 = both[1 : step + 1] * scale_e1
            gain_1 = gain_ref[0, 0:1, at(i)]
            mixed = unit_1 * gain_1 + unit_e1 * gain_ref[0, 1:2, at(i)]
            mixed = mixed.astype(bf16).astype(f32)
            d_mixed_2 = cot_ref[:, at(i)].astype(f32)
            u = d_mixed_2 * gain_ref[1, 0:1, at(i)]
            return both, unit_1, unit_e1, gain_1, mixed, d_mixed_2, u

        def products(i, carry):
            _, unit_1, _, gain_1, mixed, _, u = units(i)
            through = unit_1 * gain_1
            pairs = ((mixed, mixed), (u, mixed), (u, through), (mixed, through))
            return tuple(c + a * b for c, (a, b) in zip(carry, pairs))

        sums = lax.fori_loop(
            0, chunks, products, tuple(jnp.zeros((step, lane_step), f32) for _ in range(4))
        )
        square, along, u_back, mixed_back = (total(value) for value in sums)
        scale_2 = lax.rsqrt(square + eps_norm)
        share_2 = scale_2 * scale_2 * along
        share_1 = scale_2 * (u_back - share_2 * mixed_back)

        def grads(i, carry):
            both, unit_1, unit_e1, gain_1, mixed, d_mixed_2, u = units(i)
            unit_e2 = both[2 : step + 2] * scale_e2
            grad_1 = (u - mixed * share_2) * scale_2
            out_ref[:, at(i)] = ((grad_1 * gain_1 - unit_1 * share_1) * scale_1).astype(bf16)
            kept_1, kept_2 = grad_1 * keep, d_mixed_2 * keep
            pairs = ((kept_1, unit_1), (kept_1, unit_e1), (kept_2, mixed * scale_2), (kept_2, unit_e2))
            for k, (a, b) in enumerate(pairs):
                term = a * b
                sums_ref[k, :, at(i)] += sum(term[r : r + 8] for r in range(0, step, 8))
            return carry

        lax.fori_loop(0, chunks, grads, 0)

        @pl.when(pl.program_id(0) == steps - 1)
        def _():
            for k in range(4):
                term = jnp.sum(sums_ref[k], axis=0, keepdims=True)
                terms_ref[k : k + 1] = term + refs[1][k : k + 1] if earlier else term

    rows = pl.BlockSpec((step, width), lambda i: (first + i, 0))
    terms = pl.BlockSpec((4, width), lambda i: (0, 0))
    return pl.pallas_call(
        body,
        name=name,
        grid=(steps,),
        in_specs=[
            smem,
            smem,
            rows,
            rows,
            pl.BlockSpec((step, width), lambda i: (jnp.minimum(first + i + 1, last), 0)),
            pl.BlockSpec(next_rows.shape, lambda i: (0, 0)),
            rows,
            pl.BlockSpec(gain.shape, lambda i: (0, 0, 0)),
        ]
        + ([anywhere, terms] if earlier else [])
        + [anywhere] * len(after),
        out_specs=[rows, terms],
        out_shape=[
            jax.ShapeDtypeStruct((tokens, width), bf16),
            jax.ShapeDtypeStruct((4, width), f32),
        ],
        input_output_aliases={8: 0} if earlier else {},
        scratch_shapes=[pltpu.VMEM((4, 8, width), f32)],
        compiler_params=pltpu.CompilerParams(vmem_limit_bytes=12 << 20),
        cost_estimate=pl.CostEstimate(
            flops=60 * tokens * width // halves,
            bytes_accessed=10 * tokens * width // halves,
            transcendentals=0,
        ),
    )(token, count, hidden, embed, embed, next_rows, cotangent, gain, *earlier, *after)


def local(
    main_hidden, embedded, cotangent, slot_token, slot_count, route_gate, norm_gain, expert_weight
):
    depths, _, features = norm_gain.shape
    tokens = main_hidden.shape[2]
    slots = slot_token.shape[3]
    seqs, groups = lax.axis_size("seq"), lax.axis_size("dp")
    rows = seqs * slots
    total = groups * rows
    width = features // seqs
    share = width // groups
    hidden_units = expert_weight.shape[3]
    parts = folds(rows, width)
    where = jnp.stack([lax.axis_index("seq"), lax.axis_index("dp")]).astype(jnp.int32)
    source, embed, cot = main_hidden[0, 0], embedded[0, 0], cotangent[0, 0]
    facts = (slot_token, slot_count)
    packed = ((rows * parts, width // parts), bf16)
    part_rows = ((rows, width), f32)

    def payload(value):
        return folded(value, parts)

    asked_token = ring(slot_token, "section", -1)

    def own_rows(where, token, count, gate, embed, cot):
        first, second = token_column(token, 0), token_column(token, 1)
        live_1, live_2 = (live_column(count, k, slots) for k in range(2))
        weight_1, weight_2 = gate_column(gate, 0) * live_1, gate_column(gate, 1) * live_2
        facts = in_lanes(
            [first.astype(f32), second.astype(f32), live_1, live_2]
            + thirds(weight_1)
            + thirds(weight_2)
        )
        ahead_1, ahead_2 = pick(first + 1, embed), pick(first + 2, embed)
        block = jnp.concatenate([ahead_1, ahead_2, pick(first, cot), pick(second, cot) * weight_2], 0)
        notes = jnp.concatenate([coded(inv_rms(ahead_1)), coded(inv_rms(ahead_2)), facts, facts], 0)
        head = embed[:depths].astype(f32)
        scale = coded(inv_rms(head))
        heads = [
            jnp.concatenate([head[:, p * width : (p + 1) * width], scale], 1) for p in range(seqs)
        ]
        return [
            jnp.concatenate([jnp.concatenate([piece, notes], 1)] + heads, 0)
            for piece in pieces_of(block, where[0], seqs)
        ]

    own_sent = call(
        "own_rows", own_rows, [((4 * slots + depths * seqs, width + lanes), bf16)] * seqs,
        (where, slot_token, slot_count, route_gate), embed, cot,
    )
    own_got = trade_seq(own_sent)

    def source_rows(where, asked, source):
        first = pick(token_column(asked, 0), source)
        second = pick(token_column(asked, 1), source)
        scale = coded(inv_rms(first))
        sent = [jnp.concatenate([p, scale], 1) for p in pieces_of(first, where[0], seqs)]
        sent[0] = jnp.concatenate([sent[0], second], 1)
        return sent + [first]

    *sent, asked_rows = call(
        "source_rows", source_rows,
        [((slots, width + lanes + features), bf16)]
        + [((slots, width + lanes), bf16)] * (seqs - 1)
        + [((slots, features), bf16)],
        (where, asked_token), source, after=(own_sent[0],),
    )
    start_got = trade_seq(sent, 1)

    def own_parts(where, *got):
        got = [g.astype(f32) for g in got]
        first = 4 * slots
        block_1, block_2, block_3, block_4 = (
            in_order([g[k * slots : (k + 1) * slots] for g in got], where[0], 0) for k in range(4)
        )
        facts = block_3[:, width:]
        heads = in_order([g[first:] for g in got], where[0], 0)
        heads = [heads[j * depths * seqs : (j + 1) * depths * seqs] for j in range(seqs)]
        units = []
        for k, block in ((1, block_1), (2, block_2)):
            unit = block[:, :width] * decoded(block[:, width:])
            after = []
            for j in range(seqs):
                token = facts[j * slots : (j + 1) * slots, 0:1]
                add = jnp.zeros((slots, width), f32)
                for i in range(k if j + 1 < seqs else 0):
                    row = heads[j + 1][i : i + 1]
                    for p in range(1, seqs):
                        at = p * depths + i
                        row = jnp.where(where[0] == p, heads[j + 1][at : at + 1], row)
                    row = row[:, :width] * decoded(row[:, width:])
                    add += jnp.where(token == float(tokens + i - k), row, 0.0)
                after.append(add)
            units.append(unit + jnp.concatenate(after, 0))
        out = folded(block_4[:, :width], parts)
        none = jnp.zeros(((parts - 1) * rows, lanes), f32)
        tail = facts if parts == 1 else jnp.concatenate([facts, none], 0)
        follow = got[-1][first:, :width]
        follow = jnp.concatenate([follow[p * depths : (p + 1) * depths] for p in range(seqs)], 1)
        follow = jnp.where(where[0] == seqs - 1, 0.0, follow)
        return block_3[:, :width], jnp.concatenate([out, tail], 1), facts, *units, follow

    cot_1, dout_2, own_facts, unit_e1, unit_e2, next_rows = call(
        "own_parts", own_parts,
        [part_rows, ((rows * parts, width // parts + lanes), bf16), ((rows, lanes), f32)]
        + [part_rows] * 2
        + [((depths, features), bf16)],
        (where,), *own_got, after=(sent[0],),
    )
    dout_2_all = gather_dp(dout_2)

    def first_mixed(where, own_facts, unit_e1, gain, *got):
        start = in_order([g[:, : width + lanes].astype(f32) for g in got], where[0], 0)
        unit = start[:, :width] * decoded(start[:, width:])
        gain_h, gain_e = (piece_of(gain[0, k : k + 1], where[0], seqs, 0) for k in range(2))
        mixed = (unit * gain_h + unit_e1 * gain_e).astype(bf16).astype(f32)
        return payload(mixed * own_facts[:, 2:3]), unit

    rows_1, unit_1 = call(
        "first_mixed", first_mixed, [packed, part_rows],
        (where,), own_facts, unit_e1, norm_gain, *start_got,
    )
    rows_1_all = gather_dp(rows_1)

    def second_base(where, token, count, start, table, after, gain):
        second = token_column(token, 1)
        start = start[:, width + lanes :].astype(f32)
        ahead_1 = pick_ahead(second + 1, table, after)
        ahead_2 = pick_ahead(second + 2, table, after)
        unit = start * inv_rms(start)
        mixed = unit * gain[0, 0:1] + ahead_1 * inv_rms(ahead_1) * gain[0, 1:2]
        mixed = mixed.astype(bf16).astype(f32)
        own = mixed * inv_rms(mixed) * gain[1, 0:1] * (1.0 - met_column(token, count))
        out = (own + ahead_2 * inv_rms(ahead_2) * gain[1, 1:2]) * live_column(count, 1, slots)
        return pieces_of(out, where[0], seqs) + [ahead_1, ahead_2]

    *base_parts, ahead_21, ahead_22 = call(
        "second_base", second_base,
        [((slots, width), bf16)] * seqs + [((slots, features), bf16)] * 2,
        (where, *facts), start_got[0], embed, next_rows, norm_gain, after=(rows_1,),
    )
    base_got = trade_seq(base_parts)

    def slot_facts(*blocks):
        facts = jnp.concatenate(
            [block[:rows].astype(f32)[:, width // parts :] for block in blocks], 0
        )
        base = (iota((total, 1), 0) // slots * tokens).astype(f32)
        first, second = facts[:, 0:1] + base, facts[:, 1:2] + base
        live = (facts[:, 3:4] > 0) & (as_row(facts[:, 2:3]) > 0)
        same = ((second == as_row(first)) & live).astype(f32)
        return same, same, same[:rows, :rows], decoded(facts, 4)

    same, same_16, same_own, weight_1 = call(
        "slot_facts", slot_facts,
        [((total, total), f32), ((total, total), bf16), ((rows, rows), f32), ((total, 1), f32)],
        (), *dout_2_all, after=(rows_1,),
    )
    first_own, first_send = project(
        "gate_up_1", rows_1_all, expert_weight, 0, (0, 1), parts, after=(ahead_21, same_own)
    )
    first = pair_seq(first_own, first_send)

    def base_order(where, *got):
        return [payload(in_order([g.astype(f32) for g in got], where[0], 0))]

    (base_2,) = call("base_order", base_order, [packed], (where,), *base_got, after=(first_send,))
    base_2_all = gather_dp(base_2)

    def forward_1(own, other):
        both = own + other.astype(f32)
        gate, up = both[:, :hidden_units], both[:, hidden_units:]
        return gate * jax.nn.sigmoid(gate) * up, both

    (act_1, both_1), out_blocks = expand(
        "down_1", forward_1, first,
        [((total, hidden_units), bf16), ((total, 2 * hidden_units), f32)],
        expert_weight, 0, (2,), groups, parts, after=(base_2,),
    )
    out_got = return_dp(out_blocks)

    fixed_own, fixed_send = project(
        "fixed_2", base_2_all, expert_weight, 1, (0, 1), parts,
        others=(dout_2_all, (2,)), after=(out_blocks[0],),
    )
    fixed_pair = pair_seq(fixed_own, fixed_send)

    def second_prev(own_facts, rows_1, *got):
        value = unfolded(rows_1.astype(f32), parts) + summed(got, parts) * decoded(own_facts, 4)
        return payload(value), value.astype(bf16)

    prev, prev_own = call(
        "second_prev", second_prev, [packed, ((rows, width), bf16)],
        (), own_facts, rows_1, *out_got, after=(fixed_own,),
    )
    prev_all = gather_dp(prev)

    hidden, _ = lax.optimization_barrier((source, rows_1))
    hidden = ring(hidden, "section", 1)
    dense = dense_rows(
        "dense_a", *facts, hidden, embed, next_rows, cot, norm_gain, None, 0, 2,
        after=(prev, fixed_pair[1]),
    )

    mixed_own, mixed_send, chosen = project(
        "gate_up_2", prev_all, expert_weight, 1, (0, 1), parts,
        select=(where, same_16), gain=norm_gain, after=(dense[1],),
    )
    second = pair_seq(mixed_own, mixed_send)
    prev_w_own, prev_w_send = project(
        "prev_down", prev_all, expert_weight, 0, (2,), parts, after=(mixed_send,)
    )
    prev_pair = pair_seq(prev_w_own, prev_w_send)

    def gates_back(gate, up, d_act):
        sig = jax.nn.sigmoid(gate)
        d_gate = d_act * up * sig * (1.0 + gate * (1.0 - sig))
        return d_gate, d_act * gate * sig

    def backward_2(own, other, fixed_own, fixed_other, same):
        many = 2 * hidden_units
        square = own[:, many : many + 1] + decoded(other[:, many:])
        scale = lax.rsqrt(square / features + eps_norm)
        row = jnp.sum(same * as_row(scale), axis=1, keepdims=True)
        both = (own[:, :many] + other[:, :many].astype(f32)) * row
        fixed = fixed_own + fixed_other.astype(f32)
        both = both + fixed[:, :many]
        gate, up = both[:, :hidden_units], both[:, hidden_units:]
        d_gate, d_up = gates_back(gate, up, fixed[:, many:])
        return d_gate, d_up, gate * jax.nn.sigmoid(gate) * up, scale, row

    units = ((total, hidden_units), bf16)
    (d_gate_2, d_up_2, act_2, scale_2, row_2), d_rows_blocks = expand(
        "back_rows_2", backward_2,
        second + fixed_pair + (same,),
        [units, units, units, ((total, 1), f32), ((total, 1), f32)],
        expert_weight, 1, (0, 1), groups, parts, after=(prev_w_own,),
    )
    d_rows_got = return_dp(d_rows_blocks)
    dense, dense_terms = dense_rows(
        "dense_b", *facts, hidden, embed, next_rows, cot, norm_gain, dense, 1, 2,
        after=(d_rows_blocks[0],),
    )
    dense = ring(dense, "section", -1)

    def first_grad(where, cot, same, gain, *got):
        d_rows = summed(got, parts)
        added = lax.dot_general(
            same, d_rows, (((0,), (0,)), ((), ())),
            precision=lax.Precision.HIGHEST, preferred_element_type=f32,
        )
        d_mixed = cot + added
        u = d_mixed * piece_of(gain[1, 0:1], where[0], seqs, 0)
        return [payload(u), d_mixed] + blocks_of(d_rows, where[0], seqs)

    u, d_mixed_2, *d_rows_back = call(
        "first_grad", first_grad, [packed, part_rows] + [((slots, width), bf16)] * seqs,
        (where,), cot_1, same_own, norm_gain, *d_rows_got, after=(dense_terms,),
    )
    u_all = gather_dp(u)
    back_got = trade_seq(d_rows_back)

    def build_2(values, g):
        chosen, row, base, dout = values[0], values[1], values[2 : 2 + groups], values[2 + groups :]
        step = width // parts
        first = chosen[:, g * step : (g + 1) * step].astype(f32) * row
        first = first + column_part(base, rows, g).astype(f32)
        return first.astype(bf16), column_part(dout, rows, g)[:, :step]

    weight_grad, tick_2 = outer(
        "weight_grad_2", 1, depths, build_2, [chosen, row_2] + base_2_all + dout_2_all,
        d_gate_2, d_up_2, act_2, width, parts, None, after=(u, back_got[-1]),
    )

    back_1_own, back_1_send = project(
        "back_1", u_all, expert_weight, 0, (2,), parts, mates=prev_all, after=(tick_2,)
    )
    back_1 = pair_seq(back_1_own, back_1_send)

    def second_grad(where, token, count, start, ahead_1, ahead_2, cot, gain, terms, *got):
        d_rows = in_order([g.astype(f32) for g in got], where[0], 1)
        keep = live_column(count, 1, slots) * (1.0 - met_column(token, count))
        grad, more = backward_rows(
            start[:, width + lanes :].astype(f32), ahead_1.astype(f32), ahead_2.astype(f32),
            pick(token_column(token, 1), cot) + d_rows, keep, gain,
        )
        notes = in_lanes([live_column(count, 0, slots), keep])
        grad = jnp.concatenate([grad.astype(f32), notes], 1)
        return [grad] + pieces_of(terms + more, where[0], seqs)

    grad_2, *terms_parts = call(
        "second_grad", second_grad,
        [((slots, features + lanes), bf16)] + [((2 * depths, width), f32)] * seqs,
        (where, *facts), start_got[0], ahead_21, ahead_22, cot, norm_gain, dense_terms, *back_got,
        after=(back_1_send,),
    )
    grad_2 = ring(grad_2, "section", -1)
    terms_got = trade_seq(terms_parts)

    def backward_1(own, other, prev_own, prev_other, both, scale, weight_1):
        inner = own[:, hidden_units : hidden_units + 1] + decoded(other[:, hidden_units:])
        d_act = own[:, :hidden_units] + other[:, :hidden_units].astype(f32)
        through = scale * scale * inner / features
        d_act = d_act - through * (prev_own + prev_other.astype(f32))
        d_act = d_act * (weight_1 * scale)
        d_gate, d_up = gates_back(both[:, :hidden_units], both[:, hidden_units:], d_act)
        return d_gate, d_up, through

    (d_gate_1, d_up_1, through_1), d_rows_blocks = expand(
        "back_rows_1", backward_1,
        back_1 + prev_pair + (both_1, scale_2, weight_1),
        [units, units, ((total, 1), f32)],
        expert_weight, 0, (0, 1), groups, parts, after=(terms_parts[0],),
    )
    d_rows_got = return_dp(d_rows_blocks)

    def build_1(values, g):
        through, scale, weight = values[:3]
        first, u, prev = (values[3 + k * groups : 3 + (k + 1) * groups] for k in range(3))
        dout = column_part(u, rows, g).astype(f32) - through * column_part(prev, rows, g).astype(f32)
        return column_part(first, rows, g), (dout * (weight * scale)).astype(bf16)

    weight_grad, tick_1 = outer(
        "weight_grad_1", 0, depths, build_1,
        [through_1, scale_2, weight_1] + rows_1_all + u_all + prev_all,
        d_gate_1, d_up_1, act_1, width, parts, weight_grad, after=(d_rows_blocks[0],),
    )

    def last_grad(where, d_mixed_2, prev, scale, through, unit_1, unit_e1, unit_e2, own_facts, gain, *got):
        got, terms = got[:groups], got[groups:]
        d_rows = summed(got, parts)
        gain_1, gain_2 = (piece_of(gain[k, 0:1], where[0], seqs, 0) for k in range(2))
        scale, through = scale[:rows], through[:rows]
        live = own_facts[:, 2:3]
        prev = prev.astype(f32)
        grad_1 = (d_mixed_2 * gain_2 - through * prev) * scale
        d_mixed_1 = grad_1 + d_rows
        kept_1, kept_2 = d_mixed_1 * live, d_mixed_2 * live
        sums = [
            jnp.sum(a * b, axis=0, keepdims=True)
            for a, b in ((kept_1, unit_1), (kept_1, unit_e1), (kept_2, prev * scale), (kept_2, unit_e2))
        ]
        sums = jnp.concatenate(sums, 0) + sum(terms)
        cut = []
        for i in range(groups):
            want = lax.rem(where[1] - i + groups, groups)
            block = sums[:, :share]
            for z in range(1, groups):
                block = jnp.where(want == z, sums[:, z * share : (z + 1) * share], block)
            cut.append(block)
        return cut + blocks_of(d_mixed_1 * gain_1, where[0], seqs)

    last = call(
        "last_grad", last_grad,
        [((2 * depths, share), f32)] * groups + [((slots, width), bf16)] * seqs,
        (where,), d_mixed_2, prev_own, scale_2, through_1, unit_1, unit_e1, unit_e2,
        own_facts, norm_gain, *d_rows_got, *terms_got, after=(tick_1,),
    )
    last_got = trade_seq(last[groups:], -1)
    sums_got = return_dp(last[:groups])

    def finish(where, token, dense, asked_rows, grad_2, *got):
        part = in_order([g.astype(f32) for g in got], where[0], 1)
        asked_rows = asked_rows.astype(f32)
        scale = inv_rms(asked_rows)
        unit = asked_rows * scale
        grad_1 = (part - unit * jnp.mean(part * unit, axis=-1, keepdims=True)) * scale
        notes = grad_2[:, features:].astype(f32)
        grads = jnp.concatenate([grad_1, grad_2[:, :features].astype(f32)], 0).astype(bf16)
        lane = iota((slots, tokens), 1)
        chosen = jnp.concatenate(
            [
                jnp.where(lane == token_column(token, k), notes[:, k : k + 1], 0.0)
                for k in range(2)
            ],
            0,
        ).astype(bf16)
        taken = lax.dot_general(
            chosen, jnp.ones((2 * slots, lanes), bf16), (((0,), (0,)), ((), ())),
            preferred_element_type=f32,
        )[:, 0:1]
        out = []
        step = chunk_of(features)
        for at in range(0, features, step):
            placed = lax.dot_general(
                chosen, grads[:, at : at + step], (((0,), (0,)), ((), ())),
                preferred_element_type=f32,
            )
            out.append(jnp.where(taken > 0, placed, dense[:, at : at + step].astype(f32)).astype(bf16))
        return [jnp.concatenate(out, 1), jnp.zeros((8, lanes), f32)]

    hidden_grad, tick = call(
        "finish", finish, [((tokens, features), bf16), ((8, lanes), f32)],
        (where, asked_token), dense, asked_rows, grad_2, *last_got, limit=20,
    )

    def gain_sum(*got):
        sums = sum(got)
        return [jnp.stack([sums[2 * k : 2 * k + 2] for k in range(depths)])[None]]

    (gain_grad,) = call(
        "gain_sum", gain_sum, [((1, depths, 2, share), f32)], (), *sums_got, after=(tick,)
    )
    return (
        hidden_grad[None, None],
        weight_grad,
        gain_grad,
    )


def solution(mesh):
    return jax.shard_map(
        local,
        mesh=mesh,
        in_specs=(
            P("section", "dp", "seq", None),
            P("section", "dp", "seq", None),
            P("section", "dp", "seq", None),
            P("section", "dp", None, "seq"),
            P("section", "dp", None, "seq"),
            P("section", "dp", None, "seq"),
            P(),
            P(None, None, "seq", "dp"),
        ),
        out_specs=(
            P("section", "dp", "seq", None),
            P("section", None, None, "seq", "dp"),
            P("section", None, None, ("seq", "dp")),
        ),
        check_vma=False,
    )
```

```python
import jax
import jax.numpy as jnp
from jax import lax
from jax.experimental import pallas as pl
from jax.experimental.pallas import tpu as pltpu
from jax.sharding import PartitionSpec as P

eps_norm = 1e-06
lanes = 128
f32 = jnp.float32
bf16 = jnp.bfloat16
vmem = pl.BlockSpec(memory_space=pltpu.VMEM)
smem = pl.BlockSpec(memory_space=pltpu.SMEM)
anywhere = pl.BlockSpec(memory_space=pl.ANY)


def ring(value, axis, steps):
    count = lax.axis_size(axis)
    return lax.ppermute(value, axis, [(i, (i + steps) % count) for i in range(count)])


def hop(value, section_step, seq_step):
    sections, seqs = lax.axis_size("section"), lax.axis_size("seq")
    pairs = [
        (c * seqs + s, (c + section_step) % sections * seqs + (s + seq_step) % seqs)
        for c in range(sections)
        for s in range(seqs)
    ]
    return lax.ppermute(value, ("section", "seq"), pairs)


def trade_seq(pieces, section_step=0):
    if section_step == 0:
        return [pieces[0]] + [ring(pieces[o], "seq", o) for o in range(1, len(pieces))]
    return [hop(piece, section_step, o) for o, piece in enumerate(pieces)]


def partner(place, step, count):
    return place ^ step if count & (count - 1) == 0 else (place - step) % count


def gather_dp(block):
    count = lax.axis_size("dp")
    return [block] + [
        lax.ppermute(block, "dp", [(partner(z, i, count), z) for z in range(count)])
        for i in range(1, count)
    ]


def return_dp(blocks):
    count = lax.axis_size("dp")
    return [blocks[0]] + [
        lax.ppermute(blocks[i], "dp", [(z, partner(z, i, count)) for z in range(count)])
        for i in range(1, count)
    ]


def pair_seq(own, send):
    if lax.axis_size("seq") == 2:
        return own, ring(send, "seq", 1)
    return lax.psum(own, "seq"), jnp.zeros_like(send)


def inv_rms(value):
    return lax.rsqrt(jnp.mean(value * value, axis=-1, keepdims=True) + eps_norm)


def iota(shape, dim):
    return lax.broadcasted_iota(jnp.int32, shape, dim)


def token_column(token, depth):
    capacity = token.shape[3]
    out = jnp.full((capacity, 1), token[0, 0, depth, 0], jnp.int32)
    for c in range(1, capacity):
        out = jnp.where(iota((capacity, 1), 0) == c, token[0, 0, depth, c], out)
    return out


def gate_column(gate, depth):
    capacity = gate.shape[3]
    out = jnp.full((capacity, 1), gate[0, 0, depth, 0], f32)
    for c in range(1, capacity):
        out = jnp.where(iota((capacity, 1), 0) == c, gate[0, 0, depth, c], out)
    return out


def live_column(count, depth, capacity):
    return (iota((capacity, 1), 0) < count[0, 0, depth, 0]).astype(f32)


def met_column(token, count):
    capacity = token.shape[3]
    second = token_column(token, 1)
    out = jnp.zeros((capacity, 1), f32)
    for c in range(capacity):
        out += ((second == token[0, 0, 0, c]) & (c < count[0, 0, 0, 0])).astype(f32)
    return jnp.minimum(out, 1.0)


def pick(column, table):
    hot = (column == iota((column.shape[0], table.shape[0]), 1)).astype(bf16)
    return jnp.dot(hot, table, preferred_element_type=f32)


def pick_ahead(column, table, after):
    return pick(column, table) + pick(column - table.shape[0], after)


def thirds(column):
    high = column.astype(bf16).astype(f32)
    mid = (column - high).astype(bf16).astype(f32)
    return [high, mid, column - high - mid]


def in_lanes(columns):
    lane = iota((columns[0].shape[0], lanes), 1)
    out = jnp.zeros(lane.shape, f32)
    for k, column in enumerate(columns):
        out = jnp.where(lane == k, column, out)
    return out


def coded(column):
    return in_lanes(thirds(column))


def decoded(block, first=0):
    lane = iota(block.shape, 1)
    inside = (lane >= first) & (lane < first + 3)
    return jnp.sum(jnp.where(inside, block.astype(f32), 0.0), axis=1, keepdims=True)


def piece_of(value, place, count, step):
    width = value.shape[-1] // count
    want = lax.rem(place + step, count)
    out = value[:, :width]
    for p in range(1, count):
        out = jnp.where(want == p, value[:, p * width : (p + 1) * width], out)
    return out


def pieces_of(value, place, count):
    return [piece_of(value, place, count, o) for o in range(count)]


def blocks_of(value, place, count):
    size = value.shape[0] // count
    out = []
    for o in range(count):
        block = value[:size]
        for j in range(1, count):
            want = lax.rem(place + o, count) == j
            block = jnp.where(want, value[j * size : (j + 1) * size], block)
        out.append(block)
    return out


def in_order(got, place, axis):
    count = len(got)
    out = []
    for j in range(count):
        block = got[0]
        for o in range(1, count):
            block = jnp.where(lax.rem(place - o + count, count) == j, got[o], block)
        out.append(block)
    return jnp.concatenate(out, axis)


def as_row(column):
    size = column.shape[0]
    here = iota((size, size), 0) == iota((size, size), 1)
    return jnp.sum(jnp.where(here, column, 0.0), axis=0, keepdims=True)


def folds(rows, width):
    for count in (1, 2, 4, 8):
        if rows * count % 16 == 0 and width % (count * lanes) == 0:
            return count
    return 1


def folded(value, count):
    step = value.shape[1] // count
    return jnp.concatenate([value[:, g * step : (g + 1) * step] for g in range(count)], 0)


def unfolded(value, count):
    rows = value.shape[0] // count
    return jnp.concatenate([value[g * rows : (g + 1) * rows] for g in range(count)], 1)


def column_part(blocks, rows, g):
    return jnp.concatenate(
        [block[g * rows : (g + 1) * rows].astype(f32) for block in blocks], 0
    ).astype(bf16)


def summed(got, parts):
    return unfolded(sum(g.astype(f32) for g in got), parts)


def chunk_of(width):
    for step in (1024, 896, 512, 256, 128):
        if width % step == 0:
            return step
    return width


def call(name, fn, outs, small, *args, after=(), flops=0, limit=12):
    shapes = [jax.ShapeDtypeStruct(shape, kind) for shape, kind in outs]
    n_small, n_args, n_after = len(small), len(args), len(after)

    def body(*refs):
        values = list(refs[:n_small]) + [r[...] for r in refs[n_small : n_small + n_args]]
        for ref, value in zip(refs[n_small + n_args + n_after :], fn(*values)):
            ref[...] = value.astype(ref.dtype)

    size = sum(a.size * a.dtype.itemsize for a in list(args) + shapes)
    return pl.pallas_call(
        body,
        name=name,
        out_shape=shapes,
        in_specs=[smem] * n_small + [vmem] * n_args + [anywhere] * n_after,
        out_specs=[vmem] * len(shapes),
        compiler_params=pltpu.CompilerParams(vmem_limit_bytes=limit << 20),
        cost_estimate=pl.CostEstimate(flops=flops, bytes_accessed=size, transcendentals=0),
    )(*small, *args, *after)


def fetch(weight_ref, depth, kinds, buffer, sems, parts):
    step = weight_ref.shape[2] // parts
    copies = []
    for g in range(parts):
        row = []
        for k, kind in enumerate(kinds):
            copy = pltpu.make_async_copy(
                weight_ref.at[depth, kind, pl.ds(g * step, step)],
                buffer.at[g, k],
                sems.at[g, k],
            )
            copy.start()
            row.append(copy)
        copies.append(row)
    return copies


def fetched(weight, kinds, parts):
    hidden = weight.shape[3]
    return [
        pltpu.VMEM((parts, len(kinds), weight.shape[2] // parts, hidden), bf16),
        pltpu.SemaphoreType.DMA((parts, len(kinds))),
    ]


def project(name, blocks, weight, depth, kinds, parts, others=None, select=None, gain=None, mates=None, after=()):
    groups = len(blocks)
    rows = blocks[0].shape[0] // parts
    width, hidden = weight.shape[2:]
    step = width // parts
    other_blocks, other_kinds = others if others is not None else ([], ())
    first_kinds, kinds = kinds, kinds + other_kinds
    total, many = rows * groups, len(kinds) * hidden
    marked = select is not None or mates is not None
    extra = lanes if marked else 0

    def body(*refs):
        refs = list(refs)
        where_ref = refs.pop(0) if select is not None else None
        x_refs, w_ref, refs = refs[:groups], refs[groups], refs[groups + 1 :]
        other_refs, refs = refs[: len(other_blocks)], refs[len(other_blocks) :]
        if select is not None:
            select_ref, gain_ref = refs.pop(0), refs.pop(0)
        if mates is not None:
            mate_refs, refs = refs[:groups], refs[groups:]
        refs = refs[len(after) :]
        own_ref, send_ref = refs.pop(0), refs.pop(0)
        kept_ref = refs.pop(0) if select is not None else None
        buffer, sems = refs
        copies = fetch(w_ref, depth, kinds, buffer, sems, parts)
        x_all = [r[...] for r in x_refs]
        mate_all = [r[...] for r in mate_refs] if mates is not None else x_all
        if select is not None:
            gain_all = piece_of(gain_ref[1, 0:1, :], where_ref[0], gain.shape[2] // width, 0)
        sums = [jnp.zeros((total, hidden), f32) for _ in kinds]
        mark = jnp.zeros((total, 1), f32)
        for g in range(parts):
            x = column_part(x_all, rows, g)
            if marked:
                mate = x if mates is None else column_part(mate_all, rows, g)
                mark += jnp.sum(x.astype(f32) * mate.astype(f32), axis=1, keepdims=True)
            if select is not None:
                chosen = jnp.dot(select_ref[...], x, preferred_element_type=f32)
                x = (chosen * gain_all[:, g * step : (g + 1) * step]).astype(bf16)
                kept_ref[:, g * step : (g + 1) * step] = x
            for k in range(len(kinds)):
                if k == len(first_kinds):
                    x = column_part([r[...] for r in other_refs], rows, g)[:, :step]
                copies[g][k].wait()
                sums[k] += jnp.dot(x, buffer[g, k], preferred_element_type=f32)
        for k in range(len(kinds)):
            own_ref[:, k * hidden : (k + 1) * hidden] = sums[k]
            send_ref[:, k * hidden : (k + 1) * hidden] = sums[k].astype(bf16)
        if marked:
            own_ref[:, many:] = in_lanes([mark])
            send_ref[:, many:] = coded(mark).astype(bf16)

    args = list(blocks) + [pltpu.with_memory_space_constraint(weight, pltpu.HBM)]
    args, specs = args + list(other_blocks), [vmem] * groups + [anywhere] + [vmem] * len(other_blocks)
    outs = [
        jax.ShapeDtypeStruct((total, many + extra), f32),
        jax.ShapeDtypeStruct((total, many + extra), bf16),
    ]
    if select is not None:
        where, table = select
        args, specs = [where] + args + [table, gain], [smem] + specs + [vmem, vmem]
        outs.append(jax.ShapeDtypeStruct((total, width), bf16))
    if mates is not None:
        args, specs = args + list(mates), specs + [vmem] * groups
    return pl.pallas_call(
        body,
        name=name,
        in_specs=specs + [anywhere] * len(after),
        out_specs=[vmem] * len(outs),
        out_shape=outs,
        scratch_shapes=fetched(weight, kinds, parts),
        compiler_params=pltpu.CompilerParams(vmem_limit_bytes=16 << 20),
        cost_estimate=pl.CostEstimate(
            flops=2 * total * width * many, bytes_accessed=2 * width * many, transcendentals=0
        ),
    )(*args, *after)


def expand(name, prepare, args, saved, weight, depth, kinds, groups, parts, after=()):
    width, hidden = weight.shape[2:]
    total = saved[0][0][0]
    rows, step = total // groups, width // parts
    count, kept = len(args), len(saved)

    def body(*refs):
        in_refs, w_ref = refs[:count], refs[count]
        refs = refs[count + 1 + len(after) :]
        saved_refs, out_refs, (buffer, sems) = refs[:kept], refs[kept:-2], refs[-2:]
        copies = fetch(w_ref, depth, kinds, buffer, sems, parts)
        for ref, value in zip(saved_refs, prepare(*[r[...] for r in in_refs])):
            ref[...] = value.astype(ref.dtype)
        out = []
        for g in range(parts):
            part = jnp.zeros((total, step), f32)
            for k in range(len(kinds)):
                copies[g][k].wait()
                part += lax.dot_general(
                    saved_refs[k][...], buffer[g, k], (((1,), (1,)), ((), ())),
                    preferred_element_type=f32,
                )
            out.append(part)
        for z in range(groups):
            block = jnp.concatenate([part[z * rows : (z + 1) * rows] for part in out], 0)
            out_refs[z][...] = block.astype(bf16)

    results = pl.pallas_call(
        body,
        name=name,
        in_specs=[vmem] * count + [anywhere] * (1 + len(after)),
        out_specs=[vmem] * (kept + groups),
        out_shape=[jax.ShapeDtypeStruct(shape, kind) for shape, kind in saved]
        + [jax.ShapeDtypeStruct((rows * parts, step), bf16)] * groups,
        scratch_shapes=fetched(weight, kinds, parts),
        compiler_params=pltpu.CompilerParams(vmem_limit_bytes=16 << 20),
        cost_estimate=pl.CostEstimate(
            flops=2 * total * width * hidden * len(kinds),
            bytes_accessed=2 * width * hidden * len(kinds),
            transcendentals=0,
        ),
    )(*args, pltpu.with_memory_space_constraint(weight, pltpu.HBM), *after)
    return results[:kept], results[kept:]


def outer(name, depth, depths, build, args, d_gate, d_up, act, width, parts, before, after=()):
    total, hidden = act.shape
    step = width // parts
    count = len(args)
    earlier = [] if before is None else [pltpu.with_memory_space_constraint(before, pltpu.HBM)]

    def contract(left, right):
        return lax.dot_general(left, right, (((0,), (0,)), ((), ())), preferred_element_type=f32)

    def body(*refs):
        values = [r[...] for r in refs[:count]]
        gate_ref, up_ref, act_ref = refs[count : count + 3]
        out_ref, tick_ref, buffer, sems = refs[-4:]
        tick_ref[...] = jnp.zeros_like(tick_ref)
        copies = []
        for g in range(parts):
            rows, dout = build(values, g)
            pairs = ((rows, gate_ref), (rows, up_ref), (dout, act_ref))
            for k, (left, right_ref) in enumerate(pairs):
                buffer[g, k] = contract(left, right_ref[...]).astype(bf16)
                copy = pltpu.make_async_copy(
                    buffer.at[g, k],
                    out_ref.at[0, depth, k, pl.ds(g * step, step)],
                    sems.at[g, k],
                )
                copy.start()
                copies.append(copy)
        for copy in copies:
            copy.wait()

    return pl.pallas_call(
        body,
        name=name,
        in_specs=[vmem] * (count + 3) + [anywhere] * (len(earlier) + len(after)),
        out_specs=[anywhere, vmem],
        out_shape=[
            jax.ShapeDtypeStruct((1, depths, 3, width, hidden), bf16),
            jax.ShapeDtypeStruct((8, lanes), f32),
        ],
        input_output_aliases={} if before is None else {count + 3: 0},
        scratch_shapes=[
            pltpu.VMEM((parts, 3, step, hidden), bf16),
            pltpu.SemaphoreType.DMA((parts, 3)),
        ],
        compiler_params=pltpu.CompilerParams(vmem_limit_bytes=24 << 20),
        cost_estimate=pl.CostEstimate(
            flops=6 * total * width * hidden, bytes_accessed=6 * width * hidden, transcendentals=0
        ),
    )(*args, d_gate, d_up, act, *earlier, *after)


def backward_rows(hidden, ahead_1, ahead_2, d_mixed_2, keep, gain):
    scale_1 = inv_rms(hidden)
    unit_1 = hidden * scale_1
    unit_e1 = ahead_1 * inv_rms(ahead_1)
    unit_e2 = ahead_2 * inv_rms(ahead_2)
    mixed = (unit_1 * gain[0, 0:1] + unit_e1 * gain[0, 1:2]).astype(bf16).astype(f32)
    scale_2 = inv_rms(mixed)
    unit_2 = mixed * scale_2
    u = d_mixed_2 * gain[1, 0:1]
    grad_1 = (u - unit_2 * jnp.mean(u * unit_2, axis=-1, keepdims=True)) * scale_2
    v = grad_1 * gain[0, 0:1]
    grad_0 = (v - unit_1 * jnp.mean(v * unit_1, axis=-1, keepdims=True)) * scale_1
    kept_1, kept_2 = grad_1 * keep, d_mixed_2 * keep
    terms = [
        jnp.sum(a * b, axis=0, keepdims=True)
        for a, b in ((kept_1, unit_1), (kept_1, unit_e1), (kept_2, unit_2), (kept_2, unit_e2))
    ]
    return grad_0.astype(bf16), jnp.concatenate(terms, 0)


def dense_rows(name, token, count, hidden, embed, next_rows, cotangent, gain, before, half, halves, after=()):
    tokens, width = hidden.shape
    size = tokens // halves
    low = half * size
    spare = next_rows.shape[0]
    chunks = width // lanes
    capacity = token.shape[3]
    earlier = [] if before is None else list(before)

    def body(token_ref, count_ref, hidden_ref, embed_ref, next_ref, cot_ref, gain_ref, *refs):
        out_ref, terms_ref, mixed_ref = refs[-3:]
        here = iota((size, 1), 0) + low
        keep = jnp.ones((size, 1), f32)
        for k in range(2):
            for c in range(capacity):
                out = (here == token_ref[0, 0, k, c]) & (c < count_ref[0, 0, k, 0])
                keep = jnp.where(out, 0.0, keep)
        mine = pl.ds(low, size)
        row, column = (iota((2 * size, size + spare), dim) for dim in range(2))
        shift = (column == jnp.where(row < size, row + 1, row + 2 - size)).astype(bf16)

        def at(i):
            return pl.ds(pl.multiple_of(i * lanes, lanes), lanes)

        def embeds(i):
            if half < halves - 1:
                return embed_ref[pl.ds(low, size + spare), at(i)]
            return jnp.concatenate([embed_ref[mine, at(i)], next_ref[:, at(i)]], 0)

        def mean(value):
            return jnp.sum(value, axis=1, keepdims=True) / width

        def squares(i, carry):
            h, e = hidden_ref[mine, at(i)].astype(f32), embeds(i).astype(f32)
            return carry[0] + h * h, carry[1] + e * e

        sums = lax.fori_loop(
            0, chunks, squares,
            (jnp.zeros((size, lanes), f32), jnp.zeros((size + spare, lanes), f32)),
        )
        scale_1 = lax.rsqrt(mean(sums[0]) + eps_norm)
        scale_e = lax.rsqrt(mean(sums[1]) + eps_norm)
        scale_e1, scale_e2 = scale_e[1 : size + 1], scale_e[2 : size + 2]

        def products(i, carry):
            ahead = jnp.dot(shift[:size], embeds(i), preferred_element_type=f32)
            through = hidden_ref[mine, at(i)].astype(f32) * scale_1 * gain_ref[0, 0:1, at(i)]
            mixed = through + ahead * scale_e1 * gain_ref[0, 1:2, at(i)]
            kept = mixed.astype(bf16)
            mixed_ref[:, at(i)] = kept
            mixed = kept.astype(f32)
            u = cot_ref[mine, at(i)].astype(f32) * gain_ref[1, 0:1, at(i)]
            pairs = ((mixed, mixed), (u, mixed), (u, through), (mixed, through))
            return tuple(c + a * b for c, (a, b) in zip(carry, pairs))

        sums = lax.fori_loop(
            0, chunks, products, tuple(jnp.zeros((size, lanes), f32) for _ in range(4))
        )
        square, along, u_back, mixed_back = (mean(value) for value in sums)
        scale_2 = lax.rsqrt(square + eps_norm)
        share_2 = scale_2 * scale_2 * along
        share_1 = scale_2 * (u_back - share_2 * mixed_back)
        keep_2, keep_h, keep_e = keep * scale_2, keep * scale_1, keep * scale_e1
        keep_e2 = keep * scale_e2

        def grads(i, carry):
            ahead = jnp.dot(shift, embeds(i), preferred_element_type=f32)
            hidden = hidden_ref[mine, at(i)].astype(f32)
            mixed = mixed_ref[:, at(i)].astype(f32)
            cot = cot_ref[mine, at(i)].astype(f32)
            grad_1 = (cot * gain_ref[1, 0:1, at(i)] - mixed * share_2) * scale_2
            grad_0 = (grad_1 * gain_ref[0, 0:1, at(i)] - hidden * (scale_1 * share_1)) * scale_1
            out_ref[mine, at(i)] = grad_0.astype(bf16)
            terms = (
                grad_1 * (hidden * keep_h),
                grad_1 * (ahead[:size] * keep_e),
                cot * (mixed * keep_2),
                cot * (ahead[size:] * keep_e2),
            )
            for k, term in enumerate(terms):
                term = jnp.sum(term, axis=0, keepdims=True)
                terms_ref[k : k + 1, at(i)] = term + refs[1][k : k + 1, at(i)] if earlier else term
            return carry

        lax.fori_loop(0, chunks, grads, 0)

    return pl.pallas_call(
        body,
        name=name,
        in_specs=[smem] * 2 + [vmem] * (5 + len(earlier)) + [anywhere] * len(after),
        out_specs=[vmem] * 2,
        out_shape=[
            jax.ShapeDtypeStruct((tokens, width), bf16),
            jax.ShapeDtypeStruct((4, width), f32),
        ],
        input_output_aliases={7: 0} if earlier else {},
        scratch_shapes=[pltpu.VMEM((size, width), bf16)],
        compiler_params=pltpu.CompilerParams(vmem_limit_bytes=8 << 20),
        cost_estimate=pl.CostEstimate(
            flops=60 * tokens * width // halves,
            bytes_accessed=10 * tokens * width // halves,
            transcendentals=0,
        ),
    )(token, count, hidden, embed, next_rows, cotangent, gain, *earlier, *after)


def local(
    main_hidden, embedded, cotangent, slot_token, slot_count, route_gate, norm_gain, expert_weight
):
    depths, _, features = norm_gain.shape
    tokens = main_hidden.shape[2]
    slots = slot_token.shape[3]
    seqs, groups = lax.axis_size("seq"), lax.axis_size("dp")
    rows = seqs * slots
    total = groups * rows
    width = features // seqs
    share = width // groups
    hidden_units = expert_weight.shape[3]
    parts = folds(rows, width)
    where = jnp.stack([lax.axis_index("seq"), lax.axis_index("dp")]).astype(jnp.int32)
    source, embed, cot = main_hidden[0, 0], embedded[0, 0], cotangent[0, 0]
    facts = (slot_token, slot_count)
    packed = ((rows * parts, width // parts), bf16)
    part_rows = ((rows, width), f32)

    def payload(value):
        return folded(value, parts)

    asked_token = ring(slot_token, "section", -1)

    def source_rows(where, asked, source):
        first = pick(token_column(asked, 0), source)
        second = pick(token_column(asked, 1), source)
        scale = coded(inv_rms(first))
        sent = [jnp.concatenate([p, scale], 1) for p in pieces_of(first, where[0], seqs)]
        sent[0] = jnp.concatenate([sent[0], second], 1)
        return sent + [first]

    *sent, asked_rows = call(
        "source_rows", source_rows,
        [((slots, width + lanes + features), bf16)]
        + [((slots, width + lanes), bf16)] * (seqs - 1)
        + [((slots, features), bf16)],
        (where, asked_token), source,
    )
    start_got = trade_seq(sent, 1)

    def own_rows(where, token, count, gate, embed, cot):
        first, second = token_column(token, 0), token_column(token, 1)
        live_1, live_2 = (live_column(count, k, slots) for k in range(2))
        weight_1, weight_2 = gate_column(gate, 0) * live_1, gate_column(gate, 1) * live_2
        facts = in_lanes(
            [first.astype(f32), second.astype(f32), live_1, live_2]
            + thirds(weight_1)
            + thirds(weight_2)
        )
        ahead_1, ahead_2 = pick(first + 1, embed), pick(first + 2, embed)
        block = jnp.concatenate([ahead_1, ahead_2, pick(first, cot), pick(second, cot) * weight_2], 0)
        notes = jnp.concatenate([coded(inv_rms(ahead_1)), coded(inv_rms(ahead_2)), facts, facts], 0)
        head = embed[:depths].astype(f32)
        scale = coded(inv_rms(head))
        heads = [
            jnp.concatenate([head[:, p * width : (p + 1) * width], scale], 1) for p in range(seqs)
        ]
        return [
            jnp.concatenate([jnp.concatenate([piece, notes], 1)] + heads, 0)
            for piece in pieces_of(block, where[0], seqs)
        ]

    own_sent = call(
        "own_rows", own_rows, [((4 * slots + depths * seqs, width + lanes), bf16)] * seqs,
        (where, slot_token, slot_count, route_gate), embed, cot, after=(sent[0],),
    )
    own_got = trade_seq(own_sent)

    def own_parts(where, *got):
        got = [g.astype(f32) for g in got]
        first = 4 * slots
        block_1, block_2, block_3, block_4 = (
            in_order([g[k * slots : (k + 1) * slots] for g in got], where[0], 0) for k in range(4)
        )
        facts = block_3[:, width:]
        heads = in_order([g[first:] for g in got], where[0], 0)
        heads = [heads[j * depths * seqs : (j + 1) * depths * seqs] for j in range(seqs)]
        units = []
        for k, block in ((1, block_1), (2, block_2)):
            unit = block[:, :width] * decoded(block[:, width:])
            after = []
            for j in range(seqs):
                token = facts[j * slots : (j + 1) * slots, 0:1]
                add = jnp.zeros((slots, width), f32)
                for i in range(k if j + 1 < seqs else 0):
                    row = heads[j + 1][i : i + 1]
                    for p in range(1, seqs):
                        at = p * depths + i
                        row = jnp.where(where[0] == p, heads[j + 1][at : at + 1], row)
                    row = row[:, :width] * decoded(row[:, width:])
                    add += jnp.where(token == float(tokens + i - k), row, 0.0)
                after.append(add)
            units.append(unit + jnp.concatenate(after, 0))
        out = folded(block_4[:, :width], parts)
        none = jnp.zeros(((parts - 1) * rows, lanes), f32)
        tail = facts if parts == 1 else jnp.concatenate([facts, none], 0)
        follow = got[-1][first:, :width]
        follow = jnp.concatenate([follow[p * depths : (p + 1) * depths] for p in range(seqs)], 1)
        follow = jnp.where(where[0] == seqs - 1, 0.0, follow)
        follow = jnp.concatenate([follow, jnp.zeros((16 - depths, features), f32)], 0)
        return block_3[:, :width], jnp.concatenate([out, tail], 1), facts, *units, follow

    cot_1, dout_2, own_facts, unit_e1, unit_e2, next_rows = call(
        "own_parts", own_parts,
        [part_rows, ((rows * parts, width // parts + lanes), bf16), ((rows, lanes), f32)]
        + [part_rows] * 2
        + [((16, features), bf16)],
        (where,), *own_got,
    )

    def first_mixed(where, own_facts, unit_e1, gain, *got):
        start = in_order([g[:, : width + lanes].astype(f32) for g in got], where[0], 0)
        unit = start[:, :width] * decoded(start[:, width:])
        gain_h, gain_e = (piece_of(gain[0, k : k + 1], where[0], seqs, 0) for k in range(2))
        mixed = (unit * gain_h + unit_e1 * gain_e).astype(bf16).astype(f32)
        return payload(mixed * own_facts[:, 2:3]), unit

    rows_1, unit_1 = call(
        "first_mixed", first_mixed, [packed, part_rows],
        (where,), own_facts, unit_e1, norm_gain, *start_got,
    )
    rows_1_all = gather_dp(rows_1)
    dout_2, _ = lax.optimization_barrier((dout_2, rows_1))
    dout_2_all = gather_dp(dout_2)

    def second_base(where, token, count, start, table, after, gain):
        second = token_column(token, 1)
        start = start[:, width + lanes :].astype(f32)
        ahead_1 = pick_ahead(second + 1, table, after)
        ahead_2 = pick_ahead(second + 2, table, after)
        unit = start * inv_rms(start)
        mixed = unit * gain[0, 0:1] + ahead_1 * inv_rms(ahead_1) * gain[0, 1:2]
        mixed = mixed.astype(bf16).astype(f32)
        own = mixed * inv_rms(mixed) * gain[1, 0:1] * (1.0 - met_column(token, count))
        out = (own + ahead_2 * inv_rms(ahead_2) * gain[1, 1:2]) * live_column(count, 1, slots)
        return pieces_of(out, where[0], seqs) + [ahead_1, ahead_2]

    *base_parts, ahead_21, ahead_22 = call(
        "second_base", second_base,
        [((slots, width), bf16)] * seqs + [((slots, features), bf16)] * 2,
        (where, *facts), start_got[0], embed, next_rows, norm_gain, after=(rows_1,),
    )
    base_got = trade_seq(base_parts)

    first_own, first_send = project(
        "gate_up_1", rows_1_all, expert_weight, 0, (0, 1), parts, after=(ahead_21,)
    )
    first = pair_seq(first_own, first_send)

    def base_order(where, *got):
        return [payload(in_order([g.astype(f32) for g in got], where[0], 0))]

    (base_2,) = call("base_order", base_order, [packed], (where,), *base_got, after=(first_send,))
    base_2_all = gather_dp(base_2)

    def forward_1(own, other):
        both = own + other.astype(f32)
        gate, up = both[:, :hidden_units], both[:, hidden_units:]
        return gate * jax.nn.sigmoid(gate) * up, both

    (act_1, both_1), out_blocks = expand(
        "down_1", forward_1, first,
        [((total, hidden_units), bf16), ((total, 2 * hidden_units), f32)],
        expert_weight, 0, (2,), groups, parts, after=(base_2,),
    )
    out_got = return_dp(out_blocks)

    def slot_facts(*blocks):
        facts = jnp.concatenate(
            [block[:rows].astype(f32)[:, width // parts :] for block in blocks], 0
        )
        base = (iota((total, 1), 0) // slots * tokens).astype(f32)
        first, second = facts[:, 0:1] + base, facts[:, 1:2] + base
        live = (facts[:, 3:4] > 0) & (as_row(facts[:, 2:3]) > 0)
        same = ((second == as_row(first)) & live).astype(f32)
        return same, same, same[:rows, :rows], decoded(facts, 4)

    same, same_16, same_own, weight_1 = call(
        "slot_facts", slot_facts,
        [((total, total), f32), ((total, total), bf16), ((rows, rows), f32), ((total, 1), f32)],
        (), *dout_2_all, after=(out_blocks[0],),
    )
    fixed_own, fixed_send = project(
        "fixed_2", base_2_all, expert_weight, 1, (0, 1), parts,
        others=(dout_2_all, (2,)), after=(out_blocks[0],),
    )
    fixed_pair = pair_seq(fixed_own, fixed_send)

    def second_prev(own_facts, rows_1, *got):
        value = unfolded(rows_1.astype(f32), parts) + summed(got, parts) * decoded(own_facts, 4)
        return payload(value), value.astype(bf16)

    prev, prev_own = call(
        "second_prev", second_prev, [packed, ((rows, width), bf16)],
        (), own_facts, rows_1, *out_got, after=(fixed_own,),
    )
    prev_all = gather_dp(prev)

    hidden, _ = lax.optimization_barrier((source, rows_1))
    hidden = ring(hidden, "section", 1)
    dense = dense_rows(
        "dense_a", *facts, hidden, embed, next_rows, cot, norm_gain, None, 0, 2,
        after=(prev, fixed_pair[1]),
    )

    mixed_own, mixed_send, chosen = project(
        "gate_up_2", prev_all, expert_weight, 1, (0, 1), parts,
        select=(where, same_16), gain=norm_gain, after=(dense[1],),
    )
    second = pair_seq(mixed_own, mixed_send)
    prev_w_own, prev_w_send = project(
        "prev_down", prev_all, expert_weight, 0, (2,), parts, after=(mixed_send,)
    )
    prev_pair = pair_seq(prev_w_own, prev_w_send)

    def gates_back(gate, up, d_act):
        sig = jax.nn.sigmoid(gate)
        d_gate = d_act * up * sig * (1.0 + gate * (1.0 - sig))
        return d_gate, d_act * gate * sig

    def backward_2(own, other, fixed_own, fixed_other, same):
        many = 2 * hidden_units
        square = own[:, many : many + 1] + decoded(other[:, many:])
        scale = lax.rsqrt(square / features + eps_norm)
        row = jnp.sum(same * as_row(scale), axis=1, keepdims=True)
        both = (own[:, :many] + other[:, :many].astype(f32)) * row
        fixed = fixed_own + fixed_other.astype(f32)
        both = both + fixed[:, :many]
        gate, up = both[:, :hidden_units], both[:, hidden_units:]
        d_gate, d_up = gates_back(gate, up, fixed[:, many:])
        return d_gate, d_up, gate * jax.nn.sigmoid(gate) * up, scale, row

    units = ((total, hidden_units), bf16)
    (d_gate_2, d_up_2, act_2, scale_2, row_2), d_rows_blocks = expand(
        "back_rows_2", backward_2,
        second + fixed_pair + (same,),
        [units, units, units, ((total, 1), f32), ((total, 1), f32)],
        expert_weight, 1, (0, 1), groups, parts, after=(prev_w_own, prev_pair[1]),
    )
    d_rows_got = return_dp(d_rows_blocks)
    dense, dense_terms = dense_rows(
        "dense_b", *facts, hidden, embed, next_rows, cot, norm_gain, dense, 1, 2,
        after=(d_rows_blocks[0],),
    )
    def first_grad(where, cot, same, gain, *got):
        d_rows = summed(got, parts)
        added = lax.dot_general(
            same, d_rows, (((0,), (0,)), ((), ())),
            precision=lax.Precision.HIGHEST, preferred_element_type=f32,
        )
        d_mixed = cot + added
        u = d_mixed * piece_of(gain[1, 0:1], where[0], seqs, 0)
        return [payload(u), d_mixed] + blocks_of(d_rows, where[0], seqs)

    u, d_mixed_2, *d_rows_back = call(
        "first_grad", first_grad, [packed, part_rows] + [((slots, width), bf16)] * seqs,
        (where,), cot_1, same_own, norm_gain, *d_rows_got, after=(dense_terms,),
    )
    u_all = gather_dp(u)
    dense, _ = lax.optimization_barrier((dense, u))
    dense = ring(dense, "section", -1)
    back_got = trade_seq(d_rows_back)

    def build_2(values, g):
        chosen, row, base, dout = values[0], values[1], values[2 : 2 + groups], values[2 + groups :]
        step = width // parts
        first = chosen[:, g * step : (g + 1) * step].astype(f32) * row
        first = first + column_part(base, rows, g).astype(f32)
        return first.astype(bf16), column_part(dout, rows, g)[:, :step]

    weight_grad, tick_2 = outer(
        "weight_grad_2", 1, depths, build_2, [chosen, row_2] + base_2_all + dout_2_all,
        d_gate_2, d_up_2, act_2, width, parts, None, after=(u, back_got[-1]),
    )

    back_1_own, back_1_send = project(
        "back_1", u_all, expert_weight, 0, (2,), parts, mates=prev_all, after=(tick_2,)
    )
    back_1 = pair_seq(back_1_own, back_1_send)

    def second_grad(where, token, count, start, ahead_1, ahead_2, cot, gain, terms, *got):
        d_rows = in_order([g.astype(f32) for g in got], where[0], 1)
        keep = live_column(count, 1, slots) * (1.0 - met_column(token, count))
        grad, more = backward_rows(
            start[:, width + lanes :].astype(f32), ahead_1.astype(f32), ahead_2.astype(f32),
            pick(token_column(token, 1), cot) + d_rows, keep, gain,
        )
        notes = in_lanes([live_column(count, 0, slots), keep])
        grad = jnp.concatenate([grad.astype(f32), notes], 1)
        return [grad] + pieces_of(terms + more, where[0], seqs)

    grad_2, *terms_parts = call(
        "second_grad", second_grad,
        [((slots, features + lanes), bf16)] + [((2 * depths, width), f32)] * seqs,
        (where, *facts), start_got[0], ahead_21, ahead_22, cot, norm_gain, dense_terms, *back_got,
        after=(back_1_send,),
    )
    grad_2 = ring(grad_2, "section", -1)
    terms_got = trade_seq(terms_parts)

    def backward_1(own, other, prev_own, prev_other, both, scale, weight_1):
        inner = own[:, hidden_units : hidden_units + 1] + decoded(other[:, hidden_units:])
        d_act = own[:, :hidden_units] + other[:, :hidden_units].astype(f32)
        through = scale * scale * inner / features
        d_act = d_act - through * (prev_own + prev_other.astype(f32))
        d_act = d_act * (weight_1 * scale)
        d_gate, d_up = gates_back(both[:, :hidden_units], both[:, hidden_units:], d_act)
        return d_gate, d_up, through

    (d_gate_1, d_up_1, through_1), d_rows_blocks = expand(
        "back_rows_1", backward_1,
        back_1 + prev_pair + (both_1, scale_2, weight_1),
        [units, units, ((total, 1), f32)],
        expert_weight, 0, (0, 1), groups, parts, after=(terms_parts[0],),
    )
    d_rows_got = return_dp(d_rows_blocks)

    def build_1(values, g):
        through, scale, weight = values[:3]
        first, u, prev = (values[3 + k * groups : 3 + (k + 1) * groups] for k in range(3))
        dout = column_part(u, rows, g).astype(f32) - through * column_part(prev, rows, g).astype(f32)
        return column_part(first, rows, g), (dout * (weight * scale)).astype(bf16)

    weight_grad, tick_1 = outer(
        "weight_grad_1", 0, depths, build_1,
        [through_1, scale_2, weight_1] + rows_1_all + u_all + prev_all,
        d_gate_1, d_up_1, act_1, width, parts, weight_grad, after=(d_rows_blocks[0],),
    )

    def last_grad(where, d_mixed_2, prev, scale, through, unit_1, unit_e1, unit_e2, own_facts, gain, *got):
        got, terms = got[:groups], got[groups:]
        d_rows = summed(got, parts)
        gain_1, gain_2 = (piece_of(gain[k, 0:1], where[0], seqs, 0) for k in range(2))
        scale, through = scale[:rows], through[:rows]
        live = own_facts[:, 2:3]
        prev = prev.astype(f32)
        grad_1 = (d_mixed_2 * gain_2 - through * prev) * scale
        d_mixed_1 = grad_1 + d_rows
        kept_1, kept_2 = d_mixed_1 * live, d_mixed_2 * live
        sums = [
            jnp.sum(a * b, axis=0, keepdims=True)
            for a, b in ((kept_1, unit_1), (kept_1, unit_e1), (kept_2, prev * scale), (kept_2, unit_e2))
        ]
        sums = jnp.concatenate(sums, 0) + sum(terms)
        cut = []
        for i in range(groups):
            block = sums[:, :share]
            for z in range(groups):
                at = partner(z, i, groups) * share
                block = jnp.where(where[1] == z, sums[:, at : at + share], block)
            cut.append(block)
        return cut + blocks_of(d_mixed_1 * gain_1, where[0], seqs)

    last = call(
        "last_grad", last_grad,
        [((2 * depths, share), f32)] * groups + [((slots, width), bf16)] * seqs,
        (where,), d_mixed_2, prev_own, scale_2, through_1, unit_1, unit_e1, unit_e2,
        own_facts, norm_gain, *d_rows_got, *terms_got, after=(tick_1,),
    )
    last_got = trade_seq(last[groups:], -1)
    sums_got = return_dp(last[:groups])

    def finish(where, token, dense, asked_rows, grad_2, *got):
        part = in_order([g.astype(f32) for g in got], where[0], 1)
        asked_rows = asked_rows.astype(f32)
        scale = inv_rms(asked_rows)
        unit = asked_rows * scale
        grad_1 = (part - unit * jnp.mean(part * unit, axis=-1, keepdims=True)) * scale
        notes = grad_2[:, features:].astype(f32)
        grads = jnp.concatenate([grad_1, grad_2[:, :features].astype(f32)], 0).astype(bf16)
        lane = iota((slots, tokens), 1)
        chosen = jnp.concatenate(
            [
                jnp.where(lane == token_column(token, k), notes[:, k : k + 1], 0.0)
                for k in range(2)
            ],
            0,
        ).astype(bf16)
        taken = lax.dot_general(
            chosen, jnp.ones((2 * slots, lanes), bf16), (((0,), (0,)), ((), ())),
            preferred_element_type=f32,
        )[:, 0:1]
        out = []
        step = chunk_of(features)
        for at in range(0, features, step):
            placed = lax.dot_general(
                chosen, grads[:, at : at + step], (((0,), (0,)), ((), ())),
                preferred_element_type=f32,
            )
            out.append(jnp.where(taken > 0, placed, dense[:, at : at + step].astype(f32)).astype(bf16))
        return [jnp.concatenate(out, 1), jnp.zeros((8, lanes), f32)]

    hidden_grad, tick = call(
        "finish", finish, [((tokens, features), bf16), ((8, lanes), f32)],
        (where, asked_token), dense, asked_rows, grad_2, *last_got, limit=20,
    )

    def gain_sum(*got):
        sums = sum(got)
        return [jnp.stack([sums[2 * k : 2 * k + 2] for k in range(depths)])[None]]

    (gain_grad,) = call(
        "gain_sum", gain_sum, [((1, depths, 2, share), f32)], (), *sums_got, after=(tick,)
    )
    return (
        hidden_grad[None, None],
        weight_grad,
        gain_grad,
    )


def solution(mesh):
    return jax.shard_map(
        local,
        mesh=mesh,
        in_specs=(
            P("section", "dp", "seq", None),
            P("section", "dp", "seq", None),
            P("section", "dp", "seq", None),
            P("section", "dp", None, "seq"),
            P("section", "dp", None, "seq"),
            P("section", "dp", None, "seq"),
            P(),
            P(None, None, "seq", "dp"),
        ),
        out_specs=(
            P("section", "dp", "seq", None),
            P("section", None, None, "seq", "dp"),
            P("section", None, None, ("seq", "dp")),
        ),
        check_vma=False,
    )
```

```python
import jax
import jax.numpy as jnp
from jax import lax
from jax.experimental import pallas as pl
from jax.experimental.pallas import tpu as pltpu
from jax.sharding import PartitionSpec as P

eps_norm = 1e-06
lanes = 128
f32 = jnp.float32
bf16 = jnp.bfloat16
vmem = pl.BlockSpec(memory_space=pltpu.VMEM)
smem = pl.BlockSpec(memory_space=pltpu.SMEM)
anywhere = pl.BlockSpec(memory_space=pl.ANY)


def ring(value, axis, steps):
    count = lax.axis_size(axis)
    return lax.ppermute(value, axis, [(i, (i + steps) % count) for i in range(count)])


def hop(value, section_step, seq_step):
    sections, seqs = lax.axis_size("section"), lax.axis_size("seq")
    pairs = [
        (c * seqs + s, (c + section_step) % sections * seqs + (s + seq_step) % seqs)
        for c in range(sections)
        for s in range(seqs)
    ]
    return lax.ppermute(value, ("section", "seq"), pairs)


def trade_seq(pieces, section_step=0):
    if section_step == 0:
        return [pieces[0]] + [ring(pieces[o], "seq", o) for o in range(1, len(pieces))]
    return [hop(piece, section_step, o) for o, piece in enumerate(pieces)]


def partner(place, step, count):
    return place ^ step if count & (count - 1) == 0 else (place - step) % count


def gather_dp(block):
    count = lax.axis_size("dp")
    return [block] + [
        lax.ppermute(block, "dp", [(partner(z, i, count), z) for z in range(count)])
        for i in range(1, count)
    ]


def return_dp(blocks):
    count = lax.axis_size("dp")
    return [blocks[0]] + [
        lax.ppermute(blocks[i], "dp", [(z, partner(z, i, count)) for z in range(count)])
        for i in range(1, count)
    ]


def pair_seq(own, send):
    if lax.axis_size("seq") == 2:
        return own, ring(send, "seq", 1)
    return lax.psum(own, "seq"), jnp.zeros_like(send)


def inv_rms(value):
    return lax.rsqrt(jnp.mean(value * value, axis=-1, keepdims=True) + eps_norm)


def iota(shape, dim):
    return lax.broadcasted_iota(jnp.int32, shape, dim)


def token_column(token, depth):
    capacity = token.shape[3]
    out = jnp.full((capacity, 1), token[0, 0, depth, 0], jnp.int32)
    for c in range(1, capacity):
        out = jnp.where(iota((capacity, 1), 0) == c, token[0, 0, depth, c], out)
    return out


def gate_column(gate, depth):
    capacity = gate.shape[3]
    out = jnp.full((capacity, 1), gate[0, 0, depth, 0], f32)
    for c in range(1, capacity):
        out = jnp.where(iota((capacity, 1), 0) == c, gate[0, 0, depth, c], out)
    return out


def live_column(count, depth, capacity):
    return (iota((capacity, 1), 0) < count[0, 0, depth, 0]).astype(f32)


def met_column(token, count):
    capacity = token.shape[3]
    second = token_column(token, 1)
    out = jnp.zeros((capacity, 1), f32)
    for c in range(capacity):
        out += ((second == token[0, 0, 0, c]) & (c < count[0, 0, 0, 0])).astype(f32)
    return jnp.minimum(out, 1.0)


def pick(column, table):
    hot = (column == iota((column.shape[0], table.shape[0]), 1)).astype(bf16)
    return jnp.dot(hot, table, preferred_element_type=f32)


def pick_ahead(column, table, after):
    return pick(column, table) + pick(column - table.shape[0], after)


def thirds(column):
    high = column.astype(bf16).astype(f32)
    mid = (column - high).astype(bf16).astype(f32)
    return [high, mid, column - high - mid]


def in_lanes(columns):
    lane = iota((columns[0].shape[0], lanes), 1)
    out = jnp.zeros(lane.shape, f32)
    for k, column in enumerate(columns):
        out = jnp.where(lane == k, column, out)
    return out


def coded(column):
    return in_lanes(thirds(column))


def decoded(block, first=0):
    lane = iota(block.shape, 1)
    inside = (lane >= first) & (lane < first + 3)
    return jnp.sum(jnp.where(inside, block.astype(f32), 0.0), axis=1, keepdims=True)


def piece_of(value, place, count, step):
    width = value.shape[-1] // count
    want = lax.rem(place + step, count)
    out = value[:, :width]
    for p in range(1, count):
        out = jnp.where(want == p, value[:, p * width : (p + 1) * width], out)
    return out


def pieces_of(value, place, count):
    return [piece_of(value, place, count, o) for o in range(count)]


def blocks_of(value, place, count):
    size = value.shape[0] // count
    out = []
    for o in range(count):
        block = value[:size]
        for j in range(1, count):
            want = lax.rem(place + o, count) == j
            block = jnp.where(want, value[j * size : (j + 1) * size], block)
        out.append(block)
    return out


def in_order(got, place, axis):
    count = len(got)
    out = []
    for j in range(count):
        block = got[0]
        for o in range(1, count):
            block = jnp.where(lax.rem(place - o + count, count) == j, got[o], block)
        out.append(block)
    return jnp.concatenate(out, axis)


def as_row(column):
    size = column.shape[0]
    here = iota((size, size), 0) == iota((size, size), 1)
    return jnp.sum(jnp.where(here, column, 0.0), axis=0, keepdims=True)


def folds(rows, width):
    for count in (1, 2, 4, 8):
        if rows * count % 16 == 0 and width % (count * lanes) == 0:
            return count
    return 1


def folded(value, count):
    step = value.shape[1] // count
    return jnp.concatenate([value[:, g * step : (g + 1) * step] for g in range(count)], 0)


def unfolded(value, count):
    rows = value.shape[0] // count
    return jnp.concatenate([value[g * rows : (g + 1) * rows] for g in range(count)], 1)


def column_part(blocks, rows, g):
    return jnp.concatenate(
        [block[g * rows : (g + 1) * rows].astype(f32) for block in blocks], 0
    ).astype(bf16)


def summed(got, parts):
    return unfolded(sum(g.astype(f32) for g in got), parts)


def chunk_of(width):
    for step in (1024, 896, 512, 256, 128):
        if width % step == 0:
            return step
    return width


def call(name, fn, outs, small, *args, after=(), flops=0, limit=12):
    shapes = [jax.ShapeDtypeStruct(shape, kind) for shape, kind in outs]
    n_small, n_args, n_after = len(small), len(args), len(after)

    def body(*refs):
        values = list(refs[:n_small]) + [r[...] for r in refs[n_small : n_small + n_args]]
        for ref, value in zip(refs[n_small + n_args + n_after :], fn(*values)):
            ref[...] = value.astype(ref.dtype)

    size = sum(a.size * a.dtype.itemsize for a in list(args) + shapes)
    return pl.pallas_call(
        body,
        name=name,
        out_shape=shapes,
        in_specs=[smem] * n_small + [vmem] * n_args + [anywhere] * n_after,
        out_specs=[vmem] * len(shapes),
        compiler_params=pltpu.CompilerParams(vmem_limit_bytes=limit << 20),
        cost_estimate=pl.CostEstimate(flops=flops, bytes_accessed=size, transcendentals=0),
    )(*small, *args, *after)


def fetch(weight_ref, depth, kinds, buffer, sems, parts):
    step = weight_ref.shape[2] // parts
    copies = []
    for g in range(parts):
        row = []
        for k, kind in enumerate(kinds):
            copy = pltpu.make_async_copy(
                weight_ref.at[depth, kind, pl.ds(g * step, step)],
                buffer.at[g, k],
                sems.at[g, k],
            )
            copy.start()
            row.append(copy)
        copies.append(row)
    return copies


def fetched(weight, kinds, parts):
    hidden = weight.shape[3]
    return [
        pltpu.VMEM((parts, len(kinds), weight.shape[2] // parts, hidden), bf16),
        pltpu.SemaphoreType.DMA((parts, len(kinds))),
    ]


def project(name, blocks, weight, depth, kinds, parts, others=None, select=None, gain=None, mates=None, after=()):
    groups = len(blocks)
    rows = blocks[0].shape[0] // parts // (1 if others is None else 2)
    width, hidden = weight.shape[2:]
    step = width // parts
    other_kinds = others if others is not None else ()
    first_kinds, kinds = kinds, kinds + other_kinds
    total, many = rows * groups, len(kinds) * hidden
    marked = select is not None or mates is not None
    extra = lanes if marked else 0

    def body(*refs):
        refs = list(refs)
        where_ref = refs.pop(0) if select is not None else None
        x_refs, w_ref, refs = refs[:groups], refs[groups], refs[groups + 1 :]
        if select is not None:
            select_ref, gain_ref = refs.pop(0), refs.pop(0)
        if mates is not None:
            mate_refs, refs = refs[:groups], refs[groups:]
        refs = refs[len(after) :]
        own_ref, send_ref = refs.pop(0), refs.pop(0)
        kept_ref = refs.pop(0) if select is not None else None
        buffer, sems = refs
        copies = fetch(w_ref, depth, kinds, buffer, sems, parts)
        x_all = [r[...] for r in x_refs]
        mate_all = [r[...] for r in mate_refs] if mates is not None else x_all
        if select is not None:
            gain_all = piece_of(gain_ref[1, 0:1, :], where_ref[0], gain.shape[2] // width, 0)
        sums = [jnp.zeros((total, hidden), f32) for _ in kinds]
        mark = jnp.zeros((total, 1), f32)
        for g in range(parts):
            x = column_part(x_all, rows, g)[:, :step]
            if marked:
                mate = x if mates is None else column_part(mate_all, rows, g)
                mark += jnp.sum(x.astype(f32) * mate.astype(f32), axis=1, keepdims=True)
            if select is not None:
                chosen = jnp.dot(select_ref[...], x, preferred_element_type=f32)
                x = (chosen * gain_all[:, g * step : (g + 1) * step]).astype(bf16)
                kept_ref[:, g * step : (g + 1) * step] = x
            for k in range(len(kinds)):
                if k == len(first_kinds):
                    x = column_part(x_all, rows, parts + g)[:, :step]
                copies[g][k].wait()
                sums[k] += jnp.dot(x, buffer[g, k], preferred_element_type=f32)
        for k in range(len(kinds)):
            own_ref[:, k * hidden : (k + 1) * hidden] = sums[k]
            send_ref[:, k * hidden : (k + 1) * hidden] = sums[k].astype(bf16)
        if marked:
            own_ref[:, many:] = in_lanes([mark])
            send_ref[:, many:] = coded(mark).astype(bf16)

    args = list(blocks) + [pltpu.with_memory_space_constraint(weight, pltpu.HBM)]
    specs = [vmem] * groups + [anywhere]
    outs = [
        jax.ShapeDtypeStruct((total, many + extra), f32),
        jax.ShapeDtypeStruct((total, many + extra), bf16),
    ]
    if select is not None:
        where, table = select
        args, specs = [where] + args + [table, gain], [smem] + specs + [vmem, vmem]
        outs.append(jax.ShapeDtypeStruct((total, width), bf16))
    if mates is not None:
        args, specs = args + list(mates), specs + [vmem] * groups
    return pl.pallas_call(
        body,
        name=name,
        in_specs=specs + [anywhere] * len(after),
        out_specs=[vmem] * len(outs),
        out_shape=outs,
        scratch_shapes=fetched(weight, kinds, parts),
        compiler_params=pltpu.CompilerParams(vmem_limit_bytes=16 << 20),
        cost_estimate=pl.CostEstimate(
            flops=2 * total * width * many, bytes_accessed=2 * width * many, transcendentals=0
        ),
    )(*args, *after)


def expand(name, prepare, args, saved, weight, depth, kinds, groups, parts, after=()):
    width, hidden = weight.shape[2:]
    total = saved[0][0][0]
    rows, step = total // groups, width // parts
    count, kept = len(args), len(saved)

    def body(*refs):
        in_refs, w_ref = refs[:count], refs[count]
        refs = refs[count + 1 + len(after) :]
        saved_refs, out_refs, (buffer, sems) = refs[:kept], refs[kept:-2], refs[-2:]
        copies = fetch(w_ref, depth, kinds, buffer, sems, parts)
        for ref, value in zip(saved_refs, prepare(*[r[...] for r in in_refs])):
            ref[...] = value.astype(ref.dtype)
        out = []
        for g in range(parts):
            part = jnp.zeros((total, step), f32)
            for k in range(len(kinds)):
                copies[g][k].wait()
                part += lax.dot_general(
                    saved_refs[k][...], buffer[g, k], (((1,), (1,)), ((), ())),
                    preferred_element_type=f32,
                )
            out.append(part)
        for z in range(groups):
            block = jnp.concatenate([part[z * rows : (z + 1) * rows] for part in out], 0)
            out_refs[z][...] = block.astype(bf16)

    results = pl.pallas_call(
        body,
        name=name,
        in_specs=[vmem] * count + [anywhere] * (1 + len(after)),
        out_specs=[vmem] * (kept + groups),
        out_shape=[jax.ShapeDtypeStruct(shape, kind) for shape, kind in saved]
        + [jax.ShapeDtypeStruct((rows * parts, step), bf16)] * groups,
        scratch_shapes=fetched(weight, kinds, parts),
        compiler_params=pltpu.CompilerParams(vmem_limit_bytes=16 << 20),
        cost_estimate=pl.CostEstimate(
            flops=2 * total * width * hidden * len(kinds),
            bytes_accessed=2 * width * hidden * len(kinds),
            transcendentals=0,
        ),
    )(*args, pltpu.with_memory_space_constraint(weight, pltpu.HBM), *after)
    return results[:kept], results[kept:]


def outer(name, depth, depths, build, args, d_gate, d_up, act, width, parts, before, after=()):
    total, hidden = act.shape
    step = width // parts
    count = len(args)
    earlier = [] if before is None else [pltpu.with_memory_space_constraint(before, pltpu.HBM)]

    def contract(left, right):
        return lax.dot_general(left, right, (((0,), (0,)), ((), ())), preferred_element_type=f32)

    def body(*refs):
        values = [r[...] for r in refs[:count]]
        gate_ref, up_ref, act_ref = refs[count : count + 3]
        out_ref, tick_ref, buffer, sems = refs[-4:]
        tick_ref[...] = jnp.zeros_like(tick_ref)
        copies = []
        for g in range(parts):
            rows, dout = build(values, g)
            pairs = ((rows, gate_ref), (rows, up_ref), (dout, act_ref))
            for k, (left, right_ref) in enumerate(pairs):
                buffer[g, k] = contract(left, right_ref[...]).astype(bf16)
                copy = pltpu.make_async_copy(
                    buffer.at[g, k],
                    out_ref.at[0, depth, k, pl.ds(g * step, step)],
                    sems.at[g, k],
                )
                copy.start()
                copies.append(copy)
        for copy in copies:
            copy.wait()

    return pl.pallas_call(
        body,
        name=name,
        in_specs=[vmem] * (count + 3) + [anywhere] * (len(earlier) + len(after)),
        out_specs=[anywhere, vmem],
        out_shape=[
            jax.ShapeDtypeStruct((1, depths, 3, width, hidden), bf16),
            jax.ShapeDtypeStruct((8, lanes), f32),
        ],
        input_output_aliases={} if before is None else {count + 3: 0},
        scratch_shapes=[
            pltpu.VMEM((parts, 3, step, hidden), bf16),
            pltpu.SemaphoreType.DMA((parts, 3)),
        ],
        compiler_params=pltpu.CompilerParams(vmem_limit_bytes=24 << 20),
        cost_estimate=pl.CostEstimate(
            flops=6 * total * width * hidden, bytes_accessed=6 * width * hidden, transcendentals=0
        ),
    )(*args, d_gate, d_up, act, *earlier, *after)


def backward_rows(hidden, ahead_1, ahead_2, d_mixed_2, keep, gain):
    scale_1 = inv_rms(hidden)
    unit_1 = hidden * scale_1
    unit_e1 = ahead_1 * inv_rms(ahead_1)
    unit_e2 = ahead_2 * inv_rms(ahead_2)
    mixed = (unit_1 * gain[0, 0:1] + unit_e1 * gain[0, 1:2]).astype(bf16).astype(f32)
    scale_2 = inv_rms(mixed)
    unit_2 = mixed * scale_2
    u = d_mixed_2 * gain[1, 0:1]
    grad_1 = (u - unit_2 * jnp.mean(u * unit_2, axis=-1, keepdims=True)) * scale_2
    v = grad_1 * gain[0, 0:1]
    grad_0 = (v - unit_1 * jnp.mean(v * unit_1, axis=-1, keepdims=True)) * scale_1
    kept_1, kept_2 = grad_1 * keep, d_mixed_2 * keep
    terms = [
        jnp.sum(a * b, axis=0, keepdims=True)
        for a, b in ((kept_1, unit_1), (kept_1, unit_e1), (kept_2, unit_2), (kept_2, unit_e2))
    ]
    return grad_0.astype(bf16), jnp.concatenate(terms, 0)


def dense_rows(name, token, count, hidden, embed, next_rows, cotangent, gain, before, half, halves, after=()):
    tokens, width = hidden.shape
    step = next_rows.shape[0]
    blocks = tokens // step // halves
    low, last = half * blocks, tokens // step - 1
    size = 2 * lanes
    capacity = token.shape[3]
    earlier = [] if before is None else list(before)

    def body(token_ref, count_ref, hidden_ref, embed_ref, next_ref, cot_ref, gain_ref, *refs):
        out_ref, terms_ref, mixed_ref, sums_ref = refs[-4:]
        sums_ref[...] = jnp.zeros_like(sums_ref)
        row, column = (iota((2 * step, 2 * step), dim) for dim in range(2))
        shift = (column == jnp.where(row < step, row + 1, row + 2 - step)).astype(bf16)
        places = [pl.ds(at, size) for at in range(0, width, size)]

        def folded_lanes(value):
            return sum(value[:, at : at + lanes] for at in range(0, size, lanes))

        def mean(value):
            return jnp.sum(value, axis=1, keepdims=True) / width

        def one(i, carry):
            block = low + i
            first = pl.multiple_of(block * step, step)
            rows = pl.ds(first, step)
            follow = pl.ds(pl.multiple_of(jnp.minimum(block + 1, last) * step, step), step)
            here = iota((step, 1), 0) + first
            keep = jnp.ones((step, 1), f32)
            for k in range(2):
                for c in range(capacity):
                    out = (here == token_ref[0, 0, k, c]) & (c < count_ref[0, 0, k, 0])
                    keep = jnp.where(out, 0.0, keep)

            def ahead(at, hot):
                after = embed_ref[follow, at]
                if half == halves - 1:
                    after = jnp.where(block == last, next_ref[:, at], after)
                both = jnp.concatenate([embed_ref[rows, at], after], 0)
                return jnp.dot(hot, both, preferred_element_type=f32)

            square_h, square_e = jnp.zeros((step, lanes), f32), jnp.zeros((2 * step, lanes), f32)
            for at in places:
                h, e = hidden_ref[rows, at].astype(f32), ahead(at, shift)
                square_h += folded_lanes(h * h)
                square_e += folded_lanes(e * e)
            scale_1 = lax.rsqrt(mean(square_h) + eps_norm)
            scale_e = lax.rsqrt(mean(square_e) + eps_norm)
            scale_e1, scale_e2 = scale_e[:step], scale_e[step:]

            sums = [jnp.zeros((step, lanes), f32) for _ in range(4)]
            for at in places:
                through = hidden_ref[rows, at].astype(f32) * scale_1 * gain_ref[0, 0:1, at]
                mixed = through + ahead(at, shift[:step]) * scale_e1 * gain_ref[0, 1:2, at]
                kept = mixed.astype(bf16)
                mixed_ref[:, at] = kept
                mixed = kept.astype(f32)
                u = cot_ref[rows, at].astype(f32) * gain_ref[1, 0:1, at]
                pairs = ((mixed, mixed), (u, mixed), (u, through), (mixed, through))
                sums = [c + folded_lanes(a * b) for c, (a, b) in zip(sums, pairs)]
            square, along, u_back, mixed_back = (mean(value) for value in sums)
            scale_2 = lax.rsqrt(square + eps_norm)
            share_2 = scale_2 * scale_2 * along
            share_1 = scale_2 * (u_back - share_2 * mixed_back) * scale_1
            keep_2, keep_h = keep * scale_2, keep * scale_1
            keep_e1, keep_e2 = keep * scale_e1, keep * scale_e2

            for at in places:
                e = ahead(at, shift)
                h = hidden_ref[rows, at].astype(f32)
                mixed = mixed_ref[:, at].astype(f32)
                cot = cot_ref[rows, at].astype(f32)
                grad_1 = (cot * gain_ref[1, 0:1, at] - mixed * share_2) * scale_2
                grad_0 = (grad_1 * gain_ref[0, 0:1, at] - h * share_1) * scale_1
                out_ref[rows, at] = grad_0.astype(bf16)
                terms = (
                    grad_1 * (h * keep_h),
                    grad_1 * (e[:step] * keep_e1),
                    cot * (mixed * keep_2),
                    cot * (e[step:] * keep_e2),
                )
                for k, term in enumerate(terms):
                    sums_ref[k, :, at] += sum(term[r : r + 8] for r in range(0, step, 8))
            return carry

        lax.fori_loop(0, blocks, one, 0)
        for k in range(4):
            term = jnp.sum(sums_ref[k], axis=0, keepdims=True)
            terms_ref[k : k + 1] = term + refs[1][k : k + 1] if earlier else term

    return pl.pallas_call(
        body,
        name=name,
        in_specs=[smem] * 2 + [vmem] * (5 + len(earlier)) + [anywhere] * len(after),
        out_specs=[vmem] * 2,
        out_shape=[
            jax.ShapeDtypeStruct((tokens, width), bf16),
            jax.ShapeDtypeStruct((4, width), f32),
        ],
        input_output_aliases={7: 0} if earlier else {},
        scratch_shapes=[pltpu.VMEM((step, width), bf16), pltpu.VMEM((4, 8, width), f32)],
        compiler_params=pltpu.CompilerParams(vmem_limit_bytes=8 << 20),
        cost_estimate=pl.CostEstimate(
            flops=60 * tokens * width // halves,
            bytes_accessed=10 * tokens * width // halves,
            transcendentals=0,
        ),
    )(token, count, hidden, embed, next_rows, cotangent, gain, *earlier, *after)


def local(
    main_hidden, embedded, cotangent, slot_token, slot_count, route_gate, norm_gain, expert_weight
):
    depths, _, features = norm_gain.shape
    tokens = main_hidden.shape[2]
    slots = slot_token.shape[3]
    seqs, groups = lax.axis_size("seq"), lax.axis_size("dp")
    rows = seqs * slots
    total = groups * rows
    width = features // seqs
    share = width // groups
    hidden_units = expert_weight.shape[3]
    parts = folds(rows, width)
    where = jnp.stack([lax.axis_index("seq"), lax.axis_index("dp")]).astype(jnp.int32)
    source, embed, cot = main_hidden[0, 0], embedded[0, 0], cotangent[0, 0]
    facts = (slot_token, slot_count)
    packed = ((rows * parts, width // parts), bf16)
    part_rows = ((rows, width), f32)

    def payload(value):
        return folded(value, parts)

    asked_token = ring(slot_token, "section", -1)

    def own_rows(where, token, count, gate, embed, cot):
        first, second = token_column(token, 0), token_column(token, 1)
        live_1, live_2 = (live_column(count, k, slots) for k in range(2))
        weight_1, weight_2 = gate_column(gate, 0) * live_1, gate_column(gate, 1) * live_2
        facts = in_lanes(
            [first.astype(f32), second.astype(f32), live_1, live_2]
            + thirds(weight_1)
            + thirds(weight_2)
        )
        ahead_1, ahead_2 = pick(first + 1, embed), pick(first + 2, embed)
        block = jnp.concatenate([ahead_1, ahead_2, pick(first, cot), pick(second, cot) * weight_2], 0)
        notes = jnp.concatenate([coded(inv_rms(ahead_1)), coded(inv_rms(ahead_2)), facts, facts], 0)
        head = embed[:depths].astype(f32)
        scale = coded(inv_rms(head))
        heads = [
            jnp.concatenate([head[:, p * width : (p + 1) * width], scale], 1) for p in range(seqs)
        ]
        return [
            jnp.concatenate([jnp.concatenate([piece, notes], 1)] + heads, 0)
            for piece in pieces_of(block, where[0], seqs)
        ]

    own_sent = call(
        "own_rows", own_rows, [((4 * slots + depths * seqs, width + lanes), bf16)] * seqs,
        (where, slot_token, slot_count, route_gate), embed, cot, after=(asked_token,),
    )
    own_got = trade_seq(own_sent)

    def source_rows(where, asked, source):
        first = pick(token_column(asked, 0), source)
        second = pick(token_column(asked, 1), source)
        scale = coded(inv_rms(first))
        sent = [jnp.concatenate([p, scale], 1) for p in pieces_of(first, where[0], seqs)]
        sent[0] = jnp.concatenate([sent[0], second], 1)
        return sent + [first]

    *sent, asked_rows = call(
        "source_rows", source_rows,
        [((slots, width + lanes + features), bf16)]
        + [((slots, width + lanes), bf16)] * (seqs - 1)
        + [((slots, features), bf16)],
        (where, asked_token), source, after=(own_sent[0],),
    )
    start_got = trade_seq(sent, 1)

    def own_parts(where, *got):
        got = [g.astype(f32) for g in got]
        first = 4 * slots
        block_1, block_2, block_3, block_4 = (
            in_order([g[k * slots : (k + 1) * slots] for g in got], where[0], 0) for k in range(4)
        )
        facts = block_3[:, width:]
        heads = in_order([g[first:] for g in got], where[0], 0)
        heads = [heads[j * depths * seqs : (j + 1) * depths * seqs] for j in range(seqs)]
        units = []
        for k, block in ((1, block_1), (2, block_2)):
            unit = block[:, :width] * decoded(block[:, width:])
            after = []
            for j in range(seqs):
                token = facts[j * slots : (j + 1) * slots, 0:1]
                add = jnp.zeros((slots, width), f32)
                for i in range(k if j + 1 < seqs else 0):
                    row = heads[j + 1][i : i + 1]
                    for p in range(1, seqs):
                        at = p * depths + i
                        row = jnp.where(where[0] == p, heads[j + 1][at : at + 1], row)
                    row = row[:, :width] * decoded(row[:, width:])
                    add += jnp.where(token == float(tokens + i - k), row, 0.0)
                after.append(add)
            units.append(unit + jnp.concatenate(after, 0))
        out = folded(block_4[:, :width], parts)
        none = jnp.zeros(((parts - 1) * rows, lanes), f32)
        tail = facts if parts == 1 else jnp.concatenate([facts, none], 0)
        follow = got[-1][first:, :width]
        follow = jnp.concatenate([follow[p * depths : (p + 1) * depths] for p in range(seqs)], 1)
        follow = jnp.where(where[0] == seqs - 1, 0.0, follow)
        follow = jnp.concatenate([follow, jnp.zeros((16 - depths, features), f32)], 0)
        return block_3[:, :width], jnp.concatenate([out, tail], 1), facts, *units, follow

    cot_1, dout_2, own_facts, unit_e1, unit_e2, next_rows = call(
        "own_parts", own_parts,
        [part_rows, ((rows * parts, width // parts + lanes), bf16), ((rows, lanes), f32)]
        + [part_rows] * 2
        + [((16, features), bf16)],
        (where,), *own_got,
    )

    def first_mixed(where, own_facts, unit_e1, gain, *got):
        start = in_order([g[:, : width + lanes].astype(f32) for g in got], where[0], 0)
        unit = start[:, :width] * decoded(start[:, width:])
        gain_h, gain_e = (piece_of(gain[0, k : k + 1], where[0], seqs, 0) for k in range(2))
        mixed = (unit * gain_h + unit_e1 * gain_e).astype(bf16).astype(f32)
        return payload(mixed * own_facts[:, 2:3]), unit

    rows_1, unit_1 = call(
        "first_mixed", first_mixed, [packed, part_rows],
        (where,), own_facts, unit_e1, norm_gain, *start_got,
    )
    rows_1_all = gather_dp(rows_1)

    def second_base(where, token, count, start, table, after, gain):
        second = token_column(token, 1)
        start = start[:, width + lanes :].astype(f32)
        ahead_1 = pick_ahead(second + 1, table, after)
        ahead_2 = pick_ahead(second + 2, table, after)
        unit = start * inv_rms(start)
        mixed = unit * gain[0, 0:1] + ahead_1 * inv_rms(ahead_1) * gain[0, 1:2]
        mixed = mixed.astype(bf16).astype(f32)
        own = mixed * inv_rms(mixed) * gain[1, 0:1] * (1.0 - met_column(token, count))
        out = (own + ahead_2 * inv_rms(ahead_2) * gain[1, 1:2]) * live_column(count, 1, slots)
        return pieces_of(out, where[0], seqs) + [ahead_1, ahead_2]

    *base_parts, ahead_21, ahead_22 = call(
        "second_base", second_base,
        [((slots, width), bf16)] * seqs + [((slots, features), bf16)] * 2,
        (where, *facts), start_got[0], embed, next_rows, norm_gain, after=(rows_1,),
    )
    base_got = trade_seq(base_parts)

    first_own, first_send = project(
        "gate_up_1", rows_1_all, expert_weight, 0, (0, 1), parts, after=(ahead_21, base_got[-1])
    )
    first = pair_seq(first_own, first_send)

    def fixed_order(where, dout, *got):
        base = payload(in_order([g.astype(f32) for g in got], where[0], 0))
        none = jnp.zeros((base.shape[0], lanes), f32)
        return [jnp.concatenate([jnp.concatenate([base, none], 1), dout.astype(f32)], 0)]

    (fixed_rows,) = call(
        "fixed_order", fixed_order, [((2 * rows * parts, width // parts + lanes), bf16)],
        (where,), dout_2, *base_got, after=(first_send,),
    )
    fixed_all = gather_dp(fixed_rows)

    def forward_1(own, other):
        both = own + other.astype(f32)
        gate, up = both[:, :hidden_units], both[:, hidden_units:]
        return gate * jax.nn.sigmoid(gate) * up, both

    (act_1, both_1), out_blocks = expand(
        "down_1", forward_1, first,
        [((total, hidden_units), bf16), ((total, 2 * hidden_units), f32)],
        expert_weight, 0, (2,), groups, parts, after=(fixed_rows,),
    )
    out_got = return_dp(out_blocks)

    hidden, _ = lax.optimization_barrier((source, rows_1))
    hidden = ring(hidden, "section", 1)
    dense = dense_rows(
        "dense_a", *facts, hidden, embed, next_rows, cot, norm_gain, None, 0, 2,
        after=(out_blocks[0],),
    )

    def second_prev(own_facts, rows_1, *got):
        value = unfolded(rows_1.astype(f32), parts) + summed(got, parts) * decoded(own_facts, 4)
        return payload(value), value.astype(bf16)

    prev, prev_own = call(
        "second_prev", second_prev, [packed, ((rows, width), bf16)],
        (), own_facts, rows_1, *out_got, after=(dense[1],),
    )
    prev_all = gather_dp(prev)

    def slot_facts(*blocks):
        facts = jnp.concatenate(
            [block[rows * parts : rows * (parts + 1)].astype(f32)[:, width // parts :] for block in blocks], 0
        )
        base = (iota((total, 1), 0) // slots * tokens).astype(f32)
        first, second = facts[:, 0:1] + base, facts[:, 1:2] + base
        live = (facts[:, 3:4] > 0) & (as_row(facts[:, 2:3]) > 0)
        same = ((second == as_row(first)) & live).astype(f32)
        return same, same, same[:rows, :rows], decoded(facts, 4)

    same, same_16, same_own, weight_1 = call(
        "slot_facts", slot_facts,
        [((total, total), f32), ((total, total), bf16), ((rows, rows), f32), ((total, 1), f32)],
        (), *fixed_all, after=(prev,),
    )
    fixed_own, fixed_send = project(
        "fixed_2", fixed_all, expert_weight, 1, (0, 1), parts,
        others=(2,), after=(same_own,),
    )
    fixed_pair = pair_seq(fixed_own, fixed_send)

    mixed_own, mixed_send, chosen = project(
        "gate_up_2", prev_all, expert_weight, 1, (0, 1), parts,
        select=(where, same_16), gain=norm_gain, after=(fixed_own,),
    )
    second = pair_seq(mixed_own, mixed_send)
    prev_w_own, prev_w_send = project(
        "prev_down", prev_all, expert_weight, 0, (2,), parts, after=(mixed_send,)
    )
    prev_pair = pair_seq(prev_w_own, prev_w_send)

    def gates_back(gate, up, d_act):
        sig = jax.nn.sigmoid(gate)
        d_gate = d_act * up * sig * (1.0 + gate * (1.0 - sig))
        return d_gate, d_act * gate * sig

    def backward_2(own, other, fixed_own, fixed_other, same):
        many = 2 * hidden_units
        square = own[:, many : many + 1] + decoded(other[:, many:])
        scale = lax.rsqrt(square / features + eps_norm)
        row = jnp.sum(same * as_row(scale), axis=1, keepdims=True)
        both = (own[:, :many] + other[:, :many].astype(f32)) * row
        fixed = fixed_own + fixed_other.astype(f32)
        both = both + fixed[:, :many]
        gate, up = both[:, :hidden_units], both[:, hidden_units:]
        d_gate, d_up = gates_back(gate, up, fixed[:, many:])
        return d_gate, d_up, gate * jax.nn.sigmoid(gate) * up, scale, row

    units = ((total, hidden_units), bf16)
    (d_gate_2, d_up_2, act_2, scale_2, row_2), d_rows_blocks = expand(
        "back_rows_2", backward_2,
        second + fixed_pair + (same,),
        [units, units, units, ((total, 1), f32), ((total, 1), f32)],
        expert_weight, 1, (0, 1), groups, parts, after=(prev_w_own,),
    )
    d_rows_got = return_dp(d_rows_blocks)
    dense, dense_terms = dense_rows(
        "dense_b", *facts, hidden, embed, next_rows, cot, norm_gain, dense, 1, 2,
        after=(d_rows_blocks[0],),
    )
    def first_grad(where, cot, same, gain, *got):
        d_rows = summed(got, parts)
        added = lax.dot_general(
            same, d_rows, (((0,), (0,)), ((), ())),
            precision=lax.Precision.HIGHEST, preferred_element_type=f32,
        )
        d_mixed = cot + added
        u = d_mixed * piece_of(gain[1, 0:1], where[0], seqs, 0)
        return [payload(u), d_mixed] + blocks_of(d_rows, where[0], seqs)

    u, d_mixed_2, *d_rows_back = call(
        "first_grad", first_grad, [packed, part_rows] + [((slots, width), bf16)] * seqs,
        (where,), cot_1, same_own, norm_gain, *d_rows_got, after=(dense_terms, prev_pair[1]),
    )
    u_all = gather_dp(u)
    dense, _ = lax.optimization_barrier((dense, u))
    dense = ring(dense, "section", -1)
    back_got = trade_seq(d_rows_back)

    def build_2(values, g):
        chosen, row, *fixed = values
        step = width // parts
        first = chosen[:, g * step : (g + 1) * step].astype(f32) * row
        first = first + column_part(fixed, rows, g)[:, :step].astype(f32)
        return first.astype(bf16), column_part(fixed, rows, parts + g)[:, :step]

    weight_grad, tick_2 = outer(
        "weight_grad_2", 1, depths, build_2, [chosen, row_2] + fixed_all,
        d_gate_2, d_up_2, act_2, width, parts, None, after=(u, back_got[-1]),
    )

    back_1_own, back_1_send = project(
        "back_1", u_all, expert_weight, 0, (2,), parts, mates=prev_all, after=(tick_2,)
    )
    back_1 = pair_seq(back_1_own, back_1_send)

    def second_grad(where, token, count, start, ahead_1, ahead_2, cot, gain, terms, *got):
        d_rows = in_order([g.astype(f32) for g in got], where[0], 1)
        keep = live_column(count, 1, slots) * (1.0 - met_column(token, count))
        grad, more = backward_rows(
            start[:, width + lanes :].astype(f32), ahead_1.astype(f32), ahead_2.astype(f32),
            pick(token_column(token, 1), cot) + d_rows, keep, gain,
        )
        notes = in_lanes([live_column(count, 0, slots), keep])
        grad = jnp.concatenate([grad.astype(f32), notes], 1)
        return [grad] + pieces_of(terms + more, where[0], seqs)

    grad_2, *terms_parts = call(
        "second_grad", second_grad,
        [((slots, features + lanes), bf16)] + [((2 * depths, width), f32)] * seqs,
        (where, *facts), start_got[0], ahead_21, ahead_22, cot, norm_gain, dense_terms, *back_got,
        after=(back_1_send,),
    )
    grad_2 = ring(grad_2, "section", -1)
    terms_got = trade_seq(terms_parts)

    def backward_1(own, other, prev_own, prev_other, both, scale, weight_1):
        inner = own[:, hidden_units : hidden_units + 1] + decoded(other[:, hidden_units:])
        d_act = own[:, :hidden_units] + other[:, :hidden_units].astype(f32)
        through = scale * scale * inner / features
        d_act = d_act - through * (prev_own + prev_other.astype(f32))
        d_act = d_act * (weight_1 * scale)
        d_gate, d_up = gates_back(both[:, :hidden_units], both[:, hidden_units:], d_act)
        return d_gate, d_up, through

    (d_gate_1, d_up_1, through_1), d_rows_blocks = expand(
        "back_rows_1", backward_1,
        back_1 + prev_pair + (both_1, scale_2, weight_1),
        [units, units, ((total, 1), f32)],
        expert_weight, 0, (0, 1), groups, parts, after=(terms_parts[0],),
    )
    d_rows_got = return_dp(d_rows_blocks)

    def build_1(values, g):
        through, scale, weight = values[:3]
        first, u, prev = (values[3 + k * groups : 3 + (k + 1) * groups] for k in range(3))
        dout = column_part(u, rows, g).astype(f32) - through * column_part(prev, rows, g).astype(f32)
        return column_part(first, rows, g), (dout * (weight * scale)).astype(bf16)

    weight_grad, tick_1 = outer(
        "weight_grad_1", 0, depths, build_1,
        [through_1, scale_2, weight_1] + rows_1_all + u_all + prev_all,
        d_gate_1, d_up_1, act_1, width, parts, weight_grad, after=(d_rows_blocks[0],),
    )

    def last_grad(where, d_mixed_2, prev, scale, through, unit_1, unit_e1, unit_e2, own_facts, gain, *got):
        got, terms = got[:groups], got[groups:]
        d_rows = summed(got, parts)
        gain_1, gain_2 = (piece_of(gain[k, 0:1], where[0], seqs, 0) for k in range(2))
        scale, through = scale[:rows], through[:rows]
        live = own_facts[:, 2:3]
        prev = prev.astype(f32)
        grad_1 = (d_mixed_2 * gain_2 - through * prev) * scale
        d_mixed_1 = grad_1 + d_rows
        kept_1, kept_2 = d_mixed_1 * live, d_mixed_2 * live
        sums = [
            jnp.sum(a * b, axis=0, keepdims=True)
            for a, b in ((kept_1, unit_1), (kept_1, unit_e1), (kept_2, prev * scale), (kept_2, unit_e2))
        ]
        sums = jnp.concatenate(sums, 0) + sum(terms)
        cut = []
        for i in range(groups):
            block = sums[:, :share]
            for z in range(groups):
                at = partner(z, i, groups) * share
                block = jnp.where(where[1] == z, sums[:, at : at + share], block)
            cut.append(block)
        return cut + blocks_of(d_mixed_1 * gain_1, where[0], seqs)

    last = call(
        "last_grad", last_grad,
        [((2 * depths, share), f32)] * groups + [((slots, width), bf16)] * seqs,
        (where,), d_mixed_2, prev_own, scale_2, through_1, unit_1, unit_e1, unit_e2,
        own_facts, norm_gain, *d_rows_got, *terms_got, after=(tick_1,),
    )
    last_got = trade_seq(last[groups:], -1)
    sums_got = return_dp(last[:groups])

    def finish(where, token, dense, asked_rows, grad_2, *got):
        part = in_order([g.astype(f32) for g in got], where[0], 1)
        asked_rows = asked_rows.astype(f32)
        scale = inv_rms(asked_rows)
        unit = asked_rows * scale
        grad_1 = (part - unit * jnp.mean(part * unit, axis=-1, keepdims=True)) * scale
        notes = grad_2[:, features:].astype(f32)
        grads = jnp.concatenate([grad_1, grad_2[:, :features].astype(f32)], 0).astype(bf16)
        lane = iota((slots, tokens), 1)
        chosen = jnp.concatenate(
            [
                jnp.where(lane == token_column(token, k), notes[:, k : k + 1], 0.0)
                for k in range(2)
            ],
            0,
        ).astype(bf16)
        taken = lax.dot_general(
            chosen, jnp.ones((2 * slots, lanes), bf16), (((0,), (0,)), ((), ())),
            preferred_element_type=f32,
        )[:, 0:1]
        out = []
        step = chunk_of(features)
        for at in range(0, features, step):
            placed = lax.dot_general(
                chosen, grads[:, at : at + step], (((0,), (0,)), ((), ())),
                preferred_element_type=f32,
            )
            out.append(jnp.where(taken > 0, placed, dense[:, at : at + step].astype(f32)).astype(bf16))
        return [jnp.concatenate(out, 1), jnp.zeros((8, lanes), f32)]

    hidden_grad, tick = call(
        "finish", finish, [((tokens, features), bf16), ((8, lanes), f32)],
        (where, asked_token), dense, asked_rows, grad_2, *last_got, limit=20,
    )

    def gain_sum(*got):
        sums = sum(got)
        return [jnp.stack([sums[2 * k : 2 * k + 2] for k in range(depths)])[None]]

    (gain_grad,) = call(
        "gain_sum", gain_sum, [((1, depths, 2, share), f32)], (), *sums_got, after=(tick,)
    )
    return (
        hidden_grad[None, None],
        weight_grad,
        gain_grad,
    )


def solution(mesh):
    return jax.shard_map(
        local,
        mesh=mesh,
        in_specs=(
            P("section", "dp", "seq", None),
            P("section", "dp", "seq", None),
            P("section", "dp", "seq", None),
            P("section", "dp", None, "seq"),
            P("section", "dp", None, "seq"),
            P("section", "dp", None, "seq"),
            P(),
            P(None, None, "seq", "dp"),
        ),
        out_specs=(
            P("section", "dp", "seq", None),
            P("section", None, None, "seq", "dp"),
            P("section", None, None, ("seq", "dp")),
        ),
        check_vma=False,
    )
```

```python
import jax
import jax.numpy as jnp
from jax import lax
from jax.experimental import pallas as pl
from jax.experimental.pallas import tpu as pltpu
from jax.sharding import PartitionSpec as P

eps_norm = 1e-06
lanes = 128
f32 = jnp.float32
bf16 = jnp.bfloat16
vmem = pl.BlockSpec(memory_space=pltpu.VMEM)
smem = pl.BlockSpec(memory_space=pltpu.SMEM)
anywhere = pl.BlockSpec(memory_space=pl.ANY)


def ring(value, axis, steps):
    count = lax.axis_size(axis)
    return lax.ppermute(value, axis, [(i, (i + steps) % count) for i in range(count)])


def hop(value, section_step, seq_step):
    sections, seqs = lax.axis_size("section"), lax.axis_size("seq")
    pairs = [
        (c * seqs + s, (c + section_step) % sections * seqs + (s + seq_step) % seqs)
        for c in range(sections)
        for s in range(seqs)
    ]
    return lax.ppermute(value, ("section", "seq"), pairs)


def trade_seq(pieces, section_step=0):
    if section_step == 0:
        return [pieces[0]] + [ring(pieces[o], "seq", o) for o in range(1, len(pieces))]
    return [hop(piece, section_step, o) for o, piece in enumerate(pieces)]


def partner(place, step, count):
    return place ^ step if count & (count - 1) == 0 else (place - step) % count


def gather_dp(block):
    count = lax.axis_size("dp")
    return [block] + [
        lax.ppermute(block, "dp", [(partner(z, i, count), z) for z in range(count)])
        for i in range(1, count)
    ]


def return_dp(blocks):
    count = lax.axis_size("dp")
    return [blocks[0]] + [
        lax.ppermute(blocks[i], "dp", [(z, partner(z, i, count)) for z in range(count)])
        for i in range(1, count)
    ]


def pair_seq(own, send):
    if lax.axis_size("seq") == 2:
        return own, ring(send, "seq", 1)
    return lax.psum(own, "seq"), jnp.zeros_like(send)


def inv_rms(value):
    return lax.rsqrt(jnp.mean(value * value, axis=-1, keepdims=True) + eps_norm)


def iota(shape, dim):
    return lax.broadcasted_iota(jnp.int32, shape, dim)


def token_column(token, depth):
    capacity = token.shape[3]
    out = jnp.full((capacity, 1), token[0, 0, depth, 0], jnp.int32)
    for c in range(1, capacity):
        out = jnp.where(iota((capacity, 1), 0) == c, token[0, 0, depth, c], out)
    return out


def gate_column(gate, depth):
    capacity = gate.shape[3]
    out = jnp.full((capacity, 1), gate[0, 0, depth, 0], f32)
    for c in range(1, capacity):
        out = jnp.where(iota((capacity, 1), 0) == c, gate[0, 0, depth, c], out)
    return out


def live_column(count, depth, capacity):
    return (iota((capacity, 1), 0) < count[0, 0, depth, 0]).astype(f32)


def met_column(token, count):
    capacity = token.shape[3]
    second = token_column(token, 1)
    out = jnp.zeros((capacity, 1), f32)
    for c in range(capacity):
        out += ((second == token[0, 0, 0, c]) & (c < count[0, 0, 0, 0])).astype(f32)
    return jnp.minimum(out, 1.0)


def pick(column, table):
    hot = (column == iota((column.shape[0], table.shape[0]), 1)).astype(bf16)
    return jnp.dot(hot, table, preferred_element_type=f32)


def pick_ahead(column, table, after):
    return pick(column, table) + pick(column - table.shape[0], after)


def thirds(column):
    high = column.astype(bf16).astype(f32)
    mid = (column - high).astype(bf16).astype(f32)
    return [high, mid, column - high - mid]


def in_lanes(columns):
    lane = iota((columns[0].shape[0], lanes), 1)
    out = jnp.zeros(lane.shape, f32)
    for k, column in enumerate(columns):
        out = jnp.where(lane == k, column, out)
    return out


def coded(column):
    return in_lanes(thirds(column))


def decoded(block, first=0):
    lane = iota(block.shape, 1)
    inside = (lane >= first) & (lane < first + 3)
    return jnp.sum(jnp.where(inside, block.astype(f32), 0.0), axis=1, keepdims=True)


def piece_of(value, place, count, step):
    width = value.shape[-1] // count
    want = lax.rem(place + step, count)
    out = value[:, :width]
    for p in range(1, count):
        out = jnp.where(want == p, value[:, p * width : (p + 1) * width], out)
    return out


def pieces_of(value, place, count):
    return [piece_of(value, place, count, o) for o in range(count)]


def blocks_of(value, place, count):
    size = value.shape[0] // count
    out = []
    for o in range(count):
        block = value[:size]
        for j in range(1, count):
            want = lax.rem(place + o, count) == j
            block = jnp.where(want, value[j * size : (j + 1) * size], block)
        out.append(block)
    return out


def from_block(got, place, block):
    count = len(got)
    out = got[0]
    for o in range(1, count):
        out = jnp.where(lax.rem(place - o + count, count) == block, got[o], out)
    return out


def in_order(got, place, axis):
    return jnp.concatenate([from_block(got, place, j) for j in range(len(got))], axis)


def as_row(column):
    size = column.shape[0]
    here = iota((size, size), 0) == iota((size, size), 1)
    return jnp.sum(jnp.where(here, column, 0.0), axis=0, keepdims=True)


def folds(rows, width):
    for count in (1, 2, 4, 8):
        if rows * count % 16 == 0 and width % (count * lanes) == 0:
            return count
    return 1


def folded(value, count):
    step = value.shape[1] // count
    return jnp.concatenate([value[:, g * step : (g + 1) * step] for g in range(count)], 0)


def unfolded(value, count):
    rows = value.shape[0] // count
    return jnp.concatenate([value[g * rows : (g + 1) * rows] for g in range(count)], 1)


def column_part(blocks, rows, g):
    return jnp.concatenate(
        [block[g * rows : (g + 1) * rows].astype(f32) for block in blocks], 0
    ).astype(bf16)


def summed(got, parts):
    return unfolded(sum(g.astype(f32) for g in got), parts)


def chunk_of(width):
    for step in (1024, 896, 512, 256, 128):
        if width % step == 0:
            return step
    return width


def in_hbm(value):
    return pltpu.with_memory_space_constraint(value, pltpu.HBM)


def call(name, fn, outs, small, *args, far=(), after=(), flops=0, limit=12):
    shapes = [jax.ShapeDtypeStruct(shape, kind) for shape, kind in outs]
    n_small, n_args, n_far, n_outs = len(small), len(args), len(far), len(shapes)

    def body(*refs):
        refs = list(refs)

        def take(count):
            taken, refs[:] = refs[:count], refs[count:]
            return taken

        small_refs, arg_refs, far_refs = take(n_small), take(n_args), take(n_far)
        take(len(after))
        out_refs, buffers, sems = take(n_outs), take(n_far), take(n_far)
        copies = [pltpu.make_async_copy(*trio) for trio in zip(far_refs, buffers, sems)]
        for copy in copies:
            copy.start()
        for copy in copies:
            copy.wait()
        values = small_refs + [r[...] for r in arg_refs + buffers]
        for ref, value in zip(out_refs, fn(*values)):
            ref[...] = value.astype(ref.dtype)

    size = sum(a.size * a.dtype.itemsize for a in list(args) + list(far) + shapes)
    return pl.pallas_call(
        body,
        name=name,
        out_shape=shapes,
        in_specs=[smem] * n_small + [vmem] * n_args + [anywhere] * (n_far + len(after)),
        out_specs=[vmem] * n_outs,
        scratch_shapes=[pltpu.VMEM(a.shape, a.dtype) for a in far] + [pltpu.SemaphoreType.DMA] * n_far,
        compiler_params=pltpu.CompilerParams(vmem_limit_bytes=limit << 20),
        cost_estimate=pl.CostEstimate(flops=flops, bytes_accessed=size, transcendentals=0),
    )(*[in_hbm(a) for a in small], *args, *[in_hbm(a) for a in far], *after)


def fetch(weight_ref, depth, kinds, buffer, sems, parts, ahead=4):
    step = weight_ref.shape[2] // parts
    copies = [
        pltpu.make_async_copy(
            weight_ref.at[depth, kind, pl.ds(g * step, step)], buffer.at[g, k], sems.at[g, k]
        )
        for g in range(parts)
        for k, kind in enumerate(kinds)
    ]
    for copy in copies[:ahead]:
        copy.start()

    def wait(g, k):
        at = g * len(kinds) + k
        copies[at].wait()
        if at + ahead < len(copies):
            copies[at + ahead].start()

    return wait


def fetched(weight, kinds, parts):
    hidden = weight.shape[3]
    return [
        pltpu.VMEM((parts, len(kinds), weight.shape[2] // parts, hidden), bf16),
        pltpu.SemaphoreType.DMA((parts, len(kinds))),
    ]


def project(name, blocks, weight, depth, kinds, parts, others=None, select=None, gain=None, mates=None, after=()):
    groups = len(blocks)
    rows = blocks[0].shape[0] // parts
    width, hidden = weight.shape[2:]
    step = width // parts
    other_blocks, other_kinds = others if others is not None else ([], ())
    first_kinds, kinds = kinds, kinds + other_kinds
    total, many = rows * groups, len(kinds) * hidden
    marked = select is not None or mates is not None
    extra = lanes if marked else 0

    def body(*refs):
        refs = list(refs)
        where_ref = refs.pop(0) if select is not None else None
        x_refs, w_ref, refs = refs[:groups], refs[groups], refs[groups + 1 :]
        other_refs, refs = refs[: len(other_blocks)], refs[len(other_blocks) :]
        if select is not None:
            select_ref, gain_ref = refs.pop(0), refs.pop(0)
        if mates is not None:
            mate_refs, refs = refs[:groups], refs[groups:]
        refs = refs[len(after) :]
        own_ref, send_ref = refs.pop(0), refs.pop(0)
        kept_ref = refs.pop(0) if select is not None else None
        buffer, sems = refs
        wait = fetch(w_ref, depth, kinds, buffer, sems, parts)
        x_all = [r[...] for r in x_refs]
        mate_all = [r[...] for r in mate_refs] if mates is not None else x_all
        if select is not None:
            gain_all = piece_of(gain_ref[1, 0:1, :], where_ref[0], gain.shape[2] // width, 0)
        sums = [jnp.zeros((total, hidden), f32) for _ in kinds]
        mark = jnp.zeros((total, 1), f32)
        for g in range(parts):
            x = column_part(x_all, rows, g)
            if marked:
                mate = x if mates is None else column_part(mate_all, rows, g)
                mark += jnp.sum(x.astype(f32) * mate.astype(f32), axis=1, keepdims=True)
            if select is not None:
                chosen = jnp.dot(select_ref[...], x, preferred_element_type=f32)
                x = (chosen * gain_all[:, g * step : (g + 1) * step]).astype(bf16)
                kept_ref[:, g * step : (g + 1) * step] = x
            for k in range(len(kinds)):
                if k == len(first_kinds):
                    x = column_part([r[...] for r in other_refs], rows, g)[:, :step]
                wait(g, k)
                sums[k] += jnp.dot(x, buffer[g, k], preferred_element_type=f32)
        for k in range(len(kinds)):
            own_ref[:, k * hidden : (k + 1) * hidden] = sums[k]
            send_ref[:, k * hidden : (k + 1) * hidden] = sums[k].astype(bf16)
        if marked:
            own_ref[:, many:] = in_lanes([mark])
            send_ref[:, many:] = coded(mark).astype(bf16)

    args = list(blocks) + [in_hbm(weight)]
    args, specs = args + list(other_blocks), [vmem] * groups + [anywhere] + [vmem] * len(other_blocks)
    outs = [
        jax.ShapeDtypeStruct((total, many + extra), f32),
        jax.ShapeDtypeStruct((total, many + extra), bf16),
    ]
    if select is not None:
        where, table = select
        args, specs = [where] + args + [table, gain], [smem] + specs + [vmem, vmem]
        outs.append(jax.ShapeDtypeStruct((total, width), bf16))
    if mates is not None:
        args, specs = args + list(mates), specs + [vmem] * groups
    return pl.pallas_call(
        body,
        name=name,
        in_specs=specs + [anywhere] * len(after),
        out_specs=[vmem] * len(outs),
        out_shape=outs,
        scratch_shapes=fetched(weight, kinds, parts),
        compiler_params=pltpu.CompilerParams(vmem_limit_bytes=16 << 20),
        cost_estimate=pl.CostEstimate(
            flops=2 * total * width * many, bytes_accessed=2 * width * many, transcendentals=0
        ),
    )(*args, *after)


def expand(name, prepare, args, saved, weight, depth, kinds, groups, parts, after=()):
    width, hidden = weight.shape[2:]
    total = saved[0][0][0]
    rows, step = total // groups, width // parts
    count, kept = len(args), len(saved)

    def body(*refs):
        in_refs, w_ref = refs[:count], refs[count]
        refs = refs[count + 1 + len(after) :]
        saved_refs, out_refs, (buffer, sems) = refs[:kept], refs[kept:-2], refs[-2:]
        wait = fetch(w_ref, depth, kinds, buffer, sems, parts)
        for ref, value in zip(saved_refs, prepare(*[r[...] for r in in_refs])):
            ref[...] = value.astype(ref.dtype)
        out = []
        for g in range(parts):
            part = jnp.zeros((total, step), f32)
            for k in range(len(kinds)):
                wait(g, k)
                part += lax.dot_general(
                    saved_refs[k][...], buffer[g, k], (((1,), (1,)), ((), ())),
                    preferred_element_type=f32,
                )
            out.append(part)
        for z in range(groups):
            block = jnp.concatenate([part[z * rows : (z + 1) * rows] for part in out], 0)
            out_refs[z][...] = block.astype(bf16)

    results = pl.pallas_call(
        body,
        name=name,
        in_specs=[vmem] * count + [anywhere] * (1 + len(after)),
        out_specs=[vmem] * (kept + groups),
        out_shape=[jax.ShapeDtypeStruct(shape, kind) for shape, kind in saved]
        + [jax.ShapeDtypeStruct((rows * parts, step), bf16)] * groups,
        scratch_shapes=fetched(weight, kinds, parts),
        compiler_params=pltpu.CompilerParams(vmem_limit_bytes=16 << 20),
        cost_estimate=pl.CostEstimate(
            flops=2 * total * width * hidden * len(kinds),
            bytes_accessed=2 * width * hidden * len(kinds),
            transcendentals=0,
        ),
    )(*args, in_hbm(weight), *after)
    return results[:kept], results[kept:]


def outer(name, depth, depths, build, args, d_gate, d_up, act, width, parts, before, after=()):
    total, hidden = act.shape
    step = width // parts
    count = len(args)
    earlier = [] if before is None else [in_hbm(before)]

    def contract(left, right):
        return lax.dot_general(left, right, (((0,), (0,)), ((), ())), preferred_element_type=f32)

    def body(*refs):
        values = [r[...] for r in refs[:count]]
        gate_ref, up_ref, act_ref = refs[count : count + 3]
        out_ref, tick_ref, buffer, sems = refs[-4:]
        tick_ref[...] = jnp.zeros_like(tick_ref)
        copies = []
        for g in range(parts):
            rows, dout = build(values, g)
            pairs = ((rows, gate_ref), (rows, up_ref), (dout, act_ref))
            for k, (left, right_ref) in enumerate(pairs):
                buffer[g, k] = contract(left, right_ref[...]).astype(bf16)
                copy = pltpu.make_async_copy(
                    buffer.at[g, k],
                    out_ref.at[0, depth, k, pl.ds(g * step, step)],
                    sems.at[g, k],
                )
                copy.start()
                copies.append(copy)
        for copy in copies:
            copy.wait()

    return pl.pallas_call(
        body,
        name=name,
        in_specs=[vmem] * (count + 3) + [anywhere] * (len(earlier) + len(after)),
        out_specs=[anywhere, vmem],
        out_shape=[
            jax.ShapeDtypeStruct((1, depths, 3, width, hidden), bf16),
            jax.ShapeDtypeStruct((8, lanes), f32),
        ],
        input_output_aliases={} if before is None else {count + 3: 0},
        scratch_shapes=[
            pltpu.VMEM((parts, 3, step, hidden), bf16),
            pltpu.SemaphoreType.DMA((parts, 3)),
        ],
        compiler_params=pltpu.CompilerParams(vmem_limit_bytes=24 << 20),
        cost_estimate=pl.CostEstimate(
            flops=6 * total * width * hidden, bytes_accessed=6 * width * hidden, transcendentals=0
        ),
    )(*args, d_gate, d_up, act, *earlier, *after)


def backward_rows(hidden, ahead_1, ahead_2, d_mixed_2, keep, gain):
    scale_1 = inv_rms(hidden)
    unit_1 = hidden * scale_1
    unit_e1 = ahead_1 * inv_rms(ahead_1)
    unit_e2 = ahead_2 * inv_rms(ahead_2)
    mixed = (unit_1 * gain[0, 0:1] + unit_e1 * gain[0, 1:2]).astype(bf16).astype(f32)
    scale_2 = inv_rms(mixed)
    unit_2 = mixed * scale_2
    u = d_mixed_2 * gain[1, 0:1]
    grad_1 = (u - unit_2 * jnp.mean(u * unit_2, axis=-1, keepdims=True)) * scale_2
    v = grad_1 * gain[0, 0:1]
    grad_0 = (v - unit_1 * jnp.mean(v * unit_1, axis=-1, keepdims=True)) * scale_1
    kept_1, kept_2 = grad_1 * keep, d_mixed_2 * keep
    terms = [
        jnp.sum(a * b, axis=0, keepdims=True)
        for a, b in ((kept_1, unit_1), (kept_1, unit_e1), (kept_2, unit_2), (kept_2, unit_e2))
    ]
    return grad_0.astype(bf16), jnp.concatenate(terms, 0)


def dense_rows(name, token, count, hidden, embed, next_rows, cotangent, gain, before, half, halves, after=()):
    tokens, width = hidden.shape
    step = next_rows.shape[0]
    blocks = tokens // step // halves
    low, last = half * blocks, tokens // step - 1
    size = 2 * lanes
    capacity = token.shape[3]
    earlier = [] if before is None else list(before)

    def body(token_ref, count_ref, hidden_ref, embed_ref, next_ref, cot_ref, gain_ref, *refs):
        out_ref, terms_ref, mixed_ref, sums_ref = refs[-4:]
        sums_ref[...] = jnp.zeros_like(sums_ref)
        row, column = (iota((2 * step, 2 * step), dim) for dim in range(2))
        shift = (column == jnp.where(row < step, row + 1, row + 2 - step)).astype(bf16)
        places = [pl.ds(at, size) for at in range(0, width, size)]

        def folded_lanes(value):
            return sum(value[:, at : at + lanes] for at in range(0, size, lanes))

        def mean(value):
            return jnp.sum(value, axis=1, keepdims=True) / width

        def one(i, carry):
            block = low + i
            first = pl.multiple_of(block * step, step)
            rows = pl.ds(first, step)
            follow = pl.ds(pl.multiple_of(jnp.minimum(block + 1, last) * step, step), step)
            here = iota((step, 1), 0) + first
            keep = jnp.ones((step, 1), f32)
            for k in range(2):
                for c in range(capacity):
                    out = (here == token_ref[0, 0, k, c]) & (c < count_ref[0, 0, k, 0])
                    keep = jnp.where(out, 0.0, keep)

            def ahead(at, hot):
                after = embed_ref[follow, at]
                if half == halves - 1:
                    after = jnp.where(block == last, next_ref[:, at], after)
                both = jnp.concatenate([embed_ref[rows, at], after], 0)
                return jnp.dot(hot, both, preferred_element_type=f32)

            square_h, square_e = jnp.zeros((step, lanes), f32), jnp.zeros((2 * step, lanes), f32)
            for at in places:
                h, e = hidden_ref[rows, at].astype(f32), ahead(at, shift)
                square_h += folded_lanes(h * h)
                square_e += folded_lanes(e * e)
            scale_1 = lax.rsqrt(mean(square_h) + eps_norm)
            scale_e = lax.rsqrt(mean(square_e) + eps_norm)
            scale_e1, scale_e2 = scale_e[:step], scale_e[step:]

            sums = [jnp.zeros((step, lanes), f32) for _ in range(4)]
            for at in places:
                through = hidden_ref[rows, at].astype(f32) * scale_1 * gain_ref[0, 0:1, at]
                mixed = through + ahead(at, shift[:step]) * scale_e1 * gain_ref[0, 1:2, at]
                kept = mixed.astype(bf16)
                mixed_ref[:, at] = kept
                mixed = kept.astype(f32)
                u = cot_ref[rows, at].astype(f32) * gain_ref[1, 0:1, at]
                pairs = ((mixed, mixed), (u, mixed), (u, through), (mixed, through))
                sums = [c + folded_lanes(a * b) for c, (a, b) in zip(sums, pairs)]
            square, along, u_back, mixed_back = (mean(value) for value in sums)
            scale_2 = lax.rsqrt(square + eps_norm)
            share_2 = scale_2 * scale_2 * along
            share_1 = scale_2 * (u_back - share_2 * mixed_back) * scale_1
            keep_2, keep_h = keep * scale_2, keep * scale_1
            keep_e1, keep_e2 = keep * scale_e1, keep * scale_e2

            for at in places:
                e = ahead(at, shift)
                h = hidden_ref[rows, at].astype(f32)
                mixed = mixed_ref[:, at].astype(f32)
                cot = cot_ref[rows, at].astype(f32)
                grad_1 = (cot * gain_ref[1, 0:1, at] - mixed * share_2) * scale_2
                grad_0 = (grad_1 * gain_ref[0, 0:1, at] - h * share_1) * scale_1
                out_ref[rows, at] = grad_0.astype(bf16)
                terms = (
                    grad_1 * (h * keep_h),
                    grad_1 * (e[:step] * keep_e1),
                    cot * (mixed * keep_2),
                    cot * (e[step:] * keep_e2),
                )
                for k, term in enumerate(terms):
                    sums_ref[k, :, at] += sum(term[r : r + 8] for r in range(0, step, 8))
            return carry

        lax.fori_loop(0, blocks, one, 0)
        for k in range(4):
            term = jnp.sum(sums_ref[k], axis=0, keepdims=True)
            terms_ref[k : k + 1] = term + refs[1][k : k + 1] if earlier else term

    return pl.pallas_call(
        body,
        name=name,
        in_specs=[smem] * 2 + [vmem] * (5 + len(earlier)) + [anywhere] * len(after),
        out_specs=[vmem] * 2,
        out_shape=[
            jax.ShapeDtypeStruct((tokens, width), bf16),
            jax.ShapeDtypeStruct((4, width), f32),
        ],
        input_output_aliases={7: 0} if earlier else {},
        scratch_shapes=[pltpu.VMEM((step, width), bf16), pltpu.VMEM((4, 8, width), f32)],
        compiler_params=pltpu.CompilerParams(vmem_limit_bytes=8 << 20),
        cost_estimate=pl.CostEstimate(
            flops=60 * tokens * width // halves,
            bytes_accessed=10 * tokens * width // halves,
            transcendentals=0,
        ),
    )(in_hbm(token), in_hbm(count), hidden, embed, next_rows, cotangent, gain, *earlier, *after)


def local(
    main_hidden, embedded, cotangent, slot_token, slot_count, route_gate, norm_gain, expert_weight
):
    depths, _, features = norm_gain.shape
    tokens = main_hidden.shape[2]
    slots = slot_token.shape[3]
    seqs, groups = lax.axis_size("seq"), lax.axis_size("dp")
    rows = seqs * slots
    total = groups * rows
    width = features // seqs
    share = width // groups
    hidden_units = expert_weight.shape[3]
    parts = folds(rows, width)
    where = jnp.stack([lax.axis_index("seq"), lax.axis_index("dp")]).astype(jnp.int32)
    source, embed, cot = main_hidden[0, 0], embedded[0, 0], cotangent[0, 0]
    facts = (slot_token, slot_count)
    packed = ((rows * parts, width // parts), bf16)
    part_rows = ((rows, width), f32)

    def payload(value):
        return folded(value, parts)

    asked_token = ring(slot_token, "section", -1)

    def own_rows(where, token, count, gate, embed, cot):
        first, second = token_column(token, 0), token_column(token, 1)
        live_1, live_2 = (live_column(count, k, slots) for k in range(2))
        weight_1, weight_2 = gate_column(gate, 0) * live_1, gate_column(gate, 1) * live_2
        facts = in_lanes(
            [first.astype(f32), second.astype(f32), live_1, live_2]
            + thirds(weight_1)
            + thirds(weight_2)
        )
        ahead_1, ahead_2 = pick(first + 1, embed), pick(first + 2, embed)
        block = jnp.concatenate([ahead_1, ahead_2, pick(first, cot)], 0)
        notes = jnp.concatenate([coded(inv_rms(ahead_1)), coded(inv_rms(ahead_2)), facts], 0)
        dout = folded(pick(second, cot) * weight_2, seqs * parts)
        none = jnp.zeros(((parts - 1) * slots, lanes), f32)
        tail = facts if parts == 1 else jnp.concatenate([facts, none], 0)
        dout = jnp.concatenate([dout, jnp.concatenate([tail] * seqs, 0)], 1)
        head = embed[:depths].astype(f32)
        scale = coded(inv_rms(head))
        heads = [
            jnp.concatenate([head[:, p * width : (p + 1) * width], scale], 1) for p in range(seqs)
        ]
        return [
            jnp.concatenate([jnp.concatenate([piece, notes], 1)] + heads, 0)
            for piece in pieces_of(block, where[0], seqs)
        ] + [dout]

    fine = width // parts + lanes
    *own_sent, dout_2 = call(
        "own_rows", own_rows,
        [((3 * slots + depths * seqs, width + lanes), bf16)] * seqs
        + [((slots * parts * seqs, fine), bf16)],
        (where, slot_token, slot_count, route_gate), far=(embed, cot), after=(asked_token,),
    )
    own_got = trade_seq(own_sent)

    def source_rows(where, asked, source):
        first = pick(token_column(asked, 0), source)
        second = pick(token_column(asked, 1), source)
        scale = coded(inv_rms(first))
        sent = [jnp.concatenate([p, scale], 1) for p in pieces_of(first, where[0], seqs)]
        sent[0] = jnp.concatenate([sent[0], second], 1)
        return sent + [first]

    *sent, asked_rows = call(
        "source_rows", source_rows,
        [((slots, width + lanes + features), bf16)]
        + [((slots, width + lanes), bf16)] * (seqs - 1)
        + [((slots, features), bf16)],
        (where, asked_token), source, after=(own_sent[0],),
    )
    start_got = trade_seq(sent, 1)
    dout_2_sent = gather_dp(dout_2)

    def first_mixed(where, gain, *got):
        start_got, got = got[:seqs], [g.astype(f32) for g in got[seqs:]]
        first = 3 * slots
        block_1, block_2, block_3 = (
            in_order([g[k * slots : (k + 1) * slots] for g in got], where[0], 0) for k in range(3)
        )
        facts = block_3[:, width:]
        heads = in_order([g[first:] for g in got], where[0], 0)
        heads = [heads[j * depths * seqs : (j + 1) * depths * seqs] for j in range(seqs)]
        units = []
        for k, block in ((1, block_1), (2, block_2)):
            unit = block[:, :width] * decoded(block[:, width:])
            after = []
            for j in range(seqs):
                token = facts[j * slots : (j + 1) * slots, 0:1]
                add = jnp.zeros((slots, width), f32)
                for i in range(k if j + 1 < seqs else 0):
                    row = heads[j + 1][i : i + 1]
                    for p in range(1, seqs):
                        at = p * depths + i
                        row = jnp.where(where[0] == p, heads[j + 1][at : at + 1], row)
                    row = row[:, :width] * decoded(row[:, width:])
                    add += jnp.where(token == float(tokens + i - k), row, 0.0)
                after.append(add)
            units.append(unit + jnp.concatenate(after, 0))
        follow = got[-1][first:, :width]
        follow = jnp.concatenate([follow[p * depths : (p + 1) * depths] for p in range(seqs)], 1)
        follow = jnp.where(where[0] == seqs - 1, 0.0, follow)
        follow = jnp.concatenate([follow, jnp.zeros((16 - depths, features), f32)], 0)
        start = in_order([g[:, : width + lanes].astype(f32) for g in start_got], where[0], 0)
        unit = start[:, :width] * decoded(start[:, width:])
        gain_h, gain_e = (piece_of(gain[0, k : k + 1], where[0], seqs, 0) for k in range(2))
        mixed = (unit * gain_h + units[0] * gain_e).astype(bf16).astype(f32)
        return payload(mixed * facts[:, 2:3]), unit, *units, block_3[:, :width], facts, follow

    rows_1, unit_1, unit_e1, unit_e2, cot_1, own_facts, next_rows = call(
        "first_mixed", first_mixed,
        [packed] + [part_rows] * 4 + [((rows, lanes), f32), ((16, features), bf16)],
        (where,), norm_gain, *start_got, *own_got,
    )
    rows_1_all = gather_dp(rows_1)

    def second_base(where, token, count, start, table, after, gain, *dout):
        second = token_column(token, 1)
        start = start[:, width + lanes :].astype(f32)
        ahead_1 = pick_ahead(second + 1, table, after)
        ahead_2 = pick_ahead(second + 2, table, after)
        unit = start * inv_rms(start)
        mixed = unit * gain[0, 0:1] + ahead_1 * inv_rms(ahead_1) * gain[0, 1:2]
        mixed = mixed.astype(bf16).astype(f32)
        own = mixed * inv_rms(mixed) * gain[1, 0:1] * (1.0 - met_column(token, count))
        out = (own + ahead_2 * inv_rms(ahead_2) * gain[1, 1:2]) * live_column(count, 1, slots)
        none = jnp.zeros((slots * parts, lanes), f32)
        bases = [
            jnp.concatenate([folded(piece, parts), none], 1)
            for piece in pieces_of(out, where[0], seqs)
        ]
        douts = zip(*(blocks_of(block.astype(f32), where[0], seqs) for block in dout))
        return [jnp.concatenate([base, *more], 0) for base, more in zip(bases, douts)] + [ahead_1, ahead_2]

    *fixed_sent, ahead_21, ahead_22 = call(
        "second_base", second_base,
        [((slots * parts * (1 + groups), fine), bf16)] * seqs + [((slots, features), bf16)] * 2,
        (where, *facts), start_got[0], embed, next_rows, norm_gain, *dout_2_sent, after=(rows_1,),
    )
    fixed_got = trade_seq(fixed_sent)

    first_own, first_send = project(
        "gate_up_1", rows_1_all, expert_weight, 0, (0, 1), parts, after=(ahead_21,)
    )
    first = pair_seq(first_own, first_send)

    def fixed_order(where, *got):
        got = [g.astype(f32) for g in got]
        size = slots * parts
        out = []
        for z in range(1 + groups):
            blocks = [g[z * size : (z + 1) * size] for g in got]
            blocks = [from_block(blocks, where[0], j) for j in range(seqs)]
            pairs = [b[g * slots : (g + 1) * slots] for g in range(parts) for b in blocks]
            out.append(jnp.concatenate(pairs, 0))
        return [out[0][:, : width // parts]] + out[1:]

    base_2, *dout_2_all = call(
        "fixed_order", fixed_order, [packed] + [((rows * parts, fine), bf16)] * groups,
        (where,), *fixed_got, after=(first_send,),
    )
    base_2_all = gather_dp(base_2)

    def forward_1(own, other):
        both = own + other.astype(f32)
        gate, up = both[:, :hidden_units], both[:, hidden_units:]
        return gate * jax.nn.sigmoid(gate) * up, both

    (act_1, both_1), out_blocks = expand(
        "down_1", forward_1, first,
        [((total, hidden_units), bf16), ((total, 2 * hidden_units), f32)],
        expert_weight, 0, (2,), groups, parts, after=(base_2,),
    )
    out_got = return_dp(out_blocks)

    hidden, _ = lax.optimization_barrier((source, rows_1))
    hidden = ring(hidden, "section", 1)
    dense = dense_rows(
        "dense_a", *facts, hidden, embed, next_rows, cot, norm_gain, None, 0, 2,
        after=(out_blocks[0],),
    )

    def second_prev(own_facts, rows_1, *got):
        value = unfolded(rows_1.astype(f32), parts) + summed(got, parts) * decoded(own_facts, 4)
        return payload(value), value.astype(bf16)

    prev, prev_own = call(
        "second_prev", second_prev, [packed, ((rows, width), bf16)],
        (), own_facts, rows_1, *out_got, after=(dense[1],),
    )
    prev_all = gather_dp(prev)

    def slot_facts(*blocks):
        facts = jnp.concatenate(
            [block[:rows].astype(f32)[:, width // parts :] for block in blocks], 0
        )
        base = (iota((total, 1), 0) // slots * tokens).astype(f32)
        first, second = facts[:, 0:1] + base, facts[:, 1:2] + base
        live = (facts[:, 3:4] > 0) & (as_row(facts[:, 2:3]) > 0)
        same = ((second == as_row(first)) & live).astype(f32)
        return same, same, same[:rows, :rows], decoded(facts, 4)

    same, same_16, same_own, weight_1 = call(
        "slot_facts", slot_facts,
        [((total, total), f32), ((total, total), bf16), ((rows, rows), f32), ((total, 1), f32)],
        (), *dout_2_all, after=(prev,),
    )
    fixed_own, fixed_send = project(
        "fixed_2", base_2_all, expert_weight, 1, (0, 1), parts,
        others=(dout_2_all, (2,)), after=(same_own,),
    )
    fixed_pair = pair_seq(fixed_own, fixed_send)

    mixed_own, mixed_send, chosen = project(
        "gate_up_2", prev_all, expert_weight, 1, (0, 1), parts,
        select=(where, same_16), gain=norm_gain, after=(fixed_own,),
    )
    second = pair_seq(mixed_own, mixed_send)
    prev_w_own, prev_w_send = project(
        "prev_down", prev_all, expert_weight, 0, (2,), parts, after=(mixed_send,)
    )
    prev_pair = pair_seq(prev_w_own, prev_w_send)

    def gates_back(gate, up, d_act):
        sig = jax.nn.sigmoid(gate)
        d_gate = d_act * up * sig * (1.0 + gate * (1.0 - sig))
        return d_gate, d_act * gate * sig

    def backward_2(own, other, fixed_own, fixed_other, same):
        many = 2 * hidden_units
        square = own[:, many : many + 1] + decoded(other[:, many:])
        scale = lax.rsqrt(square / features + eps_norm)
        row = jnp.sum(same * as_row(scale), axis=1, keepdims=True)
        both = (own[:, :many] + other[:, :many].astype(f32)) * row
        fixed = fixed_own + fixed_other.astype(f32)
        both = both + fixed[:, :many]
        gate, up = both[:, :hidden_units], both[:, hidden_units:]
        d_gate, d_up = gates_back(gate, up, fixed[:, many:])
        return d_gate, d_up, gate * jax.nn.sigmoid(gate) * up, scale, row

    units = ((total, hidden_units), bf16)
    (d_gate_2, d_up_2, act_2, scale_2, row_2), d_rows_blocks = expand(
        "back_rows_2", backward_2,
        second + fixed_pair + (same,),
        [units, units, units, ((total, 1), f32), ((total, 1), f32)],
        expert_weight, 1, (0, 1), groups, parts, after=(prev_w_own,),
    )
    d_rows_got = return_dp(d_rows_blocks)
    dense, dense_terms = dense_rows(
        "dense_b", *facts, hidden, embed, next_rows, cot, norm_gain, dense, 1, 2,
        after=(d_rows_blocks[0],),
    )
    def first_grad(where, cot, same, gain, *got):
        d_rows = summed(got, parts)
        added = lax.dot_general(
            same, d_rows, (((0,), (0,)), ((), ())),
            precision=lax.Precision.HIGHEST, preferred_element_type=f32,
        )
        d_mixed = cot + added
        u = d_mixed * piece_of(gain[1, 0:1], where[0], seqs, 0)
        return [payload(u), d_mixed] + blocks_of(d_rows, where[0], seqs)

    u, d_mixed_2, *d_rows_back = call(
        "first_grad", first_grad, [packed, part_rows] + [((slots, width), bf16)] * seqs,
        (where,), cot_1, same_own, norm_gain, *d_rows_got, after=(dense_terms, prev_pair[1]),
    )
    u_all = gather_dp(u)
    dense, _ = lax.optimization_barrier((dense, u))
    dense = ring(dense, "section", -1)
    back_got = trade_seq(d_rows_back)

    def build_2(values, g):
        chosen, row, base, dout = values[0], values[1], values[2 : 2 + groups], values[2 + groups :]
        step = width // parts
        first = chosen[:, g * step : (g + 1) * step].astype(f32) * row
        first = first + column_part(base, rows, g).astype(f32)
        return first.astype(bf16), column_part(dout, rows, g)[:, :step]

    weight_grad, tick_2 = outer(
        "weight_grad_2", 1, depths, build_2, [chosen, row_2] + base_2_all + dout_2_all,
        d_gate_2, d_up_2, act_2, width, parts, None, after=(u, back_got[-1]),
    )

    back_1_own, back_1_send = project(
        "back_1", u_all, expert_weight, 0, (2,), parts, mates=prev_all, after=(tick_2,)
    )
    back_1 = pair_seq(back_1_own, back_1_send)

    def second_grad(where, token, count, start, ahead_1, ahead_2, cot, gain, terms, *got):
        d_rows = in_order([g.astype(f32) for g in got], where[0], 1)
        keep = live_column(count, 1, slots) * (1.0 - met_column(token, count))
        grad, more = backward_rows(
            start[:, width + lanes :].astype(f32), ahead_1.astype(f32), ahead_2.astype(f32),
            pick(token_column(token, 1), cot) + d_rows, keep, gain,
        )
        notes = in_lanes([live_column(count, 0, slots), keep])
        grad = jnp.concatenate([grad.astype(f32), notes], 1)
        return [grad] + pieces_of(terms + more, where[0], seqs)

    grad_2, *terms_parts = call(
        "second_grad", second_grad,
        [((slots, features + lanes), bf16)] + [((2 * depths, width), f32)] * seqs,
        (where, *facts), start_got[0], ahead_21, ahead_22, cot, norm_gain, dense_terms, *back_got,
        after=(back_1_send,),
    )
    grad_2 = ring(grad_2, "section", -1)
    terms_got = trade_seq(terms_parts)

    def backward_1(own, other, prev_own, prev_other, both, scale, weight_1):
        inner = own[:, hidden_units : hidden_units + 1] + decoded(other[:, hidden_units:])
        d_act = own[:, :hidden_units] + other[:, :hidden_units].astype(f32)
        through = scale * scale * inner / features
        d_act = d_act - through * (prev_own + prev_other.astype(f32))
        d_act = d_act * (weight_1 * scale)
        d_gate, d_up = gates_back(both[:, :hidden_units], both[:, hidden_units:], d_act)
        return d_gate, d_up, through

    (d_gate_1, d_up_1, through_1), d_rows_blocks = expand(
        "back_rows_1", backward_1,
        back_1 + prev_pair + (both_1, scale_2, weight_1),
        [units, units, ((total, 1), f32)],
        expert_weight, 0, (0, 1), groups, parts, after=(terms_parts[0],),
    )
    d_rows_got = return_dp(d_rows_blocks)

    def build_1(values, g):
        through, scale, weight = values[:3]
        first, u, prev = (values[3 + k * groups : 3 + (k + 1) * groups] for k in range(3))
        dout = column_part(u, rows, g).astype(f32) - through * column_part(prev, rows, g).astype(f32)
        return column_part(first, rows, g), (dout * (weight * scale)).astype(bf16)

    weight_grad, tick_1 = outer(
        "weight_grad_1", 0, depths, build_1,
        [through_1, scale_2, weight_1] + rows_1_all + u_all + prev_all,
        d_gate_1, d_up_1, act_1, width, parts, weight_grad, after=(d_rows_blocks[0],),
    )

    def last_grad(where, d_mixed_2, prev, scale, through, unit_1, unit_e1, unit_e2, own_facts, gain, *got):
        got, terms = got[:groups], got[groups:]
        d_rows = summed(got, parts)
        gain_1, gain_2 = (piece_of(gain[k, 0:1], where[0], seqs, 0) for k in range(2))
        scale, through = scale[:rows], through[:rows]
        live = own_facts[:, 2:3]
        prev = prev.astype(f32)
        grad_1 = (d_mixed_2 * gain_2 - through * prev) * scale
        d_mixed_1 = grad_1 + d_rows
        kept_1, kept_2 = d_mixed_1 * live, d_mixed_2 * live
        sums = [
            jnp.sum(a * b, axis=0, keepdims=True)
            for a, b in ((kept_1, unit_1), (kept_1, unit_e1), (kept_2, prev * scale), (kept_2, unit_e2))
        ]
        sums = jnp.concatenate(sums, 0) + sum(terms)
        cut = []
        for i in range(groups):
            block = sums[:, :share]
            for z in range(groups):
                at = partner(z, i, groups) * share
                block = jnp.where(where[1] == z, sums[:, at : at + share], block)
            cut.append(block)
        return cut + blocks_of(d_mixed_1 * gain_1, where[0], seqs)

    last = call(
        "last_grad", last_grad,
        [((2 * depths, share), f32)] * groups + [((slots, width), bf16)] * seqs,
        (where,), d_mixed_2, prev_own, scale_2, through_1, unit_1, unit_e1, unit_e2,
        own_facts, norm_gain, *d_rows_got, *terms_got, after=(tick_1,),
    )
    last_got = trade_seq(last[groups:], -1)
    sums_got = return_dp(last[:groups])

    def finish(where, token, dense, asked_rows, grad_2, *got):
        part = in_order([g.astype(f32) for g in got], where[0], 1)
        asked_rows = asked_rows.astype(f32)
        scale = inv_rms(asked_rows)
        unit = asked_rows * scale
        grad_1 = (part - unit * jnp.mean(part * unit, axis=-1, keepdims=True)) * scale
        notes = grad_2[:, features:].astype(f32)
        grads = jnp.concatenate([grad_1, grad_2[:, :features].astype(f32)], 0).astype(bf16)
        lane = iota((slots, tokens), 1)
        chosen = jnp.concatenate(
            [
                jnp.where(lane == token_column(token, k), notes[:, k : k + 1], 0.0)
                for k in range(2)
            ],
            0,
        ).astype(bf16)
        taken = lax.dot_general(
            chosen, jnp.ones((2 * slots, lanes), bf16), (((0,), (0,)), ((), ())),
            preferred_element_type=f32,
        )[:, 0:1]
        out = []
        step = chunk_of(features)
        for at in range(0, features, step):
            placed = lax.dot_general(
                chosen, grads[:, at : at + step], (((0,), (0,)), ((), ())),
                preferred_element_type=f32,
            )
            out.append(jnp.where(taken > 0, placed, dense[:, at : at + step].astype(f32)).astype(bf16))
        return [jnp.concatenate(out, 1), jnp.zeros((8, lanes), f32)]

    hidden_grad, tick = call(
        "finish", finish, [((tokens, features), bf16), ((8, lanes), f32)],
        (where, asked_token), dense, asked_rows, grad_2, *last_got, limit=20,
    )

    def gain_sum(*got):
        sums = sum(got)
        return [jnp.stack([sums[2 * k : 2 * k + 2] for k in range(depths)])[None]]

    (gain_grad,) = call(
        "gain_sum", gain_sum, [((1, depths, 2, share), f32)], (), *sums_got, after=(tick,)
    )
    return (
        hidden_grad[None, None],
        weight_grad,
        gain_grad,
    )


def solution(mesh):
    return jax.shard_map(
        local,
        mesh=mesh,
        in_specs=(
            P("section", "dp", "seq", None),
            P("section", "dp", "seq", None),
            P("section", "dp", "seq", None),
            P("section", "dp", None, "seq"),
            P("section", "dp", None, "seq"),
            P("section", "dp", None, "seq"),
            P(),
            P(None, None, "seq", "dp"),
        ),
        out_specs=(
            P("section", "dp", "seq", None),
            P("section", None, None, "seq", "dp"),
            P("section", None, None, ("seq", "dp")),
        ),
        check_vma=False,
    )
```

```python
import jax
import jax.numpy as jnp
from jax import lax
from jax.experimental import pallas as pl
from jax.experimental.pallas import tpu as pltpu
from jax.sharding import PartitionSpec as P

eps_norm = 1e-06
lanes = 128
f32 = jnp.float32
bf16 = jnp.bfloat16
vmem = pl.BlockSpec(memory_space=pltpu.VMEM)
smem = pl.BlockSpec(memory_space=pltpu.SMEM)
anywhere = pl.BlockSpec(memory_space=pl.ANY)


def ring(value, axis, steps):
    count = lax.axis_size(axis)
    return lax.ppermute(value, axis, [(i, (i + steps) % count) for i in range(count)])


def hop(value, section_step, seq_step):
    sections, seqs = lax.axis_size("section"), lax.axis_size("seq")
    pairs = [
        (c * seqs + s, (c + section_step) % sections * seqs + (s + seq_step) % seqs)
        for c in range(sections)
        for s in range(seqs)
    ]
    return lax.ppermute(value, ("section", "seq"), pairs)


def trade_seq(pieces, section_step=0):
    if section_step == 0:
        return [pieces[0]] + [ring(pieces[o], "seq", o) for o in range(1, len(pieces))]
    return [hop(piece, section_step, o) for o, piece in enumerate(pieces)]


def partner(place, step, count):
    return place ^ step if count & (count - 1) == 0 else (place - step) % count


def gather_dp(block):
    count = lax.axis_size("dp")
    return [block] + [
        lax.ppermute(block, "dp", [(partner(z, i, count), z) for z in range(count)])
        for i in range(1, count)
    ]


def return_dp(blocks):
    count = lax.axis_size("dp")
    return [blocks[0]] + [
        lax.ppermute(blocks[i], "dp", [(z, partner(z, i, count)) for z in range(count)])
        for i in range(1, count)
    ]


def pair_seq(own, send):
    if lax.axis_size("seq") == 2:
        return own, ring(send, "seq", 1)
    return lax.psum(own, "seq"), jnp.zeros_like(send)


def inv_rms(value):
    return lax.rsqrt(jnp.mean(value * value, axis=-1, keepdims=True) + eps_norm)


def iota(shape, dim):
    return lax.broadcasted_iota(jnp.int32, shape, dim)


def token_column(token, depth):
    capacity = token.shape[3]
    out = jnp.full((capacity, 1), token[0, 0, depth, 0], jnp.int32)
    for c in range(1, capacity):
        out = jnp.where(iota((capacity, 1), 0) == c, token[0, 0, depth, c], out)
    return out


def gate_column(gate, depth):
    capacity = gate.shape[3]
    out = jnp.full((capacity, 1), gate[0, 0, depth, 0], f32)
    for c in range(1, capacity):
        out = jnp.where(iota((capacity, 1), 0) == c, gate[0, 0, depth, c], out)
    return out


def live_column(count, depth, capacity):
    return (iota((capacity, 1), 0) < count[0, 0, depth, 0]).astype(f32)


def met_column(token, count):
    capacity = token.shape[3]
    second = token_column(token, 1)
    out = jnp.zeros((capacity, 1), f32)
    for c in range(capacity):
        out += ((second == token[0, 0, 0, c]) & (c < count[0, 0, 0, 0])).astype(f32)
    return jnp.minimum(out, 1.0)


def pick(column, table):
    hot = (column == iota((column.shape[0], table.shape[0]), 1)).astype(bf16)
    return jnp.dot(hot, table, preferred_element_type=f32)


def pick_ahead(column, table, after):
    return pick(column, table) + pick(column - table.shape[0], after)


def thirds(column):
    high = column.astype(bf16).astype(f32)
    mid = (column - high).astype(bf16).astype(f32)
    return [high, mid, column - high - mid]


def in_lanes(columns):
    lane = iota((columns[0].shape[0], lanes), 1)
    out = jnp.zeros(lane.shape, f32)
    for k, column in enumerate(columns):
        out = jnp.where(lane == k, column, out)
    return out


def coded(column):
    return in_lanes(thirds(column))


def decoded(block, first=0):
    lane = iota(block.shape, 1)
    inside = (lane >= first) & (lane < first + 3)
    return jnp.sum(jnp.where(inside, block.astype(f32), 0.0), axis=1, keepdims=True)


def piece_of(value, place, count, step):
    width = value.shape[-1] // count
    want = lax.rem(place + step, count)
    out = value[:, :width]
    for p in range(1, count):
        out = jnp.where(want == p, value[:, p * width : (p + 1) * width], out)
    return out


def pieces_of(value, place, count):
    return [piece_of(value, place, count, o) for o in range(count)]


def blocks_of(value, place, count):
    size = value.shape[0] // count
    out = []
    for o in range(count):
        block = value[:size]
        for j in range(1, count):
            want = lax.rem(place + o, count) == j
            block = jnp.where(want, value[j * size : (j + 1) * size], block)
        out.append(block)
    return out


def from_block(got, place, block):
    count = len(got)
    out = got[0]
    for o in range(1, count):
        out = jnp.where(lax.rem(place - o + count, count) == block, got[o], out)
    return out


def in_order(got, place, axis):
    return jnp.concatenate([from_block(got, place, j) for j in range(len(got))], axis)


def as_row(column):
    size = column.shape[0]
    here = iota((size, size), 0) == iota((size, size), 1)
    return jnp.sum(jnp.where(here, column, 0.0), axis=0, keepdims=True)


def folds(rows, width):
    for count in (1, 2, 4, 8):
        if rows * count % 16 == 0 and width % (count * lanes) == 0:
            return count
    return 1


def folded(value, count):
    step = value.shape[1] // count
    return jnp.concatenate([value[:, g * step : (g + 1) * step] for g in range(count)], 0)


def unfolded(value, count):
    rows = value.shape[0] // count
    return jnp.concatenate([value[g * rows : (g + 1) * rows] for g in range(count)], 1)


def column_part(blocks, rows, g):
    return jnp.concatenate(
        [block[g * rows : (g + 1) * rows].astype(f32) for block in blocks], 0
    ).astype(bf16)


def summed(got, parts):
    return unfolded(sum(g.astype(f32) for g in got), parts)


def chunk_of(width):
    for step in (1024, 896, 512, 256, 128):
        if width % step == 0:
            return step
    return width


def in_hbm(value):
    return pltpu.with_memory_space_constraint(value, pltpu.HBM)


def call(name, fn, outs, small, *args, far=(), after=(), flops=0, limit=12):
    shapes = [jax.ShapeDtypeStruct(shape, kind) for shape, kind in outs]
    n_small, n_args, n_far, n_outs = len(small), len(args), len(far), len(shapes)

    def body(*refs):
        refs = list(refs)

        def take(count):
            taken, refs[:] = refs[:count], refs[count:]
            return taken

        small_refs, arg_refs, far_refs = take(n_small), take(n_args), take(n_far)
        take(len(after))
        out_refs, buffers, sems = take(n_outs), take(n_far), take(n_far)
        copies = [pltpu.make_async_copy(*trio) for trio in zip(far_refs, buffers, sems)]
        for copy in copies:
            copy.start()
        for copy in copies:
            copy.wait()
        values = small_refs + [r[...] for r in arg_refs + buffers]
        for ref, value in zip(out_refs, fn(*values)):
            ref[...] = value.astype(ref.dtype)

    size = sum(a.size * a.dtype.itemsize for a in list(args) + list(far) + shapes)
    return pl.pallas_call(
        body,
        name=name,
        out_shape=shapes,
        in_specs=[smem] * n_small + [vmem] * n_args + [anywhere] * (n_far + len(after)),
        out_specs=[vmem] * n_outs,
        scratch_shapes=[pltpu.VMEM(a.shape, a.dtype) for a in far] + [pltpu.SemaphoreType.DMA] * n_far,
        compiler_params=pltpu.CompilerParams(vmem_limit_bytes=limit << 20),
        cost_estimate=pl.CostEstimate(flops=flops, bytes_accessed=size, transcendentals=0),
    )(*[in_hbm(a) for a in small], *args, *[in_hbm(a) for a in far], *after)


def fetch(weight_ref, depth, kinds, buffer, sems, parts):
    step = weight_ref.shape[2] // parts
    copies = [
        [
            pltpu.make_async_copy(
                weight_ref.at[depth, kind, pl.ds(g * step, step)], buffer.at[g, k], sems.at[g, k]
            )
            for k, kind in enumerate(kinds)
        ]
        for g in range(parts)
    ]
    for row in copies:
        for copy in row:
            copy.start()
    return copies


def fetched(weight, kinds, parts):
    hidden = weight.shape[3]
    return [
        pltpu.VMEM((parts, len(kinds), weight.shape[2] // parts, hidden), bf16),
        pltpu.SemaphoreType.DMA((parts, len(kinds))),
    ]


def project(name, blocks, weight, depth, kinds, parts, others=None, select=None, gain=None, mates=None, after=()):
    groups = len(blocks)
    rows = blocks[0].shape[0] // parts
    width, hidden = weight.shape[2:]
    step = width // parts
    other_blocks, other_kinds = others if others is not None else ([], ())
    first_kinds, kinds = kinds, kinds + other_kinds
    total, many = rows * groups, len(kinds) * hidden
    marked = select is not None or mates is not None
    extra = lanes if marked else 0

    def body(*refs):
        refs = list(refs)
        where_ref = refs.pop(0) if select is not None else None
        x_refs, w_ref, refs = refs[:groups], refs[groups], refs[groups + 1 :]
        other_refs, refs = refs[: len(other_blocks)], refs[len(other_blocks) :]
        if select is not None:
            select_ref, gain_ref = refs.pop(0), refs.pop(0)
        if mates is not None:
            mate_refs, refs = refs[:groups], refs[groups:]
        refs = refs[len(after) :]
        own_ref, send_ref = refs.pop(0), refs.pop(0)
        kept_ref = refs.pop(0) if select is not None else None
        buffer, sems = refs
        copies = fetch(w_ref, depth, kinds, buffer, sems, parts)
        x_all = [r[...] for r in x_refs]
        mate_all = [r[...] for r in mate_refs] if mates is not None else x_all
        if select is not None:
            gain_all = piece_of(gain_ref[1, 0:1, :], where_ref[0], gain.shape[2] // width, 0)
        sums = [jnp.zeros((total, hidden), f32) for _ in kinds]
        mark = jnp.zeros((total, 1), f32)
        for g in range(parts):
            x = column_part(x_all, rows, g)
            if marked:
                mate = x if mates is None else column_part(mate_all, rows, g)
                mark += jnp.sum(x.astype(f32) * mate.astype(f32), axis=1, keepdims=True)
            if select is not None:
                chosen = jnp.dot(select_ref[...], x, preferred_element_type=f32)
                x = (chosen * gain_all[:, g * step : (g + 1) * step]).astype(bf16)
                kept_ref[:, g * step : (g + 1) * step] = x
            for k in range(len(kinds)):
                if k == len(first_kinds):
                    x = column_part([r[...] for r in other_refs], rows, g)[:, :step]
                copies[g][k].wait()
                sums[k] += jnp.dot(x, buffer[g, k], preferred_element_type=f32)
        for k in range(len(kinds)):
            own_ref[:, k * hidden : (k + 1) * hidden] = sums[k]
            send_ref[:, k * hidden : (k + 1) * hidden] = sums[k].astype(bf16)
        if marked:
            own_ref[:, many:] = in_lanes([mark])
            send_ref[:, many:] = coded(mark).astype(bf16)

    args = list(blocks) + [in_hbm(weight)]
    args, specs = args + list(other_blocks), [vmem] * groups + [anywhere] + [vmem] * len(other_blocks)
    outs = [
        jax.ShapeDtypeStruct((total, many + extra), f32),
        jax.ShapeDtypeStruct((total, many + extra), bf16),
    ]
    if select is not None:
        where, table = select
        args, specs = [where] + args + [table, gain], [smem] + specs + [vmem, vmem]
        outs.append(jax.ShapeDtypeStruct((total, width), bf16))
    if mates is not None:
        args, specs = args + list(mates), specs + [vmem] * groups
    return pl.pallas_call(
        body,
        name=name,
        in_specs=specs + [anywhere] * len(after),
        out_specs=[vmem] * len(outs),
        out_shape=outs,
        scratch_shapes=fetched(weight, kinds, parts),
        compiler_params=pltpu.CompilerParams(vmem_limit_bytes=16 << 20),
        cost_estimate=pl.CostEstimate(
            flops=2 * total * width * many, bytes_accessed=2 * width * many, transcendentals=0
        ),
    )(*args, *after)


def expand(name, prepare, args, saved, weight, depth, kinds, groups, parts, after=()):
    width, hidden = weight.shape[2:]
    total = saved[0][0][0]
    rows, step = total // groups, width // parts
    count, kept = len(args), len(saved)

    def body(*refs):
        in_refs, w_ref = refs[:count], refs[count]
        refs = refs[count + 1 + len(after) :]
        saved_refs, out_refs, (buffer, sems) = refs[:kept], refs[kept:-2], refs[-2:]
        copies = fetch(w_ref, depth, kinds, buffer, sems, parts)
        for ref, value in zip(saved_refs, prepare(*[r[...] for r in in_refs])):
            ref[...] = value.astype(ref.dtype)
        out = []
        for g in range(parts):
            part = jnp.zeros((total, step), f32)
            for k in range(len(kinds)):
                copies[g][k].wait()
                part += lax.dot_general(
                    saved_refs[k][...], buffer[g, k], (((1,), (1,)), ((), ())),
                    preferred_element_type=f32,
                )
            out.append(part)
        for z in range(groups):
            block = jnp.concatenate([part[z * rows : (z + 1) * rows] for part in out], 0)
            out_refs[z][...] = block.astype(bf16)

    results = pl.pallas_call(
        body,
        name=name,
        in_specs=[vmem] * count + [anywhere] * (1 + len(after)),
        out_specs=[vmem] * (kept + groups),
        out_shape=[jax.ShapeDtypeStruct(shape, kind) for shape, kind in saved]
        + [jax.ShapeDtypeStruct((rows * parts, step), bf16)] * groups,
        scratch_shapes=fetched(weight, kinds, parts),
        compiler_params=pltpu.CompilerParams(vmem_limit_bytes=16 << 20),
        cost_estimate=pl.CostEstimate(
            flops=2 * total * width * hidden * len(kinds),
            bytes_accessed=2 * width * hidden * len(kinds),
            transcendentals=0,
        ),
    )(*args, in_hbm(weight), *after)
    return results[:kept], results[kept:]


def outer(name, depth, depths, build, args, d_gate, d_up, act, width, parts, before, after=()):
    total, hidden = act.shape
    step = width // parts
    count = len(args)
    earlier = [] if before is None else [in_hbm(before)]

    def contract(left, right):
        return lax.dot_general(left, right, (((0,), (0,)), ((), ())), preferred_element_type=f32)

    def body(*refs):
        values = [r[...] for r in refs[:count]]
        gate_ref, up_ref, act_ref = refs[count : count + 3]
        out_ref, tick_ref, buffer, sems = refs[-4:]
        tick_ref[...] = jnp.zeros_like(tick_ref)
        copies = []
        for g in range(parts):
            rows, dout = build(values, g)
            pairs = ((rows, gate_ref), (rows, up_ref), (dout, act_ref))
            for k, (left, right_ref) in enumerate(pairs):
                buffer[g, k] = contract(left, right_ref[...]).astype(bf16)
                copy = pltpu.make_async_copy(
                    buffer.at[g, k],
                    out_ref.at[0, depth, k, pl.ds(g * step, step)],
                    sems.at[g, k],
                )
                copy.start()
                copies.append(copy)
        for copy in copies:
            copy.wait()

    return pl.pallas_call(
        body,
        name=name,
        in_specs=[vmem] * (count + 3) + [anywhere] * (len(earlier) + len(after)),
        out_specs=[anywhere, vmem],
        out_shape=[
            jax.ShapeDtypeStruct((1, depths, 3, width, hidden), bf16),
            jax.ShapeDtypeStruct((8, lanes), f32),
        ],
        input_output_aliases={} if before is None else {count + 3: 0},
        scratch_shapes=[
            pltpu.VMEM((parts, 3, step, hidden), bf16),
            pltpu.SemaphoreType.DMA((parts, 3)),
        ],
        compiler_params=pltpu.CompilerParams(vmem_limit_bytes=24 << 20),
        cost_estimate=pl.CostEstimate(
            flops=6 * total * width * hidden, bytes_accessed=6 * width * hidden, transcendentals=0
        ),
    )(*args, d_gate, d_up, act, *earlier, *after)


def backward_rows(hidden, ahead_1, ahead_2, d_mixed_2, keep, gain):
    scale_1 = inv_rms(hidden)
    unit_1 = hidden * scale_1
    unit_e1 = ahead_1 * inv_rms(ahead_1)
    unit_e2 = ahead_2 * inv_rms(ahead_2)
    mixed = (unit_1 * gain[0, 0:1] + unit_e1 * gain[0, 1:2]).astype(bf16).astype(f32)
    scale_2 = inv_rms(mixed)
    unit_2 = mixed * scale_2
    u = d_mixed_2 * gain[1, 0:1]
    grad_1 = (u - unit_2 * jnp.mean(u * unit_2, axis=-1, keepdims=True)) * scale_2
    v = grad_1 * gain[0, 0:1]
    grad_0 = (v - unit_1 * jnp.mean(v * unit_1, axis=-1, keepdims=True)) * scale_1
    kept_1, kept_2 = grad_1 * keep, d_mixed_2 * keep
    terms = [
        jnp.sum(a * b, axis=0, keepdims=True)
        for a, b in ((kept_1, unit_1), (kept_1, unit_e1), (kept_2, unit_2), (kept_2, unit_e2))
    ]
    return grad_0.astype(bf16), jnp.concatenate(terms, 0)


def dense_rows(name, token, count, hidden, embed, next_rows, cotangent, gain, before, half, halves, after=()):
    tokens, width = hidden.shape
    step = next_rows.shape[0]
    blocks = tokens // step // halves
    low, last = half * blocks, tokens // step - 1
    size = 2 * lanes
    capacity = token.shape[3]
    earlier = [] if before is None else list(before)

    def body(token_ref, count_ref, hidden_ref, embed_ref, next_ref, cot_ref, gain_ref, *refs):
        out_ref, terms_ref, mixed_ref, sums_ref = refs[-4:]
        sums_ref[...] = jnp.zeros_like(sums_ref)
        row, column = (iota((2 * step, 2 * step), dim) for dim in range(2))
        shift = (column == jnp.where(row < step, row + 1, row + 2 - step)).astype(bf16)
        places = [pl.ds(at, size) for at in range(0, width, size)]

        def folded_lanes(value):
            return sum(value[:, at : at + lanes] for at in range(0, size, lanes))

        def mean(value):
            return jnp.sum(value, axis=1, keepdims=True) / width

        def one(i, carry):
            block = low + i
            first = pl.multiple_of(block * step, step)
            rows = pl.ds(first, step)
            follow = pl.ds(pl.multiple_of(jnp.minimum(block + 1, last) * step, step), step)
            here = iota((step, 1), 0) + first
            keep = jnp.ones((step, 1), f32)
            for k in range(2):
                for c in range(capacity):
                    out = (here == token_ref[0, 0, k, c]) & (c < count_ref[0, 0, k, 0])
                    keep = jnp.where(out, 0.0, keep)

            def ahead(at, hot):
                after = embed_ref[follow, at]
                if half == halves - 1:
                    after = jnp.where(block == last, next_ref[:, at], after)
                both = jnp.concatenate([embed_ref[rows, at], after], 0)
                return jnp.dot(hot, both, preferred_element_type=f32)

            square_h, square_e = jnp.zeros((step, lanes), f32), jnp.zeros((2 * step, lanes), f32)
            for at in places:
                h, e = hidden_ref[rows, at].astype(f32), ahead(at, shift)
                square_h += folded_lanes(h * h)
                square_e += folded_lanes(e * e)
            scale_1 = lax.rsqrt(mean(square_h) + eps_norm)
            scale_e = lax.rsqrt(mean(square_e) + eps_norm)
            scale_e1, scale_e2 = scale_e[:step], scale_e[step:]

            sums = [jnp.zeros((step, lanes), f32) for _ in range(4)]
            for at in places:
                through = hidden_ref[rows, at].astype(f32) * scale_1 * gain_ref[0, 0:1, at]
                mixed = through + ahead(at, shift[:step]) * scale_e1 * gain_ref[0, 1:2, at]
                kept = mixed.astype(bf16)
                mixed_ref[:, at] = kept
                mixed = kept.astype(f32)
                u = cot_ref[rows, at].astype(f32) * gain_ref[1, 0:1, at]
                pairs = ((mixed, mixed), (u, mixed), (u, through), (mixed, through))
                sums = [c + folded_lanes(a * b) for c, (a, b) in zip(sums, pairs)]
            square, along, u_back, mixed_back = (mean(value) for value in sums)
            scale_2 = lax.rsqrt(square + eps_norm)
            share_2 = scale_2 * scale_2 * along
            share_1 = scale_2 * (u_back - share_2 * mixed_back) * scale_1
            keep_2, keep_h = keep * scale_2, keep * scale_1
            keep_e1, keep_e2 = keep * scale_e1, keep * scale_e2

            for at in places:
                e = ahead(at, shift)
                h = hidden_ref[rows, at].astype(f32)
                mixed = mixed_ref[:, at].astype(f32)
                cot = cot_ref[rows, at].astype(f32)
                grad_1 = (cot * gain_ref[1, 0:1, at] - mixed * share_2) * scale_2
                grad_0 = (grad_1 * gain_ref[0, 0:1, at] - h * share_1) * scale_1
                out_ref[rows, at] = grad_0.astype(bf16)
                terms = (
                    grad_1 * (h * keep_h),
                    grad_1 * (e[:step] * keep_e1),
                    cot * (mixed * keep_2),
                    cot * (e[step:] * keep_e2),
                )
                for k, term in enumerate(terms):
                    sums_ref[k, :, at] += sum(term[r : r + 8] for r in range(0, step, 8))
            return carry

        lax.fori_loop(0, blocks, one, 0)
        for k in range(4):
            term = jnp.sum(sums_ref[k], axis=0, keepdims=True)
            terms_ref[k : k + 1] = term + refs[1][k : k + 1] if earlier else term

    return pl.pallas_call(
        body,
        name=name,
        in_specs=[smem] * 2 + [vmem] * (5 + len(earlier)) + [anywhere] * len(after),
        out_specs=[vmem] * 2,
        out_shape=[
            jax.ShapeDtypeStruct((tokens, width), bf16),
            jax.ShapeDtypeStruct((4, width), f32),
        ],
        input_output_aliases={7: 0} if earlier else {},
        scratch_shapes=[pltpu.VMEM((step, width), bf16), pltpu.VMEM((4, 8, width), f32)],
        compiler_params=pltpu.CompilerParams(vmem_limit_bytes=8 << 20),
        cost_estimate=pl.CostEstimate(
            flops=60 * tokens * width // halves,
            bytes_accessed=10 * tokens * width // halves,
            transcendentals=0,
        ),
    )(in_hbm(token), in_hbm(count), hidden, embed, next_rows, cotangent, gain, *earlier, *after)


def local(
    main_hidden, embedded, cotangent, slot_token, slot_count, route_gate, norm_gain, expert_weight
):
    depths, _, features = norm_gain.shape
    tokens = main_hidden.shape[2]
    slots = slot_token.shape[3]
    seqs, groups = lax.axis_size("seq"), lax.axis_size("dp")
    rows = seqs * slots
    total = groups * rows
    width = features // seqs
    share = width // groups
    hidden_units = expert_weight.shape[3]
    parts = folds(rows, width)
    where = jnp.stack([lax.axis_index("seq"), lax.axis_index("dp")]).astype(jnp.int32)
    source, embed, cot = main_hidden[0, 0], embedded[0, 0], cotangent[0, 0]
    facts = (slot_token, slot_count)
    packed = ((rows * parts, width // parts), bf16)
    part_rows = ((rows, width), f32)

    def payload(value):
        return folded(value, parts)

    asked_token = ring(slot_token, "section", -1)

    def own_rows(where, token, count, gate, embed, cot):
        first, second = token_column(token, 0), token_column(token, 1)
        live_1, live_2 = (live_column(count, k, slots) for k in range(2))
        weight_1, weight_2 = gate_column(gate, 0) * live_1, gate_column(gate, 1) * live_2
        facts = in_lanes(
            [first.astype(f32), second.astype(f32), live_1, live_2]
            + thirds(weight_1)
            + thirds(weight_2)
        )
        ahead_1, ahead_2 = pick(first + 1, embed), pick(first + 2, embed)
        block = jnp.concatenate([ahead_1, ahead_2, pick(first, cot)], 0)
        notes = jnp.concatenate([coded(inv_rms(ahead_1)), coded(inv_rms(ahead_2)), facts], 0)
        dout = folded(pick(second, cot) * weight_2, seqs * parts)
        none = jnp.zeros(((parts - 1) * slots, lanes), f32)
        tail = facts if parts == 1 else jnp.concatenate([facts, none], 0)
        dout = jnp.concatenate([dout, jnp.concatenate([tail] * seqs, 0)], 1)
        head = embed[:depths].astype(f32)
        scale = coded(inv_rms(head))
        heads = [
            jnp.concatenate([head[:, p * width : (p + 1) * width], scale], 1) for p in range(seqs)
        ]
        return [
            jnp.concatenate([jnp.concatenate([piece, notes], 1)] + heads, 0)
            for piece in pieces_of(block, where[0], seqs)
        ] + [dout]

    fine = width // parts + lanes
    *own_sent, dout_2 = call(
        "own_rows", own_rows,
        [((3 * slots + depths * seqs, width + lanes), bf16)] * seqs
        + [((slots * parts * seqs, fine), bf16)],
        (where, slot_token, slot_count, route_gate), far=(embed, cot), after=(asked_token,),
    )
    own_got = trade_seq(own_sent)

    def source_rows(where, asked, source):
        first = pick(token_column(asked, 0), source)
        second = pick(token_column(asked, 1), source)
        scale = coded(inv_rms(first))
        sent = [jnp.concatenate([p, scale], 1) for p in pieces_of(first, where[0], seqs)]
        sent[0] = jnp.concatenate([sent[0], second], 1)
        return sent + [first]

    *sent, asked_rows = call(
        "source_rows", source_rows,
        [((slots, width + lanes + features), bf16)]
        + [((slots, width + lanes), bf16)] * (seqs - 1)
        + [((slots, features), bf16)],
        (where, asked_token), source, after=(own_sent[0],),
    )
    start_got = trade_seq(sent, 1)
    dout_2, _ = lax.optimization_barrier((dout_2, sent[0]))
    dout_2_got = gather_dp(dout_2)

    def first_mixed(where, gain, *got):
        start_got, dout = got[:seqs], [g.astype(f32) for g in got[2 * seqs :]]
        got = [g.astype(f32) for g in got[seqs : 2 * seqs]]
        first = 3 * slots
        block_1, block_2, block_3 = (
            in_order([g[k * slots : (k + 1) * slots] for g in got], where[0], 0) for k in range(3)
        )
        facts = block_3[:, width:]
        heads = in_order([g[first:] for g in got], where[0], 0)
        heads = [heads[j * depths * seqs : (j + 1) * depths * seqs] for j in range(seqs)]
        units = []
        for k, block in ((1, block_1), (2, block_2)):
            unit = block[:, :width] * decoded(block[:, width:])
            after = []
            for j in range(seqs):
                token = facts[j * slots : (j + 1) * slots, 0:1]
                add = jnp.zeros((slots, width), f32)
                for i in range(k if j + 1 < seqs else 0):
                    row = heads[j + 1][i : i + 1]
                    for p in range(1, seqs):
                        at = p * depths + i
                        row = jnp.where(where[0] == p, heads[j + 1][at : at + 1], row)
                    row = row[:, :width] * decoded(row[:, width:])
                    add += jnp.where(token == float(tokens + i - k), row, 0.0)
                after.append(add)
            units.append(unit + jnp.concatenate(after, 0))
        follow = got[-1][first:, :width]
        follow = jnp.concatenate([follow[p * depths : (p + 1) * depths] for p in range(seqs)], 1)
        follow = jnp.where(where[0] == seqs - 1, 0.0, follow)
        follow = jnp.concatenate([follow, jnp.zeros((16 - depths, features), f32)], 0)
        start = in_order([g[:, : width + lanes].astype(f32) for g in start_got], where[0], 0)
        unit = start[:, :width] * decoded(start[:, width:])
        gain_h, gain_e = (piece_of(gain[0, k : k + 1], where[0], seqs, 0) for k in range(2))
        mixed = (unit * gain_h + units[0] * gain_e).astype(bf16).astype(f32)
        douts = zip(*(blocks_of(block, where[0], seqs) for block in dout))
        douts = [jnp.concatenate(blocks, 0) for blocks in douts]
        return payload(mixed * facts[:, 2:3]), unit, *units, block_3[:, :width], facts, follow, *douts

    rows_1, unit_1, unit_e1, unit_e2, cot_1, own_facts, next_rows, *dout_2_sent = call(
        "first_mixed", first_mixed,
        [packed] + [part_rows] * 4 + [((rows, lanes), f32), ((16, features), bf16)]
        + [((groups * slots * parts, fine), bf16)] * seqs,
        (where,), norm_gain, *start_got, *own_got, *dout_2_got,
    )
    rows_1_all = gather_dp(rows_1)

    def second_base(where, token, count, start, table, after, gain):
        second = token_column(token, 1)
        start = start[:, width + lanes :].astype(f32)
        ahead_1 = pick_ahead(second + 1, table, after)
        ahead_2 = pick_ahead(second + 2, table, after)
        unit = start * inv_rms(start)
        mixed = unit * gain[0, 0:1] + ahead_1 * inv_rms(ahead_1) * gain[0, 1:2]
        mixed = mixed.astype(bf16).astype(f32)
        own = mixed * inv_rms(mixed) * gain[1, 0:1] * (1.0 - met_column(token, count))
        out = (own + ahead_2 * inv_rms(ahead_2) * gain[1, 1:2]) * live_column(count, 1, slots)
        bases = [folded(piece, parts) for piece in pieces_of(out, where[0], seqs)]
        return bases + [ahead_1, ahead_2]

    *base_sent, ahead_21, ahead_22 = call(
        "second_base", second_base,
        [((slots * parts, width // parts), bf16)] * seqs + [((slots, features), bf16)] * 2,
        (where, *facts), start_got[0], embed, next_rows, norm_gain, after=(rows_1,),
    )
    base_got = trade_seq(base_sent)

    first_own, first_send = project(
        "gate_up_1", rows_1_all, expert_weight, 0, (0, 1), parts, after=(ahead_21, base_got[-1])
    )
    first = pair_seq(first_own, first_send)

    def by_slots(got, place):
        blocks = [from_block(got, place, j) for j in range(seqs)]
        pairs = [b[g * slots : (g + 1) * slots] for g in range(parts) for b in blocks]
        return jnp.concatenate(pairs, 0)

    (base_2,) = call(
        "base_order", lambda where, *got: [by_slots([g.astype(f32) for g in got], where[0])], [packed],
        (where,), *base_got, after=(first_send,),
    )
    base_2_all = gather_dp(base_2)

    def forward_1(own, other):
        both = own + other.astype(f32)
        gate, up = both[:, :hidden_units], both[:, hidden_units:]
        return gate * jax.nn.sigmoid(gate) * up, both

    (act_1, both_1), out_blocks = expand(
        "down_1", forward_1, first,
        [((total, hidden_units), bf16), ((total, 2 * hidden_units), f32)],
        expert_weight, 0, (2,), groups, parts, after=(base_2,),
    )
    out_got = return_dp(out_blocks)

    hidden, _ = lax.optimization_barrier((source, rows_1))
    hidden = ring(hidden, "section", 1)
    dense = dense_rows(
        "dense_a", *facts, hidden, embed, next_rows, cot, norm_gain, None, 0, 2,
        after=(out_blocks[0],),
    )

    def second_prev(own_facts, rows_1, *got):
        value = unfolded(rows_1.astype(f32), parts) + summed(got, parts) * decoded(own_facts, 4)
        return payload(value), value.astype(bf16)

    prev, prev_own = call(
        "second_prev", second_prev, [packed, ((rows, width), bf16)],
        (), own_facts, rows_1, *out_got, after=(dense[1],),
    )
    prev_all = gather_dp(prev)

    dout_2_sent = lax.optimization_barrier((*dout_2_sent, out_blocks[0]))[:-1]
    dout_2_traded = trade_seq(dout_2_sent)

    def slot_facts(where, *got):
        got, size = [g.astype(f32) for g in got], slots * parts
        blocks = [
            by_slots([g[z * size : (z + 1) * size] for g in got], where[0]) for z in range(groups)
        ]
        facts = jnp.concatenate([block[:rows, width // parts :] for block in blocks], 0)
        base = (iota((total, 1), 0) // slots * tokens).astype(f32)
        first, second = facts[:, 0:1] + base, facts[:, 1:2] + base
        live = (facts[:, 3:4] > 0) & (as_row(facts[:, 2:3]) > 0)
        same = ((second == as_row(first)) & live).astype(f32)
        return same, same, same[:rows, :rows], decoded(facts, 4), *blocks

    same, same_16, same_own, weight_1, *dout_2_all = call(
        "slot_facts", slot_facts,
        [((total, total), f32), ((total, total), bf16), ((rows, rows), f32), ((total, 1), f32)]
        + [((rows * parts, fine), bf16)] * groups,
        (where,), *dout_2_traded, after=(prev,),
    )
    fixed_own, fixed_send = project(
        "fixed_2", base_2_all, expert_weight, 1, (0, 1), parts,
        others=(dout_2_all, (2,)), after=(same_own,),
    )
    fixed_pair = pair_seq(fixed_own, fixed_send)

    mixed_own, mixed_send, chosen = project(
        "gate_up_2", prev_all, expert_weight, 1, (0, 1), parts,
        select=(where, same_16), gain=norm_gain, after=(fixed_own,),
    )
    second = pair_seq(mixed_own, mixed_send)
    prev_w_own, prev_w_send = project(
        "prev_down", prev_all, expert_weight, 0, (2,), parts, after=(mixed_send,)
    )
    prev_pair = pair_seq(prev_w_own, prev_w_send)

    def gates_back(gate, up, d_act):
        sig = jax.nn.sigmoid(gate)
        d_gate = d_act * up * sig * (1.0 + gate * (1.0 - sig))
        return d_gate, d_act * gate * sig

    def backward_2(own, other, fixed_own, fixed_other, same):
        many = 2 * hidden_units
        square = own[:, many : many + 1] + decoded(other[:, many:])
        scale = lax.rsqrt(square / features + eps_norm)
        row = jnp.sum(same * as_row(scale), axis=1, keepdims=True)
        both = (own[:, :many] + other[:, :many].astype(f32)) * row
        fixed = fixed_own + fixed_other.astype(f32)
        both = both + fixed[:, :many]
        gate, up = both[:, :hidden_units], both[:, hidden_units:]
        d_gate, d_up = gates_back(gate, up, fixed[:, many:])
        return d_gate, d_up, gate * jax.nn.sigmoid(gate) * up, scale, row

    units = ((total, hidden_units), bf16)
    (d_gate_2, d_up_2, act_2, scale_2, row_2), d_rows_blocks = expand(
        "back_rows_2", backward_2,
        second + fixed_pair + (same,),
        [units, units, units, ((total, 1), f32), ((total, 1), f32)],
        expert_weight, 1, (0, 1), groups, parts, after=(prev_w_own,),
    )
    d_rows_got = return_dp(d_rows_blocks)
    dense, dense_terms = dense_rows(
        "dense_b", *facts, hidden, embed, next_rows, cot, norm_gain, dense, 1, 2,
        after=(d_rows_blocks[0],),
    )
    def first_grad(where, cot, same, gain, *got):
        d_rows = summed(got, parts)
        added = lax.dot_general(
            same, d_rows, (((0,), (0,)), ((), ())),
            precision=lax.Precision.HIGHEST, preferred_element_type=f32,
        )
        d_mixed = cot + added
        u = d_mixed * piece_of(gain[1, 0:1], where[0], seqs, 0)
        return [payload(u), d_mixed] + blocks_of(d_rows, where[0], seqs)

    u, d_mixed_2, *d_rows_back = call(
        "first_grad", first_grad, [packed, part_rows] + [((slots, width), bf16)] * seqs,
        (where,), cot_1, same_own, norm_gain, *d_rows_got, after=(dense_terms, prev_pair[1]),
    )
    u_all = gather_dp(u)
    dense, _ = lax.optimization_barrier((dense, u))
    dense = ring(dense, "section", -1)
    back_got = trade_seq(d_rows_back)

    def build_2(values, g):
        chosen, row, base, dout = values[0], values[1], values[2 : 2 + groups], values[2 + groups :]
        step = width // parts
        first = chosen[:, g * step : (g + 1) * step].astype(f32) * row
        first = first + column_part(base, rows, g).astype(f32)
        return first.astype(bf16), column_part(dout, rows, g)[:, :step]

    weight_grad, tick_2 = outer(
        "weight_grad_2", 1, depths, build_2, [chosen, row_2] + base_2_all + dout_2_all,
        d_gate_2, d_up_2, act_2, width, parts, None, after=(u, back_got[-1]),
    )

    back_1_own, back_1_send = project(
        "back_1", u_all, expert_weight, 0, (2,), parts, mates=prev_all, after=(tick_2,)
    )
    back_1 = pair_seq(back_1_own, back_1_send)

    def second_grad(where, token, count, start, ahead_1, ahead_2, cot, gain, terms, *got):
        d_rows = in_order([g.astype(f32) for g in got], where[0], 1)
        keep = live_column(count, 1, slots) * (1.0 - met_column(token, count))
        grad, more = backward_rows(
            start[:, width + lanes :].astype(f32), ahead_1.astype(f32), ahead_2.astype(f32),
            pick(token_column(token, 1), cot) + d_rows, keep, gain,
        )
        notes = in_lanes([live_column(count, 0, slots), keep])
        grad = jnp.concatenate([grad.astype(f32), notes], 1)
        return [grad] + pieces_of(terms + more, where[0], seqs)

    grad_2, *terms_parts = call(
        "second_grad", second_grad,
        [((slots, features + lanes), bf16)] + [((2 * depths, width), f32)] * seqs,
        (where, *facts), start_got[0], ahead_21, ahead_22, cot, norm_gain, dense_terms, *back_got,
        after=(back_1_send,),
    )
    grad_2 = ring(grad_2, "section", -1)
    terms_got = trade_seq(terms_parts)

    def backward_1(own, other, prev_own, prev_other, both, scale, weight_1):
        inner = own[:, hidden_units : hidden_units + 1] + decoded(other[:, hidden_units:])
        d_act = own[:, :hidden_units] + other[:, :hidden_units].astype(f32)
        through = scale * scale * inner / features
        d_act = d_act - through * (prev_own + prev_other.astype(f32))
        d_act = d_act * (weight_1 * scale)
        d_gate, d_up = gates_back(both[:, :hidden_units], both[:, hidden_units:], d_act)
        return d_gate, d_up, through

    (d_gate_1, d_up_1, through_1), d_rows_blocks = expand(
        "back_rows_1", backward_1,
        back_1 + prev_pair + (both_1, scale_2, weight_1),
        [units, units, ((total, 1), f32)],
        expert_weight, 0, (0, 1), groups, parts, after=(terms_parts[0],),
    )
    d_rows_got = return_dp(d_rows_blocks)

    def build_1(values, g):
        through, scale, weight = values[:3]
        first, u, prev = (values[3 + k * groups : 3 + (k + 1) * groups] for k in range(3))
        dout = column_part(u, rows, g).astype(f32) - through * column_part(prev, rows, g).astype(f32)
        return column_part(first, rows, g), (dout * (weight * scale)).astype(bf16)

    weight_grad, tick_1 = outer(
        "weight_grad_1", 0, depths, build_1,
        [through_1, scale_2, weight_1] + rows_1_all + u_all + prev_all,
        d_gate_1, d_up_1, act_1, width, parts, weight_grad, after=(d_rows_blocks[0],),
    )

    def last_grad(where, d_mixed_2, prev, scale, through, unit_1, unit_e1, unit_e2, own_facts, gain, *got):
        got, terms = got[:groups], got[groups:]
        d_rows = summed(got, parts)
        gain_1, gain_2 = (piece_of(gain[k, 0:1], where[0], seqs, 0) for k in range(2))
        scale, through = scale[:rows], through[:rows]
        live = own_facts[:, 2:3]
        prev = prev.astype(f32)
        grad_1 = (d_mixed_2 * gain_2 - through * prev) * scale
        d_mixed_1 = grad_1 + d_rows
        kept_1, kept_2 = d_mixed_1 * live, d_mixed_2 * live
        sums = [
            jnp.sum(a * b, axis=0, keepdims=True)
            for a, b in ((kept_1, unit_1), (kept_1, unit_e1), (kept_2, prev * scale), (kept_2, unit_e2))
        ]
        sums = jnp.concatenate(sums, 0) + sum(terms)
        cut = []
        for i in range(groups):
            block = sums[:, :share]
            for z in range(groups):
                at = partner(z, i, groups) * share
                block = jnp.where(where[1] == z, sums[:, at : at + share], block)
            cut.append(block)
        return cut + blocks_of(d_mixed_1 * gain_1, where[0], seqs)

    last = call(
        "last_grad", last_grad,
        [((2 * depths, share), f32)] * groups + [((slots, width), bf16)] * seqs,
        (where,), d_mixed_2, prev_own, scale_2, through_1, unit_1, unit_e1, unit_e2,
        own_facts, norm_gain, *d_rows_got, *terms_got, after=(tick_1,),
    )
    last_got = trade_seq(last[groups:], -1)
    sums_got = return_dp(last[:groups])

    def finish(where, token, dense, asked_rows, grad_2, *got):
        part = in_order([g.astype(f32) for g in got], where[0], 1)
        asked_rows = asked_rows.astype(f32)
        scale = inv_rms(asked_rows)
        unit = asked_rows * scale
        grad_1 = (part - unit * jnp.mean(part * unit, axis=-1, keepdims=True)) * scale
        notes = grad_2[:, features:].astype(f32)
        grads = jnp.concatenate([grad_1, grad_2[:, :features].astype(f32)], 0).astype(bf16)
        lane = iota((slots, tokens), 1)
        chosen = jnp.concatenate(
            [
                jnp.where(lane == token_column(token, k), notes[:, k : k + 1], 0.0)
                for k in range(2)
            ],
            0,
        ).astype(bf16)
        taken = lax.dot_general(
            chosen, jnp.ones((2 * slots, lanes), bf16), (((0,), (0,)), ((), ())),
            preferred_element_type=f32,
        )[:, 0:1]
        out = []
        step = chunk_of(features)
        for at in range(0, features, step):
            placed = lax.dot_general(
                chosen, grads[:, at : at + step], (((0,), (0,)), ((), ())),
                preferred_element_type=f32,
            )
            out.append(jnp.where(taken > 0, placed, dense[:, at : at + step].astype(f32)).astype(bf16))
        return [jnp.concatenate(out, 1), jnp.zeros((8, lanes), f32)]

    hidden_grad, tick = call(
        "finish", finish, [((tokens, features), bf16), ((8, lanes), f32)],
        (where, asked_token), dense, asked_rows, grad_2, *last_got, limit=20,
    )

    def gain_sum(*got):
        sums = sum(got)
        return [jnp.stack([sums[2 * k : 2 * k + 2] for k in range(depths)])[None]]

    (gain_grad,) = call(
        "gain_sum", gain_sum, [((1, depths, 2, share), f32)], (), *sums_got, after=(tick,)
    )
    return (
        hidden_grad[None, None],
        weight_grad,
        gain_grad,
    )


def solution(mesh):
    return jax.shard_map(
        local,
        mesh=mesh,
        in_specs=(
            P("section", "dp", "seq", None),
            P("section", "dp", "seq", None),
            P("section", "dp", "seq", None),
            P("section", "dp", None, "seq"),
            P("section", "dp", None, "seq"),
            P("section", "dp", None, "seq"),
            P(),
            P(None, None, "seq", "dp"),
        ),
        out_specs=(
            P("section", "dp", "seq", None),
            P("section", None, None, "seq", "dp"),
            P("section", None, None, ("seq", "dp")),
        ),
        check_vma=False,
    )
```

```python
import jax
import jax.numpy as jnp
from jax import lax
from jax.experimental import pallas as pl
from jax.experimental.pallas import tpu as pltpu
from jax.sharding import PartitionSpec as P

eps_norm = 1e-06
lanes = 128
f32 = jnp.float32
bf16 = jnp.bfloat16
vmem = pl.BlockSpec(memory_space=pltpu.VMEM)
smem = pl.BlockSpec(memory_space=pltpu.SMEM)
anywhere = pl.BlockSpec(memory_space=pl.ANY)


def ring(value, axis, steps):
    count = lax.axis_size(axis)
    return lax.ppermute(value, axis, [(i, (i + steps) % count) for i in range(count)])


def hop(value, section_step, seq_step):
    sections, seqs = lax.axis_size("section"), lax.axis_size("seq")
    pairs = [
        (c * seqs + s, (c + section_step) % sections * seqs + (s + seq_step) % seqs)
        for c in range(sections)
        for s in range(seqs)
    ]
    return lax.ppermute(value, ("section", "seq"), pairs)


def trade_seq(pieces, section_step=0):
    if section_step == 0:
        return [pieces[0]] + [ring(pieces[o], "seq", o) for o in range(1, len(pieces))]
    return [hop(piece, section_step, o) for o, piece in enumerate(pieces)]


def partner(place, step, count):
    return place ^ step if count & (count - 1) == 0 else (place - step) % count


def gather_dp(block):
    count = lax.axis_size("dp")
    return [block] + [
        lax.ppermute(block, "dp", [(partner(z, i, count), z) for z in range(count)])
        for i in range(1, count)
    ]


def return_dp(blocks):
    count = lax.axis_size("dp")
    return [blocks[0]] + [
        lax.ppermute(blocks[i], "dp", [(z, partner(z, i, count)) for z in range(count)])
        for i in range(1, count)
    ]


def pair_seq(own, send):
    if lax.axis_size("seq") == 2:
        return own, ring(send, "seq", 1)
    return lax.psum(own, "seq"), jnp.zeros_like(send)


def inv_rms(value):
    return lax.rsqrt(jnp.mean(value * value, axis=-1, keepdims=True) + eps_norm)


def iota(shape, dim):
    return lax.broadcasted_iota(jnp.int32, shape, dim)


def seq_place():
    return lax.axis_index("seq").astype(jnp.int32)


def token_column(token, depth):
    capacity = token.shape[3]
    out = jnp.full((capacity, 1), token[0, 0, depth, 0], jnp.int32)
    for c in range(1, capacity):
        out = jnp.where(iota((capacity, 1), 0) == c, token[0, 0, depth, c], out)
    return out


def gate_column(gate, depth):
    capacity = gate.shape[3]
    out = jnp.full((capacity, 1), gate[0, 0, depth, 0], f32)
    for c in range(1, capacity):
        out = jnp.where(iota((capacity, 1), 0) == c, gate[0, 0, depth, c], out)
    return out


def live_column(count, depth, capacity):
    return (iota((capacity, 1), 0) < count[depth]).astype(f32)


def met_column(token, count):
    capacity = token.shape[3]
    second = token_column(token, 1)
    out = jnp.zeros((capacity, 1), f32)
    for c in range(capacity):
        out += ((second == token[0, 0, 0, c]) & (c < count[0])).astype(f32)
    return jnp.minimum(out, 1.0)


def pick(column, table):
    hot = (column == iota((column.shape[0], table.shape[0]), 1)).astype(bf16)
    return jnp.dot(hot, table, preferred_element_type=f32)


def pick_ahead(column, table, after):
    return pick(column, table) + pick(column - table.shape[0], after)


def thirds(column):
    high = column.astype(bf16).astype(f32)
    mid = (column - high).astype(bf16).astype(f32)
    return [high, mid, column - high - mid]


def in_lanes(columns):
    lane = iota((columns[0].shape[0], lanes), 1)
    out = jnp.zeros(lane.shape, f32)
    for k, column in enumerate(columns):
        out = jnp.where(lane == k, column, out)
    return out


def coded(column):
    return in_lanes(thirds(column))


def decoded(block, first=0):
    lane = iota(block.shape, 1)
    inside = (lane >= first) & (lane < first + 3)
    return jnp.sum(jnp.where(inside, block.astype(f32), 0.0), axis=1, keepdims=True)


def piece_of(value, place, count, step):
    width = value.shape[-1] // count
    want = lax.rem(place + step, count)
    out = value[:, :width]
    for p in range(1, count):
        out = jnp.where(want == p, value[:, p * width : (p + 1) * width], out)
    return out


def pieces_of(value, place, count):
    return [piece_of(value, place, count, o) for o in range(count)]


def blocks_of(value, place, count):
    size = value.shape[0] // count
    out = []
    for o in range(count):
        block = value[:size]
        for j in range(1, count):
            want = lax.rem(place + o, count) == j
            block = jnp.where(want, value[j * size : (j + 1) * size], block)
        out.append(block)
    return out


def from_block(got, place, block):
    count = len(got)
    out = got[0]
    for o in range(1, count):
        out = jnp.where(lax.rem(place - o + count, count) == block, got[o], out)
    return out


def in_order(got, place, axis):
    return jnp.concatenate([from_block(got, place, j) for j in range(len(got))], axis)


def as_row(column):
    size = column.shape[0]
    here = iota((size, size), 0) == iota((size, size), 1)
    return jnp.sum(jnp.where(here, column, 0.0), axis=0, keepdims=True)


def folds(rows, width):
    for count in (1, 2, 4, 8):
        if rows * count % 16 == 0 and width % (count * lanes) == 0:
            return count
    return 1


def folded(value, count):
    step = value.shape[1] // count
    return jnp.concatenate([value[:, g * step : (g + 1) * step] for g in range(count)], 0)


def unfolded(value, count):
    rows = value.shape[0] // count
    return jnp.concatenate([value[g * rows : (g + 1) * rows] for g in range(count)], 1)


def column_part(blocks, rows, g):
    return jnp.concatenate(
        [block[g * rows : (g + 1) * rows].astype(f32) for block in blocks], 0
    ).astype(bf16)


def summed(got, parts):
    return unfolded(sum(g.astype(f32) for g in got), parts)


def chunk_of(width):
    for step in (1024, 896, 512, 256, 128):
        if width % step == 0:
            return step
    return width


def in_hbm(value):
    return pltpu.with_memory_space_constraint(value, pltpu.HBM)


def call(name, fn, outs, small, *args, far=(), after=(), flops=0, limit=12):
    shapes = [jax.ShapeDtypeStruct(shape, kind) for shape, kind in outs]
    n_small, n_args, n_far, n_outs = len(small), len(args), len(far), len(shapes)

    def body(*refs):
        refs = list(refs)

        def take(count):
            taken, refs[:] = refs[:count], refs[count:]
            return taken

        small_refs, arg_refs, far_refs = take(n_small), take(n_args), take(n_far)
        take(len(after))
        out_refs, buffers, sems = take(n_outs), take(n_far), take(n_far)
        copies = [pltpu.make_async_copy(*trio) for trio in zip(far_refs, buffers, sems)]
        for copy in copies:
            copy.start()
        for copy in copies:
            copy.wait()
        values = small_refs + [r[...] for r in arg_refs + buffers]
        for ref, value in zip(out_refs, fn(*values)):
            ref[...] = value.astype(ref.dtype)

    size = sum(a.size * a.dtype.itemsize for a in list(args) + list(far) + shapes)
    return pl.pallas_call(
        body,
        name=name,
        out_shape=shapes,
        in_specs=[smem] * n_small + [vmem] * n_args + [anywhere] * (n_far + len(after)),
        out_specs=[vmem] * n_outs,
        scratch_shapes=[pltpu.VMEM(a.shape, a.dtype) for a in far] + [pltpu.SemaphoreType.DMA] * n_far,
        compiler_params=pltpu.CompilerParams(vmem_limit_bytes=limit << 20),
        cost_estimate=pl.CostEstimate(flops=flops, bytes_accessed=size, transcendentals=0),
    )(*[in_hbm(a) for a in small], *args, *[in_hbm(a) for a in far], *after)


def held(name, weight, depth, after=()):
    _, kinds, width, hidden = weight.shape

    def body(*refs):
        weight_ref, out_ref, tick_ref, sem = refs[0], *refs[-3:]
        copy = pltpu.make_async_copy(weight_ref.at[depth], out_ref, sem)
        copy.start()
        tick_ref[...] = jnp.zeros_like(tick_ref)
        copy.wait()

    return pl.pallas_call(
        body,
        name=name,
        in_specs=[anywhere] * (1 + len(after)),
        out_specs=[vmem] * 2,
        out_shape=[
            jax.ShapeDtypeStruct((kinds, width, hidden), bf16),
            jax.ShapeDtypeStruct((8, lanes), f32),
        ],
        scratch_shapes=[pltpu.SemaphoreType.DMA],
        compiler_params=pltpu.CompilerParams(vmem_limit_bytes=2 << 20),
        cost_estimate=pl.CostEstimate(
            flops=0, bytes_accessed=4 * kinds * width * hidden, transcendentals=0
        ),
    )(in_hbm(weight), *after)


def project(name, blocks, weight, kinds, parts, others=None, select=None, gain=None, mates=None, after=()):
    groups = len(blocks)
    rows = blocks[0].shape[0] // parts
    width, hidden = weight.shape[1:]
    step = width // parts
    other_blocks, other_kinds = others if others is not None else ([], ())
    first_kinds, kinds = kinds, kinds + other_kinds
    total, many = rows * groups, len(kinds) * hidden
    marked = select is not None or mates is not None
    extra = lanes if marked else 0

    def body(*refs):
        refs = list(refs)
        x_refs, w_ref, refs = refs[:groups], refs[groups], refs[groups + 1 :]
        other_refs, refs = refs[: len(other_blocks)], refs[len(other_blocks) :]
        if select is not None:
            select_ref, gain_ref = refs.pop(0), refs.pop(0)
        if mates is not None:
            mate_refs, refs = refs[:groups], refs[groups:]
        refs = refs[len(after) :]
        own_ref, send_ref = refs.pop(0), refs.pop(0)
        kept_ref = refs.pop(0) if select is not None else None
        x_all = [r[...] for r in x_refs]
        mate_all = [r[...] for r in mate_refs] if mates is not None else x_all
        if select is not None:
            gain_all = piece_of(gain_ref[1, 0:1, :], seq_place(), gain.shape[2] // width, 0)
        sums = [jnp.zeros((total, hidden), f32) for _ in kinds]
        mark = jnp.zeros((total, 1), f32)
        for g in range(parts):
            x = column_part(x_all, rows, g)
            if marked:
                mate = x if mates is None else column_part(mate_all, rows, g)
                mark += jnp.sum(x.astype(f32) * mate.astype(f32), axis=1, keepdims=True)
            if select is not None:
                chosen = jnp.dot(select_ref[...], x, preferred_element_type=f32)
                x = (chosen * gain_all[:, g * step : (g + 1) * step]).astype(bf16)
                kept_ref[:, g * step : (g + 1) * step] = x
            for k in range(len(kinds)):
                if k == len(first_kinds):
                    x = column_part([r[...] for r in other_refs], rows, g)[:, :step]
                part_ref = w_ref.at[kinds[k], pl.ds(g * step, step)]
                sums[k] += jnp.dot(x, part_ref[...], preferred_element_type=f32)
        for k in range(len(kinds)):
            own_ref[:, k * hidden : (k + 1) * hidden] = sums[k]
            send_ref[:, k * hidden : (k + 1) * hidden] = sums[k].astype(bf16)
        if marked:
            own_ref[:, many:] = in_lanes([mark])
            send_ref[:, many:] = coded(mark).astype(bf16)

    args = list(blocks) + [weight]
    args, specs = args + list(other_blocks), [vmem] * groups + [vmem] + [vmem] * len(other_blocks)
    outs = [
        jax.ShapeDtypeStruct((total, many + extra), f32),
        jax.ShapeDtypeStruct((total, many + extra), bf16),
    ]
    if select is not None:
        args, specs = args + [select, gain], specs + [vmem, vmem]
        outs.append(jax.ShapeDtypeStruct((total, width), bf16))
    if mates is not None:
        args, specs = args + list(mates), specs + [vmem] * groups
    return pl.pallas_call(
        body,
        name=name,
        in_specs=specs + [anywhere] * len(after),
        out_specs=[vmem] * len(outs),
        out_shape=outs,
        compiler_params=pltpu.CompilerParams(vmem_limit_bytes=8 << 20),
        cost_estimate=pl.CostEstimate(
            flops=2 * total * width * many, bytes_accessed=2 * width * many, transcendentals=0
        ),
    )(*args, *after)


def expand(name, prepare, args, saved, weight, kinds, groups, parts, after=()):
    width, hidden = weight.shape[1:]
    total = saved[0][0][0]
    rows, step = total // groups, width // parts
    count, kept = len(args), len(saved)

    def body(*refs):
        in_refs, w_ref = refs[:count], refs[count]
        refs = refs[count + 1 + len(after) :]
        saved_refs, out_refs = refs[:kept], refs[kept:]
        for ref, value in zip(saved_refs, prepare(*[r[...] for r in in_refs])):
            ref[...] = value.astype(ref.dtype)
        out = []
        for g in range(parts):
            part = jnp.zeros((total, step), f32)
            for k in range(len(kinds)):
                part_ref = w_ref.at[kinds[k], pl.ds(g * step, step)]
                part += lax.dot_general(
                    saved_refs[k][...], part_ref[...], (((1,), (1,)), ((), ())),
                    preferred_element_type=f32,
                )
            out.append(part)
        for z in range(groups):
            block = jnp.concatenate([part[z * rows : (z + 1) * rows] for part in out], 0)
            out_refs[z][...] = block.astype(bf16)

    results = pl.pallas_call(
        body,
        name=name,
        in_specs=[vmem] * (count + 1) + [anywhere] * len(after),
        out_specs=[vmem] * (kept + groups),
        out_shape=[jax.ShapeDtypeStruct(shape, kind) for shape, kind in saved]
        + [jax.ShapeDtypeStruct((rows * parts, step), bf16)] * groups,
        compiler_params=pltpu.CompilerParams(vmem_limit_bytes=8 << 20),
        cost_estimate=pl.CostEstimate(
            flops=2 * total * width * hidden * len(kinds),
            bytes_accessed=2 * width * hidden * len(kinds),
            transcendentals=0,
        ),
    )(*args, weight, *after)
    return results[:kept], results[kept:]


def outer(name, depth, depths, build, args, d_gate, d_up, act, width, parts, before, after=()):
    total, hidden = act.shape
    step = width // parts
    count = len(args)
    earlier = [] if before is None else [in_hbm(before)]

    def contract(left, right):
        return lax.dot_general(left, right, (((0,), (0,)), ((), ())), preferred_element_type=f32)

    def body(*refs):
        values = [r[...] for r in refs[:count]]
        gate_ref, up_ref, act_ref = refs[count : count + 3]
        out_ref, tick_ref, buffer, sems = refs[-4:]
        tick_ref[...] = jnp.zeros_like(tick_ref)
        copies = []
        for g in range(parts):
            rows, dout = build(values, g)
            pairs = ((rows, gate_ref), (rows, up_ref), (dout, act_ref))
            for k, (left, right_ref) in enumerate(pairs):
                buffer[g, k] = contract(left, right_ref[...]).astype(bf16)
                copy = pltpu.make_async_copy(
                    buffer.at[g, k],
                    out_ref.at[0, depth, k, pl.ds(g * step, step)],
                    sems.at[g, k],
                )
                copy.start()
                copies.append(copy)
        for copy in copies:
            copy.wait()

    return pl.pallas_call(
        body,
        name=name,
        in_specs=[vmem] * (count + 3) + [anywhere] * (len(earlier) + len(after)),
        out_specs=[anywhere, vmem],
        out_shape=[
            jax.ShapeDtypeStruct((1, depths, 3, width, hidden), bf16),
            jax.ShapeDtypeStruct((8, lanes), f32),
        ],
        input_output_aliases={} if before is None else {count + 3: 0},
        scratch_shapes=[
            pltpu.VMEM((parts, 3, step, hidden), bf16),
            pltpu.SemaphoreType.DMA((parts, 3)),
        ],
        compiler_params=pltpu.CompilerParams(vmem_limit_bytes=24 << 20),
        cost_estimate=pl.CostEstimate(
            flops=6 * total * width * hidden, bytes_accessed=6 * width * hidden, transcendentals=0
        ),
    )(*args, d_gate, d_up, act, *earlier, *after)


def backward_rows(hidden, ahead_1, ahead_2, d_mixed_2, keep, gain):
    scale_1 = inv_rms(hidden)
    unit_1 = hidden * scale_1
    unit_e1 = ahead_1 * inv_rms(ahead_1)
    unit_e2 = ahead_2 * inv_rms(ahead_2)
    mixed = (unit_1 * gain[0, 0:1] + unit_e1 * gain[0, 1:2]).astype(bf16).astype(f32)
    scale_2 = inv_rms(mixed)
    unit_2 = mixed * scale_2
    u = d_mixed_2 * gain[1, 0:1]
    grad_1 = (u - unit_2 * jnp.mean(u * unit_2, axis=-1, keepdims=True)) * scale_2
    v = grad_1 * gain[0, 0:1]
    grad_0 = (v - unit_1 * jnp.mean(v * unit_1, axis=-1, keepdims=True)) * scale_1
    kept_1, kept_2 = grad_1 * keep, d_mixed_2 * keep
    terms = [
        jnp.sum(a * b, axis=0, keepdims=True)
        for a, b in ((kept_1, unit_1), (kept_1, unit_e1), (kept_2, unit_2), (kept_2, unit_e2))
    ]
    return grad_0.astype(bf16), jnp.concatenate(terms, 0)


def dense_rows(name, token, count, hidden, embed, next_rows, cotangent, gain, before, half, halves, after=()):
    tokens, width = hidden.shape
    step = next_rows.shape[0]
    blocks = tokens // step // halves
    low, last = half * blocks, tokens // step - 1
    size = 2 * lanes
    capacity = token.shape[3]
    earlier = [] if before is None else list(before)

    def body(token_ref, count_ref, hidden_ref, embed_ref, next_ref, cot_ref, gain_ref, *refs):
        out_ref, terms_ref, mixed_ref, sums_ref = refs[-4:]
        sums_ref[...] = jnp.zeros_like(sums_ref)
        row, column = (iota((2 * step, 2 * step), dim) for dim in range(2))
        shift = (column == jnp.where(row < step, row + 1, row + 2 - step)).astype(bf16)
        places = [pl.ds(at, size) for at in range(0, width, size)]

        def folded_lanes(value):
            return sum(value[:, at : at + lanes] for at in range(0, size, lanes))

        def mean(value):
            return jnp.sum(value, axis=1, keepdims=True) / width

        def one(i, carry):
            block = low + i
            first = pl.multiple_of(block * step, step)
            rows = pl.ds(first, step)
            follow = pl.ds(pl.multiple_of(jnp.minimum(block + 1, last) * step, step), step)
            here = iota((step, 1), 0) + first
            keep = jnp.ones((step, 1), f32)
            for k in range(2):
                for c in range(capacity):
                    out = (here == token_ref[0, 0, k, c]) & (c < count_ref[k])
                    keep = jnp.where(out, 0.0, keep)

            def ahead(at, hot):
                after = embed_ref[follow, at]
                if half == halves - 1:
                    after = jnp.where(block == last, next_ref[:, at], after)
                both = jnp.concatenate([embed_ref[rows, at], after], 0)
                return jnp.dot(hot, both, preferred_element_type=f32)

            square_h, square_e = jnp.zeros((step, lanes), f32), jnp.zeros((2 * step, lanes), f32)
            for at in places:
                h, e = hidden_ref[rows, at].astype(f32), ahead(at, shift)
                square_h += folded_lanes(h * h)
                square_e += folded_lanes(e * e)
            scale_1 = lax.rsqrt(mean(square_h) + eps_norm)
            scale_e = lax.rsqrt(mean(square_e) + eps_norm)
            scale_e1, scale_e2 = scale_e[:step], scale_e[step:]

            sums = [jnp.zeros((step, lanes), f32) for _ in range(4)]
            for at in places:
                through = hidden_ref[rows, at].astype(f32) * scale_1 * gain_ref[0, 0:1, at]
                mixed = through + ahead(at, shift[:step]) * scale_e1 * gain_ref[0, 1:2, at]
                kept = mixed.astype(bf16)
                mixed_ref[:, at] = kept
                mixed = kept.astype(f32)
                u = cot_ref[rows, at].astype(f32) * gain_ref[1, 0:1, at]
                pairs = ((mixed, mixed), (u, mixed), (u, through), (mixed, through))
                sums = [c + folded_lanes(a * b) for c, (a, b) in zip(sums, pairs)]
            square, along, u_back, mixed_back = (mean(value) for value in sums)
            scale_2 = lax.rsqrt(square + eps_norm)
            share_2 = scale_2 * scale_2 * along
            share_1 = scale_2 * (u_back - share_2 * mixed_back) * scale_1
            keep_2, keep_h = keep * scale_2, keep * scale_1
            keep_e1, keep_e2 = keep * scale_e1, keep * scale_e2

            for at in places:
                e = ahead(at, shift)
                h = hidden_ref[rows, at].astype(f32)
                mixed = mixed_ref[:, at].astype(f32)
                cot = cot_ref[rows, at].astype(f32)
                grad_1 = (cot * gain_ref[1, 0:1, at] - mixed * share_2) * scale_2
                grad_0 = (grad_1 * gain_ref[0, 0:1, at] - h * share_1) * scale_1
                out_ref[rows, at] = grad_0.astype(bf16)
                terms = (
                    grad_1 * (h * keep_h),
                    grad_1 * (e[:step] * keep_e1),
                    cot * (mixed * keep_2),
                    cot * (e[step:] * keep_e2),
                )
                for k, term in enumerate(terms):
                    sums_ref[k, :, at] += sum(term[r : r + 8] for r in range(0, step, 8))
            return carry

        lax.fori_loop(0, blocks, one, 0)
        for k in range(4):
            term = jnp.sum(sums_ref[k], axis=0, keepdims=True)
            terms_ref[k : k + 1] = term + refs[1][k : k + 1] if earlier else term

    return pl.pallas_call(
        body,
        name=name,
        in_specs=[smem] * 2 + [vmem] * (5 + len(earlier)) + [anywhere] * len(after),
        out_specs=[vmem] * 2,
        out_shape=[
            jax.ShapeDtypeStruct((tokens, width), bf16),
            jax.ShapeDtypeStruct((4, width), f32),
        ],
        input_output_aliases={7: 0} if earlier else {},
        scratch_shapes=[pltpu.VMEM((step, width), bf16), pltpu.VMEM((4, 8, width), f32)],
        compiler_params=pltpu.CompilerParams(vmem_limit_bytes=8 << 20),
        cost_estimate=pl.CostEstimate(
            flops=60 * tokens * width // halves,
            bytes_accessed=10 * tokens * width // halves,
            transcendentals=0,
        ),
    )(in_hbm(token), in_hbm(count), hidden, embed, next_rows, cotangent, gain, *earlier, *after)


def local(
    main_hidden, embedded, cotangent, slot_token, slot_count, route_gate, norm_gain, expert_weight
):
    depths, _, features = norm_gain.shape
    tokens = main_hidden.shape[2]
    slots = slot_token.shape[3]
    seqs, groups = lax.axis_size("seq"), lax.axis_size("dp")
    rows = seqs * slots
    total = groups * rows
    width = features // seqs
    share = width // groups
    hidden_units = expert_weight.shape[3]
    parts = folds(rows, width)
    source, embed, cot = main_hidden[0, 0], embedded[0, 0], cotangent[0, 0]
    slot_count = slot_count.reshape(-1)
    facts = (slot_token, slot_count)
    packed = ((rows * parts, width // parts), bf16)
    part_rows = ((rows, width), f32)

    def payload(value):
        return folded(value, parts)

    asked_token = ring(slot_token, "section", -1)

    def own_rows(token, count, gate, embed, cot):
        first, second = token_column(token, 0), token_column(token, 1)
        live_1, live_2 = (live_column(count, k, slots) for k in range(2))
        weight_1, weight_2 = gate_column(gate, 0) * live_1, gate_column(gate, 1) * live_2
        facts = in_lanes(
            [first.astype(f32), second.astype(f32), live_1, live_2]
            + thirds(weight_1)
            + thirds(weight_2)
        )
        ahead_1, ahead_2 = pick(first + 1, embed), pick(first + 2, embed)
        block = jnp.concatenate([ahead_1, ahead_2, pick(first, cot)], 0)
        notes = jnp.concatenate([coded(inv_rms(ahead_1)), coded(inv_rms(ahead_2)), facts], 0)
        dout = folded(pick(second, cot) * weight_2, seqs * parts)
        none = jnp.zeros(((parts - 1) * slots, lanes), f32)
        tail = facts if parts == 1 else jnp.concatenate([facts, none], 0)
        dout = jnp.concatenate([dout, jnp.concatenate([tail] * seqs, 0)], 1)
        head = embed[:depths].astype(f32)
        scale = coded(inv_rms(head))
        heads = [
            jnp.concatenate([head[:, p * width : (p + 1) * width], scale], 1) for p in range(seqs)
        ]
        return [
            jnp.concatenate([jnp.concatenate([piece, notes], 1)] + heads, 0)
            for piece in pieces_of(block, seq_place(), seqs)
        ] + [dout]

    fine = width // parts + lanes
    *own_sent, dout_2 = call(
        "own_rows", own_rows,
        [((3 * slots + depths * seqs, width + lanes), bf16)] * seqs
        + [((slots * parts * seqs, fine), bf16)],
        (slot_token, slot_count, route_gate), far=(embed, cot), after=(asked_token,),
    )
    own_got = trade_seq(own_sent)

    def source_rows(asked, source):
        first = pick(token_column(asked, 0), source)
        second = pick(token_column(asked, 1), source)
        scale = coded(inv_rms(first))
        sent = [jnp.concatenate([p, scale], 1) for p in pieces_of(first, seq_place(), seqs)]
        sent[0] = jnp.concatenate([sent[0], second], 1)
        return sent + [first]

    *sent, asked_rows = call(
        "source_rows", source_rows,
        [((slots, width + lanes + features), bf16)]
        + [((slots, width + lanes), bf16)] * (seqs - 1)
        + [((slots, features), bf16)],
        (asked_token,), source, after=(own_sent[0],),
    )
    start_got = trade_seq(sent, 1)
    dout_2, _ = lax.optimization_barrier((dout_2, sent[0]))
    dout_2_got = gather_dp(dout_2)

    def second_base(token, count, start, table, got, gain):
        after = got[3 * slots :, :width].astype(f32)
        after = jnp.concatenate([after[p * depths : (p + 1) * depths] for p in range(seqs)], 1)
        after = jnp.where(seq_place() == seqs - 1, 0.0, after)
        after = jnp.concatenate([after, jnp.zeros((16 - depths, features), f32)], 0).astype(bf16)
        second = token_column(token, 1)
        start = start[:, width + lanes :].astype(f32)
        ahead_1 = pick_ahead(second + 1, table, after)
        ahead_2 = pick_ahead(second + 2, table, after)
        unit = start * inv_rms(start)
        mixed = unit * gain[0, 0:1] + ahead_1 * inv_rms(ahead_1) * gain[0, 1:2]
        mixed = mixed.astype(bf16).astype(f32)
        own = mixed * inv_rms(mixed) * gain[1, 0:1] * (1.0 - met_column(token, count))
        out = (own + ahead_2 * inv_rms(ahead_2) * gain[1, 1:2]) * live_column(count, 1, slots)
        bases = [folded(piece, parts) for piece in pieces_of(out, seq_place(), seqs)]
        return bases + [after, ahead_1, ahead_2]

    *base_sent, next_rows, ahead_21, ahead_22 = call(
        "second_base", second_base,
        [((slots * parts, width // parts), bf16)] * seqs
        + [((16, features), bf16)]
        + [((slots, features), bf16)] * 2,
        facts, start_got[0], embed, own_got[-1], norm_gain, after=(start_got[-1],),
    )
    base_got = trade_seq(base_sent)

    weight_1st, tick_a = held("held_1", expert_weight, 0, after=(sent[0],))

    def first_mixed(gain, *got):
        start_got, dout = got[:seqs], [g.astype(f32) for g in got[2 * seqs :]]
        got = [g.astype(f32) for g in got[seqs : 2 * seqs]]
        first = 3 * slots
        block_1, block_2, block_3 = (
            in_order([g[k * slots : (k + 1) * slots] for g in got], seq_place(), 0) for k in range(3)
        )
        facts = block_3[:, width:]
        heads = in_order([g[first:] for g in got], seq_place(), 0)
        heads = [heads[j * depths * seqs : (j + 1) * depths * seqs] for j in range(seqs)]
        units = []
        for k, block in ((1, block_1), (2, block_2)):
            unit = block[:, :width] * decoded(block[:, width:])
            after = []
            for j in range(seqs):
                token = facts[j * slots : (j + 1) * slots, 0:1]
                add = jnp.zeros((slots, width), f32)
                for i in range(k if j + 1 < seqs else 0):
                    row = heads[j + 1][i : i + 1]
                    for p in range(1, seqs):
                        at = p * depths + i
                        row = jnp.where(seq_place() == p, heads[j + 1][at : at + 1], row)
                    row = row[:, :width] * decoded(row[:, width:])
                    add += jnp.where(token == float(tokens + i - k), row, 0.0)
                after.append(add)
            units.append(unit + jnp.concatenate(after, 0))
        start = in_order([g[:, : width + lanes].astype(f32) for g in start_got], seq_place(), 0)
        unit = start[:, :width] * decoded(start[:, width:])
        gain_h, gain_e = (piece_of(gain[0, k : k + 1], seq_place(), seqs, 0) for k in range(2))
        mixed = (unit * gain_h + units[0] * gain_e).astype(bf16).astype(f32)
        douts = zip(*(blocks_of(block, seq_place(), seqs) for block in dout))
        douts = [jnp.concatenate(blocks, 0) for blocks in douts]
        return payload(mixed * facts[:, 2:3]), unit, *units, block_3[:, :width], facts, *douts

    rows_1, unit_1, unit_e1, unit_e2, cot_1, own_facts, *dout_2_sent = call(
        "first_mixed", first_mixed,
        [packed] + [part_rows] * 4 + [((rows, lanes), f32)]
        + [((groups * slots * parts, fine), bf16)] * seqs,
        (), norm_gain, *start_got, *own_got, *dout_2_got, after=(ahead_21, tick_a),
    )
    rows_1_all = gather_dp(rows_1)

    def by_slots(got, place):
        blocks = [from_block(got, place, j) for j in range(seqs)]
        pairs = [b[g * slots : (g + 1) * slots] for g in range(parts) for b in blocks]
        return jnp.concatenate(pairs, 0)

    (base_2,) = call(
        "base_order", lambda *got: [by_slots([g.astype(f32) for g in got], seq_place())], [packed],
        (), *base_got, after=(rows_1,),
    )
    base_2_all = gather_dp(base_2)

    weight_2nd, tick_b = held("held_2", expert_weight, 1, after=(rows_1,))
    first_own, first_send = project(
        "gate_up_1", rows_1_all, weight_1st, (0, 1), parts, after=(base_2, tick_b)
    )
    first = pair_seq(first_own, first_send)

    def forward_1(own, other):
        both = own + other.astype(f32)
        gate, up = both[:, :hidden_units], both[:, hidden_units:]
        return gate * jax.nn.sigmoid(gate) * up, both

    (act_1, both_1), out_blocks = expand(
        "down_1", forward_1, first,
        [((total, hidden_units), bf16), ((total, 2 * hidden_units), f32)],
        weight_1st, (2,), groups, parts,
    )
    out_blocks = lax.optimization_barrier((*out_blocks, *base_2_all))[:groups]
    out_got = return_dp(out_blocks)

    hidden, _ = lax.optimization_barrier((source, rows_1))
    hidden = ring(hidden, "section", 1)
    dense = dense_rows(
        "dense_a", *facts, hidden, embed, next_rows, cot, norm_gain, None, 0, 2,
        after=(out_blocks[0],),
    )

    def second_prev(own_facts, rows_1, *got):
        value = unfolded(rows_1.astype(f32), parts) + summed(got, parts) * decoded(own_facts, 4)
        return payload(value), value.astype(bf16)

    prev, prev_own = call(
        "second_prev", second_prev, [packed, ((rows, width), bf16)],
        (), own_facts, rows_1, *out_got, after=(dense[1],),
    )
    prev_all = gather_dp(prev)

    dout_2_sent = lax.optimization_barrier((*dout_2_sent, out_blocks[0]))[:-1]
    dout_2_traded = trade_seq(dout_2_sent)

    def slot_facts(*got):
        got, size = [g.astype(f32) for g in got], slots * parts
        blocks = [
            by_slots([g[z * size : (z + 1) * size] for g in got], seq_place()) for z in range(groups)
        ]
        facts = jnp.concatenate([block[:rows, width // parts :] for block in blocks], 0)
        base = (iota((total, 1), 0) // slots * tokens).astype(f32)
        first, second = facts[:, 0:1] + base, facts[:, 1:2] + base
        live = (facts[:, 3:4] > 0) & (as_row(facts[:, 2:3]) > 0)
        same = ((second == as_row(first)) & live).astype(f32)
        return same, same, same[:rows, :rows], decoded(facts, 4), *blocks

    same, same_16, same_own, weight_1, *dout_2_all = call(
        "slot_facts", slot_facts,
        [((total, total), f32), ((total, total), bf16), ((rows, rows), f32), ((total, 1), f32)]
        + [((rows * parts, fine), bf16)] * groups,
        (), *dout_2_traded, after=(prev,),
    )
    fixed_own, fixed_send = project(
        "fixed_2", base_2_all, weight_2nd, (0, 1), parts,
        others=(dout_2_all, (2,)), after=(same_own,),
    )
    fixed_pair = pair_seq(fixed_own, fixed_send)

    mixed_own, mixed_send, chosen = project(
        "gate_up_2", prev_all, weight_2nd, (0, 1), parts,
        select=same_16, gain=norm_gain, after=(fixed_own,),
    )
    second = pair_seq(mixed_own, mixed_send)
    prev_w_own, prev_w_send = project(
        "prev_down", prev_all, weight_1st, (2,), parts, after=(mixed_send,)
    )
    prev_pair = pair_seq(prev_w_own, prev_w_send)

    def gates_back(gate, up, d_act):
        sig = jax.nn.sigmoid(gate)
        d_gate = d_act * up * sig * (1.0 + gate * (1.0 - sig))
        return d_gate, d_act * gate * sig

    def backward_2(own, other, fixed_own, fixed_other, same):
        many = 2 * hidden_units
        square = own[:, many : many + 1] + decoded(other[:, many:])
        scale = lax.rsqrt(square / features + eps_norm)
        row = jnp.sum(same * as_row(scale), axis=1, keepdims=True)
        both = (own[:, :many] + other[:, :many].astype(f32)) * row
        fixed = fixed_own + fixed_other.astype(f32)
        both = both + fixed[:, :many]
        gate, up = both[:, :hidden_units], both[:, hidden_units:]
        d_gate, d_up = gates_back(gate, up, fixed[:, many:])
        return d_gate, d_up, gate * jax.nn.sigmoid(gate) * up, scale, row

    units = ((total, hidden_units), bf16)
    (d_gate_2, d_up_2, act_2, scale_2, row_2), d_rows_blocks = expand(
        "back_rows_2", backward_2,
        second + fixed_pair + (same,),
        [units, units, units, ((total, 1), f32), ((total, 1), f32)],
        weight_2nd, (0, 1), groups, parts, after=(prev_w_own,),
    )
    d_rows_got = return_dp(d_rows_blocks)
    dense, dense_terms = dense_rows(
        "dense_b", *facts, hidden, embed, next_rows, cot, norm_gain, dense, 1, 2,
        after=(d_rows_blocks[0],),
    )
    def first_grad(cot, same, gain, *got):
        d_rows = summed(got, parts)
        added = lax.dot_general(
            same, d_rows, (((0,), (0,)), ((), ())),
            precision=lax.Precision.HIGHEST, preferred_element_type=f32,
        )
        d_mixed = cot + added
        u = d_mixed * piece_of(gain[1, 0:1], seq_place(), seqs, 0)
        return [payload(u), d_mixed] + blocks_of(d_rows, seq_place(), seqs)

    u, d_mixed_2, *d_rows_back = call(
        "first_grad", first_grad, [packed, part_rows] + [((slots, width), bf16)] * seqs,
        (), cot_1, same_own, norm_gain, *d_rows_got, after=(dense_terms, prev_pair[1]),
    )
    u_all = gather_dp(u)
    dense, _ = lax.optimization_barrier((dense, u))
    dense = ring(dense, "section", -1)
    back_got = trade_seq(d_rows_back)

    def build_2(values, g):
        chosen, row, base, dout = values[0], values[1], values[2 : 2 + groups], values[2 + groups :]
        step = width // parts
        first = chosen[:, g * step : (g + 1) * step].astype(f32) * row
        first = first + column_part(base, rows, g).astype(f32)
        return first.astype(bf16), column_part(dout, rows, g)[:, :step]

    weight_grad, tick_2 = outer(
        "weight_grad_2", 1, depths, build_2, [chosen, row_2] + base_2_all + dout_2_all,
        d_gate_2, d_up_2, act_2, width, parts, None, after=(u, back_got[-1]),
    )

    back_1_own, back_1_send = project(
        "back_1", u_all, weight_1st, (2,), parts, mates=prev_all, after=(tick_2,)
    )
    back_1 = pair_seq(back_1_own, back_1_send)

    def second_grad(token, count, start, ahead_1, ahead_2, cot, gain, terms, *got):
        d_rows = in_order([g.astype(f32) for g in got], seq_place(), 1)
        keep = live_column(count, 1, slots) * (1.0 - met_column(token, count))
        grad, more = backward_rows(
            start[:, width + lanes :].astype(f32), ahead_1.astype(f32), ahead_2.astype(f32),
            pick(token_column(token, 1), cot) + d_rows, keep, gain,
        )
        notes = in_lanes([live_column(count, 0, slots), keep])
        grad = jnp.concatenate([grad.astype(f32), notes], 1)
        return [grad] + pieces_of(terms + more, seq_place(), seqs)

    grad_2, *terms_parts = call(
        "second_grad", second_grad,
        [((slots, features + lanes), bf16)] + [((2 * depths, width), f32)] * seqs,
        facts, start_got[0], ahead_21, ahead_22, cot, norm_gain, dense_terms, *back_got,
        after=(back_1_send,),
    )
    grad_2 = ring(grad_2, "section", -1)
    terms_got = trade_seq(terms_parts)

    def backward_1(own, other, prev_own, prev_other, both, scale, weight_1):
        inner = own[:, hidden_units : hidden_units + 1] + decoded(other[:, hidden_units:])
        d_act = own[:, :hidden_units] + other[:, :hidden_units].astype(f32)
        through = scale * scale * inner / features
        d_act = d_act - through * (prev_own + prev_other.astype(f32))
        d_act = d_act * (weight_1 * scale)
        d_gate, d_up = gates_back(both[:, :hidden_units], both[:, hidden_units:], d_act)
        return d_gate, d_up, through

    (d_gate_1, d_up_1, through_1), d_rows_blocks = expand(
        "back_rows_1", backward_1,
        back_1 + prev_pair + (both_1, scale_2, weight_1),
        [units, units, ((total, 1), f32)],
        weight_1st, (0, 1), groups, parts, after=(terms_parts[0],),
    )
    d_rows_got = return_dp(d_rows_blocks)

    def build_1(values, g):
        through, scale, weight = values[:3]
        first, u, prev = (values[3 + k * groups : 3 + (k + 1) * groups] for k in range(3))
        dout = column_part(u, rows, g).astype(f32) - through * column_part(prev, rows, g).astype(f32)
        return column_part(first, rows, g), (dout * (weight * scale)).astype(bf16)

    weight_grad, tick_1 = outer(
        "weight_grad_1", 0, depths, build_1,
        [through_1, scale_2, weight_1] + rows_1_all + u_all + prev_all,
        d_gate_1, d_up_1, act_1, width, parts, weight_grad, after=(d_rows_blocks[0],),
    )

    def last_grad(d_mixed_2, prev, scale, through, unit_1, unit_e1, unit_e2, own_facts, gain, *got):
        got, terms = got[:groups], got[groups:]
        d_rows = summed(got, parts)
        gain_1, gain_2 = (piece_of(gain[k, 0:1], seq_place(), seqs, 0) for k in range(2))
        scale, through = scale[:rows], through[:rows]
        live = own_facts[:, 2:3]
        prev = prev.astype(f32)
        grad_1 = (d_mixed_2 * gain_2 - through * prev) * scale
        d_mixed_1 = grad_1 + d_rows
        kept_1, kept_2 = d_mixed_1 * live, d_mixed_2 * live
        sums = [
            jnp.sum(a * b, axis=0, keepdims=True)
            for a, b in ((kept_1, unit_1), (kept_1, unit_e1), (kept_2, prev * scale), (kept_2, unit_e2))
        ]
        sums = jnp.concatenate(sums, 0) + sum(terms)
        cut = []
        for i in range(groups):
            block = sums[:, :share]
            for z in range(groups):
                at = partner(z, i, groups) * share
                block = jnp.where(lax.axis_index("dp") == z, sums[:, at : at + share], block)
            cut.append(block)
        return cut + blocks_of(d_mixed_1 * gain_1, seq_place(), seqs)

    last = call(
        "last_grad", last_grad,
        [((2 * depths, share), f32)] * groups + [((slots, width), bf16)] * seqs,
        (), d_mixed_2, prev_own, scale_2, through_1, unit_1, unit_e1, unit_e2,
        own_facts, norm_gain, *d_rows_got, *terms_got, after=(tick_1,),
    )
    last_got = trade_seq(last[groups:], -1)
    sums_got = return_dp(last[:groups])

    def finish(token, dense, asked_rows, grad_2, *got):
        part = in_order([g.astype(f32) for g in got], seq_place(), 1)
        asked_rows = asked_rows.astype(f32)
        scale = inv_rms(asked_rows)
        unit = asked_rows * scale
        grad_1 = (part - unit * jnp.mean(part * unit, axis=-1, keepdims=True)) * scale
        notes = grad_2[:, features:].astype(f32)
        grads = jnp.concatenate([grad_1, grad_2[:, :features].astype(f32)], 0).astype(bf16)
        lane = iota((slots, tokens), 1)
        chosen = jnp.concatenate(
            [
                jnp.where(lane == token_column(token, k), notes[:, k : k + 1], 0.0)
                for k in range(2)
            ],
            0,
        ).astype(bf16)
        taken = lax.dot_general(
            chosen, jnp.ones((2 * slots, lanes), bf16), (((0,), (0,)), ((), ())),
            preferred_element_type=f32,
        )[:, 0:1]
        out = []
        step = chunk_of(features)
        for at in range(0, features, step):
            placed = lax.dot_general(
                chosen, grads[:, at : at + step], (((0,), (0,)), ((), ())),
                preferred_element_type=f32,
            )
            out.append(jnp.where(taken > 0, placed, dense[:, at : at + step].astype(f32)).astype(bf16))
        return [jnp.concatenate(out, 1), jnp.zeros((8, lanes), f32)]

    hidden_grad, tick = call(
        "finish", finish, [((tokens, features), bf16), ((8, lanes), f32)],
        (asked_token,), dense, asked_rows, grad_2, *last_got, limit=20,
    )

    def gain_sum(*got):
        sums = sum(got)
        return [jnp.stack([sums[2 * k : 2 * k + 2] for k in range(depths)])[None]]

    (gain_grad,) = call(
        "gain_sum", gain_sum, [((1, depths, 2, share), f32)], (), *sums_got, after=(tick,)
    )
    return (
        hidden_grad[None, None],
        weight_grad,
        gain_grad,
    )


def solution(mesh):
    return jax.shard_map(
        local,
        mesh=mesh,
        in_specs=(
            P("section", "dp", "seq", None),
            P("section", "dp", "seq", None),
            P("section", "dp", "seq", None),
            P("section", "dp", None, "seq"),
            P("section", "dp", None, "seq"),
            P("section", "dp", None, "seq"),
            P(),
            P(None, None, "seq", "dp"),
        ),
        out_specs=(
            P("section", "dp", "seq", None),
            P("section", None, None, "seq", "dp"),
            P("section", None, None, ("seq", "dp")),
        ),
        check_vma=False,
    )
```

```python
import jax
import jax.numpy as jnp
from jax import lax
from jax.experimental import pallas as pl
from jax.experimental.pallas import tpu as pltpu
from jax.sharding import PartitionSpec as P

eps_norm = 1e-06
lanes = 128
f32 = jnp.float32
bf16 = jnp.bfloat16
vmem = pl.BlockSpec(memory_space=pltpu.VMEM)
smem = pl.BlockSpec(memory_space=pltpu.SMEM)
anywhere = pl.BlockSpec(memory_space=pl.ANY)


def ring(value, axis, steps):
    count = lax.axis_size(axis)
    return lax.ppermute(value, axis, [(i, (i + steps) % count) for i in range(count)])


def hop(value, section_step, seq_step):
    sections, seqs = lax.axis_size("section"), lax.axis_size("seq")
    pairs = [
        (c * seqs + s, (c + section_step) % sections * seqs + (s + seq_step) % seqs)
        for c in range(sections)
        for s in range(seqs)
    ]
    return lax.ppermute(value, ("section", "seq"), pairs)


def trade_seq(pieces, section_step=0):
    if section_step == 0:
        return [pieces[0]] + [ring(pieces[o], "seq", o) for o in range(1, len(pieces))]
    return [hop(piece, section_step, o) for o, piece in enumerate(pieces)]


def partner(place, step, count):
    return place ^ step if count & (count - 1) == 0 else (place - step) % count


def gather_dp(block, before_last=None):
    count = lax.axis_size("dp")
    got = [block]
    for i in range(1, count):
        if i == count - 1 and before_last is not None:
            block, _ = lax.optimization_barrier((block, before_last))
        got.append(lax.ppermute(block, "dp", [(partner(z, i, count), z) for z in range(count)]))
    return got


def return_dp(blocks):
    count = lax.axis_size("dp")
    return [blocks[0]] + [
        lax.ppermute(blocks[i], "dp", [(z, partner(z, i, count)) for z in range(count)])
        for i in range(1, count)
    ]


def pair_seq(own, send):
    if lax.axis_size("seq") == 2:
        return own, ring(send, "seq", 1)
    return lax.psum(own, "seq"), jnp.zeros_like(send)


def inv_rms(value):
    return lax.rsqrt(jnp.mean(value * value, axis=-1, keepdims=True) + eps_norm)


def iota(shape, dim):
    return lax.broadcasted_iota(jnp.int32, shape, dim)


def seq_place():
    return lax.axis_index("seq").astype(jnp.int32)


def token_column(token, depth):
    capacity = token.shape[3]
    out = jnp.full((capacity, 1), token[0, 0, depth, 0], jnp.int32)
    for c in range(1, capacity):
        out = jnp.where(iota((capacity, 1), 0) == c, token[0, 0, depth, c], out)
    return out


def gate_column(gate, depth):
    capacity = gate.shape[3]
    out = jnp.full((capacity, 1), gate[0, 0, depth, 0], f32)
    for c in range(1, capacity):
        out = jnp.where(iota((capacity, 1), 0) == c, gate[0, 0, depth, c], out)
    return out


def live_column(count, depth, capacity):
    return (iota((capacity, 1), 0) < count[depth]).astype(f32)


def met_column(token, count):
    capacity = token.shape[3]
    second = token_column(token, 1)
    out = jnp.zeros((capacity, 1), f32)
    for c in range(capacity):
        out += ((second == token[0, 0, 0, c]) & (c < count[0])).astype(f32)
    return jnp.minimum(out, 1.0)


def pick(column, table):
    hot = (column == iota((column.shape[0], table.shape[0]), 1)).astype(bf16)
    return jnp.dot(hot, table, preferred_element_type=f32)


def pick_ahead(column, table, after):
    return pick(column, table) + pick(column - table.shape[0], after)


def thirds(column):
    high = column.astype(bf16).astype(f32)
    mid = (column - high).astype(bf16).astype(f32)
    return [high, mid, column - high - mid]


def in_lanes(columns):
    lane = iota((columns[0].shape[0], lanes), 1)
    out = jnp.zeros(lane.shape, f32)
    for k, column in enumerate(columns):
        out = jnp.where(lane == k, column, out)
    return out


def coded(column):
    return in_lanes(thirds(column))


def decoded(block, first=0):
    lane = iota(block.shape, 1)
    inside = (lane >= first) & (lane < first + 3)
    return jnp.sum(jnp.where(inside, block.astype(f32), 0.0), axis=1, keepdims=True)


def piece_of(value, place, count, step):
    width = value.shape[-1] // count
    want = lax.rem(place + step, count)
    out = value[:, :width]
    for p in range(1, count):
        out = jnp.where(want == p, value[:, p * width : (p + 1) * width], out)
    return out


def pieces_of(value, place, count):
    return [piece_of(value, place, count, o) for o in range(count)]


def blocks_of(value, place, count):
    size = value.shape[0] // count
    out = []
    for o in range(count):
        block = value[:size]
        for j in range(1, count):
            want = lax.rem(place + o, count) == j
            block = jnp.where(want, value[j * size : (j + 1) * size], block)
        out.append(block)
    return out


def from_block(got, place, block):
    count = len(got)
    out = got[0]
    for o in range(1, count):
        out = jnp.where(lax.rem(place - o + count, count) == block, got[o], out)
    return out


def in_order(got, place, axis):
    return jnp.concatenate([from_block(got, place, j) for j in range(len(got))], axis)


def as_row(column):
    size = column.shape[0]
    here = iota((size, size), 0) == iota((size, size), 1)
    return jnp.sum(jnp.where(here, column, 0.0), axis=0, keepdims=True)


def folds(rows, width):
    for count in (1, 2, 4, 8):
        if rows * count % 16 == 0 and width % (count * lanes) == 0:
            return count
    return 1


def folded(value, count):
    step = value.shape[1] // count
    return jnp.concatenate([value[:, g * step : (g + 1) * step] for g in range(count)], 0)


def unfolded(value, count):
    rows = value.shape[0] // count
    return jnp.concatenate([value[g * rows : (g + 1) * rows] for g in range(count)], 1)


def column_part(blocks, rows, g):
    return jnp.concatenate(
        [block[g * rows : (g + 1) * rows].astype(f32) for block in blocks], 0
    ).astype(bf16)


def summed(got, parts):
    return unfolded(sum(g.astype(f32) for g in got), parts)


def chunk_of(width):
    for step in (1024, 896, 512, 256, 128):
        if width % step == 0:
            return step
    return width


def in_hbm(value):
    return pltpu.with_memory_space_constraint(value, pltpu.HBM)


def call(name, fn, outs, small, *args, far=(), hold=(), after=(), flops=0, limit=12):
    outs = list(outs) + [(weight.shape[2:], bf16) for weight, _, _ in hold]
    shapes = [jax.ShapeDtypeStruct(shape, kind) for shape, kind in outs]
    n_small, n_args, n_far, n_outs = len(small), len(args), len(far), len(shapes) - len(hold)

    def body(*refs):
        refs = list(refs)

        def take(count):
            taken, refs[:] = refs[:count], refs[count:]
            return taken

        small_refs, arg_refs, far_refs = take(n_small), take(n_args), take(n_far)
        hold_refs = take(len(hold))
        take(len(after))
        out_refs, held_refs, buffers = take(n_outs), take(len(hold)), take(n_far)
        copies = [pltpu.make_async_copy(*trio) for trio in zip(far_refs, buffers, take(n_far))]
        holds = [
            pltpu.make_async_copy(ref.at[depth, kind], held_ref, sem)
            for ref, (_, depth, kind), held_ref, sem in zip(hold_refs, hold, held_refs, refs)
        ]
        for copy in copies + holds:
            copy.start()
        for copy in copies:
            copy.wait()
        values = small_refs + [r[...] for r in arg_refs + buffers]
        for ref, value in zip(out_refs, fn(*values)):
            ref[...] = value.astype(ref.dtype)
        for copy in holds:
            copy.wait()

    size = sum(a.size * a.dtype.itemsize for a in list(args) + list(far) + shapes)
    return pl.pallas_call(
        body,
        name=name,
        out_shape=shapes,
        in_specs=[smem] * n_small + [vmem] * n_args + [anywhere] * (n_far + len(hold) + len(after)),
        out_specs=[vmem] * len(shapes),
        scratch_shapes=[pltpu.VMEM(a.shape, a.dtype) for a in far]
        + [pltpu.SemaphoreType.DMA] * (n_far + len(hold)),
        compiler_params=pltpu.CompilerParams(vmem_limit_bytes=limit << 20),
        cost_estimate=pl.CostEstimate(flops=flops, bytes_accessed=size, transcendentals=0),
    )(*[in_hbm(a) for a in small], *args, *[in_hbm(a) for a in far], *[in_hbm(a) for a, _, _ in hold], *after)


def project(name, blocks, weights, kinds, parts, others=None, select=None, gain=None, mates=None, after=()):
    groups = len(blocks)
    rows = blocks[0].shape[0] // parts
    width, hidden = weights[0].shape
    step = width // parts
    other_blocks, other_kinds = others if others is not None else ([], ())
    first_kinds, kinds = kinds, kinds + other_kinds
    many_kinds = len(kinds)
    total, many = rows * groups, len(kinds) * hidden
    marked = select is not None or mates is not None
    extra = lanes if marked else 0

    def body(*refs):
        refs = list(refs)
        x_refs, w_refs, refs = refs[:groups], refs[groups : groups + many_kinds], refs[groups + many_kinds :]
        other_refs, refs = refs[: len(other_blocks)], refs[len(other_blocks) :]
        if select is not None:
            select_ref, gain_ref = refs.pop(0), refs.pop(0)
        if mates is not None:
            mate_refs, refs = refs[:groups], refs[groups:]
        refs = refs[len(after) :]
        own_ref, send_ref = refs.pop(0), refs.pop(0)
        kept_ref = refs.pop(0) if select is not None else None
        x_all = [r[...] for r in x_refs]
        mate_all = [r[...] for r in mate_refs] if mates is not None else x_all
        if select is not None:
            gain_all = piece_of(gain_ref[1, 0:1, :], seq_place(), gain.shape[2] // width, 0)
        sums = [jnp.zeros((total, hidden), f32) for _ in kinds]
        mark = jnp.zeros((total, 1), f32)
        for g in range(parts):
            x = column_part(x_all, rows, g)
            if marked:
                mate = x if mates is None else column_part(mate_all, rows, g)
                mark += jnp.sum(x.astype(f32) * mate.astype(f32), axis=1, keepdims=True)
            if select is not None:
                chosen = jnp.dot(select_ref[...], x, preferred_element_type=f32)
                x = (chosen * gain_all[:, g * step : (g + 1) * step]).astype(bf16)
                kept_ref[:, g * step : (g + 1) * step] = x
            for k in range(len(kinds)):
                if k == len(first_kinds):
                    x = column_part([r[...] for r in other_refs], rows, g)[:, :step]
                part_ref = w_refs[k].at[pl.ds(g * step, step)]
                sums[k] += jnp.dot(x, part_ref[...], preferred_element_type=f32)
        for k in range(len(kinds)):
            own_ref[:, k * hidden : (k + 1) * hidden] = sums[k]
            send_ref[:, k * hidden : (k + 1) * hidden] = sums[k].astype(bf16)
        if marked:
            own_ref[:, many:] = in_lanes([mark])
            send_ref[:, many:] = coded(mark).astype(bf16)

    args = list(blocks) + [weights[k] for k in kinds]
    args, specs = args + list(other_blocks), [vmem] * (groups + many_kinds) + [vmem] * len(other_blocks)
    outs = [
        jax.ShapeDtypeStruct((total, many + extra), f32),
        jax.ShapeDtypeStruct((total, many + extra), bf16),
    ]
    if select is not None:
        args, specs = args + [select, gain], specs + [vmem, vmem]
        outs.append(jax.ShapeDtypeStruct((total, width), bf16))
    if mates is not None:
        args, specs = args + list(mates), specs + [vmem] * groups
    return pl.pallas_call(
        body,
        name=name,
        in_specs=specs + [anywhere] * len(after),
        out_specs=[vmem] * len(outs),
        out_shape=outs,
        compiler_params=pltpu.CompilerParams(vmem_limit_bytes=8 << 20),
        cost_estimate=pl.CostEstimate(
            flops=2 * total * width * many, bytes_accessed=2 * width * many, transcendentals=0
        ),
    )(*args, *after)


def expand(name, prepare, args, saved, weights, kinds, groups, parts, after=()):
    width, hidden = weights[0].shape
    total = saved[0][0][0]
    rows, step = total // groups, width // parts
    count, kept = len(args), len(saved)

    def body(*refs):
        in_refs, w_refs = refs[:count], refs[count : count + len(kinds)]
        refs = refs[count + len(kinds) + len(after) :]
        saved_refs, out_refs = refs[:kept], refs[kept:]
        for ref, value in zip(saved_refs, prepare(*[r[...] for r in in_refs])):
            ref[...] = value.astype(ref.dtype)
        out = []
        for g in range(parts):
            part = jnp.zeros((total, step), f32)
            for k in range(len(kinds)):
                part_ref = w_refs[k].at[pl.ds(g * step, step)]
                part += lax.dot_general(
                    saved_refs[k][...], part_ref[...], (((1,), (1,)), ((), ())),
                    preferred_element_type=f32,
                )
            out.append(part)
        for z in range(groups):
            block = jnp.concatenate([part[z * rows : (z + 1) * rows] for part in out], 0)
            out_refs[z][...] = block.astype(bf16)

    results = pl.pallas_call(
        body,
        name=name,
        in_specs=[vmem] * (count + len(kinds)) + [anywhere] * len(after),
        out_specs=[vmem] * (kept + groups),
        out_shape=[jax.ShapeDtypeStruct(shape, kind) for shape, kind in saved]
        + [jax.ShapeDtypeStruct((rows * parts, step), bf16)] * groups,
        compiler_params=pltpu.CompilerParams(vmem_limit_bytes=8 << 20),
        cost_estimate=pl.CostEstimate(
            flops=2 * total * width * hidden * len(kinds),
            bytes_accessed=2 * width * hidden * len(kinds),
            transcendentals=0,
        ),
    )(*args, *[weights[k] for k in kinds], *after)
    return results[:kept], results[kept:]


def outer(name, depth, depths, build, args, d_gate, d_up, act, width, parts, before, after=()):
    total, hidden = act.shape
    step = width // parts
    count = len(args)
    earlier = [] if before is None else [in_hbm(before)]

    def contract(left, right):
        return lax.dot_general(left, right, (((0,), (0,)), ((), ())), preferred_element_type=f32)

    def body(*refs):
        values = [r[...] for r in refs[:count]]
        gate_ref, up_ref, act_ref = refs[count : count + 3]
        out_ref, tick_ref, buffer, sems = refs[-4:]
        tick_ref[...] = jnp.zeros_like(tick_ref)
        copies = []
        for g in range(parts):
            rows, dout = build(values, g)
            pairs = ((rows, gate_ref), (rows, up_ref), (dout, act_ref))
            for k, (left, right_ref) in enumerate(pairs):
                buffer[g, k] = contract(left, right_ref[...]).astype(bf16)
                copy = pltpu.make_async_copy(
                    buffer.at[g, k],
                    out_ref.at[0, depth, k, pl.ds(g * step, step)],
                    sems.at[g, k],
                )
                copy.start()
                copies.append(copy)
        for copy in copies:
            copy.wait()

    return pl.pallas_call(
        body,
        name=name,
        in_specs=[vmem] * (count + 3) + [anywhere] * (len(earlier) + len(after)),
        out_specs=[anywhere, vmem],
        out_shape=[
            jax.ShapeDtypeStruct((1, depths, 3, width, hidden), bf16),
            jax.ShapeDtypeStruct((8, lanes), f32),
        ],
        input_output_aliases={} if before is None else {count + 3: 0},
        scratch_shapes=[
            pltpu.VMEM((parts, 3, step, hidden), bf16),
            pltpu.SemaphoreType.DMA((parts, 3)),
        ],
        compiler_params=pltpu.CompilerParams(vmem_limit_bytes=24 << 20),
        cost_estimate=pl.CostEstimate(
            flops=6 * total * width * hidden, bytes_accessed=6 * width * hidden, transcendentals=0
        ),
    )(*args, d_gate, d_up, act, *earlier, *after)


def backward_rows(hidden, ahead_1, ahead_2, d_mixed_2, keep, gain):
    scale_1 = inv_rms(hidden)
    unit_1 = hidden * scale_1
    unit_e1 = ahead_1 * inv_rms(ahead_1)
    unit_e2 = ahead_2 * inv_rms(ahead_2)
    mixed = (unit_1 * gain[0, 0:1] + unit_e1 * gain[0, 1:2]).astype(bf16).astype(f32)
    scale_2 = inv_rms(mixed)
    unit_2 = mixed * scale_2
    u = d_mixed_2 * gain[1, 0:1]
    grad_1 = (u - unit_2 * jnp.mean(u * unit_2, axis=-1, keepdims=True)) * scale_2
    v = grad_1 * gain[0, 0:1]
    grad_0 = (v - unit_1 * jnp.mean(v * unit_1, axis=-1, keepdims=True)) * scale_1
    kept_1, kept_2 = grad_1 * keep, d_mixed_2 * keep
    terms = [
        jnp.sum(a * b, axis=0, keepdims=True)
        for a, b in ((kept_1, unit_1), (kept_1, unit_e1), (kept_2, unit_2), (kept_2, unit_e2))
    ]
    return grad_0.astype(bf16), jnp.concatenate(terms, 0)


def dense_rows(name, token, count, hidden, embed, next_rows, cotangent, gain, before, half, halves, hold=(), after=()):
    tokens, width = hidden.shape
    step = next_rows.shape[0]
    blocks = tokens // step // halves
    low, last = half * blocks, tokens // step - 1
    size = 2 * lanes
    capacity = token.shape[3]
    earlier = [] if before is None else list(before)

    def body(token_ref, count_ref, hidden_ref, embed_ref, next_ref, cot_ref, gain_ref, *refs):
        skip, kept = len(earlier), len(hold)
        hold_refs, refs = refs[skip : skip + kept], refs[:skip] + refs[skip + kept :]
        held_refs, sems = refs[len(refs) - 2 * kept - 2 : len(refs) - kept - 2], refs[len(refs) - kept :]
        out_ref, terms_ref = refs[skip + len(after) : skip + len(after) + 2]
        mixed_ref, sums_ref = refs[len(refs) - kept - 2 : len(refs) - kept]
        holds = [
            pltpu.make_async_copy(ref.at[depth, kind], held_ref, sem)
            for ref, (_, depth, kind), held_ref, sem in zip(hold_refs, hold, held_refs, sems)
        ]
        for copy in holds:
            copy.start()
        sums_ref[...] = jnp.zeros_like(sums_ref)
        row, column = (iota((2 * step, 2 * step), dim) for dim in range(2))
        shift = (column == jnp.where(row < step, row + 1, row + 2 - step)).astype(bf16)
        places = [pl.ds(at, size) for at in range(0, width, size)]

        def folded_lanes(value):
            return sum(value[:, at : at + lanes] for at in range(0, size, lanes))

        def mean(value):
            return jnp.sum(value, axis=1, keepdims=True) / width

        def one(i, carry):
            block = low + i
            first = pl.multiple_of(block * step, step)
            rows = pl.ds(first, step)
            follow = pl.ds(pl.multiple_of(jnp.minimum(block + 1, last) * step, step), step)
            here = iota((step, 1), 0) + first
            keep = jnp.ones((step, 1), f32)
            for k in range(2):
                for c in range(capacity):
                    out = (here == token_ref[0, 0, k, c]) & (c < count_ref[k])
                    keep = jnp.where(out, 0.0, keep)

            def ahead(at, hot):
                after = embed_ref[follow, at]
                if half == halves - 1:
                    after = jnp.where(block == last, next_ref[:, at], after)
                both = jnp.concatenate([embed_ref[rows, at], after], 0)
                return jnp.dot(hot, both, preferred_element_type=f32)

            square_h, square_e = jnp.zeros((step, lanes), f32), jnp.zeros((2 * step, lanes), f32)
            for at in places:
                h, e = hidden_ref[rows, at].astype(f32), ahead(at, shift)
                square_h += folded_lanes(h * h)
                square_e += folded_lanes(e * e)
            scale_1 = lax.rsqrt(mean(square_h) + eps_norm)
            scale_e = lax.rsqrt(mean(square_e) + eps_norm)
            scale_e1, scale_e2 = scale_e[:step], scale_e[step:]

            sums = [jnp.zeros((step, lanes), f32) for _ in range(4)]
            for at in places:
                through = hidden_ref[rows, at].astype(f32) * scale_1 * gain_ref[0, 0:1, at]
                mixed = through + ahead(at, shift[:step]) * scale_e1 * gain_ref[0, 1:2, at]
                kept = mixed.astype(bf16)
                mixed_ref[:, at] = kept
                mixed = kept.astype(f32)
                u = cot_ref[rows, at].astype(f32) * gain_ref[1, 0:1, at]
                pairs = ((mixed, mixed), (u, mixed), (u, through), (mixed, through))
                sums = [c + folded_lanes(a * b) for c, (a, b) in zip(sums, pairs)]
            square, along, u_back, mixed_back = (mean(value) for value in sums)
            scale_2 = lax.rsqrt(square + eps_norm)
            share_2 = scale_2 * scale_2 * along
            share_1 = scale_2 * (u_back - share_2 * mixed_back) * scale_1
            keep_2, keep_h = keep * scale_2, keep * scale_1
            keep_e1, keep_e2 = keep * scale_e1, keep * scale_e2

            for at in places:
                e = ahead(at, shift)
                h = hidden_ref[rows, at].astype(f32)
                mixed = mixed_ref[:, at].astype(f32)
                cot = cot_ref[rows, at].astype(f32)
                grad_1 = (cot * gain_ref[1, 0:1, at] - mixed * share_2) * scale_2
                grad_0 = (grad_1 * gain_ref[0, 0:1, at] - h * share_1) * scale_1
                out_ref[rows, at] = grad_0.astype(bf16)
                terms = (
                    grad_1 * (h * keep_h),
                    grad_1 * (e[:step] * keep_e1),
                    cot * (mixed * keep_2),
                    cot * (e[step:] * keep_e2),
                )
                for k, term in enumerate(terms):
                    sums_ref[k, :, at] += sum(term[r : r + 8] for r in range(0, step, 8))
            return carry

        lax.fori_loop(0, blocks, one, 0)
        for k in range(4):
            term = jnp.sum(sums_ref[k], axis=0, keepdims=True)
            terms_ref[k : k + 1] = term + refs[1][k : k + 1] if earlier else term
        for copy in holds:
            copy.wait()

    return pl.pallas_call(
        body,
        name=name,
        in_specs=[smem] * 2 + [vmem] * (5 + len(earlier)) + [anywhere] * (len(hold) + len(after)),
        out_specs=[vmem] * (2 + len(hold)),
        out_shape=[
            jax.ShapeDtypeStruct((tokens, width), bf16),
            jax.ShapeDtypeStruct((4, width), f32),
        ]
        + [jax.ShapeDtypeStruct(weight.shape[2:], bf16) for weight, _, _ in hold],
        input_output_aliases={7: 0} if earlier else {},
        scratch_shapes=[pltpu.VMEM((step, width), bf16), pltpu.VMEM((4, 8, width), f32)]
        + [pltpu.SemaphoreType.DMA] * len(hold),
        compiler_params=pltpu.CompilerParams(vmem_limit_bytes=8 << 20),
        cost_estimate=pl.CostEstimate(
            flops=60 * tokens * width // halves,
            bytes_accessed=10 * tokens * width // halves,
            transcendentals=0,
        ),
    )(in_hbm(token), in_hbm(count), hidden, embed, next_rows, cotangent, gain, *earlier, *[in_hbm(a) for a, _, _ in hold], *after)


def local(
    main_hidden, embedded, cotangent, slot_token, slot_count, route_gate, norm_gain, expert_weight
):
    depths, _, features = norm_gain.shape
    tokens = main_hidden.shape[2]
    slots = slot_token.shape[3]
    seqs, groups = lax.axis_size("seq"), lax.axis_size("dp")
    rows = seqs * slots
    total = groups * rows
    width = features // seqs
    share = width // groups
    hidden_units = expert_weight.shape[3]
    parts = folds(rows, width)
    source, embed, cot = main_hidden[0, 0], embedded[0, 0], cotangent[0, 0]
    slot_count = slot_count.reshape(-1)
    facts = (slot_token, slot_count)
    packed = ((rows * parts, width // parts), bf16)
    part_rows = ((rows, width), f32)

    def payload(value):
        return folded(value, parts)

    asked_token = ring(slot_token, "section", -1)

    def own_rows(token, count, gate, embed, cot):
        first, second = token_column(token, 0), token_column(token, 1)
        live_1, live_2 = (live_column(count, k, slots) for k in range(2))
        weight_1, weight_2 = gate_column(gate, 0) * live_1, gate_column(gate, 1) * live_2
        facts = in_lanes(
            [first.astype(f32), second.astype(f32), live_1, live_2]
            + thirds(weight_1)
            + thirds(weight_2)
        )
        ahead_1, ahead_2 = pick(first + 1, embed), pick(first + 2, embed)
        block = jnp.concatenate([ahead_1, ahead_2, pick(first, cot)], 0)
        notes = jnp.concatenate([coded(inv_rms(ahead_1)), coded(inv_rms(ahead_2)), facts], 0)
        dout = folded(pick(second, cot) * weight_2, seqs * parts)
        none = jnp.zeros(((parts - 1) * slots, lanes), f32)
        tail = facts if parts == 1 else jnp.concatenate([facts, none], 0)
        dout = jnp.concatenate([dout, jnp.concatenate([tail] * seqs, 0)], 1)
        head = embed[:depths].astype(f32)
        scale = coded(inv_rms(head))
        heads = [
            jnp.concatenate([head[:, p * width : (p + 1) * width], scale], 1) for p in range(seqs)
        ]
        return [
            jnp.concatenate([jnp.concatenate([piece, notes], 1)] + heads, 0)
            for piece in pieces_of(block, seq_place(), seqs)
        ] + [dout]

    fine = width // parts + lanes
    *own_sent, dout_2, gate_1st = call(
        "own_rows", own_rows,
        [((3 * slots + depths * seqs, width + lanes), bf16)] * seqs
        + [((slots * parts * seqs, fine), bf16)],
        (slot_token, slot_count, route_gate), far=(embed, cot),
        hold=((expert_weight, 0, 0),), after=(asked_token,),
    )
    own_got = trade_seq(own_sent)

    def source_rows(asked, source):
        first = pick(token_column(asked, 0), source)
        second = pick(token_column(asked, 1), source)
        scale = coded(inv_rms(first))
        sent = [jnp.concatenate([p, scale], 1) for p in pieces_of(first, seq_place(), seqs)]
        sent[0] = jnp.concatenate([sent[0], second], 1)
        return sent + [first]

    *sent, asked_rows, up_1st = call(
        "source_rows", source_rows,
        [((slots, width + lanes + features), bf16)]
        + [((slots, width + lanes), bf16)] * (seqs - 1)
        + [((slots, features), bf16)],
        (asked_token,), source, hold=((expert_weight, 0, 1),), after=(own_sent[0],),
    )
    start_got = trade_seq(sent, 1)
    dout_2, _ = lax.optimization_barrier((dout_2, sent[0]))

    def second_base(token, count, start, table, got, gain):
        after = got[3 * slots :, :width].astype(f32)
        after = jnp.concatenate([after[p * depths : (p + 1) * depths] for p in range(seqs)], 1)
        after = jnp.where(seq_place() == seqs - 1, 0.0, after)
        after = jnp.concatenate([after, jnp.zeros((16 - depths, features), f32)], 0).astype(bf16)
        second = token_column(token, 1)
        start = start[:, width + lanes :].astype(f32)
        ahead_1 = pick_ahead(second + 1, table, after)
        ahead_2 = pick_ahead(second + 2, table, after)
        unit = start * inv_rms(start)
        mixed = unit * gain[0, 0:1] + ahead_1 * inv_rms(ahead_1) * gain[0, 1:2]
        mixed = mixed.astype(bf16).astype(f32)
        own = mixed * inv_rms(mixed) * gain[1, 0:1] * (1.0 - met_column(token, count))
        out = (own + ahead_2 * inv_rms(ahead_2) * gain[1, 1:2]) * live_column(count, 1, slots)
        bases = [folded(piece, parts) for piece in pieces_of(out, seq_place(), seqs)]
        return bases + [after, ahead_1, ahead_2]

    *base_sent, next_rows, ahead_21, ahead_22, down_1st = call(
        "second_base", second_base,
        [((slots * parts, width // parts), bf16)] * seqs
        + [((16, features), bf16)]
        + [((slots, features), bf16)] * 2,
        facts, start_got[0], embed, own_got[-1], norm_gain,
        hold=((expert_weight, 0, 2),), after=(start_got[-1],),
    )
    base_got = trade_seq(base_sent)

    dout_2_got = gather_dp(dout_2, ahead_21)

    def first_mixed(gain, *got):
        start_got, dout = got[:seqs], [g.astype(f32) for g in got[2 * seqs :]]
        got = [g.astype(f32) for g in got[seqs : 2 * seqs]]
        first = 3 * slots
        block_1, block_2, block_3 = (
            in_order([g[k * slots : (k + 1) * slots] for g in got], seq_place(), 0) for k in range(3)
        )
        facts = block_3[:, width:]
        heads = in_order([g[first:] for g in got], seq_place(), 0)
        heads = [heads[j * depths * seqs : (j + 1) * depths * seqs] for j in range(seqs)]
        units = []
        for k, block in ((1, block_1), (2, block_2)):
            unit = block[:, :width] * decoded(block[:, width:])
            after = []
            for j in range(seqs):
                token = facts[j * slots : (j + 1) * slots, 0:1]
                add = jnp.zeros((slots, width), f32)
                for i in range(k if j + 1 < seqs else 0):
                    row = heads[j + 1][i : i + 1]
                    for p in range(1, seqs):
                        at = p * depths + i
                        row = jnp.where(seq_place() == p, heads[j + 1][at : at + 1], row)
                    row = row[:, :width] * decoded(row[:, width:])
                    add += jnp.where(token == float(tokens + i - k), row, 0.0)
                after.append(add)
            units.append(unit + jnp.concatenate(after, 0))
        start = in_order([g[:, : width + lanes].astype(f32) for g in start_got], seq_place(), 0)
        unit = start[:, :width] * decoded(start[:, width:])
        gain_h, gain_e = (piece_of(gain[0, k : k + 1], seq_place(), seqs, 0) for k in range(2))
        mixed = (unit * gain_h + units[0] * gain_e).astype(bf16).astype(f32)
        douts = zip(*(blocks_of(block, seq_place(), seqs) for block in dout))
        douts = [jnp.concatenate(blocks, 0) for blocks in douts]
        return payload(mixed * facts[:, 2:3]), unit, *units, block_3[:, :width], facts, *douts

    rows_1, unit_1, unit_e1, unit_e2, cot_1, own_facts, *dout_2_sent = call(
        "first_mixed", first_mixed,
        [packed] + [part_rows] * 4 + [((rows, lanes), f32)]
        + [((groups * slots * parts, fine), bf16)] * seqs,
        (), norm_gain, *start_got, *own_got, *dout_2_got, after=(ahead_21,),
    )
    rows_1_all = gather_dp(rows_1)

    def by_slots(got, place):
        blocks = [from_block(got, place, j) for j in range(seqs)]
        pairs = [b[g * slots : (g + 1) * slots] for g in range(parts) for b in blocks]
        return jnp.concatenate(pairs, 0)

    (base_2,) = call(
        "base_order", lambda *got: [by_slots([g.astype(f32) for g in got], seq_place())], [packed],
        (), *base_got, after=(rows_1,),
    )
    base_2_all = gather_dp(base_2)

    weight_1st = (gate_1st, up_1st, down_1st)
    first_own, first_send = project(
        "gate_up_1", rows_1_all, weight_1st, (0, 1), parts, after=(base_2,)
    )
    first = pair_seq(first_own, first_send)

    def forward_1(own, other):
        both = own + other.astype(f32)
        gate, up = both[:, :hidden_units], both[:, hidden_units:]
        return gate * jax.nn.sigmoid(gate) * up, both

    (act_1, both_1), out_blocks = expand(
        "down_1", forward_1, first,
        [((total, hidden_units), bf16), ((total, 2 * hidden_units), f32)],
        weight_1st, (2,), groups, parts,
    )
    out_blocks = lax.optimization_barrier((*out_blocks, *base_2_all))[:groups]
    out_got = return_dp(out_blocks)

    hidden, _ = lax.optimization_barrier((source, rows_1))
    hidden = ring(hidden, "section", 1)
    *dense, gate_2nd, up_2nd, down_2nd = dense_rows(
        "dense_a", *facts, hidden, embed, next_rows, cot, norm_gain, None, 0, 2,
        hold=tuple((expert_weight, 1, k) for k in range(3)), after=(out_blocks[0],),
    )
    weight_2nd = (gate_2nd, up_2nd, down_2nd)

    def second_prev(own_facts, rows_1, *got):
        value = unfolded(rows_1.astype(f32), parts) + summed(got, parts) * decoded(own_facts, 4)
        return payload(value), value.astype(bf16)

    prev, prev_own = call(
        "second_prev", second_prev, [packed, ((rows, width), bf16)],
        (), own_facts, rows_1, *out_got, after=(dense[1],),
    )
    prev_all = gather_dp(prev)

    dout_2_sent = lax.optimization_barrier((*dout_2_sent, out_blocks[0]))[:-1]
    dout_2_traded = trade_seq(dout_2_sent)

    def slot_facts(*got):
        got, size = [g.astype(f32) for g in got], slots * parts
        blocks = [
            by_slots([g[z * size : (z + 1) * size] for g in got], seq_place()) for z in range(groups)
        ]
        facts = jnp.concatenate([block[:rows, width // parts :] for block in blocks], 0)
        base = (iota((total, 1), 0) // slots * tokens).astype(f32)
        first, second = facts[:, 0:1] + base, facts[:, 1:2] + base
        live = (facts[:, 3:4] > 0) & (as_row(facts[:, 2:3]) > 0)
        same = ((second == as_row(first)) & live).astype(f32)
        return same, same, same[:rows, :rows], decoded(facts, 4), *blocks

    same, same_16, same_own, weight_1, *dout_2_all = call(
        "slot_facts", slot_facts,
        [((total, total), f32), ((total, total), bf16), ((rows, rows), f32), ((total, 1), f32)]
        + [((rows * parts, fine), bf16)] * groups,
        (), *dout_2_traded, after=(prev,),
    )
    fixed_own, fixed_send = project(
        "fixed_2", base_2_all, weight_2nd, (0, 1), parts,
        others=(dout_2_all, (2,)), after=(same_own,),
    )
    fixed_pair = pair_seq(fixed_own, fixed_send)

    mixed_own, mixed_send, chosen = project(
        "gate_up_2", prev_all, weight_2nd, (0, 1), parts,
        select=same_16, gain=norm_gain, after=(fixed_own,),
    )
    second = pair_seq(mixed_own, mixed_send)
    prev_w_own, prev_w_send = project(
        "prev_down", prev_all, weight_1st, (2,), parts, after=(mixed_send,)
    )
    prev_pair = pair_seq(prev_w_own, prev_w_send)

    def gates_back(gate, up, d_act):
        sig = jax.nn.sigmoid(gate)
        d_gate = d_act * up * sig * (1.0 + gate * (1.0 - sig))
        return d_gate, d_act * gate * sig

    def backward_2(own, other, fixed_own, fixed_other, same):
        many = 2 * hidden_units
        square = own[:, many : many + 1] + decoded(other[:, many:])
        scale = lax.rsqrt(square / features + eps_norm)
        row = jnp.sum(same * as_row(scale), axis=1, keepdims=True)
        both = (own[:, :many] + other[:, :many].astype(f32)) * row
        fixed = fixed_own + fixed_other.astype(f32)
        both = both + fixed[:, :many]
        gate, up = both[:, :hidden_units], both[:, hidden_units:]
        d_gate, d_up = gates_back(gate, up, fixed[:, many:])
        return d_gate, d_up, gate * jax.nn.sigmoid(gate) * up, scale, row

    units = ((total, hidden_units), bf16)
    (d_gate_2, d_up_2, act_2, scale_2, row_2), d_rows_blocks = expand(
        "back_rows_2", backward_2,
        second + fixed_pair + (same,),
        [units, units, units, ((total, 1), f32), ((total, 1), f32)],
        weight_2nd, (0, 1), groups, parts, after=(prev_w_own,),
    )
    d_rows_got = return_dp(d_rows_blocks)
    dense, dense_terms = dense_rows(
        "dense_b", *facts, hidden, embed, next_rows, cot, norm_gain, dense, 1, 2,
        after=(d_rows_blocks[0],),
    )
    def first_grad(cot, same, gain, *got):
        d_rows = summed(got, parts)
        added = lax.dot_general(
            same, d_rows, (((0,), (0,)), ((), ())),
            precision=lax.Precision.HIGHEST, preferred_element_type=f32,
        )
        d_mixed = cot + added
        u = d_mixed * piece_of(gain[1, 0:1], seq_place(), seqs, 0)
        return [payload(u), d_mixed] + blocks_of(d_rows, seq_place(), seqs)

    u, d_mixed_2, *d_rows_back = call(
        "first_grad", first_grad, [packed, part_rows] + [((slots, width), bf16)] * seqs,
        (), cot_1, same_own, norm_gain, *d_rows_got, after=(dense_terms, prev_pair[1]),
    )
    u_all = gather_dp(u)
    dense, _ = lax.optimization_barrier((dense, u))
    dense = ring(dense, "section", -1)
    back_got = trade_seq(d_rows_back)

    def build_2(values, g):
        chosen, row, base, dout = values[0], values[1], values[2 : 2 + groups], values[2 + groups :]
        step = width // parts
        first = chosen[:, g * step : (g + 1) * step].astype(f32) * row
        first = first + column_part(base, rows, g).astype(f32)
        return first.astype(bf16), column_part(dout, rows, g)[:, :step]

    weight_grad, tick_2 = outer(
        "weight_grad_2", 1, depths, build_2, [chosen, row_2] + base_2_all + dout_2_all,
        d_gate_2, d_up_2, act_2, width, parts, None, after=(u, back_got[-1]),
    )

    back_1_own, back_1_send = project(
        "back_1", u_all, weight_1st, (2,), parts, mates=prev_all, after=(tick_2,)
    )
    back_1 = pair_seq(back_1_own, back_1_send)

    def second_grad(token, count, start, ahead_1, ahead_2, cot, gain, terms, *got):
        d_rows = in_order([g.astype(f32) for g in got], seq_place(), 1)
        keep = live_column(count, 1, slots) * (1.0 - met_column(token, count))
        grad, more = backward_rows(
            start[:, width + lanes :].astype(f32), ahead_1.astype(f32), ahead_2.astype(f32),
            pick(token_column(token, 1), cot) + d_rows, keep, gain,
        )
        notes = in_lanes([live_column(count, 0, slots), keep])
        grad = jnp.concatenate([grad.astype(f32), notes], 1)
        return [grad] + pieces_of(terms + more, seq_place(), seqs)

    grad_2, *terms_parts = call(
        "second_grad", second_grad,
        [((slots, features + lanes), bf16)] + [((2 * depths, width), f32)] * seqs,
        facts, start_got[0], ahead_21, ahead_22, cot, norm_gain, dense_terms, *back_got,
        after=(back_1_send,),
    )
    grad_2 = ring(grad_2, "section", -1)
    terms_got = trade_seq(terms_parts)

    def backward_1(own, other, prev_own, prev_other, both, scale, weight_1):
        inner = own[:, hidden_units : hidden_units + 1] + decoded(other[:, hidden_units:])
        d_act = own[:, :hidden_units] + other[:, :hidden_units].astype(f32)
        through = scale * scale * inner / features
        d_act = d_act - through * (prev_own + prev_other.astype(f32))
        d_act = d_act * (weight_1 * scale)
        d_gate, d_up = gates_back(both[:, :hidden_units], both[:, hidden_units:], d_act)
        return d_gate, d_up, through

    (d_gate_1, d_up_1, through_1), d_rows_blocks = expand(
        "back_rows_1", backward_1,
        back_1 + prev_pair + (both_1, scale_2, weight_1),
        [units, units, ((total, 1), f32)],
        weight_1st, (0, 1), groups, parts, after=(terms_parts[0],),
    )
    d_rows_got = return_dp(d_rows_blocks)

    def build_1(values, g):
        through, scale, weight = values[:3]
        first, u, prev = (values[3 + k * groups : 3 + (k + 1) * groups] for k in range(3))
        dout = column_part(u, rows, g).astype(f32) - through * column_part(prev, rows, g).astype(f32)
        return column_part(first, rows, g), (dout * (weight * scale)).astype(bf16)

    weight_grad, tick_1 = outer(
        "weight_grad_1", 0, depths, build_1,
        [through_1, scale_2, weight_1] + rows_1_all + u_all + prev_all,
        d_gate_1, d_up_1, act_1, width, parts, weight_grad, after=(d_rows_blocks[0],),
    )

    def last_grad(d_mixed_2, prev, scale, through, unit_1, unit_e1, unit_e2, own_facts, gain, *got):
        got, terms = got[:groups], got[groups:]
        d_rows = summed(got, parts)
        gain_1, gain_2 = (piece_of(gain[k, 0:1], seq_place(), seqs, 0) for k in range(2))
        scale, through = scale[:rows], through[:rows]
        live = own_facts[:, 2:3]
        prev = prev.astype(f32)
        grad_1 = (d_mixed_2 * gain_2 - through * prev) * scale
        d_mixed_1 = grad_1 + d_rows
        kept_1, kept_2 = d_mixed_1 * live, d_mixed_2 * live
        sums = [
            jnp.sum(a * b, axis=0, keepdims=True)
            for a, b in ((kept_1, unit_1), (kept_1, unit_e1), (kept_2, prev * scale), (kept_2, unit_e2))
        ]
        sums = jnp.concatenate(sums, 0) + sum(terms)
        cut = []
        for i in range(groups):
            block = sums[:, :share]
            for z in range(groups):
                at = partner(z, i, groups) * share
                block = jnp.where(lax.axis_index("dp") == z, sums[:, at : at + share], block)
            cut.append(block)
        return cut + blocks_of(d_mixed_1 * gain_1, seq_place(), seqs)

    last = call(
        "last_grad", last_grad,
        [((2 * depths, share), f32)] * groups + [((slots, width), bf16)] * seqs,
        (), d_mixed_2, prev_own, scale_2, through_1, unit_1, unit_e1, unit_e2,
        own_facts, norm_gain, *d_rows_got, *terms_got, after=(tick_1,),
    )
    last_got = trade_seq(last[groups:], -1)
    sums_got = return_dp(last[:groups])

    def finish(token, dense, asked_rows, grad_2, *got):
        part = in_order([g.astype(f32) for g in got], seq_place(), 1)
        asked_rows = asked_rows.astype(f32)
        scale = inv_rms(asked_rows)
        unit = asked_rows * scale
        grad_1 = (part - unit * jnp.mean(part * unit, axis=-1, keepdims=True)) * scale
        notes = grad_2[:, features:].astype(f32)
        grads = jnp.concatenate([grad_1, grad_2[:, :features].astype(f32)], 0).astype(bf16)
        lane = iota((slots, tokens), 1)
        chosen = jnp.concatenate(
            [
                jnp.where(lane == token_column(token, k), notes[:, k : k + 1], 0.0)
                for k in range(2)
            ],
            0,
        ).astype(bf16)
        taken = lax.dot_general(
            chosen, jnp.ones((2 * slots, lanes), bf16), (((0,), (0,)), ((), ())),
            preferred_element_type=f32,
        )[:, 0:1]
        out = []
        step = chunk_of(features)
        for at in range(0, features, step):
            placed = lax.dot_general(
                chosen, grads[:, at : at + step], (((0,), (0,)), ((), ())),
                preferred_element_type=f32,
            )
            out.append(jnp.where(taken > 0, placed, dense[:, at : at + step].astype(f32)).astype(bf16))
        return [jnp.concatenate(out, 1), jnp.zeros((8, lanes), f32)]

    hidden_grad, tick = call(
        "finish", finish, [((tokens, features), bf16), ((8, lanes), f32)],
        (asked_token,), dense, asked_rows, grad_2, *last_got, limit=20,
    )

    def gain_sum(*got):
        sums = sum(got)
        return [jnp.stack([sums[2 * k : 2 * k + 2] for k in range(depths)])[None]]

    (gain_grad,) = call(
        "gain_sum", gain_sum, [((1, depths, 2, share), f32)], (), *sums_got, after=(tick,)
    )
    return (
        hidden_grad[None, None],
        weight_grad,
        gain_grad,
    )


def solution(mesh):
    return jax.shard_map(
        local,
        mesh=mesh,
        in_specs=(
            P("section", "dp", "seq", None),
            P("section", "dp", "seq", None),
            P("section", "dp", "seq", None),
            P("section", "dp", None, "seq"),
            P("section", "dp", None, "seq"),
            P("section", "dp", None, "seq"),
            P(),
            P(None, None, "seq", "dp"),
        ),
        out_specs=(
            P("section", "dp", "seq", None),
            P("section", None, None, "seq", "dp"),
            P("section", None, None, ("seq", "dp")),
        ),
        check_vma=False,
    )
```

```python
import jax
import jax.numpy as jnp
from jax import lax
from jax.experimental import pallas as pl
from jax.experimental.pallas import tpu as pltpu
from jax.sharding import PartitionSpec as P

eps_norm = 1e-06
lanes = 128
f32 = jnp.float32
bf16 = jnp.bfloat16
vmem = pl.BlockSpec(memory_space=pltpu.VMEM)
smem = pl.BlockSpec(memory_space=pltpu.SMEM)
anywhere = pl.BlockSpec(memory_space=pl.ANY)


def ring(value, axis, steps):
    count = lax.axis_size(axis)
    return lax.ppermute(value, axis, [(i, (i + steps) % count) for i in range(count)])


def hop(value, section_step, seq_step):
    sections, seqs = lax.axis_size("section"), lax.axis_size("seq")
    pairs = [
        (c * seqs + s, (c + section_step) % sections * seqs + (s + seq_step) % seqs)
        for c in range(sections)
        for s in range(seqs)
    ]
    return lax.ppermute(value, ("section", "seq"), pairs)


def trade_seq(pieces, section_step=0):
    if section_step == 0:
        return [pieces[0]] + [ring(pieces[o], "seq", o) for o in range(1, len(pieces))]
    return [hop(piece, section_step, o) for o, piece in enumerate(pieces)]


def partner(place, step, count):
    return place ^ step if count & (count - 1) == 0 else (place - step) % count


def gather_dp(block):
    count = lax.axis_size("dp")
    return [block] + [
        lax.ppermute(block, "dp", [(partner(z, i, count), z) for z in range(count)])
        for i in range(1, count)
    ]


def return_dp(blocks):
    count = lax.axis_size("dp")
    return [blocks[0]] + [
        lax.ppermute(blocks[i], "dp", [(z, partner(z, i, count)) for z in range(count)])
        for i in range(1, count)
    ]


def pair_seq(own, send):
    if lax.axis_size("seq") == 2:
        return own, ring(send, "seq", 1)
    return lax.psum(own, "seq"), jnp.zeros_like(send)


def inv_rms(value):
    return lax.rsqrt(jnp.mean(value * value, axis=-1, keepdims=True) + eps_norm)


def iota(shape, dim):
    return lax.broadcasted_iota(jnp.int32, shape, dim)


def seq_place():
    return lax.axis_index("seq").astype(jnp.int32)


def token_column(token, depth):
    capacity = token.shape[3]
    out = jnp.full((capacity, 1), token[0, 0, depth, 0], jnp.int32)
    for c in range(1, capacity):
        out = jnp.where(iota((capacity, 1), 0) == c, token[0, 0, depth, c], out)
    return out


def gate_column(gate, depth):
    capacity = gate.shape[3]
    out = jnp.full((capacity, 1), gate[0, 0, depth, 0], f32)
    for c in range(1, capacity):
        out = jnp.where(iota((capacity, 1), 0) == c, gate[0, 0, depth, c], out)
    return out


def live_column(count, depth, capacity):
    return (iota((capacity, 1), 0) < count[depth]).astype(f32)


def met_column(token, count):
    capacity = token.shape[3]
    second = token_column(token, 1)
    out = jnp.zeros((capacity, 1), f32)
    for c in range(capacity):
        out += ((second == token[0, 0, 0, c]) & (c < count[0])).astype(f32)
    return jnp.minimum(out, 1.0)


def pick(column, table):
    hot = (column == iota((column.shape[0], table.shape[0]), 1)).astype(bf16)
    return jnp.dot(hot, table, preferred_element_type=f32)


def pick_ahead(column, table, after):
    return pick(column, table) + pick(column - table.shape[0], after)


def thirds(column):
    high = column.astype(bf16).astype(f32)
    mid = (column - high).astype(bf16).astype(f32)
    return [high, mid, column - high - mid]


def in_lanes(columns):
    lane = iota((columns[0].shape[0], lanes), 1)
    out = jnp.zeros(lane.shape, f32)
    for k, column in enumerate(columns):
        out = jnp.where(lane == k, column, out)
    return out


def coded(column):
    return in_lanes(thirds(column))


def decoded(block, first=0):
    lane = iota(block.shape, 1)
    inside = (lane >= first) & (lane < first + 3)
    return jnp.sum(jnp.where(inside, block.astype(f32), 0.0), axis=1, keepdims=True)


def piece_of(value, place, count, step):
    width = value.shape[-1] // count
    want = lax.rem(place + step, count)
    out = value[:, :width]
    for p in range(1, count):
        out = jnp.where(want == p, value[:, p * width : (p + 1) * width], out)
    return out


def pieces_of(value, place, count):
    return [piece_of(value, place, count, o) for o in range(count)]


def blocks_of(value, place, count):
    size = value.shape[0] // count
    out = []
    for o in range(count):
        block = value[:size]
        for j in range(1, count):
            want = lax.rem(place + o, count) == j
            block = jnp.where(want, value[j * size : (j + 1) * size], block)
        out.append(block)
    return out


def from_block(got, place, block):
    count = len(got)
    out = got[0]
    for o in range(1, count):
        out = jnp.where(lax.rem(place - o + count, count) == block, got[o], out)
    return out


def in_order(got, place, axis):
    return jnp.concatenate([from_block(got, place, j) for j in range(len(got))], axis)


def as_row(column):
    size = column.shape[0]
    here = iota((size, size), 0) == iota((size, size), 1)
    return jnp.sum(jnp.where(here, column, 0.0), axis=0, keepdims=True)


def folds(rows, width):
    for count in (1, 2, 4, 8):
        if rows * count % 16 == 0 and width % (count * lanes) == 0:
            return count
    return 1


def folded(value, count):
    step = value.shape[1] // count
    return jnp.concatenate([value[:, g * step : (g + 1) * step] for g in range(count)], 0)


def unfolded(value, count):
    rows = value.shape[0] // count
    return jnp.concatenate([value[g * rows : (g + 1) * rows] for g in range(count)], 1)


def column_part(blocks, rows, g):
    return jnp.concatenate(
        [block[g * rows : (g + 1) * rows].astype(f32) for block in blocks], 0
    ).astype(bf16)


def summed(got, parts):
    return unfolded(sum(g.astype(f32) for g in got), parts)


def chunk_of(width):
    for step in (1024, 896, 512, 256, 128):
        if width % step == 0:
            return step
    return width


def in_hbm(value):
    return pltpu.with_memory_space_constraint(value, pltpu.HBM)


def call(name, fn, outs, small, *args, far=(), hold=(), after=(), flops=0, limit=12):
    outs = list(outs) + [(weight.shape[2:], bf16) for weight, _, _ in hold]
    shapes = [jax.ShapeDtypeStruct(shape, kind) for shape, kind in outs]
    n_small, n_args, n_far, n_outs = len(small), len(args), len(far), len(shapes) - len(hold)

    def body(*refs):
        refs = list(refs)

        def take(count):
            taken, refs[:] = refs[:count], refs[count:]
            return taken

        small_refs, arg_refs, far_refs = take(n_small), take(n_args), take(n_far)
        hold_refs = take(len(hold))
        take(len(after))
        out_refs, held_refs, buffers = take(n_outs), take(len(hold)), take(n_far)
        copies = [pltpu.make_async_copy(*trio) for trio in zip(far_refs, buffers, take(n_far))]
        holds = [
            pltpu.make_async_copy(ref.at[depth, kind], held_ref, sem)
            for ref, (_, depth, kind), held_ref, sem in zip(hold_refs, hold, held_refs, refs)
        ]
        for copy in copies + holds:
            copy.start()
        for copy in copies:
            copy.wait()
        values = small_refs + [r[...] for r in arg_refs + buffers]
        for ref, value in zip(out_refs, fn(*values)):
            ref[...] = value.astype(ref.dtype)
        for copy in holds:
            copy.wait()

    size = sum(a.size * a.dtype.itemsize for a in list(args) + list(far) + shapes)
    return pl.pallas_call(
        body,
        name=name,
        out_shape=shapes,
        in_specs=[smem] * n_small + [vmem] * n_args + [anywhere] * (n_far + len(hold) + len(after)),
        out_specs=[vmem] * len(shapes),
        scratch_shapes=[pltpu.VMEM(a.shape, a.dtype) for a in far]
        + [pltpu.SemaphoreType.DMA] * (n_far + len(hold)),
        compiler_params=pltpu.CompilerParams(vmem_limit_bytes=limit << 20),
        cost_estimate=pl.CostEstimate(flops=flops, bytes_accessed=size, transcendentals=0),
    )(*[in_hbm(a) for a in small], *args, *[in_hbm(a) for a in far], *[in_hbm(a) for a, _, _ in hold], *after)


def project(name, blocks, weights, kinds, parts, others=None, select=None, gain=None, mates=None, after=()):
    groups = len(blocks)
    rows = blocks[0].shape[0] // parts
    width, hidden = weights[0].shape
    step = width // parts
    other_blocks, other_kinds = others if others is not None else ([], ())
    first_kinds, kinds = kinds, kinds + other_kinds
    many_kinds = len(kinds)
    total, many = rows * groups, len(kinds) * hidden
    marked = select is not None or mates is not None
    extra = lanes if marked else 0

    def body(*refs):
        refs = list(refs)
        x_refs, w_refs, refs = refs[:groups], refs[groups : groups + many_kinds], refs[groups + many_kinds :]
        other_refs, refs = refs[: len(other_blocks)], refs[len(other_blocks) :]
        if select is not None:
            select_ref, gain_ref = refs.pop(0), refs.pop(0)
        if mates is not None:
            mate_refs, refs = refs[:groups], refs[groups:]
        refs = refs[len(after) :]
        own_ref, send_ref = refs.pop(0), refs.pop(0)
        kept_ref = refs.pop(0) if select is not None else None
        x_all = [r[...] for r in x_refs]
        mate_all = [r[...] for r in mate_refs] if mates is not None else x_all
        if select is not None:
            gain_all = piece_of(gain_ref[1, 0:1, :], seq_place(), gain.shape[2] // width, 0)
        sums = [jnp.zeros((total, hidden), f32) for _ in kinds]
        mark = jnp.zeros((total, 1), f32)
        for g in range(parts):
            x = column_part(x_all, rows, g)
            if marked:
                mate = x if mates is None else column_part(mate_all, rows, g)
                mark += jnp.sum(x.astype(f32) * mate.astype(f32), axis=1, keepdims=True)
            if select is not None:
                chosen = jnp.dot(select_ref[...], x, preferred_element_type=f32)
                x = (chosen * gain_all[:, g * step : (g + 1) * step]).astype(bf16)
                kept_ref[:, g * step : (g + 1) * step] = x
            for k in range(len(kinds)):
                if k == len(first_kinds):
                    x = column_part([r[...] for r in other_refs], rows, g)[:, :step]
                part_ref = w_refs[k].at[pl.ds(g * step, step)]
                sums[k] += jnp.dot(x, part_ref[...], preferred_element_type=f32)
        for k in range(len(kinds)):
            own_ref[:, k * hidden : (k + 1) * hidden] = sums[k]
            send_ref[:, k * hidden : (k + 1) * hidden] = sums[k].astype(bf16)
        if marked:
            own_ref[:, many:] = in_lanes([mark])
            send_ref[:, many:] = coded(mark).astype(bf16)

    args = list(blocks) + [weights[k] for k in kinds]
    args, specs = args + list(other_blocks), [vmem] * (groups + many_kinds) + [vmem] * len(other_blocks)
    outs = [
        jax.ShapeDtypeStruct((total, many + extra), f32),
        jax.ShapeDtypeStruct((total, many + extra), bf16),
    ]
    if select is not None:
        args, specs = args + [select, gain], specs + [vmem, vmem]
        outs.append(jax.ShapeDtypeStruct((total, width), bf16))
    if mates is not None:
        args, specs = args + list(mates), specs + [vmem] * groups
    return pl.pallas_call(
        body,
        name=name,
        in_specs=specs + [anywhere] * len(after),
        out_specs=[vmem] * len(outs),
        out_shape=outs,
        compiler_params=pltpu.CompilerParams(vmem_limit_bytes=8 << 20),
        cost_estimate=pl.CostEstimate(
            flops=2 * total * width * many, bytes_accessed=2 * width * many, transcendentals=0
        ),
    )(*args, *after)


def expand(name, prepare, args, saved, weights, kinds, groups, parts, after=()):
    width, hidden = weights[0].shape
    total = saved[0][0][0]
    rows, step = total // groups, width // parts
    count, kept = len(args), len(saved)

    def body(*refs):
        in_refs, w_refs = refs[:count], refs[count : count + len(kinds)]
        refs = refs[count + len(kinds) + len(after) :]
        saved_refs, out_refs = refs[:kept], refs[kept:]
        for ref, value in zip(saved_refs, prepare(*[r[...] for r in in_refs])):
            ref[...] = value.astype(ref.dtype)
        out = []
        for g in range(parts):
            part = jnp.zeros((total, step), f32)
            for k in range(len(kinds)):
                part_ref = w_refs[k].at[pl.ds(g * step, step)]
                part += lax.dot_general(
                    saved_refs[k][...], part_ref[...], (((1,), (1,)), ((), ())),
                    preferred_element_type=f32,
                )
            out.append(part)
        for z in range(groups):
            block = jnp.concatenate([part[z * rows : (z + 1) * rows] for part in out], 0)
            out_refs[z][...] = block.astype(bf16)

    results = pl.pallas_call(
        body,
        name=name,
        in_specs=[vmem] * (count + len(kinds)) + [anywhere] * len(after),
        out_specs=[vmem] * (kept + groups),
        out_shape=[jax.ShapeDtypeStruct(shape, kind) for shape, kind in saved]
        + [jax.ShapeDtypeStruct((rows * parts, step), bf16)] * groups,
        compiler_params=pltpu.CompilerParams(vmem_limit_bytes=8 << 20),
        cost_estimate=pl.CostEstimate(
            flops=2 * total * width * hidden * len(kinds),
            bytes_accessed=2 * width * hidden * len(kinds),
            transcendentals=0,
        ),
    )(*args, *[weights[k] for k in kinds], *after)
    return results[:kept], results[kept:]


def outer(name, depth, depths, build, args, d_gate, d_up, act, width, parts, before, after=()):
    total, hidden = act.shape
    step = width // parts
    count = len(args)
    earlier = [] if before is None else [in_hbm(before)]

    def contract(left, right):
        return lax.dot_general(left, right, (((0,), (0,)), ((), ())), preferred_element_type=f32)

    def body(*refs):
        values = [r[...] for r in refs[:count]]
        gate_ref, up_ref, act_ref = refs[count : count + 3]
        out_ref, tick_ref, buffer, sems = refs[-4:]
        tick_ref[...] = jnp.zeros_like(tick_ref)
        copies = []
        for g in range(parts):
            rows, dout = build(values, g)
            pairs = ((rows, gate_ref), (rows, up_ref), (dout, act_ref))
            for k, (left, right_ref) in enumerate(pairs):
                buffer[g, k] = contract(left, right_ref[...]).astype(bf16)
                copy = pltpu.make_async_copy(
                    buffer.at[g, k],
                    out_ref.at[0, depth, k, pl.ds(g * step, step)],
                    sems.at[g, k],
                )
                copy.start()
                copies.append(copy)
        for copy in copies:
            copy.wait()

    return pl.pallas_call(
        body,
        name=name,
        in_specs=[vmem] * (count + 3) + [anywhere] * (len(earlier) + len(after)),
        out_specs=[anywhere, vmem],
        out_shape=[
            jax.ShapeDtypeStruct((1, depths, 3, width, hidden), bf16),
            jax.ShapeDtypeStruct((8, lanes), f32),
        ],
        input_output_aliases={} if before is None else {count + 3: 0},
        scratch_shapes=[
            pltpu.VMEM((parts, 3, step, hidden), bf16),
            pltpu.SemaphoreType.DMA((parts, 3)),
        ],
        compiler_params=pltpu.CompilerParams(vmem_limit_bytes=24 << 20),
        cost_estimate=pl.CostEstimate(
            flops=6 * total * width * hidden, bytes_accessed=6 * width * hidden, transcendentals=0
        ),
    )(*args, d_gate, d_up, act, *earlier, *after)


def backward_rows(hidden, ahead_1, ahead_2, d_mixed_2, keep, gain):
    scale_1 = inv_rms(hidden)
    unit_1 = hidden * scale_1
    unit_e1 = ahead_1 * inv_rms(ahead_1)
    unit_e2 = ahead_2 * inv_rms(ahead_2)
    mixed = (unit_1 * gain[0, 0:1] + unit_e1 * gain[0, 1:2]).astype(bf16).astype(f32)
    scale_2 = inv_rms(mixed)
    unit_2 = mixed * scale_2
    u = d_mixed_2 * gain[1, 0:1]
    grad_1 = (u - unit_2 * jnp.mean(u * unit_2, axis=-1, keepdims=True)) * scale_2
    v = grad_1 * gain[0, 0:1]
    grad_0 = (v - unit_1 * jnp.mean(v * unit_1, axis=-1, keepdims=True)) * scale_1
    kept_1, kept_2 = grad_1 * keep, d_mixed_2 * keep
    terms = [
        jnp.sum(a * b, axis=0, keepdims=True)
        for a, b in ((kept_1, unit_1), (kept_1, unit_e1), (kept_2, unit_2), (kept_2, unit_e2))
    ]
    return grad_0.astype(bf16), jnp.concatenate(terms, 0)


def dense_rows(name, token, count, hidden, embed, next_rows, cotangent, gain, before, half, halves, hold=(), after=()):
    tokens, width = hidden.shape
    step = next_rows.shape[0]
    blocks = tokens // step // halves
    low, last = half * blocks, tokens // step - 1
    size = 2 * lanes
    capacity = token.shape[3]
    earlier = [] if before is None else list(before)

    def body(token_ref, count_ref, hidden_ref, embed_ref, next_ref, cot_ref, gain_ref, *refs):
        skip, kept = len(earlier), len(hold)
        hold_refs, refs = refs[skip : skip + kept], refs[:skip] + refs[skip + kept :]
        held_refs, sems = refs[len(refs) - 2 * kept - 2 : len(refs) - kept - 2], refs[len(refs) - kept :]
        out_ref, terms_ref = refs[skip + len(after) : skip + len(after) + 2]
        mixed_ref, sums_ref = refs[len(refs) - kept - 2 : len(refs) - kept]
        holds = [
            pltpu.make_async_copy(ref.at[depth, kind], held_ref, sem)
            for ref, (_, depth, kind), held_ref, sem in zip(hold_refs, hold, held_refs, sems)
        ]
        for copy in holds:
            copy.start()
        sums_ref[...] = jnp.zeros_like(sums_ref)
        row, column = (iota((2 * step, 2 * step), dim) for dim in range(2))
        shift = (column == jnp.where(row < step, row + 1, row + 2 - step)).astype(bf16)
        places = [pl.ds(at, size) for at in range(0, width, size)]

        def folded_lanes(value):
            return sum(value[:, at : at + lanes] for at in range(0, size, lanes))

        def mean(value):
            return jnp.sum(value, axis=1, keepdims=True) / width

        def one(i, carry):
            block = low + i
            first = pl.multiple_of(block * step, step)
            rows = pl.ds(first, step)
            follow = pl.ds(pl.multiple_of(jnp.minimum(block + 1, last) * step, step), step)
            here = iota((step, 1), 0) + first
            keep = jnp.ones((step, 1), f32)
            for k in range(2):
                for c in range(capacity):
                    out = (here == token_ref[0, 0, k, c]) & (c < count_ref[k])
                    keep = jnp.where(out, 0.0, keep)

            def ahead(at, hot):
                after = embed_ref[follow, at]
                if half == halves - 1:
                    after = jnp.where(block == last, next_ref[:, at], after)
                both = jnp.concatenate([embed_ref[rows, at], after], 0)
                return jnp.dot(hot, both, preferred_element_type=f32)

            square_h, square_e = jnp.zeros((step, lanes), f32), jnp.zeros((2 * step, lanes), f32)
            for at in places:
                h, e = hidden_ref[rows, at].astype(f32), ahead(at, shift)
                square_h += folded_lanes(h * h)
                square_e += folded_lanes(e * e)
            scale_1 = lax.rsqrt(mean(square_h) + eps_norm)
            scale_e = lax.rsqrt(mean(square_e) + eps_norm)
            scale_e1, scale_e2 = scale_e[:step], scale_e[step:]

            sums = [jnp.zeros((step, lanes), f32) for _ in range(4)]
            for at in places:
                through = hidden_ref[rows, at].astype(f32) * scale_1 * gain_ref[0, 0:1, at]
                mixed = through + ahead(at, shift[:step]) * scale_e1 * gain_ref[0, 1:2, at]
                kept = mixed.astype(bf16)
                mixed_ref[:, at] = kept
                mixed = kept.astype(f32)
                u = cot_ref[rows, at].astype(f32) * gain_ref[1, 0:1, at]
                pairs = ((mixed, mixed), (u, mixed), (u, through), (mixed, through))
                sums = [c + folded_lanes(a * b) for c, (a, b) in zip(sums, pairs)]
            square, along, u_back, mixed_back = (mean(value) for value in sums)
            scale_2 = lax.rsqrt(square + eps_norm)
            share_2 = scale_2 * scale_2 * along
            share_1 = scale_2 * (u_back - share_2 * mixed_back) * scale_1
            keep_2, keep_h = keep * scale_2, keep * scale_1
            keep_e1, keep_e2 = keep * scale_e1, keep * scale_e2

            for at in places:
                e = ahead(at, shift)
                h = hidden_ref[rows, at].astype(f32)
                mixed = mixed_ref[:, at].astype(f32)
                cot = cot_ref[rows, at].astype(f32)
                grad_1 = (cot * gain_ref[1, 0:1, at] - mixed * share_2) * scale_2
                grad_0 = (grad_1 * gain_ref[0, 0:1, at] - h * share_1) * scale_1
                out_ref[rows, at] = grad_0.astype(bf16)
                terms = (
                    grad_1 * (h * keep_h),
                    grad_1 * (e[:step] * keep_e1),
                    cot * (mixed * keep_2),
                    cot * (e[step:] * keep_e2),
                )
                for k, term in enumerate(terms):
                    sums_ref[k, :, at] += sum(term[r : r + 8] for r in range(0, step, 8))
            return carry

        lax.fori_loop(0, blocks, one, 0)
        for k in range(4):
            term = jnp.sum(sums_ref[k], axis=0, keepdims=True)
            terms_ref[k : k + 1] = term + refs[1][k : k + 1] if earlier else term
        for copy in holds:
            copy.wait()

    return pl.pallas_call(
        body,
        name=name,
        in_specs=[smem] * 2 + [vmem] * (5 + len(earlier)) + [anywhere] * (len(hold) + len(after)),
        out_specs=[vmem] * (2 + len(hold)),
        out_shape=[
            jax.ShapeDtypeStruct((tokens, width), bf16),
            jax.ShapeDtypeStruct((4, width), f32),
        ]
        + [jax.ShapeDtypeStruct(weight.shape[2:], bf16) for weight, _, _ in hold],
        input_output_aliases={7: 0} if earlier else {},
        scratch_shapes=[pltpu.VMEM((step, width), bf16), pltpu.VMEM((4, 8, width), f32)]
        + [pltpu.SemaphoreType.DMA] * len(hold),
        compiler_params=pltpu.CompilerParams(vmem_limit_bytes=8 << 20),
        cost_estimate=pl.CostEstimate(
            flops=60 * tokens * width // halves,
            bytes_accessed=10 * tokens * width // halves,
            transcendentals=0,
        ),
    )(in_hbm(token), in_hbm(count), hidden, embed, next_rows, cotangent, gain, *earlier, *[in_hbm(a) for a, _, _ in hold], *after)


def local(
    main_hidden, embedded, cotangent, slot_token, slot_count, route_gate, norm_gain, expert_weight
):
    depths, _, features = norm_gain.shape
    tokens = main_hidden.shape[2]
    slots = slot_token.shape[3]
    seqs, groups = lax.axis_size("seq"), lax.axis_size("dp")
    rows = seqs * slots
    total = groups * rows
    width = features // seqs
    share = width // groups
    hidden_units = expert_weight.shape[3]
    parts = folds(rows, width)
    source, embed, cot = main_hidden[0, 0], embedded[0, 0], cotangent[0, 0]
    slot_count = slot_count.reshape(-1)
    facts = (slot_token, slot_count)
    packed = ((rows * parts, width // parts), bf16)
    part_rows = ((rows, width), f32)

    def payload(value):
        return folded(value, parts)

    asked_token = ring(slot_token, "section", -1)

    def own_rows(token, count, gate, embed, cot):
        first, second = token_column(token, 0), token_column(token, 1)
        live_1, live_2 = (live_column(count, k, slots) for k in range(2))
        weight_1, weight_2 = gate_column(gate, 0) * live_1, gate_column(gate, 1) * live_2
        facts = in_lanes(
            [first.astype(f32), second.astype(f32), live_1, live_2]
            + thirds(weight_1)
            + thirds(weight_2)
        )
        ahead_1, ahead_2 = pick(first + 1, embed), pick(first + 2, embed)
        block = jnp.concatenate([ahead_1, ahead_2, pick(first, cot)], 0)
        notes = jnp.concatenate([coded(inv_rms(ahead_1)), coded(inv_rms(ahead_2)), facts], 0)
        dout = folded(pick(second, cot) * weight_2, seqs * parts)
        none = jnp.zeros(((parts - 1) * slots, lanes), f32)
        tail = facts if parts == 1 else jnp.concatenate([facts, none], 0)
        dout = jnp.concatenate([dout, jnp.concatenate([tail] * seqs, 0)], 1)
        head = embed[:depths].astype(f32)
        scale = coded(inv_rms(head))
        heads = [
            jnp.concatenate([head[:, p * width : (p + 1) * width], scale], 1) for p in range(seqs)
        ]
        return [
            jnp.concatenate([jnp.concatenate([piece, notes], 1)] + heads, 0)
            for piece in pieces_of(block, seq_place(), seqs)
        ] + [dout]

    fine = width // parts + lanes
    *own_sent, dout_2, gate_1st = call(
        "own_rows", own_rows,
        [((3 * slots + depths * seqs, width + lanes), bf16)] * seqs
        + [((slots * parts * seqs, fine), bf16)],
        (slot_token, slot_count, route_gate), far=(embed, cot),
        hold=((expert_weight, 0, 0),),
    )
    own_sent = lax.optimization_barrier((*own_sent, asked_token))[:-1]
    own_got = trade_seq(own_sent)

    def source_rows(asked, source):
        first = pick(token_column(asked, 0), source)
        second = pick(token_column(asked, 1), source)
        scale = coded(inv_rms(first))
        sent = [jnp.concatenate([p, scale], 1) for p in pieces_of(first, seq_place(), seqs)]
        sent[0] = jnp.concatenate([sent[0], second], 1)
        return sent + [first]

    *sent, asked_rows = call(
        "source_rows", source_rows,
        [((slots, width + lanes + features), bf16)]
        + [((slots, width + lanes), bf16)] * (seqs - 1)
        + [((slots, features), bf16)],
        (asked_token,), source, after=(own_sent[0],),
    )
    start_got = trade_seq(sent, 1)
    dout_2, _ = lax.optimization_barrier((dout_2, sent[0]))

    def second_base(token, count, start, table, got, gain):
        after = got[3 * slots :, :width].astype(f32)
        after = jnp.concatenate([after[p * depths : (p + 1) * depths] for p in range(seqs)], 1)
        after = jnp.where(seq_place() == seqs - 1, 0.0, after)
        after = jnp.concatenate([after, jnp.zeros((16 - depths, features), f32)], 0).astype(bf16)
        second = token_column(token, 1)
        start = start[:, width + lanes :].astype(f32)
        ahead_1 = pick_ahead(second + 1, table, after)
        ahead_2 = pick_ahead(second + 2, table, after)
        unit = start * inv_rms(start)
        mixed = unit * gain[0, 0:1] + ahead_1 * inv_rms(ahead_1) * gain[0, 1:2]
        mixed = mixed.astype(bf16).astype(f32)
        own = mixed * inv_rms(mixed) * gain[1, 0:1] * (1.0 - met_column(token, count))
        out = (own + ahead_2 * inv_rms(ahead_2) * gain[1, 1:2]) * live_column(count, 1, slots)
        bases = [folded(piece, parts) for piece in pieces_of(out, seq_place(), seqs)]
        return bases + [after, ahead_1, ahead_2]

    *base_sent, next_rows, ahead_21, ahead_22 = call(
        "second_base", second_base,
        [((slots * parts, width // parts), bf16)] * seqs
        + [((16, features), bf16)]
        + [((slots, features), bf16)] * 2,
        facts, start_got[0], embed, own_got[-1], norm_gain, after=(start_got[-1],),
    )
    base_got = trade_seq(base_sent)

    dout_2_got = gather_dp(dout_2)

    def first_mixed(gain, *got):
        start_got, dout = got[:seqs], [g.astype(f32) for g in got[2 * seqs :]]
        got = [g.astype(f32) for g in got[seqs : 2 * seqs]]
        first = 3 * slots
        block_1, block_2, block_3 = (
            in_order([g[k * slots : (k + 1) * slots] for g in got], seq_place(), 0) for k in range(3)
        )
        facts = block_3[:, width:]
        heads = in_order([g[first:] for g in got], seq_place(), 0)
        heads = [heads[j * depths * seqs : (j + 1) * depths * seqs] for j in range(seqs)]
        units = []
        for k, block in ((1, block_1), (2, block_2)):
            unit = block[:, :width] * decoded(block[:, width:])
            after = []
            for j in range(seqs):
                token = facts[j * slots : (j + 1) * slots, 0:1]
                add = jnp.zeros((slots, width), f32)
                for i in range(k if j + 1 < seqs else 0):
                    row = heads[j + 1][i : i + 1]
                    for p in range(1, seqs):
                        at = p * depths + i
                        row = jnp.where(seq_place() == p, heads[j + 1][at : at + 1], row)
                    row = row[:, :width] * decoded(row[:, width:])
                    add += jnp.where(token == float(tokens + i - k), row, 0.0)
                after.append(add)
            units.append(unit + jnp.concatenate(after, 0))
        start = in_order([g[:, : width + lanes].astype(f32) for g in start_got], seq_place(), 0)
        unit = start[:, :width] * decoded(start[:, width:])
        gain_h, gain_e = (piece_of(gain[0, k : k + 1], seq_place(), seqs, 0) for k in range(2))
        mixed = (unit * gain_h + units[0] * gain_e).astype(bf16).astype(f32)
        douts = zip(*(blocks_of(block, seq_place(), seqs) for block in dout))
        douts = [jnp.concatenate(blocks, 0) for blocks in douts]
        return payload(mixed * facts[:, 2:3]), unit, *units, block_3[:, :width], facts, *douts

    rows_1, unit_1, unit_e1, unit_e2, cot_1, own_facts, *dout_2_sent = call(
        "first_mixed", first_mixed,
        [packed] + [part_rows] * 4 + [((rows, lanes), f32)]
        + [((groups * slots * parts, fine), bf16)] * seqs,
        (), norm_gain, *start_got, *own_got, *dout_2_got, after=(ahead_21,),
    )
    rows_1_all = gather_dp(rows_1)

    def by_slots(got, place):
        blocks = [from_block(got, place, j) for j in range(seqs)]
        pairs = [b[g * slots : (g + 1) * slots] for g in range(parts) for b in blocks]
        return jnp.concatenate(pairs, 0)

    (base_2,) = call(
        "base_order", lambda *got: [by_slots([g.astype(f32) for g in got], seq_place())], [packed],
        (), *base_got, after=(rows_1,),
    )
    base_2_all = gather_dp(base_2)

    up_1st, down_1st = call(
        "held_1", lambda: [], [], (),
        hold=((expert_weight, 0, 1), (expert_weight, 0, 2)), after=(rows_1,), limit=2,
    )
    weight_1st = (gate_1st, up_1st, down_1st)
    first_own, first_send = project(
        "gate_up_1", rows_1_all, weight_1st, (0, 1), parts, after=(base_2,)
    )
    first = pair_seq(first_own, first_send)

    def forward_1(own, other):
        both = own + other.astype(f32)
        gate, up = both[:, :hidden_units], both[:, hidden_units:]
        return gate * jax.nn.sigmoid(gate) * up, both

    (act_1, both_1), out_blocks = expand(
        "down_1", forward_1, first,
        [((total, hidden_units), bf16), ((total, 2 * hidden_units), f32)],
        weight_1st, (2,), groups, parts,
    )
    out_blocks = lax.optimization_barrier((*out_blocks, *base_2_all))[:groups]
    out_got = return_dp(out_blocks)

    hidden, _ = lax.optimization_barrier((source, rows_1))
    hidden = ring(hidden, "section", 1)
    *dense, gate_2nd, up_2nd, down_2nd = dense_rows(
        "dense_a", *facts, hidden, embed, next_rows, cot, norm_gain, None, 0, 2,
        hold=tuple((expert_weight, 1, k) for k in range(3)), after=(out_blocks[0],),
    )
    weight_2nd = (gate_2nd, up_2nd, down_2nd)

    def second_prev(own_facts, rows_1, *got):
        value = unfolded(rows_1.astype(f32), parts) + summed(got, parts) * decoded(own_facts, 4)
        return payload(value), value.astype(bf16)

    prev, prev_own = call(
        "second_prev", second_prev, [packed, ((rows, width), bf16)],
        (), own_facts, rows_1, *out_got, after=(dense[1],),
    )
    prev_all = gather_dp(prev)

    dout_2_sent = lax.optimization_barrier((*dout_2_sent, out_blocks[0]))[:-1]
    dout_2_traded = trade_seq(dout_2_sent)

    def slot_facts(*got):
        got, size = [g.astype(f32) for g in got], slots * parts
        blocks = [
            by_slots([g[z * size : (z + 1) * size] for g in got], seq_place()) for z in range(groups)
        ]
        facts = jnp.concatenate([block[:rows, width // parts :] for block in blocks], 0)
        base = (iota((total, 1), 0) // slots * tokens).astype(f32)
        first, second = facts[:, 0:1] + base, facts[:, 1:2] + base
        live = (facts[:, 3:4] > 0) & (as_row(facts[:, 2:3]) > 0)
        same = ((second == as_row(first)) & live).astype(f32)
        return same, same, same[:rows, :rows], decoded(facts, 4), *blocks

    same, same_16, same_own, weight_1, *dout_2_all = call(
        "slot_facts", slot_facts,
        [((total, total), f32), ((total, total), bf16), ((rows, rows), f32), ((total, 1), f32)]
        + [((rows * parts, fine), bf16)] * groups,
        (), *dout_2_traded, after=(prev,),
    )
    fixed_own, fixed_send = project(
        "fixed_2", base_2_all, weight_2nd, (0, 1), parts,
        others=(dout_2_all, (2,)), after=(same_own,),
    )
    fixed_pair = pair_seq(fixed_own, fixed_send)

    mixed_own, mixed_send, chosen = project(
        "gate_up_2", prev_all, weight_2nd, (0, 1), parts,
        select=same_16, gain=norm_gain, after=(fixed_own,),
    )
    second = pair_seq(mixed_own, mixed_send)
    prev_w_own, prev_w_send = project(
        "prev_down", prev_all, weight_1st, (2,), parts, after=(mixed_send,)
    )
    prev_pair = pair_seq(prev_w_own, prev_w_send)

    def gates_back(gate, up, d_act):
        sig = jax.nn.sigmoid(gate)
        d_gate = d_act * up * sig * (1.0 + gate * (1.0 - sig))
        return d_gate, d_act * gate * sig

    def backward_2(own, other, fixed_own, fixed_other, same):
        many = 2 * hidden_units
        square = own[:, many : many + 1] + decoded(other[:, many:])
        scale = lax.rsqrt(square / features + eps_norm)
        row = jnp.sum(same * as_row(scale), axis=1, keepdims=True)
        both = (own[:, :many] + other[:, :many].astype(f32)) * row
        fixed = fixed_own + fixed_other.astype(f32)
        both = both + fixed[:, :many]
        gate, up = both[:, :hidden_units], both[:, hidden_units:]
        d_gate, d_up = gates_back(gate, up, fixed[:, many:])
        return d_gate, d_up, gate * jax.nn.sigmoid(gate) * up, scale, row

    units = ((total, hidden_units), bf16)
    (d_gate_2, d_up_2, act_2, scale_2, row_2), d_rows_blocks = expand(
        "back_rows_2", backward_2,
        second + fixed_pair + (same,),
        [units, units, units, ((total, 1), f32), ((total, 1), f32)],
        weight_2nd, (0, 1), groups, parts, after=(prev_w_own,),
    )
    d_rows_got = return_dp(d_rows_blocks)
    dense, dense_terms = dense_rows(
        "dense_b", *facts, hidden, embed, next_rows, cot, norm_gain, dense, 1, 2,
        after=(d_rows_blocks[0],),
    )
    def first_grad(cot, same, gain, *got):
        d_rows = summed(got, parts)
        added = lax.dot_general(
            same, d_rows, (((0,), (0,)), ((), ())),
            precision=lax.Precision.HIGHEST, preferred_element_type=f32,
        )
        d_mixed = cot + added
        u = d_mixed * piece_of(gain[1, 0:1], seq_place(), seqs, 0)
        return [payload(u), d_mixed] + blocks_of(d_rows, seq_place(), seqs)

    u, d_mixed_2, *d_rows_back = call(
        "first_grad", first_grad, [packed, part_rows] + [((slots, width), bf16)] * seqs,
        (), cot_1, same_own, norm_gain, *d_rows_got, after=(dense_terms, prev_pair[1]),
    )
    u_all = gather_dp(u)
    dense, _ = lax.optimization_barrier((dense, u))
    dense = ring(dense, "section", -1)
    back_got = trade_seq(d_rows_back)

    def build_2(values, g):
        chosen, row, base, dout = values[0], values[1], values[2 : 2 + groups], values[2 + groups :]
        step = width // parts
        first = chosen[:, g * step : (g + 1) * step].astype(f32) * row
        first = first + column_part(base, rows, g).astype(f32)
        return first.astype(bf16), column_part(dout, rows, g)[:, :step]

    weight_grad, tick_2 = outer(
        "weight_grad_2", 1, depths, build_2, [chosen, row_2] + base_2_all + dout_2_all,
        d_gate_2, d_up_2, act_2, width, parts, None, after=(u, back_got[-1]),
    )

    back_1_own, back_1_send = project(
        "back_1", u_all, weight_1st, (2,), parts, mates=prev_all, after=(tick_2,)
    )
    back_1 = pair_seq(back_1_own, back_1_send)

    def second_grad(token, count, start, ahead_1, ahead_2, cot, gain, terms, *got):
        d_rows = in_order([g.astype(f32) for g in got], seq_place(), 1)
        keep = live_column(count, 1, slots) * (1.0 - met_column(token, count))
        grad, more = backward_rows(
            start[:, width + lanes :].astype(f32), ahead_1.astype(f32), ahead_2.astype(f32),
            pick(token_column(token, 1), cot) + d_rows, keep, gain,
        )
        notes = in_lanes([live_column(count, 0, slots), keep])
        grad = jnp.concatenate([grad.astype(f32), notes], 1)
        return [grad] + pieces_of(terms + more, seq_place(), seqs)

    grad_2, *terms_parts = call(
        "second_grad", second_grad,
        [((slots, features + lanes), bf16)] + [((2 * depths, width), f32)] * seqs,
        facts, start_got[0], ahead_21, ahead_22, cot, norm_gain, dense_terms, *back_got,
        after=(back_1_send,),
    )
    grad_2 = ring(grad_2, "section", -1)
    terms_got = trade_seq(terms_parts)

    def backward_1(own, other, prev_own, prev_other, both, scale, weight_1):
        inner = own[:, hidden_units : hidden_units + 1] + decoded(other[:, hidden_units:])
        d_act = own[:, :hidden_units] + other[:, :hidden_units].astype(f32)
        through = scale * scale * inner / features
        d_act = d_act - through * (prev_own + prev_other.astype(f32))
        d_act = d_act * (weight_1 * scale)
        d_gate, d_up = gates_back(both[:, :hidden_units], both[:, hidden_units:], d_act)
        return d_gate, d_up, through

    (d_gate_1, d_up_1, through_1), d_rows_blocks = expand(
        "back_rows_1", backward_1,
        back_1 + prev_pair + (both_1, scale_2, weight_1),
        [units, units, ((total, 1), f32)],
        weight_1st, (0, 1), groups, parts, after=(terms_parts[0],),
    )
    d_rows_got = return_dp(d_rows_blocks)

    def build_1(values, g):
        through, scale, weight = values[:3]
        first, u, prev = (values[3 + k * groups : 3 + (k + 1) * groups] for k in range(3))
        dout = column_part(u, rows, g).astype(f32) - through * column_part(prev, rows, g).astype(f32)
        return column_part(first, rows, g), (dout * (weight * scale)).astype(bf16)

    weight_grad, tick_1 = outer(
        "weight_grad_1", 0, depths, build_1,
        [through_1, scale_2, weight_1] + rows_1_all + u_all + prev_all,
        d_gate_1, d_up_1, act_1, width, parts, weight_grad, after=(d_rows_blocks[0],),
    )

    def last_grad(d_mixed_2, prev, scale, through, unit_1, unit_e1, unit_e2, own_facts, gain, *got):
        got, terms = got[:groups], got[groups:]
        d_rows = summed(got, parts)
        gain_1, gain_2 = (piece_of(gain[k, 0:1], seq_place(), seqs, 0) for k in range(2))
        scale, through = scale[:rows], through[:rows]
        live = own_facts[:, 2:3]
        prev = prev.astype(f32)
        grad_1 = (d_mixed_2 * gain_2 - through * prev) * scale
        d_mixed_1 = grad_1 + d_rows
        kept_1, kept_2 = d_mixed_1 * live, d_mixed_2 * live
        sums = [
            jnp.sum(a * b, axis=0, keepdims=True)
            for a, b in ((kept_1, unit_1), (kept_1, unit_e1), (kept_2, prev * scale), (kept_2, unit_e2))
        ]
        sums = jnp.concatenate(sums, 0) + sum(terms)
        cut = []
        for i in range(groups):
            block = sums[:, :share]
            for z in range(groups):
                at = partner(z, i, groups) * share
                block = jnp.where(lax.axis_index("dp") == z, sums[:, at : at + share], block)
            cut.append(block)
        return cut + blocks_of(d_mixed_1 * gain_1, seq_place(), seqs)

    last = call(
        "last_grad", last_grad,
        [((2 * depths, share), f32)] * groups + [((slots, width), bf16)] * seqs,
        (), d_mixed_2, prev_own, scale_2, through_1, unit_1, unit_e1, unit_e2,
        own_facts, norm_gain, *d_rows_got, *terms_got, after=(tick_1,),
    )
    last_got = trade_seq(last[groups:], -1)
    sums_got = return_dp(last[:groups])

    def finish(token, dense, asked_rows, grad_2, *got):
        part = in_order([g.astype(f32) for g in got], seq_place(), 1)
        asked_rows = asked_rows.astype(f32)
        scale = inv_rms(asked_rows)
        unit = asked_rows * scale
        grad_1 = (part - unit * jnp.mean(part * unit, axis=-1, keepdims=True)) * scale
        notes = grad_2[:, features:].astype(f32)
        grads = jnp.concatenate([grad_1, grad_2[:, :features].astype(f32)], 0).astype(bf16)
        lane = iota((slots, tokens), 1)
        chosen = jnp.concatenate(
            [
                jnp.where(lane == token_column(token, k), notes[:, k : k + 1], 0.0)
                for k in range(2)
            ],
            0,
        ).astype(bf16)
        taken = lax.dot_general(
            chosen, jnp.ones((2 * slots, lanes), bf16), (((0,), (0,)), ((), ())),
            preferred_element_type=f32,
        )[:, 0:1]
        out = []
        step = chunk_of(features)
        for at in range(0, features, step):
            placed = lax.dot_general(
                chosen, grads[:, at : at + step], (((0,), (0,)), ((), ())),
                preferred_element_type=f32,
            )
            out.append(jnp.where(taken > 0, placed, dense[:, at : at + step].astype(f32)).astype(bf16))
        return [jnp.concatenate(out, 1), jnp.zeros((8, lanes), f32)]

    hidden_grad, tick = call(
        "finish", finish, [((tokens, features), bf16), ((8, lanes), f32)],
        (asked_token,), dense, asked_rows, grad_2, *last_got, limit=20,
    )

    def gain_sum(*got):
        sums = sum(got)
        return [jnp.stack([sums[2 * k : 2 * k + 2] for k in range(depths)])[None]]

    (gain_grad,) = call(
        "gain_sum", gain_sum, [((1, depths, 2, share), f32)], (), *sums_got, after=(tick,)
    )
    return (
        hidden_grad[None, None],
        weight_grad,
        gain_grad,
    )


def solution(mesh):
    return jax.shard_map(
        local,
        mesh=mesh,
        in_specs=(
            P("section", "dp", "seq", None),
            P("section", "dp", "seq", None),
            P("section", "dp", "seq", None),
            P("section", "dp", None, "seq"),
            P("section", "dp", None, "seq"),
            P("section", "dp", None, "seq"),
            P(),
            P(None, None, "seq", "dp"),
        ),
        out_specs=(
            P("section", "dp", "seq", None),
            P("section", None, None, "seq", "dp"),
            P("section", None, None, ("seq", "dp")),
        ),
        check_vma=False,
    )
```

```python
import jax
import jax.numpy as jnp
from jax import lax
from jax.experimental import pallas as pl
from jax.experimental.pallas import tpu as pltpu
from jax.sharding import PartitionSpec as P

eps_norm = 1e-06
lanes = 128
f32 = jnp.float32
bf16 = jnp.bfloat16
vmem = pl.BlockSpec(memory_space=pltpu.VMEM)
smem = pl.BlockSpec(memory_space=pltpu.SMEM)
anywhere = pl.BlockSpec(memory_space=pl.ANY)


def ring(value, axis, steps):
    count = lax.axis_size(axis)
    return lax.ppermute(value, axis, [(i, (i + steps) % count) for i in range(count)])


def hop(value, section_step, seq_step):
    sections, seqs = lax.axis_size("section"), lax.axis_size("seq")
    pairs = [
        (c * seqs + s, (c + section_step) % sections * seqs + (s + seq_step) % seqs)
        for c in range(sections)
        for s in range(seqs)
    ]
    return lax.ppermute(value, ("section", "seq"), pairs)


def trade_seq(pieces, section_step=0):
    if section_step == 0:
        return [pieces[0]] + [ring(pieces[o], "seq", o) for o in range(1, len(pieces))]
    return [hop(piece, section_step, o) for o, piece in enumerate(pieces)]


def partner(place, step, count):
    return place ^ step if count & (count - 1) == 0 else (place - step) % count


def gather_dp(block):
    count = lax.axis_size("dp")
    return [block] + [
        lax.ppermute(block, "dp", [(partner(z, i, count), z) for z in range(count)])
        for i in range(1, count)
    ]


def return_dp(blocks):
    count = lax.axis_size("dp")
    return [blocks[0]] + [
        lax.ppermute(blocks[i], "dp", [(z, partner(z, i, count)) for z in range(count)])
        for i in range(1, count)
    ]


def pair_seq(own, send):
    if lax.axis_size("seq") == 2:
        return own, ring(send, "seq", 1)
    return lax.psum(own, "seq"), jnp.zeros_like(send)


def inv_rms(value):
    return lax.rsqrt(jnp.mean(value * value, axis=-1, keepdims=True) + eps_norm)


def iota(shape, dim):
    return lax.broadcasted_iota(jnp.int32, shape, dim)


def seq_place():
    return lax.axis_index("seq").astype(jnp.int32)


def token_column(token, depth):
    capacity = token.shape[3]
    out = jnp.full((capacity, 1), token[0, 0, depth, 0], jnp.int32)
    for c in range(1, capacity):
        out = jnp.where(iota((capacity, 1), 0) == c, token[0, 0, depth, c], out)
    return out


def gate_column(gate, depth):
    capacity = gate.shape[3]
    out = jnp.full((capacity, 1), gate[0, 0, depth, 0], f32)
    for c in range(1, capacity):
        out = jnp.where(iota((capacity, 1), 0) == c, gate[0, 0, depth, c], out)
    return out


def live_column(count, depth, capacity):
    return (iota((capacity, 1), 0) < count[depth]).astype(f32)


def met_column(token, count):
    capacity = token.shape[3]
    second = token_column(token, 1)
    out = jnp.zeros((capacity, 1), f32)
    for c in range(capacity):
        out += ((second == token[0, 0, 0, c]) & (c < count[0])).astype(f32)
    return jnp.minimum(out, 1.0)


def pick(column, table):
    hot = (column == iota((column.shape[0], table.shape[0]), 1)).astype(bf16)
    return jnp.dot(hot, table, preferred_element_type=f32)


def pick_ahead(column, table, after):
    return pick(column, table) + pick(column - table.shape[0], after)


def thirds(column):
    high = column.astype(bf16).astype(f32)
    mid = (column - high).astype(bf16).astype(f32)
    return [high, mid, column - high - mid]


def in_lanes(columns):
    lane = iota((columns[0].shape[0], lanes), 1)
    out = jnp.zeros(lane.shape, f32)
    for k, column in enumerate(columns):
        out = jnp.where(lane == k, column, out)
    return out


def coded(column):
    return in_lanes(thirds(column))


def decoded(block, first=0):
    lane = iota(block.shape, 1)
    inside = (lane >= first) & (lane < first + 3)
    return jnp.sum(jnp.where(inside, block.astype(f32), 0.0), axis=1, keepdims=True)


def piece_of(value, place, count, step):
    width = value.shape[-1] // count
    want = lax.rem(place + step, count)
    out = value[:, :width]
    for p in range(1, count):
        out = jnp.where(want == p, value[:, p * width : (p + 1) * width], out)
    return out


def pieces_of(value, place, count):
    return [piece_of(value, place, count, o) for o in range(count)]


def blocks_of(value, place, count):
    size = value.shape[0] // count
    out = []
    for o in range(count):
        block = value[:size]
        for j in range(1, count):
            want = lax.rem(place + o, count) == j
            block = jnp.where(want, value[j * size : (j + 1) * size], block)
        out.append(block)
    return out


def from_block(got, place, block):
    count = len(got)
    out = got[0]
    for o in range(1, count):
        out = jnp.where(lax.rem(place - o + count, count) == block, got[o], out)
    return out


def in_order(got, place, axis):
    return jnp.concatenate([from_block(got, place, j) for j in range(len(got))], axis)


def as_row(column):
    size = column.shape[0]
    here = iota((size, size), 0) == iota((size, size), 1)
    return jnp.sum(jnp.where(here, column, 0.0), axis=0, keepdims=True)


def folds(rows, width):
    for count in (1, 2, 4, 8):
        if rows * count % 16 == 0 and width % (count * lanes) == 0:
            return count
    return 1


def folded(value, count):
    step = value.shape[1] // count
    return jnp.concatenate([value[:, g * step : (g + 1) * step] for g in range(count)], 0)


def unfolded(value, count):
    rows = value.shape[0] // count
    return jnp.concatenate([value[g * rows : (g + 1) * rows] for g in range(count)], 1)


def column_part(blocks, rows, g):
    return jnp.concatenate(
        [block[g * rows : (g + 1) * rows].astype(f32) for block in blocks], 0
    ).astype(bf16)


def summed(got, parts):
    return unfolded(sum(g.astype(f32) for g in got), parts)


def chunk_of(width):
    for step in (1024, 896, 512, 256, 128):
        if width % step == 0:
            return step
    return width


def in_hbm(value):
    return pltpu.with_memory_space_constraint(value, pltpu.HBM)


def call(name, fn, outs, small, *args, far=(), hold=(), after=(), stream=False, flops=0, limit=12):
    outs = list(outs) + [(weight.shape[2:], bf16) for weight, _, _ in hold]
    shapes = [jax.ShapeDtypeStruct(shape, kind) for shape, kind in outs]
    n_small, n_args, n_far, n_outs = len(small), len(args), len(far), len(shapes) - len(hold)

    def body(*refs):
        refs = list(refs)

        def take(count):
            taken, refs[:] = refs[:count], refs[count:]
            return taken

        small_refs, arg_refs, far_refs = take(n_small), take(n_args), take(n_far)
        hold_refs = take(len(hold))
        take(len(after))
        out_refs, held_refs, buffers = take(n_outs), take(len(hold)), take(n_far)
        if stream:
            stage_ref, stage_sem = refs.pop(), refs.pop()
        copies = [pltpu.make_async_copy(*trio) for trio in zip(far_refs, buffers, take(n_far))]
        holds = [
            pltpu.make_async_copy(ref.at[depth, kind], held_ref, sem)
            for ref, (_, depth, kind), held_ref, sem in zip(hold_refs, hold, held_refs, refs)
        ]
        for copy in copies + holds:
            copy.start()
        for copy in copies:
            copy.wait()
        values = small_refs + [r[...] for r in arg_refs + buffers]
        results = fn(*values)
        if stream:
            chunks, results, target = results[0], results[1:], out_refs.pop(0)
            width = target.shape[1] // len(chunks)
            for k, chunk in enumerate(chunks):
                at = pl.ds(k * width, width)
                stage_ref[:, at] = chunk.astype(target.dtype)
                copy = pltpu.make_async_copy(stage_ref.at[:, at], target.at[:, at], stage_sem.at[k])
                copy.start()
                holds.append(copy)
        for ref, value in zip(out_refs, results):
            ref[...] = value.astype(ref.dtype)
        for copy in holds:
            copy.wait()

    size = sum(a.size * a.dtype.itemsize for a in list(args) + list(far) + shapes)
    return pl.pallas_call(
        body,
        name=name,
        out_shape=shapes,
        in_specs=[smem] * n_small + [vmem] * n_args + [anywhere] * (n_far + len(hold) + len(after)),
        out_specs=[anywhere if stream and k == 0 else vmem for k in range(len(shapes))],
        scratch_shapes=[pltpu.VMEM(a.shape, a.dtype) for a in far]
        + [pltpu.SemaphoreType.DMA] * (n_far + len(hold))
        + ([pltpu.SemaphoreType.DMA((stream,)), pltpu.VMEM(*outs[0])] if stream else []),
        compiler_params=pltpu.CompilerParams(vmem_limit_bytes=limit << 20),
        cost_estimate=pl.CostEstimate(flops=flops, bytes_accessed=size, transcendentals=0),
    )(*[in_hbm(a) for a in small], *args, *[in_hbm(a) for a in far], *[in_hbm(a) for a, _, _ in hold], *after)


def project(name, blocks, weights, kinds, parts, others=None, select=None, gain=None, mates=None, after=()):
    groups = len(blocks)
    rows = blocks[0].shape[0] // parts
    width, hidden = weights[0].shape
    step = width // parts
    other_blocks, other_kinds = others if others is not None else ([], ())
    first_kinds, kinds = kinds, kinds + other_kinds
    many_kinds = len(kinds)
    total, many = rows * groups, len(kinds) * hidden
    marked = select is not None or mates is not None
    extra = lanes if marked else 0

    def body(*refs):
        refs = list(refs)
        x_refs, w_refs, refs = refs[:groups], refs[groups : groups + many_kinds], refs[groups + many_kinds :]
        other_refs, refs = refs[: len(other_blocks)], refs[len(other_blocks) :]
        if select is not None:
            select_ref, gain_ref = refs.pop(0), refs.pop(0)
        if mates is not None:
            mate_refs, refs = refs[:groups], refs[groups:]
        refs = refs[len(after) :]
        own_ref, send_ref = refs.pop(0), refs.pop(0)
        kept_ref = refs.pop(0) if select is not None else None
        x_all = [r[...] for r in x_refs]
        mate_all = [r[...] for r in mate_refs] if mates is not None else x_all
        if select is not None:
            gain_all = piece_of(gain_ref[1, 0:1, :], seq_place(), gain.shape[2] // width, 0)
        sums = [jnp.zeros((total, hidden), f32) for _ in kinds]
        mark = jnp.zeros((total, 1), f32)
        for g in range(parts):
            x = column_part(x_all, rows, g)
            if marked:
                mate = x if mates is None else column_part(mate_all, rows, g)
                mark += jnp.sum(x.astype(f32) * mate.astype(f32), axis=1, keepdims=True)
            if select is not None:
                chosen = jnp.dot(select_ref[...], x, preferred_element_type=f32)
                x = (chosen * gain_all[:, g * step : (g + 1) * step]).astype(bf16)
                kept_ref[:, g * step : (g + 1) * step] = x
            for k in range(len(kinds)):
                if k == len(first_kinds):
                    x = column_part([r[...] for r in other_refs], rows, g)[:, :step]
                part_ref = w_refs[k].at[pl.ds(g * step, step)]
                sums[k] += jnp.dot(x, part_ref[...], preferred_element_type=f32)
        for k in range(len(kinds)):
            own_ref[:, k * hidden : (k + 1) * hidden] = sums[k]
            send_ref[:, k * hidden : (k + 1) * hidden] = sums[k].astype(bf16)
        if marked:
            own_ref[:, many:] = in_lanes([mark])
            send_ref[:, many:] = coded(mark).astype(bf16)

    args = list(blocks) + [weights[k] for k in kinds]
    args, specs = args + list(other_blocks), [vmem] * (groups + many_kinds) + [vmem] * len(other_blocks)
    outs = [
        jax.ShapeDtypeStruct((total, many + extra), f32),
        jax.ShapeDtypeStruct((total, many + extra), bf16),
    ]
    if select is not None:
        args, specs = args + [select, gain], specs + [vmem, vmem]
        outs.append(jax.ShapeDtypeStruct((total, width), bf16))
    if mates is not None:
        args, specs = args + list(mates), specs + [vmem] * groups
    return pl.pallas_call(
        body,
        name=name,
        in_specs=specs + [anywhere] * len(after),
        out_specs=[vmem] * len(outs),
        out_shape=outs,
        compiler_params=pltpu.CompilerParams(vmem_limit_bytes=8 << 20),
        cost_estimate=pl.CostEstimate(
            flops=2 * total * width * many, bytes_accessed=2 * width * many, transcendentals=0
        ),
    )(*args, *after)


def expand(name, prepare, args, saved, weights, kinds, groups, parts, after=()):
    width, hidden = weights[0].shape
    total = saved[0][0][0]
    rows, step = total // groups, width // parts
    count, kept = len(args), len(saved)

    def body(*refs):
        in_refs, w_refs = refs[:count], refs[count : count + len(kinds)]
        refs = refs[count + len(kinds) + len(after) :]
        saved_refs, out_refs = refs[:kept], refs[kept:]
        for ref, value in zip(saved_refs, prepare(*[r[...] for r in in_refs])):
            ref[...] = value.astype(ref.dtype)
        out = []
        for g in range(parts):
            part = jnp.zeros((total, step), f32)
            for k in range(len(kinds)):
                part_ref = w_refs[k].at[pl.ds(g * step, step)]
                part += lax.dot_general(
                    saved_refs[k][...], part_ref[...], (((1,), (1,)), ((), ())),
                    preferred_element_type=f32,
                )
            out.append(part)
        for z in range(groups):
            block = jnp.concatenate([part[z * rows : (z + 1) * rows] for part in out], 0)
            out_refs[z][...] = block.astype(bf16)

    results = pl.pallas_call(
        body,
        name=name,
        in_specs=[vmem] * (count + len(kinds)) + [anywhere] * len(after),
        out_specs=[vmem] * (kept + groups),
        out_shape=[jax.ShapeDtypeStruct(shape, kind) for shape, kind in saved]
        + [jax.ShapeDtypeStruct((rows * parts, step), bf16)] * groups,
        compiler_params=pltpu.CompilerParams(vmem_limit_bytes=8 << 20),
        cost_estimate=pl.CostEstimate(
            flops=2 * total * width * hidden * len(kinds),
            bytes_accessed=2 * width * hidden * len(kinds),
            transcendentals=0,
        ),
    )(*args, *[weights[k] for k in kinds], *after)
    return results[:kept], results[kept:]


def outer(name, depth, depths, build, args, d_gate, d_up, act, width, parts, before, after=()):
    total, hidden = act.shape
    step = width // parts
    count = len(args)
    earlier = [] if before is None else [in_hbm(before)]

    def contract(left, right):
        return lax.dot_general(left, right, (((0,), (0,)), ((), ())), preferred_element_type=f32)

    def body(*refs):
        values = [r[...] for r in refs[:count]]
        gate_ref, up_ref, act_ref = refs[count : count + 3]
        out_ref, tick_ref, buffer, sems = refs[-4:]
        tick_ref[...] = jnp.zeros_like(tick_ref)
        copies = []
        for g in range(parts):
            rows, dout = build(values, g)
            pairs = ((rows, gate_ref), (rows, up_ref), (dout, act_ref))
            for k, (left, right_ref) in enumerate(pairs):
                buffer[g, k] = contract(left, right_ref[...]).astype(bf16)
                copy = pltpu.make_async_copy(
                    buffer.at[g, k],
                    out_ref.at[0, depth, k, pl.ds(g * step, step)],
                    sems.at[g, k],
                )
                copy.start()
                copies.append(copy)
        for copy in copies:
            copy.wait()

    return pl.pallas_call(
        body,
        name=name,
        in_specs=[vmem] * (count + 3) + [anywhere] * (len(earlier) + len(after)),
        out_specs=[anywhere, vmem],
        out_shape=[
            jax.ShapeDtypeStruct((1, depths, 3, width, hidden), bf16),
            jax.ShapeDtypeStruct((8, lanes), f32),
        ],
        input_output_aliases={} if before is None else {count + 3: 0},
        scratch_shapes=[
            pltpu.VMEM((parts, 3, step, hidden), bf16),
            pltpu.SemaphoreType.DMA((parts, 3)),
        ],
        compiler_params=pltpu.CompilerParams(vmem_limit_bytes=24 << 20),
        cost_estimate=pl.CostEstimate(
            flops=6 * total * width * hidden, bytes_accessed=6 * width * hidden, transcendentals=0
        ),
    )(*args, d_gate, d_up, act, *earlier, *after)


def backward_rows(hidden, ahead_1, ahead_2, d_mixed_2, keep, gain):
    scale_1 = inv_rms(hidden)
    unit_1 = hidden * scale_1
    unit_e1 = ahead_1 * inv_rms(ahead_1)
    unit_e2 = ahead_2 * inv_rms(ahead_2)
    mixed = (unit_1 * gain[0, 0:1] + unit_e1 * gain[0, 1:2]).astype(bf16).astype(f32)
    scale_2 = inv_rms(mixed)
    unit_2 = mixed * scale_2
    u = d_mixed_2 * gain[1, 0:1]
    grad_1 = (u - unit_2 * jnp.mean(u * unit_2, axis=-1, keepdims=True)) * scale_2
    v = grad_1 * gain[0, 0:1]
    grad_0 = (v - unit_1 * jnp.mean(v * unit_1, axis=-1, keepdims=True)) * scale_1
    kept_1, kept_2 = grad_1 * keep, d_mixed_2 * keep
    terms = [
        jnp.sum(a * b, axis=0, keepdims=True)
        for a, b in ((kept_1, unit_1), (kept_1, unit_e1), (kept_2, unit_2), (kept_2, unit_e2))
    ]
    return grad_0.astype(bf16), jnp.concatenate(terms, 0)


def dense_rows(name, token, count, hidden, embed, next_rows, cotangent, gain, before, half, halves, hold=(), after=()):
    tokens, width = hidden.shape
    step = next_rows.shape[0]
    blocks = tokens // step // halves
    low, last = half * blocks, tokens // step - 1
    size = 2 * lanes
    capacity = token.shape[3]
    earlier = [] if before is None else list(before)

    def body(token_ref, count_ref, hidden_ref, embed_ref, next_ref, cot_ref, gain_ref, *refs):
        skip, kept = len(earlier), len(hold)
        hold_refs, refs = refs[skip : skip + kept], refs[:skip] + refs[skip + kept :]
        held_refs, sems = refs[len(refs) - 2 * kept - 2 : len(refs) - kept - 2], refs[len(refs) - kept :]
        out_ref, terms_ref = refs[skip + len(after) : skip + len(after) + 2]
        mixed_ref, sums_ref = refs[len(refs) - kept - 2 : len(refs) - kept]
        holds = [
            pltpu.make_async_copy(ref.at[depth, kind], held_ref, sem)
            for ref, (_, depth, kind), held_ref, sem in zip(hold_refs, hold, held_refs, sems)
        ]
        for copy in holds:
            copy.start()
        sums_ref[...] = jnp.zeros_like(sums_ref)
        row, column = (iota((2 * step, 2 * step), dim) for dim in range(2))
        shift = (column == jnp.where(row < step, row + 1, row + 2 - step)).astype(bf16)
        places = [pl.ds(at, size) for at in range(0, width, size)]

        def folded_lanes(value):
            return sum(value[:, at : at + lanes] for at in range(0, size, lanes))

        def mean(value):
            return jnp.sum(value, axis=1, keepdims=True) / width

        def one(i, carry):
            block = low + i
            first = pl.multiple_of(block * step, step)
            rows = pl.ds(first, step)
            follow = pl.ds(pl.multiple_of(jnp.minimum(block + 1, last) * step, step), step)
            here = iota((step, 1), 0) + first
            keep = jnp.ones((step, 1), f32)
            for k in range(2):
                for c in range(capacity):
                    out = (here == token_ref[0, 0, k, c]) & (c < count_ref[k])
                    keep = jnp.where(out, 0.0, keep)

            def ahead(at, hot):
                after = embed_ref[follow, at]
                if half == halves - 1:
                    after = jnp.where(block == last, next_ref[:, at], after)
                both = jnp.concatenate([embed_ref[rows, at], after], 0)
                return jnp.dot(hot, both, preferred_element_type=f32)

            square_h, square_e = jnp.zeros((step, lanes), f32), jnp.zeros((2 * step, lanes), f32)
            for at in places:
                h, e = hidden_ref[rows, at].astype(f32), ahead(at, shift)
                square_h += folded_lanes(h * h)
                square_e += folded_lanes(e * e)
            scale_1 = lax.rsqrt(mean(square_h) + eps_norm)
            scale_e = lax.rsqrt(mean(square_e) + eps_norm)
            scale_e1, scale_e2 = scale_e[:step], scale_e[step:]

            sums = [jnp.zeros((step, lanes), f32) for _ in range(4)]
            for at in places:
                through = hidden_ref[rows, at].astype(f32) * scale_1 * gain_ref[0, 0:1, at]
                mixed = through + ahead(at, shift[:step]) * scale_e1 * gain_ref[0, 1:2, at]
                kept = mixed.astype(bf16)
                mixed_ref[:, at] = kept
                mixed = kept.astype(f32)
                u = cot_ref[rows, at].astype(f32) * gain_ref[1, 0:1, at]
                pairs = ((mixed, mixed), (u, mixed), (u, through), (mixed, through))
                sums = [c + folded_lanes(a * b) for c, (a, b) in zip(sums, pairs)]
            square, along, u_back, mixed_back = (mean(value) for value in sums)
            scale_2 = lax.rsqrt(square + eps_norm)
            share_2 = scale_2 * scale_2 * along
            share_1 = scale_2 * (u_back - share_2 * mixed_back) * scale_1
            keep_2, keep_h = keep * scale_2, keep * scale_1
            keep_e1, keep_e2 = keep * scale_e1, keep * scale_e2

            for at in places:
                e = ahead(at, shift)
                h = hidden_ref[rows, at].astype(f32)
                mixed = mixed_ref[:, at].astype(f32)
                cot = cot_ref[rows, at].astype(f32)
                grad_1 = (cot * gain_ref[1, 0:1, at] - mixed * share_2) * scale_2
                grad_0 = (grad_1 * gain_ref[0, 0:1, at] - h * share_1) * scale_1
                out_ref[rows, at] = grad_0.astype(bf16)
                terms = (
                    grad_1 * (h * keep_h),
                    grad_1 * (e[:step] * keep_e1),
                    cot * (mixed * keep_2),
                    cot * (e[step:] * keep_e2),
                )
                for k, term in enumerate(terms):
                    sums_ref[k, :, at] += sum(term[r : r + 8] for r in range(0, step, 8))
            return carry

        lax.fori_loop(0, blocks, one, 0)
        for k in range(4):
            term = jnp.sum(sums_ref[k], axis=0, keepdims=True)
            terms_ref[k : k + 1] = term + refs[1][k : k + 1] if earlier else term
        for copy in holds:
            copy.wait()

    return pl.pallas_call(
        body,
        name=name,
        in_specs=[smem] * 2 + [vmem] * (5 + len(earlier)) + [anywhere] * (len(hold) + len(after)),
        out_specs=[vmem] * (2 + len(hold)),
        out_shape=[
            jax.ShapeDtypeStruct((tokens, width), bf16),
            jax.ShapeDtypeStruct((4, width), f32),
        ]
        + [jax.ShapeDtypeStruct(weight.shape[2:], bf16) for weight, _, _ in hold],
        input_output_aliases={7: 0} if earlier else {},
        scratch_shapes=[pltpu.VMEM((step, width), bf16), pltpu.VMEM((4, 8, width), f32)]
        + [pltpu.SemaphoreType.DMA] * len(hold),
        compiler_params=pltpu.CompilerParams(vmem_limit_bytes=8 << 20),
        cost_estimate=pl.CostEstimate(
            flops=60 * tokens * width // halves,
            bytes_accessed=10 * tokens * width // halves,
            transcendentals=0,
        ),
    )(in_hbm(token), in_hbm(count), hidden, embed, next_rows, cotangent, gain, *earlier, *[in_hbm(a) for a, _, _ in hold], *after)


def local(
    main_hidden, embedded, cotangent, slot_token, slot_count, route_gate, norm_gain, expert_weight
):
    depths, _, features = norm_gain.shape
    tokens = main_hidden.shape[2]
    slots = slot_token.shape[3]
    seqs, groups = lax.axis_size("seq"), lax.axis_size("dp")
    rows = seqs * slots
    total = groups * rows
    width = features // seqs
    share = width // groups
    hidden_units = expert_weight.shape[3]
    parts = folds(rows, width)
    source, embed, cot = main_hidden[0, 0], embedded[0, 0], cotangent[0, 0]
    slot_count = slot_count.reshape(-1)
    facts = (slot_token, slot_count)
    packed = ((rows * parts, width // parts), bf16)
    part_rows = ((rows, width), f32)

    def payload(value):
        return folded(value, parts)

    asked_token = ring(slot_token, "section", -1)

    def own_rows(token, count, gate, embed, cot):
        first, second = token_column(token, 0), token_column(token, 1)
        live_1, live_2 = (live_column(count, k, slots) for k in range(2))
        weight_1, weight_2 = gate_column(gate, 0) * live_1, gate_column(gate, 1) * live_2
        facts = in_lanes(
            [first.astype(f32), second.astype(f32), live_1, live_2]
            + thirds(weight_1)
            + thirds(weight_2)
        )
        ahead_1, ahead_2 = pick(first + 1, embed), pick(first + 2, embed)
        block = jnp.concatenate([ahead_1, ahead_2, pick(first, cot)], 0)
        notes = jnp.concatenate([coded(inv_rms(ahead_1)), coded(inv_rms(ahead_2)), facts], 0)
        dout = folded(pick(second, cot) * weight_2, seqs * parts)
        none = jnp.zeros(((parts - 1) * slots, lanes), f32)
        tail = facts if parts == 1 else jnp.concatenate([facts, none], 0)
        dout = jnp.concatenate([dout, jnp.concatenate([tail] * seqs, 0)], 1)
        head = embed[:depths].astype(f32)
        scale = coded(inv_rms(head))
        heads = [
            jnp.concatenate([head[:, p * width : (p + 1) * width], scale], 1) for p in range(seqs)
        ]
        return [
            jnp.concatenate([jnp.concatenate([piece, notes], 1)] + heads, 0)
            for piece in pieces_of(block, seq_place(), seqs)
        ] + [dout]

    fine = width // parts + lanes
    *own_sent, dout_2, gate_1st = call(
        "own_rows", own_rows,
        [((3 * slots + depths * seqs, width + lanes), bf16)] * seqs
        + [((slots * parts * seqs, fine), bf16)],
        (slot_token, slot_count, route_gate), far=(embed, cot),
        hold=((expert_weight, 0, 0),),
    )
    own_sent = lax.optimization_barrier((*own_sent, asked_token))[:-1]
    own_got = trade_seq(own_sent)

    def source_rows(asked, source):
        first = pick(token_column(asked, 0), source)
        second = pick(token_column(asked, 1), source)
        scale = coded(inv_rms(first))
        sent = [jnp.concatenate([p, scale], 1) for p in pieces_of(first, seq_place(), seqs)]
        sent[0] = jnp.concatenate([sent[0], second], 1)
        return sent + [first]

    *sent, asked_rows = call(
        "source_rows", source_rows,
        [((slots, width + lanes + features), bf16)]
        + [((slots, width + lanes), bf16)] * (seqs - 1)
        + [((slots, features), bf16)],
        (asked_token,), source, after=(own_sent[0],),
    )
    start_got = trade_seq(sent, 1)
    dout_2, _ = lax.optimization_barrier((dout_2, sent[0]))

    def second_base(token, count, start, table, got, gain):
        after = got[3 * slots :, :width].astype(f32)
        after = jnp.concatenate([after[p * depths : (p + 1) * depths] for p in range(seqs)], 1)
        after = jnp.where(seq_place() == seqs - 1, 0.0, after)
        after = jnp.concatenate([after, jnp.zeros((16 - depths, features), f32)], 0).astype(bf16)
        second = token_column(token, 1)
        start = start[:, width + lanes :].astype(f32)
        ahead_1 = pick_ahead(second + 1, table, after)
        ahead_2 = pick_ahead(second + 2, table, after)
        unit = start * inv_rms(start)
        mixed = unit * gain[0, 0:1] + ahead_1 * inv_rms(ahead_1) * gain[0, 1:2]
        mixed = mixed.astype(bf16).astype(f32)
        own = mixed * inv_rms(mixed) * gain[1, 0:1] * (1.0 - met_column(token, count))
        out = (own + ahead_2 * inv_rms(ahead_2) * gain[1, 1:2]) * live_column(count, 1, slots)
        bases = [folded(piece, parts) for piece in pieces_of(out, seq_place(), seqs)]
        return bases + [after, ahead_1, ahead_2]

    *base_sent, next_rows, ahead_21, ahead_22 = call(
        "second_base", second_base,
        [((slots * parts, width // parts), bf16)] * seqs
        + [((16, features), bf16)]
        + [((slots, features), bf16)] * 2,
        facts, start_got[0], embed, own_got[-1], norm_gain,
    )
    base_got = trade_seq(base_sent)

    dout_2_got = gather_dp(dout_2)

    def first_mixed(gain, *got):
        start_got = got[:seqs]
        got = [g.astype(f32) for g in got[seqs : 2 * seqs]]
        first = 3 * slots
        block_1, block_2, block_3 = (
            in_order([g[k * slots : (k + 1) * slots] for g in got], seq_place(), 0) for k in range(3)
        )
        facts = block_3[:, width:]
        heads = in_order([g[first:] for g in got], seq_place(), 0)
        heads = [heads[j * depths * seqs : (j + 1) * depths * seqs] for j in range(seqs)]
        units = []
        for k, block in ((1, block_1), (2, block_2)):
            unit = block[:, :width] * decoded(block[:, width:])
            after = []
            for j in range(seqs):
                token = facts[j * slots : (j + 1) * slots, 0:1]
                add = jnp.zeros((slots, width), f32)
                for i in range(k if j + 1 < seqs else 0):
                    row = heads[j + 1][i : i + 1]
                    for p in range(1, seqs):
                        at = p * depths + i
                        row = jnp.where(seq_place() == p, heads[j + 1][at : at + 1], row)
                    row = row[:, :width] * decoded(row[:, width:])
                    add += jnp.where(token == float(tokens + i - k), row, 0.0)
                after.append(add)
            units.append(unit + jnp.concatenate(after, 0))
        start = in_order([g[:, : width + lanes].astype(f32) for g in start_got], seq_place(), 0)
        unit = start[:, :width] * decoded(start[:, width:])
        gain_h, gain_e = (piece_of(gain[0, k : k + 1], seq_place(), seqs, 0) for k in range(2))
        mixed = (unit * gain_h + units[0] * gain_e).astype(bf16).astype(f32)
        return payload(mixed * facts[:, 2:3]), unit, *units, block_3[:, :width], facts

    rows_1, unit_1, unit_e1, unit_e2, cot_1, own_facts = call(
        "first_mixed", first_mixed,
        [packed] + [part_rows] * 4 + [((rows, lanes), f32)],
        (), norm_gain, *start_got, *own_got, after=(ahead_21, *dout_2_got[1:-1]),
    )
    rows_1_all = gather_dp(rows_1)

    def by_slots(got, place):
        blocks = [from_block(got, place, j) for j in range(seqs)]
        pairs = [b[g * slots : (g + 1) * slots] for g in range(parts) for b in blocks]
        return jnp.concatenate(pairs, 0)

    (base_2,) = call(
        "base_order", lambda *got: [by_slots([g.astype(f32) for g in got], seq_place())], [packed],
        (), *base_got, after=(rows_1,),
    )
    base_2_all = gather_dp(base_2)

    def dout_pieces(*dout):
        pieces = zip(*(blocks_of(block.astype(f32), seq_place(), seqs) for block in dout))
        return [jnp.concatenate(blocks, 0) for blocks in pieces]

    dout_2_sent = call(
        "dout_pieces", dout_pieces, [((groups * slots * parts, fine), bf16)] * seqs,
        (), *dout_2_got, after=(rows_1,),
    )
    up_1st, down_1st = call(
        "held_1", lambda: [], [], (),
        hold=((expert_weight, 0, 1), (expert_weight, 0, 2)), after=(dout_2_sent[0],), limit=2,
    )
    weight_1st = (gate_1st, up_1st, down_1st)
    first_own, first_send = project(
        "gate_up_1", rows_1_all, weight_1st, (0, 1), parts, after=(base_2,)
    )
    first = pair_seq(first_own, first_send)

    def forward_1(own, other):
        both = own + other.astype(f32)
        gate, up = both[:, :hidden_units], both[:, hidden_units:]
        return gate * jax.nn.sigmoid(gate) * up, both

    (act_1, both_1), out_blocks = expand(
        "down_1", forward_1, first,
        [((total, hidden_units), bf16), ((total, 2 * hidden_units), f32)],
        weight_1st, (2,), groups, parts,
    )
    out_blocks = lax.optimization_barrier((*out_blocks, *base_2_all))[:groups]
    out_got = return_dp(out_blocks)

    hidden, _ = lax.optimization_barrier((source, rows_1))
    hidden = ring(hidden, "section", 1)
    *dense, gate_2nd, up_2nd, down_2nd = dense_rows(
        "dense_a", *facts, hidden, embed, next_rows, cot, norm_gain, None, 0, 2,
        hold=tuple((expert_weight, 1, k) for k in range(3)), after=(out_blocks[0],),
    )
    weight_2nd = (gate_2nd, up_2nd, down_2nd)

    def second_prev(own_facts, rows_1, *got):
        value = unfolded(rows_1.astype(f32), parts) + summed(got, parts) * decoded(own_facts, 4)
        return payload(value), value.astype(bf16)

    prev, prev_own = call(
        "second_prev", second_prev, [packed, ((rows, width), bf16)],
        (), own_facts, rows_1, *out_got, after=(dense[1],),
    )
    prev_all = gather_dp(prev)

    dout_2_sent = lax.optimization_barrier((*dout_2_sent, out_blocks[0]))[:-1]
    dout_2_traded = trade_seq(dout_2_sent)

    def slot_facts(*got):
        got, size = [g.astype(f32) for g in got], slots * parts
        blocks = [
            by_slots([g[z * size : (z + 1) * size] for g in got], seq_place()) for z in range(groups)
        ]
        facts = jnp.concatenate([block[:rows, width // parts :] for block in blocks], 0)
        base = (iota((total, 1), 0) // slots * tokens).astype(f32)
        first, second = facts[:, 0:1] + base, facts[:, 1:2] + base
        live = (facts[:, 3:4] > 0) & (as_row(facts[:, 2:3]) > 0)
        same = ((second == as_row(first)) & live).astype(f32)
        return same, same, same[:rows, :rows], decoded(facts, 4), *blocks

    same, same_16, same_own, weight_1, *dout_2_all = call(
        "slot_facts", slot_facts,
        [((total, total), f32), ((total, total), bf16), ((rows, rows), f32), ((total, 1), f32)]
        + [((rows * parts, fine), bf16)] * groups,
        (), *dout_2_traded, after=(prev,),
    )
    fixed_own, fixed_send = project(
        "fixed_2", base_2_all, weight_2nd, (0, 1), parts,
        others=(dout_2_all, (2,)), after=(same_own,),
    )
    fixed_pair = pair_seq(fixed_own, fixed_send)

    mixed_own, mixed_send, chosen = project(
        "gate_up_2", prev_all, weight_2nd, (0, 1), parts,
        select=same_16, gain=norm_gain, after=(fixed_own,),
    )
    second = pair_seq(mixed_own, mixed_send)
    prev_w_own, prev_w_send = project(
        "prev_down", prev_all, weight_1st, (2,), parts, after=(mixed_send,)
    )
    prev_pair = pair_seq(prev_w_own, prev_w_send)

    def gates_back(gate, up, d_act):
        sig = jax.nn.sigmoid(gate)
        d_gate = d_act * up * sig * (1.0 + gate * (1.0 - sig))
        return d_gate, d_act * gate * sig

    def backward_2(own, other, fixed_own, fixed_other, same):
        many = 2 * hidden_units
        square = own[:, many : many + 1] + decoded(other[:, many:])
        scale = lax.rsqrt(square / features + eps_norm)
        row = jnp.sum(same * as_row(scale), axis=1, keepdims=True)
        both = (own[:, :many] + other[:, :many].astype(f32)) * row
        fixed = fixed_own + fixed_other.astype(f32)
        both = both + fixed[:, :many]
        gate, up = both[:, :hidden_units], both[:, hidden_units:]
        d_gate, d_up = gates_back(gate, up, fixed[:, many:])
        return d_gate, d_up, gate * jax.nn.sigmoid(gate) * up, scale, row

    units = ((total, hidden_units), bf16)
    (d_gate_2, d_up_2, act_2, scale_2, row_2), d_rows_blocks = expand(
        "back_rows_2", backward_2,
        second + fixed_pair + (same,),
        [units, units, units, ((total, 1), f32), ((total, 1), f32)],
        weight_2nd, (0, 1), groups, parts, after=(prev_w_own,),
    )
    d_rows_got = return_dp(d_rows_blocks)
    dense, dense_terms = dense_rows(
        "dense_b", *facts, hidden, embed, next_rows, cot, norm_gain, dense, 1, 2,
        after=(d_rows_blocks[0],),
    )
    def first_grad(cot, same, gain, *got):
        d_rows = summed(got, parts)
        added = lax.dot_general(
            same, d_rows, (((0,), (0,)), ((), ())),
            precision=lax.Precision.HIGHEST, preferred_element_type=f32,
        )
        d_mixed = cot + added
        u = d_mixed * piece_of(gain[1, 0:1], seq_place(), seqs, 0)
        return [payload(u), d_mixed] + blocks_of(d_rows, seq_place(), seqs)

    u, d_mixed_2, *d_rows_back = call(
        "first_grad", first_grad, [packed, part_rows] + [((slots, width), bf16)] * seqs,
        (), cot_1, same_own, norm_gain, *d_rows_got, after=(dense_terms, prev_pair[1]),
    )
    u_all = gather_dp(u)
    dense, _ = lax.optimization_barrier((dense, u))
    dense = ring(dense, "section", -1)
    back_got = trade_seq(d_rows_back)

    def build_2(values, g):
        chosen, row, base, dout = values[0], values[1], values[2 : 2 + groups], values[2 + groups :]
        step = width // parts
        first = chosen[:, g * step : (g + 1) * step].astype(f32) * row
        first = first + column_part(base, rows, g).astype(f32)
        return first.astype(bf16), column_part(dout, rows, g)[:, :step]

    weight_grad, tick_2 = outer(
        "weight_grad_2", 1, depths, build_2, [chosen, row_2] + base_2_all + dout_2_all,
        d_gate_2, d_up_2, act_2, width, parts, None, after=(u, back_got[-1]),
    )

    back_1_own, back_1_send = project(
        "back_1", u_all, weight_1st, (2,), parts, mates=prev_all, after=(tick_2,)
    )
    back_1 = pair_seq(back_1_own, back_1_send)

    def second_grad(token, count, start, ahead_1, ahead_2, cot, gain, terms, *got):
        d_rows = in_order([g.astype(f32) for g in got], seq_place(), 1)
        keep = live_column(count, 1, slots) * (1.0 - met_column(token, count))
        grad, more = backward_rows(
            start[:, width + lanes :].astype(f32), ahead_1.astype(f32), ahead_2.astype(f32),
            pick(token_column(token, 1), cot) + d_rows, keep, gain,
        )
        notes = in_lanes([live_column(count, 0, slots), keep])
        grad = jnp.concatenate([grad.astype(f32), notes], 1)
        return [grad] + pieces_of(terms + more, seq_place(), seqs)

    grad_2, *terms_parts = call(
        "second_grad", second_grad,
        [((slots, features + lanes), bf16)] + [((2 * depths, width), f32)] * seqs,
        facts, start_got[0], ahead_21, ahead_22, cot, norm_gain, dense_terms, *back_got,
        after=(back_1_send,),
    )
    grad_2 = ring(grad_2, "section", -1)
    terms_got = trade_seq(terms_parts)

    def backward_1(own, other, prev_own, prev_other, both, scale, weight_1):
        inner = own[:, hidden_units : hidden_units + 1] + decoded(other[:, hidden_units:])
        d_act = own[:, :hidden_units] + other[:, :hidden_units].astype(f32)
        through = scale * scale * inner / features
        d_act = d_act - through * (prev_own + prev_other.astype(f32))
        d_act = d_act * (weight_1 * scale)
        d_gate, d_up = gates_back(both[:, :hidden_units], both[:, hidden_units:], d_act)
        return d_gate, d_up, through

    (d_gate_1, d_up_1, through_1), d_rows_blocks = expand(
        "back_rows_1", backward_1,
        back_1 + prev_pair + (both_1, scale_2, weight_1),
        [units, units, ((total, 1), f32)],
        weight_1st, (0, 1), groups, parts, after=(terms_parts[0],),
    )
    d_rows_got = return_dp(d_rows_blocks)

    def build_1(values, g):
        through, scale, weight = values[:3]
        first, u, prev = (values[3 + k * groups : 3 + (k + 1) * groups] for k in range(3))
        dout = column_part(u, rows, g).astype(f32) - through * column_part(prev, rows, g).astype(f32)
        return column_part(first, rows, g), (dout * (weight * scale)).astype(bf16)

    weight_grad, tick_1 = outer(
        "weight_grad_1", 0, depths, build_1,
        [through_1, scale_2, weight_1] + rows_1_all + u_all + prev_all,
        d_gate_1, d_up_1, act_1, width, parts, weight_grad, after=(d_rows_blocks[0],),
    )

    def last_grad(d_mixed_2, prev, scale, through, unit_1, unit_e1, unit_e2, own_facts, gain, *got):
        got, terms = got[:groups], got[groups:]
        d_rows = summed(got, parts)
        gain_1, gain_2 = (piece_of(gain[k, 0:1], seq_place(), seqs, 0) for k in range(2))
        scale, through = scale[:rows], through[:rows]
        live = own_facts[:, 2:3]
        prev = prev.astype(f32)
        grad_1 = (d_mixed_2 * gain_2 - through * prev) * scale
        d_mixed_1 = grad_1 + d_rows
        kept_1, kept_2 = d_mixed_1 * live, d_mixed_2 * live
        sums = [
            jnp.sum(a * b, axis=0, keepdims=True)
            for a, b in ((kept_1, unit_1), (kept_1, unit_e1), (kept_2, prev * scale), (kept_2, unit_e2))
        ]
        sums = jnp.concatenate(sums, 0) + sum(terms)
        cut = []
        for i in range(groups):
            block = sums[:, :share]
            for z in range(groups):
                at = partner(z, i, groups) * share
                block = jnp.where(lax.axis_index("dp") == z, sums[:, at : at + share], block)
            cut.append(block)
        return cut + blocks_of(d_mixed_1 * gain_1, seq_place(), seqs)

    last = call(
        "last_grad", last_grad,
        [((2 * depths, share), f32)] * groups + [((slots, width), bf16)] * seqs,
        (), d_mixed_2, prev_own, scale_2, through_1, unit_1, unit_e1, unit_e2,
        own_facts, norm_gain, *d_rows_got, *terms_got, after=(tick_1,),
    )
    last_got = trade_seq(last[groups:], -1)
    sums_got = return_dp(last[:groups])

    def finish(token, dense, asked_rows, grad_2, *got):
        part = in_order([g.astype(f32) for g in got], seq_place(), 1)
        asked_rows = asked_rows.astype(f32)
        scale = inv_rms(asked_rows)
        unit = asked_rows * scale
        grad_1 = (part - unit * jnp.mean(part * unit, axis=-1, keepdims=True)) * scale
        notes = grad_2[:, features:].astype(f32)
        grads = jnp.concatenate([grad_1, grad_2[:, :features].astype(f32)], 0).astype(bf16)
        lane = iota((slots, tokens), 1)
        chosen = jnp.concatenate(
            [
                jnp.where(lane == token_column(token, k), notes[:, k : k + 1], 0.0)
                for k in range(2)
            ],
            0,
        ).astype(bf16)
        taken = lax.dot_general(
            chosen, jnp.ones((2 * slots, lanes), bf16), (((0,), (0,)), ((), ())),
            preferred_element_type=f32,
        )[:, 0:1]
        out = []
        step = chunk_of(features)
        for at in range(0, features, step):
            placed = lax.dot_general(
                chosen, grads[:, at : at + step], (((0,), (0,)), ((), ())),
                preferred_element_type=f32,
            )
            out.append(jnp.where(taken > 0, placed, dense[:, at : at + step].astype(f32)).astype(bf16))
        return [out, jnp.zeros((8, lanes), f32)]

    hidden_grad, tick = call(
        "finish", finish, [((tokens, features), bf16), ((8, lanes), f32)],
        (asked_token,), dense, asked_rows, grad_2, *last_got,
        stream=features // chunk_of(features), limit=20,
    )

    def gain_sum(*got):
        sums = sum(got)
        return [jnp.stack([sums[2 * k : 2 * k + 2] for k in range(depths)])[None]]

    (gain_grad,) = call(
        "gain_sum", gain_sum, [((1, depths, 2, share), f32)], (), *sums_got, after=(tick,)
    )
    return (
        hidden_grad[None, None],
        weight_grad,
        gain_grad,
    )


def solution(mesh):
    return jax.shard_map(
        local,
        mesh=mesh,
        in_specs=(
            P("section", "dp", "seq", None),
            P("section", "dp", "seq", None),
            P("section", "dp", "seq", None),
            P("section", "dp", None, "seq"),
            P("section", "dp", None, "seq"),
            P("section", "dp", None, "seq"),
            P(),
            P(None, None, "seq", "dp"),
        ),
        out_specs=(
            P("section", "dp", "seq", None),
            P("section", None, None, "seq", "dp"),
            P("section", None, None, ("seq", "dp")),
        ),
        check_vma=False,
    )
```

```python
import jax
import jax.numpy as jnp
from jax import lax
from jax.experimental import pallas as pl
from jax.experimental.pallas import tpu as pltpu
from jax.sharding import PartitionSpec as P

eps_norm = 1e-06
lanes = 128
f32 = jnp.float32
bf16 = jnp.bfloat16
vmem = pl.BlockSpec(memory_space=pltpu.VMEM)
smem = pl.BlockSpec(memory_space=pltpu.SMEM)
anywhere = pl.BlockSpec(memory_space=pl.ANY)


def ring(value, axis, steps):
    count = lax.axis_size(axis)
    return lax.ppermute(value, axis, [(i, (i + steps) % count) for i in range(count)])


def hop(value, section_step, seq_step):
    sections, seqs = lax.axis_size("section"), lax.axis_size("seq")
    pairs = [
        (c * seqs + s, (c + section_step) % sections * seqs + (s + seq_step) % seqs)
        for c in range(sections)
        for s in range(seqs)
    ]
    return lax.ppermute(value, ("section", "seq"), pairs)


def trade_seq(pieces, section_step=0):
    if section_step == 0:
        return [pieces[0]] + [ring(pieces[o], "seq", o) for o in range(1, len(pieces))]
    return [hop(piece, section_step, o) for o, piece in enumerate(pieces)]


def partner(place, step, count):
    return place ^ step if count & (count - 1) == 0 else (place - step) % count


def gather_dp(block):
    count = lax.axis_size("dp")
    return [block] + [
        lax.ppermute(block, "dp", [(partner(z, i, count), z) for z in range(count)])
        for i in range(1, count)
    ]


def return_dp(blocks):
    count = lax.axis_size("dp")
    return [blocks[0]] + [
        lax.ppermute(blocks[i], "dp", [(z, partner(z, i, count)) for z in range(count)])
        for i in range(1, count)
    ]


def pair_seq(own, send):
    if lax.axis_size("seq") == 2:
        return own, ring(send, "seq", 1)
    return lax.psum(own, "seq"), jnp.zeros_like(send)


def inv_rms(value):
    return lax.rsqrt(jnp.mean(value * value, axis=-1, keepdims=True) + eps_norm)


def iota(shape, dim):
    return lax.broadcasted_iota(jnp.int32, shape, dim)


def seq_place():
    return lax.axis_index("seq").astype(jnp.int32)


def token_column(token, depth):
    capacity = token.shape[3]
    out = jnp.full((capacity, 1), token[0, 0, depth, 0], jnp.int32)
    for c in range(1, capacity):
        out = jnp.where(iota((capacity, 1), 0) == c, token[0, 0, depth, c], out)
    return out


def gate_column(gate, depth):
    capacity = gate.shape[3]
    out = jnp.full((capacity, 1), gate[0, 0, depth, 0], f32)
    for c in range(1, capacity):
        out = jnp.where(iota((capacity, 1), 0) == c, gate[0, 0, depth, c], out)
    return out


def live_column(count, depth, capacity):
    return (iota((capacity, 1), 0) < count[depth]).astype(f32)


def met_column(token, count):
    capacity = token.shape[3]
    second = token_column(token, 1)
    out = jnp.zeros((capacity, 1), f32)
    for c in range(capacity):
        out += ((second == token[0, 0, 0, c]) & (c < count[0])).astype(f32)
    return jnp.minimum(out, 1.0)


def pick(column, table):
    hot = (column == iota((column.shape[0], table.shape[0]), 1)).astype(bf16)
    return jnp.dot(hot, table, preferred_element_type=f32)


def pick_ahead(column, table, after):
    return pick(column, table) + pick(column - table.shape[0], after)


def thirds(column):
    high = column.astype(bf16).astype(f32)
    mid = (column - high).astype(bf16).astype(f32)
    return [high, mid, column - high - mid]


def in_lanes(columns):
    lane = iota((columns[0].shape[0], lanes), 1)
    out = jnp.zeros(lane.shape, f32)
    for k, column in enumerate(columns):
        out = jnp.where(lane == k, column, out)
    return out


def coded(column):
    return in_lanes(thirds(column))


def decoded(block, first=0):
    lane = iota(block.shape, 1)
    inside = (lane >= first) & (lane < first + 3)
    return jnp.sum(jnp.where(inside, block.astype(f32), 0.0), axis=1, keepdims=True)


def piece_of(value, place, count, step):
    width = value.shape[-1] // count
    want = lax.rem(place + step, count)
    out = value[:, :width]
    for p in range(1, count):
        out = jnp.where(want == p, value[:, p * width : (p + 1) * width], out)
    return out


def pieces_of(value, place, count):
    return [piece_of(value, place, count, o) for o in range(count)]


def blocks_of(value, place, count):
    size = value.shape[0] // count
    out = []
    for o in range(count):
        block = value[:size]
        for j in range(1, count):
            want = lax.rem(place + o, count) == j
            block = jnp.where(want, value[j * size : (j + 1) * size], block)
        out.append(block)
    return out


def from_block(got, place, block):
    count = len(got)
    out = got[0]
    for o in range(1, count):
        out = jnp.where(lax.rem(place - o + count, count) == block, got[o], out)
    return out


def in_order(got, place, axis):
    return jnp.concatenate([from_block(got, place, j) for j in range(len(got))], axis)


def as_row(column):
    size = column.shape[0]
    here = iota((size, size), 0) == iota((size, size), 1)
    return jnp.sum(jnp.where(here, column, 0.0), axis=0, keepdims=True)


def folds(rows, width):
    for count in (1, 2, 4, 8):
        if rows * count % 16 == 0 and width % (count * lanes) == 0:
            return count
    return 1


def folded(value, count):
    step = value.shape[1] // count
    return jnp.concatenate([value[:, g * step : (g + 1) * step] for g in range(count)], 0)


def unfolded(value, count):
    rows = value.shape[0] // count
    return jnp.concatenate([value[g * rows : (g + 1) * rows] for g in range(count)], 1)


def column_part(blocks, rows, g):
    return jnp.concatenate(
        [block[g * rows : (g + 1) * rows].astype(f32) for block in blocks], 0
    ).astype(bf16)


def summed(got, parts):
    return unfolded(sum(g.astype(f32) for g in got), parts)


def chunk_of(width):
    for step in (1024, 896, 512, 256, 128):
        if width % step == 0:
            return step
    return width


def in_hbm(value):
    return pltpu.with_memory_space_constraint(value, pltpu.HBM)


def call(name, fn, outs, small, *args, far=(), hold=(), after=(), stream=False, flops=0, limit=12):
    outs = list(outs) + [(weight.shape[2:], bf16) for weight, _, _ in hold]
    shapes = [jax.ShapeDtypeStruct(shape, kind) for shape, kind in outs]
    n_small, n_args, n_far, n_outs = len(small), len(args), len(far), len(shapes) - len(hold)

    def body(*refs):
        refs = list(refs)

        def take(count):
            taken, refs[:] = refs[:count], refs[count:]
            return taken

        small_refs, arg_refs, far_refs = take(n_small), take(n_args), take(n_far)
        hold_refs = take(len(hold))
        take(len(after))
        out_refs, held_refs, buffers = take(n_outs), take(len(hold)), take(n_far)
        if stream:
            stage_ref, stage_sem = refs.pop(), refs.pop()
        copies = [pltpu.make_async_copy(*trio) for trio in zip(far_refs, buffers, take(n_far))]
        holds = [
            pltpu.make_async_copy(ref.at[depth, kind], held_ref, sem)
            for ref, (_, depth, kind), held_ref, sem in zip(hold_refs, hold, held_refs, refs)
        ]
        for copy in copies + holds:
            copy.start()
        for copy in copies:
            copy.wait()
        values = small_refs + [r[...] for r in arg_refs + buffers]
        results = fn(*values)
        if stream:
            chunks, results, target = results[0], results[1:], out_refs.pop(0)
            width = target.shape[1] // len(chunks)
            for k, chunk in enumerate(chunks):
                at = pl.ds(k * width, width)
                stage_ref[:, at] = chunk.astype(target.dtype)
                copy = pltpu.make_async_copy(stage_ref.at[:, at], target.at[:, at], stage_sem.at[k])
                copy.start()
                holds.append(copy)
        for ref, value in zip(out_refs, results):
            ref[...] = value.astype(ref.dtype)
        for copy in holds:
            copy.wait()

    size = sum(a.size * a.dtype.itemsize for a in list(args) + list(far) + shapes)
    return pl.pallas_call(
        body,
        name=name,
        out_shape=shapes,
        in_specs=[smem] * n_small + [vmem] * n_args + [anywhere] * (n_far + len(hold) + len(after)),
        out_specs=[anywhere if stream and k == 0 else vmem for k in range(len(shapes))],
        scratch_shapes=[pltpu.VMEM(a.shape, a.dtype) for a in far]
        + [pltpu.SemaphoreType.DMA] * (n_far + len(hold))
        + ([pltpu.SemaphoreType.DMA((stream,)), pltpu.VMEM(*outs[0])] if stream else []),
        compiler_params=pltpu.CompilerParams(vmem_limit_bytes=limit << 20),
        cost_estimate=pl.CostEstimate(flops=flops, bytes_accessed=size, transcendentals=0),
    )(*[in_hbm(a) for a in small], *args, *[in_hbm(a) for a in far], *[in_hbm(a) for a, _, _ in hold], *after)


def project(name, blocks, weights, kinds, parts, others=None, select=None, gain=None, mates=None, after=()):
    groups = len(blocks)
    rows = blocks[0].shape[0] // parts
    width, hidden = weights[0].shape
    step = width // parts
    other_blocks, other_kinds = others if others is not None else ([], ())
    first_kinds, kinds = kinds, kinds + other_kinds
    many_kinds = len(kinds)
    total, many = rows * groups, len(kinds) * hidden
    marked = select is not None or mates is not None
    extra = lanes if marked else 0

    def body(*refs):
        refs = list(refs)
        x_refs, w_refs, refs = refs[:groups], refs[groups : groups + many_kinds], refs[groups + many_kinds :]
        other_refs, refs = refs[: len(other_blocks)], refs[len(other_blocks) :]
        if select is not None:
            select_ref, gain_ref = refs.pop(0), refs.pop(0)
        if mates is not None:
            mate_refs, refs = refs[:groups], refs[groups:]
        refs = refs[len(after) :]
        own_ref, send_ref = refs.pop(0), refs.pop(0)
        kept_ref = refs.pop(0) if select is not None else None
        x_all = [r[...] for r in x_refs]
        mate_all = [r[...] for r in mate_refs] if mates is not None else x_all
        if select is not None:
            gain_all = piece_of(gain_ref[1, 0:1, :], seq_place(), gain.shape[2] // width, 0)
        sums = [jnp.zeros((total, hidden), f32) for _ in kinds]
        mark = jnp.zeros((total, 1), f32)
        for g in range(parts):
            x = column_part(x_all, rows, g)
            if marked:
                mate = x if mates is None else column_part(mate_all, rows, g)
                mark += jnp.sum(x.astype(f32) * mate.astype(f32), axis=1, keepdims=True)
            if select is not None:
                chosen = jnp.dot(select_ref[...], x, preferred_element_type=f32)
                x = (chosen * gain_all[:, g * step : (g + 1) * step]).astype(bf16)
                kept_ref[:, g * step : (g + 1) * step] = x
            for k in range(len(kinds)):
                if k == len(first_kinds):
                    x = column_part([r[...] for r in other_refs], rows, g)[:, :step]
                part_ref = w_refs[k].at[pl.ds(g * step, step)]
                sums[k] += jnp.dot(x, part_ref[...], preferred_element_type=f32)
        for k in range(len(kinds)):
            own_ref[:, k * hidden : (k + 1) * hidden] = sums[k]
            send_ref[:, k * hidden : (k + 1) * hidden] = sums[k].astype(bf16)
        if marked:
            own_ref[:, many:] = in_lanes([mark])
            send_ref[:, many:] = coded(mark).astype(bf16)

    args = list(blocks) + [weights[k] for k in kinds]
    args, specs = args + list(other_blocks), [vmem] * (groups + many_kinds) + [vmem] * len(other_blocks)
    outs = [
        jax.ShapeDtypeStruct((total, many + extra), f32),
        jax.ShapeDtypeStruct((total, many + extra), bf16),
    ]
    if select is not None:
        args, specs = args + [select, gain], specs + [vmem, vmem]
        outs.append(jax.ShapeDtypeStruct((total, width), bf16))
    if mates is not None:
        args, specs = args + list(mates), specs + [vmem] * groups
    return pl.pallas_call(
        body,
        name=name,
        in_specs=specs + [anywhere] * len(after),
        out_specs=[vmem] * len(outs),
        out_shape=outs,
        compiler_params=pltpu.CompilerParams(vmem_limit_bytes=8 << 20),
        cost_estimate=pl.CostEstimate(
            flops=2 * total * width * many, bytes_accessed=2 * width * many, transcendentals=0
        ),
    )(*args, *after)


def expand(name, prepare, args, saved, weights, kinds, groups, parts, after=()):
    width, hidden = weights[0].shape
    total = saved[0][0][0]
    rows, step = total // groups, width // parts
    count, kept = len(args), len(saved)

    def body(*refs):
        in_refs, w_refs = refs[:count], refs[count : count + len(kinds)]
        refs = refs[count + len(kinds) + len(after) :]
        saved_refs, out_refs = refs[:kept], refs[kept:]
        for ref, value in zip(saved_refs, prepare(*[r[...] for r in in_refs])):
            ref[...] = value.astype(ref.dtype)
        out = []
        for g in range(parts):
            part = jnp.zeros((total, step), f32)
            for k in range(len(kinds)):
                part_ref = w_refs[k].at[pl.ds(g * step, step)]
                part += lax.dot_general(
                    saved_refs[k][...], part_ref[...], (((1,), (1,)), ((), ())),
                    preferred_element_type=f32,
                )
            out.append(part)
        for z in range(groups):
            block = jnp.concatenate([part[z * rows : (z + 1) * rows] for part in out], 0)
            out_refs[z][...] = block.astype(bf16)

    results = pl.pallas_call(
        body,
        name=name,
        in_specs=[vmem] * (count + len(kinds)) + [anywhere] * len(after),
        out_specs=[vmem] * (kept + groups),
        out_shape=[jax.ShapeDtypeStruct(shape, kind) for shape, kind in saved]
        + [jax.ShapeDtypeStruct((rows * parts, step), bf16)] * groups,
        compiler_params=pltpu.CompilerParams(vmem_limit_bytes=8 << 20),
        cost_estimate=pl.CostEstimate(
            flops=2 * total * width * hidden * len(kinds),
            bytes_accessed=2 * width * hidden * len(kinds),
            transcendentals=0,
        ),
    )(*args, *[weights[k] for k in kinds], *after)
    return results[:kept], results[kept:]


def outer(name, depth, depths, build, args, d_gate, d_up, act, width, parts, before, after=()):
    total, hidden = act.shape
    step = width // parts
    count = len(args)
    earlier = [] if before is None else [in_hbm(before)]

    def contract(left, right):
        return lax.dot_general(left, right, (((0,), (0,)), ((), ())), preferred_element_type=f32)

    def body(*refs):
        values = [r[...] for r in refs[:count]]
        gate_ref, up_ref, act_ref = refs[count : count + 3]
        out_ref, tick_ref, buffer, sems = refs[-4:]
        tick_ref[...] = jnp.zeros_like(tick_ref)
        copies = []
        for g in range(parts):
            rows, dout = build(values, g)
            pairs = ((rows, gate_ref), (rows, up_ref), (dout, act_ref))
            for k, (left, right_ref) in enumerate(pairs):
                buffer[g, k] = contract(left, right_ref[...]).astype(bf16)
                copy = pltpu.make_async_copy(
                    buffer.at[g, k],
                    out_ref.at[0, depth, k, pl.ds(g * step, step)],
                    sems.at[g, k],
                )
                copy.start()
                copies.append(copy)
        for copy in copies:
            copy.wait()

    return pl.pallas_call(
        body,
        name=name,
        in_specs=[vmem] * (count + 3) + [anywhere] * (len(earlier) + len(after)),
        out_specs=[anywhere, vmem],
        out_shape=[
            jax.ShapeDtypeStruct((1, depths, 3, width, hidden), bf16),
            jax.ShapeDtypeStruct((8, lanes), f32),
        ],
        input_output_aliases={} if before is None else {count + 3: 0},
        scratch_shapes=[
            pltpu.VMEM((parts, 3, step, hidden), bf16),
            pltpu.SemaphoreType.DMA((parts, 3)),
        ],
        compiler_params=pltpu.CompilerParams(vmem_limit_bytes=24 << 20),
        cost_estimate=pl.CostEstimate(
            flops=6 * total * width * hidden, bytes_accessed=6 * width * hidden, transcendentals=0
        ),
    )(*args, d_gate, d_up, act, *earlier, *after)


def backward_rows(hidden, ahead_1, ahead_2, d_mixed_2, keep, gain):
    scale_1 = inv_rms(hidden)
    unit_1 = hidden * scale_1
    unit_e1 = ahead_1 * inv_rms(ahead_1)
    unit_e2 = ahead_2 * inv_rms(ahead_2)
    mixed = (unit_1 * gain[0, 0:1] + unit_e1 * gain[0, 1:2]).astype(bf16).astype(f32)
    scale_2 = inv_rms(mixed)
    unit_2 = mixed * scale_2
    u = d_mixed_2 * gain[1, 0:1]
    grad_1 = (u - unit_2 * jnp.mean(u * unit_2, axis=-1, keepdims=True)) * scale_2
    v = grad_1 * gain[0, 0:1]
    grad_0 = (v - unit_1 * jnp.mean(v * unit_1, axis=-1, keepdims=True)) * scale_1
    kept_1, kept_2 = grad_1 * keep, d_mixed_2 * keep
    terms = [
        jnp.sum(a * b, axis=0, keepdims=True)
        for a, b in ((kept_1, unit_1), (kept_1, unit_e1), (kept_2, unit_2), (kept_2, unit_e2))
    ]
    return grad_0.astype(bf16), jnp.concatenate(terms, 0)


def dense_rows(name, token, count, hidden, embed, next_rows, cotangent, gain, before, half, halves, hold=(), after=()):
    tokens, width = hidden.shape
    step = next_rows.shape[0]
    blocks = tokens // step // halves
    low, last = half * blocks, tokens // step - 1
    size = 2 * lanes
    capacity = token.shape[3]
    earlier = [] if before is None else list(before)

    def body(token_ref, count_ref, hidden_ref, embed_ref, next_ref, cot_ref, gain_ref, *refs):
        skip, kept = len(earlier), len(hold)
        hold_refs, refs = refs[skip : skip + kept], refs[:skip] + refs[skip + kept :]
        held_refs, sems = refs[len(refs) - 2 * kept - 2 : len(refs) - kept - 2], refs[len(refs) - kept :]
        out_ref, terms_ref = refs[skip + len(after) : skip + len(after) + 2]
        mixed_ref, sums_ref = refs[len(refs) - kept - 2 : len(refs) - kept]
        holds = [
            pltpu.make_async_copy(ref.at[depth, kind], held_ref, sem)
            for ref, (_, depth, kind), held_ref, sem in zip(hold_refs, hold, held_refs, sems)
        ]
        for copy in holds:
            copy.start()
        sums_ref[...] = jnp.zeros_like(sums_ref)
        row, column = (iota((2 * step, 2 * step), dim) for dim in range(2))
        shift = (column == jnp.where(row < step, row + 1, row + 2 - step)).astype(bf16)
        places = [pl.ds(at, size) for at in range(0, width, size)]

        def folded_lanes(value):
            return sum(value[:, at : at + lanes] for at in range(0, size, lanes))

        def mean(value):
            return jnp.sum(value, axis=1, keepdims=True) / width

        def one(i, carry):
            block = low + i
            first = pl.multiple_of(block * step, step)
            rows = pl.ds(first, step)
            follow = pl.ds(pl.multiple_of(jnp.minimum(block + 1, last) * step, step), step)
            here = iota((step, 1), 0) + first
            keep = jnp.ones((step, 1), f32)
            for k in range(2):
                for c in range(capacity):
                    out = (here == token_ref[0, 0, k, c]) & (c < count_ref[k])
                    keep = jnp.where(out, 0.0, keep)

            def ahead(at, hot):
                after = embed_ref[follow, at]
                if half == halves - 1:
                    after = jnp.where(block == last, next_ref[:, at], after)
                both = jnp.concatenate([embed_ref[rows, at], after], 0)
                return jnp.dot(hot, both, preferred_element_type=f32)

            square_h, square_e = jnp.zeros((step, lanes), f32), jnp.zeros((2 * step, lanes), f32)
            for at in places:
                h, e = hidden_ref[rows, at].astype(f32), ahead(at, shift)
                square_h += folded_lanes(h * h)
                square_e += folded_lanes(e * e)
            scale_1 = lax.rsqrt(mean(square_h) + eps_norm)
            scale_e = lax.rsqrt(mean(square_e) + eps_norm)
            scale_e1, scale_e2 = scale_e[:step], scale_e[step:]

            sums = [jnp.zeros((step, lanes), f32) for _ in range(4)]
            for at in places:
                through = hidden_ref[rows, at].astype(f32) * scale_1 * gain_ref[0, 0:1, at]
                mixed = through + ahead(at, shift[:step]) * scale_e1 * gain_ref[0, 1:2, at]
                kept = mixed.astype(bf16)
                mixed_ref[:, at] = kept
                mixed = kept.astype(f32)
                u = cot_ref[rows, at].astype(f32) * gain_ref[1, 0:1, at]
                pairs = ((mixed, mixed), (u, mixed), (u, through), (mixed, through))
                sums = [c + folded_lanes(a * b) for c, (a, b) in zip(sums, pairs)]
            square, along, u_back, mixed_back = (mean(value) for value in sums)
            scale_2 = lax.rsqrt(square + eps_norm)
            share_2 = scale_2 * scale_2 * along
            share_1 = scale_2 * (u_back - share_2 * mixed_back) * scale_1
            keep_2, keep_h = keep * scale_2, keep * scale_1
            keep_e1, keep_e2 = keep * scale_e1, keep * scale_e2

            for at in places:
                e = ahead(at, shift)
                h = hidden_ref[rows, at].astype(f32)
                mixed = mixed_ref[:, at].astype(f32)
                cot = cot_ref[rows, at].astype(f32)
                grad_1 = (cot * gain_ref[1, 0:1, at] - mixed * share_2) * scale_2
                grad_0 = (grad_1 * gain_ref[0, 0:1, at] - h * share_1) * scale_1
                out_ref[rows, at] = grad_0.astype(bf16)
                terms = (
                    grad_1 * (h * keep_h),
                    grad_1 * (e[:step] * keep_e1),
                    cot * (mixed * keep_2),
                    cot * (e[step:] * keep_e2),
                )
                for k, term in enumerate(terms):
                    sums_ref[k, :, at] += sum(term[r : r + 8] for r in range(0, step, 8))
            return carry

        lax.fori_loop(0, blocks, one, 0)
        for k in range(4):
            term = jnp.sum(sums_ref[k], axis=0, keepdims=True)
            terms_ref[k : k + 1] = term + refs[1][k : k + 1] if earlier else term
        for copy in holds:
            copy.wait()

    return pl.pallas_call(
        body,
        name=name,
        in_specs=[smem] * 2 + [vmem] * (5 + len(earlier)) + [anywhere] * (len(hold) + len(after)),
        out_specs=[vmem] * (2 + len(hold)),
        out_shape=[
            jax.ShapeDtypeStruct((tokens, width), bf16),
            jax.ShapeDtypeStruct((4, width), f32),
        ]
        + [jax.ShapeDtypeStruct(weight.shape[2:], bf16) for weight, _, _ in hold],
        input_output_aliases={7: 0} if earlier else {},
        scratch_shapes=[pltpu.VMEM((step, width), bf16), pltpu.VMEM((4, 8, width), f32)]
        + [pltpu.SemaphoreType.DMA] * len(hold),
        compiler_params=pltpu.CompilerParams(vmem_limit_bytes=8 << 20),
        cost_estimate=pl.CostEstimate(
            flops=60 * tokens * width // halves,
            bytes_accessed=10 * tokens * width // halves,
            transcendentals=0,
        ),
    )(in_hbm(token), in_hbm(count), hidden, embed, next_rows, cotangent, gain, *earlier, *[in_hbm(a) for a, _, _ in hold], *after)


def local(
    main_hidden, embedded, cotangent, slot_token, slot_count, route_gate, norm_gain, expert_weight
):
    depths, _, features = norm_gain.shape
    tokens = main_hidden.shape[2]
    slots = slot_token.shape[3]
    seqs, groups = lax.axis_size("seq"), lax.axis_size("dp")
    rows = seqs * slots
    total = groups * rows
    width = features // seqs
    share = width // groups
    hidden_units = expert_weight.shape[3]
    parts = folds(rows, width)
    source, embed, cot = main_hidden[0, 0], embedded[0, 0], cotangent[0, 0]
    slot_count = slot_count.reshape(-1)
    facts = (slot_token, slot_count)
    packed = ((rows * parts, width // parts), bf16)
    part_rows = ((rows, width), f32)

    def payload(value):
        return folded(value, parts)

    asked_token = ring(slot_token, "section", -1)

    def own_rows(token, count, gate, embed, cot):
        first, second = token_column(token, 0), token_column(token, 1)
        live_1, live_2 = (live_column(count, k, slots) for k in range(2))
        weight_1, weight_2 = gate_column(gate, 0) * live_1, gate_column(gate, 1) * live_2
        facts = in_lanes(
            [first.astype(f32), second.astype(f32), live_1, live_2]
            + thirds(weight_1)
            + thirds(weight_2)
        )
        ahead_1, ahead_2 = pick(first + 1, embed), pick(first + 2, embed)
        block = jnp.concatenate([ahead_1, ahead_2, pick(first, cot)], 0)
        notes = jnp.concatenate([coded(inv_rms(ahead_1)), coded(inv_rms(ahead_2)), facts], 0)
        dout = folded(pick(second, cot) * weight_2, seqs * parts)
        none = jnp.zeros(((parts - 1) * slots, lanes), f32)
        tail = facts if parts == 1 else jnp.concatenate([facts, none], 0)
        dout = jnp.concatenate([dout, jnp.concatenate([tail] * seqs, 0)], 1)
        head = embed[:depths].astype(f32)
        scale = coded(inv_rms(head))
        heads = [
            jnp.concatenate([head[:, p * width : (p + 1) * width], scale], 1) for p in range(seqs)
        ]
        return [
            jnp.concatenate([jnp.concatenate([piece, notes], 1)] + heads, 0)
            for piece in pieces_of(block, seq_place(), seqs)
        ] + [dout]

    fine = width // parts + lanes
    *own_sent, dout_2, gate_1st = call(
        "own_rows", own_rows,
        [((3 * slots + depths * seqs, width + lanes), bf16)] * seqs
        + [((slots * parts * seqs, fine), bf16)],
        (slot_token, slot_count, route_gate), far=(embed, cot),
        hold=((expert_weight, 0, 0),),
    )
    own_sent = lax.optimization_barrier((*own_sent, asked_token))[:-1]
    own_got = trade_seq(own_sent)

    def source_rows(asked, source):
        first = pick(token_column(asked, 0), source)
        second = pick(token_column(asked, 1), source)
        scale = coded(inv_rms(first))
        sent = [jnp.concatenate([p, scale], 1) for p in pieces_of(first, seq_place(), seqs)]
        sent[0] = jnp.concatenate([sent[0], second], 1)
        return sent + [first]

    *sent, asked_rows = call(
        "source_rows", source_rows,
        [((slots, width + lanes + features), bf16)]
        + [((slots, width + lanes), bf16)] * (seqs - 1)
        + [((slots, features), bf16)],
        (asked_token,), source, after=(own_sent[0],),
    )
    start_got = trade_seq(sent, 1)
    dout_2, _ = lax.optimization_barrier((dout_2, sent[0]))

    def second_base(token, count, start, table, got, gain):
        after = got[3 * slots :, :width].astype(f32)
        after = jnp.concatenate([after[p * depths : (p + 1) * depths] for p in range(seqs)], 1)
        after = jnp.where(seq_place() == seqs - 1, 0.0, after)
        after = jnp.concatenate([after, jnp.zeros((16 - depths, features), f32)], 0).astype(bf16)
        second = token_column(token, 1)
        start = start[:, width + lanes :].astype(f32)
        ahead_1 = pick_ahead(second + 1, table, after)
        ahead_2 = pick_ahead(second + 2, table, after)
        unit = start * inv_rms(start)
        mixed = unit * gain[0, 0:1] + ahead_1 * inv_rms(ahead_1) * gain[0, 1:2]
        mixed = mixed.astype(bf16).astype(f32)
        own = mixed * inv_rms(mixed) * gain[1, 0:1] * (1.0 - met_column(token, count))
        out = (own + ahead_2 * inv_rms(ahead_2) * gain[1, 1:2]) * live_column(count, 1, slots)
        bases = [folded(piece, parts) for piece in pieces_of(out, seq_place(), seqs)]
        return bases + [after, ahead_1, ahead_2]

    *base_sent, next_rows, ahead_21, ahead_22 = call(
        "second_base", second_base,
        [((slots * parts, width // parts), bf16)] * seqs
        + [((16, features), bf16)]
        + [((slots, features), bf16)] * 2,
        facts, start_got[0], embed, own_got[-1], norm_gain,
    )
    base_got = trade_seq(base_sent)

    dout_2_got = gather_dp(dout_2)

    def first_mixed(gain, *got):
        start_got = got[:seqs]
        got = [g.astype(f32) for g in got[seqs : 2 * seqs]]
        first = 3 * slots
        block_1, block_2, block_3 = (
            in_order([g[k * slots : (k + 1) * slots] for g in got], seq_place(), 0) for k in range(3)
        )
        facts = block_3[:, width:]
        heads = in_order([g[first:] for g in got], seq_place(), 0)
        heads = [heads[j * depths * seqs : (j + 1) * depths * seqs] for j in range(seqs)]
        units = []
        for k, block in ((1, block_1), (2, block_2)):
            unit = block[:, :width] * decoded(block[:, width:])
            after = []
            for j in range(seqs):
                token = facts[j * slots : (j + 1) * slots, 0:1]
                add = jnp.zeros((slots, width), f32)
                for i in range(k if j + 1 < seqs else 0):
                    row = heads[j + 1][i : i + 1]
                    for p in range(1, seqs):
                        at = p * depths + i
                        row = jnp.where(seq_place() == p, heads[j + 1][at : at + 1], row)
                    row = row[:, :width] * decoded(row[:, width:])
                    add += jnp.where(token == float(tokens + i - k), row, 0.0)
                after.append(add)
            units.append(unit + jnp.concatenate(after, 0))
        start = in_order([g[:, : width + lanes].astype(f32) for g in start_got], seq_place(), 0)
        unit = start[:, :width] * decoded(start[:, width:])
        gain_h, gain_e = (piece_of(gain[0, k : k + 1], seq_place(), seqs, 0) for k in range(2))
        mixed = (unit * gain_h + units[0] * gain_e).astype(bf16).astype(f32)
        return payload(mixed * facts[:, 2:3]), unit, *units, block_3[:, :width], facts

    rows_1, unit_1, unit_e1, unit_e2, cot_1, own_facts = call(
        "first_mixed", first_mixed,
        [packed] + [part_rows] * 4 + [((rows, lanes), f32)],
        (), norm_gain, *start_got, *own_got, after=(ahead_21, *dout_2_got[1:-1]),
    )
    rows_1_all = gather_dp(rows_1)

    def by_slots(got, place):
        blocks = [from_block(got, place, j) for j in range(seqs)]
        pairs = [b[g * slots : (g + 1) * slots] for g in range(parts) for b in blocks]
        return jnp.concatenate(pairs, 0)

    (base_2,) = call(
        "base_order", lambda *got: [by_slots([g.astype(f32) for g in got], seq_place())], [packed],
        (), *base_got, after=(rows_1,),
    )
    base_2_all = gather_dp(base_2)

    def dout_pieces(*dout):
        pieces = zip(*(blocks_of(block.astype(f32), seq_place(), seqs) for block in dout))
        return [jnp.concatenate(blocks, 0) for blocks in pieces]

    dout_2_sent = call(
        "dout_pieces", dout_pieces, [((groups * slots * parts, fine), bf16)] * seqs,
        (), *dout_2_got, after=(rows_1,),
    )
    up_1st, down_1st = call(
        "held_1", lambda: [], [], (),
        hold=((expert_weight, 0, 1), (expert_weight, 0, 2)), after=(dout_2_sent[0],), limit=2,
    )
    weight_1st = (gate_1st, up_1st, down_1st)
    first_own, first_send = project(
        "gate_up_1", rows_1_all, weight_1st, (0, 1), parts, after=(base_2,)
    )
    first = pair_seq(first_own, first_send)

    def forward_1(own, other):
        both = own + other.astype(f32)
        gate, up = both[:, :hidden_units], both[:, hidden_units:]
        return gate * jax.nn.sigmoid(gate) * up, both

    (act_1, both_1), out_blocks = expand(
        "down_1", forward_1, first,
        [((total, hidden_units), bf16), ((total, 2 * hidden_units), f32)],
        weight_1st, (2,), groups, parts,
    )
    out_blocks = lax.optimization_barrier((*out_blocks, *base_2_all[1:-1]))[:groups]
    out_got = return_dp(out_blocks)

    hidden, _ = lax.optimization_barrier((source, rows_1))
    hidden = ring(hidden, "section", 1)
    *dense, gate_2nd, up_2nd, down_2nd = dense_rows(
        "dense_a", *facts, hidden, embed, next_rows, cot, norm_gain, None, 0, 2,
        hold=tuple((expert_weight, 1, k) for k in range(3)), after=(out_blocks[0],),
    )
    weight_2nd = (gate_2nd, up_2nd, down_2nd)

    def second_prev(own_facts, rows_1, *got):
        value = unfolded(rows_1.astype(f32), parts) + summed(got, parts) * decoded(own_facts, 4)
        return payload(value), value.astype(bf16)

    prev, prev_own = call(
        "second_prev", second_prev, [packed, ((rows, width), bf16)],
        (), own_facts, rows_1, *out_got, after=(dense[1],),
    )
    prev_all = gather_dp(prev)

    dout_2_sent = lax.optimization_barrier((*dout_2_sent, out_blocks[0]))[:-1]
    dout_2_traded = trade_seq(dout_2_sent)

    def slot_facts(*got):
        got, size = [g.astype(f32) for g in got], slots * parts
        blocks = [
            by_slots([g[z * size : (z + 1) * size] for g in got], seq_place()) for z in range(groups)
        ]
        facts = jnp.concatenate([block[:rows, width // parts :] for block in blocks], 0)
        base = (iota((total, 1), 0) // slots * tokens).astype(f32)
        first, second = facts[:, 0:1] + base, facts[:, 1:2] + base
        live = (facts[:, 3:4] > 0) & (as_row(facts[:, 2:3]) > 0)
        same = ((second == as_row(first)) & live).astype(f32)
        return same, same, same[:rows, :rows], decoded(facts, 4), *blocks

    same, same_16, same_own, weight_1, *dout_2_all = call(
        "slot_facts", slot_facts,
        [((total, total), f32), ((total, total), bf16), ((rows, rows), f32), ((total, 1), f32)]
        + [((rows * parts, fine), bf16)] * groups,
        (), *dout_2_traded, after=(prev,),
    )
    fixed_own, fixed_send = project(
        "fixed_2", base_2_all, weight_2nd, (0, 1), parts,
        others=(dout_2_all, (2,)), after=(same_own,),
    )
    fixed_pair = pair_seq(fixed_own, fixed_send)

    mixed_own, mixed_send, chosen = project(
        "gate_up_2", prev_all, weight_2nd, (0, 1), parts,
        select=same_16, gain=norm_gain, after=(fixed_own,),
    )
    second = pair_seq(mixed_own, mixed_send)
    def gates_back(gate, up, d_act):
        sig = jax.nn.sigmoid(gate)
        d_gate = d_act * up * sig * (1.0 + gate * (1.0 - sig))
        return d_gate, d_act * gate * sig

    def backward_2(own, other, fixed_own, fixed_other, same):
        many = 2 * hidden_units
        square = own[:, many : many + 1] + decoded(other[:, many:])
        scale = lax.rsqrt(square / features + eps_norm)
        row = jnp.sum(same * as_row(scale), axis=1, keepdims=True)
        both = (own[:, :many] + other[:, :many].astype(f32)) * row
        fixed = fixed_own + fixed_other.astype(f32)
        both = both + fixed[:, :many]
        gate, up = both[:, :hidden_units], both[:, hidden_units:]
        d_gate, d_up = gates_back(gate, up, fixed[:, many:])
        return d_gate, d_up, gate * jax.nn.sigmoid(gate) * up, scale, row

    units = ((total, hidden_units), bf16)
    (d_gate_2, d_up_2, act_2, scale_2, row_2), d_rows_blocks = expand(
        "back_rows_2", backward_2,
        second + fixed_pair + (same,),
        [units, units, units, ((total, 1), f32), ((total, 1), f32)],
        weight_2nd, (0, 1), groups, parts,
    )
    d_rows_got = return_dp(d_rows_blocks)
    dense, dense_terms = dense_rows(
        "dense_b", *facts, hidden, embed, next_rows, cot, norm_gain, dense, 1, 2,
        after=(d_rows_blocks[0],),
    )
    def first_grad(cot, same, gain, *got):
        d_rows = summed(got, parts)
        added = lax.dot_general(
            same, d_rows, (((0,), (0,)), ((), ())),
            precision=lax.Precision.HIGHEST, preferred_element_type=f32,
        )
        d_mixed = cot + added
        u = d_mixed * piece_of(gain[1, 0:1], seq_place(), seqs, 0)
        return [payload(u), d_mixed] + blocks_of(d_rows, seq_place(), seqs)

    u, d_mixed_2, *d_rows_back = call(
        "first_grad", first_grad, [packed, part_rows] + [((slots, width), bf16)] * seqs,
        (), cot_1, same_own, norm_gain, *d_rows_got, after=(dense_terms,),
    )
    u_all = gather_dp(u)
    dense, _ = lax.optimization_barrier((dense, u))
    dense = ring(dense, "section", -1)
    back_got = trade_seq(d_rows_back)

    def build_2(values, g):
        chosen, row, base, dout = values[0], values[1], values[2 : 2 + groups], values[2 + groups :]
        step = width // parts
        first = chosen[:, g * step : (g + 1) * step].astype(f32) * row
        first = first + column_part(base, rows, g).astype(f32)
        return first.astype(bf16), column_part(dout, rows, g)[:, :step]

    weight_grad, tick_2 = outer(
        "weight_grad_2", 1, depths, build_2, [chosen, row_2] + base_2_all + dout_2_all,
        d_gate_2, d_up_2, act_2, width, parts, None, after=(u, back_got[-1]),
    )

    back_1_own, back_1_send = project(
        "back_1", u_all, weight_1st, (2,), parts, others=(prev_all, (2,)), mates=prev_all, after=(tick_2,)
    )
    back_1 = pair_seq(back_1_own, back_1_send)

    def second_grad(token, count, start, ahead_1, ahead_2, cot, gain, terms, *got):
        d_rows = in_order([g.astype(f32) for g in got], seq_place(), 1)
        keep = live_column(count, 1, slots) * (1.0 - met_column(token, count))
        grad, more = backward_rows(
            start[:, width + lanes :].astype(f32), ahead_1.astype(f32), ahead_2.astype(f32),
            pick(token_column(token, 1), cot) + d_rows, keep, gain,
        )
        notes = in_lanes([live_column(count, 0, slots), keep])
        grad = jnp.concatenate([grad.astype(f32), notes], 1)
        return [grad] + pieces_of(terms + more, seq_place(), seqs)

    grad_2, *terms_parts = call(
        "second_grad", second_grad,
        [((slots, features + lanes), bf16)] + [((2 * depths, width), f32)] * seqs,
        facts, start_got[0], ahead_21, ahead_22, cot, norm_gain, dense_terms, *back_got,
        after=(back_1_send,),
    )
    grad_2 = ring(grad_2, "section", -1)
    terms_got = trade_seq(terms_parts)

    def backward_1(own, other, both, scale, weight_1):
        many = 2 * hidden_units
        inner = own[:, many : many + 1] + decoded(other[:, many:])
        sums = own[:, :many] + other[:, :many].astype(f32)
        through = scale * scale * inner / features
        d_act = sums[:, :hidden_units] - through * sums[:, hidden_units:]
        d_act = d_act * (weight_1 * scale)
        d_gate, d_up = gates_back(both[:, :hidden_units], both[:, hidden_units:], d_act)
        return d_gate, d_up, through

    (d_gate_1, d_up_1, through_1), d_rows_blocks = expand(
        "back_rows_1", backward_1,
        back_1 + (both_1, scale_2, weight_1),
        [units, units, ((total, 1), f32)],
        weight_1st, (0, 1), groups, parts, after=(terms_parts[0],),
    )
    d_rows_got = return_dp(d_rows_blocks)

    def build_1(values, g):
        through, scale, weight = values[:3]
        first, u, prev = (values[3 + k * groups : 3 + (k + 1) * groups] for k in range(3))
        dout = column_part(u, rows, g).astype(f32) - through * column_part(prev, rows, g).astype(f32)
        return column_part(first, rows, g), (dout * (weight * scale)).astype(bf16)

    weight_grad, tick_1 = outer(
        "weight_grad_1", 0, depths, build_1,
        [through_1, scale_2, weight_1] + rows_1_all + u_all + prev_all,
        d_gate_1, d_up_1, act_1, width, parts, weight_grad, after=(d_rows_blocks[0],),
    )

    def last_grad(d_mixed_2, prev, scale, through, unit_1, unit_e1, unit_e2, own_facts, gain, *got):
        got, terms = got[:groups], got[groups:]
        d_rows = summed(got, parts)
        gain_1, gain_2 = (piece_of(gain[k, 0:1], seq_place(), seqs, 0) for k in range(2))
        scale, through = scale[:rows], through[:rows]
        live = own_facts[:, 2:3]
        prev = prev.astype(f32)
        grad_1 = (d_mixed_2 * gain_2 - through * prev) * scale
        d_mixed_1 = grad_1 + d_rows
        kept_1, kept_2 = d_mixed_1 * live, d_mixed_2 * live
        sums = [
            jnp.sum(a * b, axis=0, keepdims=True)
            for a, b in ((kept_1, unit_1), (kept_1, unit_e1), (kept_2, prev * scale), (kept_2, unit_e2))
        ]
        sums = jnp.concatenate(sums, 0) + sum(terms)
        cut = []
        for i in range(groups):
            block = sums[:, :share]
            for z in range(groups):
                at = partner(z, i, groups) * share
                block = jnp.where(lax.axis_index("dp") == z, sums[:, at : at + share], block)
            cut.append(block)
        return cut + blocks_of(d_mixed_1 * gain_1, seq_place(), seqs)

    last = call(
        "last_grad", last_grad,
        [((2 * depths, share), f32)] * groups + [((slots, width), bf16)] * seqs,
        (), d_mixed_2, prev_own, scale_2, through_1, unit_1, unit_e1, unit_e2,
        own_facts, norm_gain, *d_rows_got, *terms_got, after=(tick_1,),
    )
    last_got = trade_seq(last[groups:], -1)
    sums_got = return_dp(last[:groups])

    def finish(token, dense, asked_rows, grad_2, *got):
        part = in_order([g.astype(f32) for g in got], seq_place(), 1)
        asked_rows = asked_rows.astype(f32)
        scale = inv_rms(asked_rows)
        unit = asked_rows * scale
        grad_1 = (part - unit * jnp.mean(part * unit, axis=-1, keepdims=True)) * scale
        notes = grad_2[:, features:].astype(f32)
        grads = jnp.concatenate([grad_1, grad_2[:, :features].astype(f32)], 0).astype(bf16)
        lane = iota((slots, tokens), 1)
        chosen = jnp.concatenate(
            [
                jnp.where(lane == token_column(token, k), notes[:, k : k + 1], 0.0)
                for k in range(2)
            ],
            0,
        ).astype(bf16)
        taken = lax.dot_general(
            chosen, jnp.ones((2 * slots, lanes), bf16), (((0,), (0,)), ((), ())),
            preferred_element_type=f32,
        )[:, 0:1]
        out = []
        step = chunk_of(features)
        for at in range(0, features, step):
            placed = lax.dot_general(
                chosen, grads[:, at : at + step], (((0,), (0,)), ((), ())),
                preferred_element_type=f32,
            )
            out.append(jnp.where(taken > 0, placed, dense[:, at : at + step].astype(f32)).astype(bf16))
        return [out, jnp.zeros((8, lanes), f32)]

    hidden_grad, tick = call(
        "finish", finish, [((tokens, features), bf16), ((8, lanes), f32)],
        (asked_token,), dense, asked_rows, grad_2, *last_got,
        stream=features // chunk_of(features), limit=20,
    )

    def gain_sum(*got):
        sums = sum(got)
        return [jnp.stack([sums[2 * k : 2 * k + 2] for k in range(depths)])[None]]

    (gain_grad,) = call(
        "gain_sum", gain_sum, [((1, depths, 2, share), f32)], (), *sums_got, after=(tick,)
    )
    return (
        hidden_grad[None, None],
        weight_grad,
        gain_grad,
    )


def solution(mesh):
    return jax.shard_map(
        local,
        mesh=mesh,
        in_specs=(
            P("section", "dp", "seq", None),
            P("section", "dp", "seq", None),
            P("section", "dp", "seq", None),
            P("section", "dp", None, "seq"),
            P("section", "dp", None, "seq"),
            P("section", "dp", None, "seq"),
            P(),
            P(None, None, "seq", "dp"),
        ),
        out_specs=(
            P("section", "dp", "seq", None),
            P("section", None, None, "seq", "dp"),
            P("section", None, None, ("seq", "dp")),
        ),
        check_vma=False,
    )
```
